32 devices in a mesh: dp: 8 (over z, x), seq: 4 (over y, core).
Axes of the slice: x: 2, y: 2, z: 4, core: 2. Of those that a mesh axis runs over, the one named last changes fastest.
Arguments:
- inputs: bfloat16 [24, 1024, 1024], P('dp', 'seq'), may hold values from -6 to 6
- segment_ids: int32 [24, 1024], P('dp', 'seq'), may hold values from 0 to 7, as said below
- doc_times: int32 [24, 8], P('dp'), may hold values from 0 to 999
- time_weight: bfloat16 [256, 1024], replicated, may hold values from -0.375 to 0.375
- time_bias: bfloat16 [1024], replicated, may hold values from -3 to 3
- norm1_gain: bfloat16 [1024], replicated, may hold values from 0.099609375 to 1.8984375
- norm1_bias: bfloat16 [1024], replicated, may hold values from -3 to 3
- qkv_weight: bfloat16 [1024, 3072], replicated, may hold values from -0.1875 to 0.1875
- qkv_bias: bfloat16 [3072], replicated, may hold values from -3 to 3
- out_weight: bfloat16 [1024, 1024], replicated, may hold values from -1.5 to 1.5
- out_bias: bfloat16 [1024], replicated, may hold values from -3 to 3
- norm2_gain: bfloat16 [1024], replicated, may hold values from 0.099609375 to 1.8984375
- norm2_bias: bfloat16 [1024], replicated, may hold values from -3 to 3
- up_weight: bfloat16 [1024, 4096], replicated, may hold values from -0.1875 to 0.1875
- up_bias: bfloat16 [4096], replicated, may hold values from -3 to 3
- down_weight: bfloat16 [4096, 1024], replicated, may hold values from -0.09375 to 0.09375
- down_bias: bfloat16 [1024], replicated, may hold values from -3 to 3
- cotangent: bfloat16 [24, 1024, 1024], P('dp', 'seq'), may hold values from -6 to 6
Outputs:
- output: bfloat16 [24, 1024, 1024], P('dp', 'seq')
- input_grad: bfloat16 [24, 1024, 1024], P('dp', 'seq')
- time_weight_grad: float32 [256, 1024], P('dp')
- time_bias_grad: float32 [1024], P('dp')
- norm1_gain_grad: float32 [1024], P('dp')
- norm1_bias_grad: float32 [1024], P('dp')
- qkv_weight_grad: float32 [1024, 3072], P('dp')
- qkv_bias_grad: float32 [3072], P('dp')
- out_weight_grad: float32 [1024, 1024], P('dp')
- out_bias_grad: float32 [1024], P('dp')
- norm2_gain_grad: float32 [1024], P('dp')
- norm2_bias_grad: float32 [1024], P('dp')
- up_weight_grad: float32 [1024, 4096], P('dp')
- up_bias_grad: float32 [4096], P('dp')
- down_weight_grad: float32 [4096, 1024], P('dp')
- down_bias_grad: float32 [1024], P('dp')
The draws below stay inside these ranges and needn't reach their ends.
Inputs may be any that keep to these rules, and one draw needn't show every extreme that they name: `segment_ids`: along each row the ids never fall and the last token has id 8 - 1. In each aligned block of 3 rows one row holds a document that begins among the first 256 tokens and ends among the last 256.
All inputs are finite; a program needn't handle non-finite values.
Results may differ from the reference program's by a relative error of at most 0.014.
Values may be sent and summed in bfloat16 or wider, within the bound.
No kernel may reach another device: no remote copies, remote signals or barrier semaphores. Data moves between devices by JAX's collectives and lax.ppermute only.
A program may use at most 320 MiB of HBM per device.

```python
import math
import jax
import jax.numpy as jnp
from jax import lax

D = 1024
HEADS = 16
HEAD_DIM = 64
FF = 4096
TEMB = 256
ROW_LEN = 1024
SEGS = 8
TSTEPS = 1000
ROWS_DEV = 3
ROWS = 24
SHARD = 256


def draw_segment_ids(key, part):
    key = jax.random.fold_in(key, 7)
    keys_all = jax.random.split(key, 6)
    groups = ROWS // ROWS_DEV
    free_cuts = jax.random.randint(keys_all[0], (ROWS, SEGS - 1), 1, ROW_LEN)
    opening = jax.random.randint(keys_all[1], (ROWS, 1), 1, SHARD)
    closing = jax.random.randint(keys_all[2], (ROWS, 1), ROW_LEN - SHARD + 1, ROW_LEN)
    before = jax.random.randint(keys_all[3], (ROWS, 1), 0, SEGS - 2)
    spread_bits = jax.random.randint(keys_all[4], (ROWS, SEGS - 1), 0, 1 << 20)
    prefix = 1 + spread_bits % opening
    suffix = closing + spread_bits % (ROW_LEN - closing)
    slot_order = jnp.arange(SEGS - 1, dtype=jnp.int32)[None, :]
    long_cuts = jnp.where(slot_order < before, prefix, jnp.where(slot_order == before, opening, jnp.where(slot_order == before + 1, closing, suffix)))
    chosen = jax.random.randint(keys_all[5], (groups,), 0, ROWS_DEV)
    row_pick = jnp.repeat(chosen, ROWS_DEV) == jnp.arange(ROWS, dtype=jnp.int32) % ROWS_DEV
    cut_points = jnp.where(row_pick[:, None], long_cuts, free_cuts)
    places = jnp.arange(ROW_LEN, dtype=jnp.int32)
    return jnp.sum((cut_points[:, None, :] <= places[None, :, None]).astype(jnp.int32), axis=-1)


def place_ends(values, stream_key, smallest, largest):
    extent = values.shape
    spot = [jax.random.randint(jax.random.fold_in(stream_key, axis), (), 0, extent[axis]) for axis in range(len(extent))]
    values = values.at[tuple(spot)].set(smallest)
    longest = extent.index(max(extent))
    spot[longest] = (spot[longest] + 1) % extent[longest]
    return values.at[tuple(spot)].set(largest)


def levels(key, extent, pieces, low, largest):
    factor_of, own = 1.0, jax.random.fold_in(key, 6)
    for axis_at, parts in pieces:
        heights = jnp.exp(jax.random.uniform(jax.random.fold_in(own, axis_at), (parts,), jnp.float32, low / len(pieces), largest / len(pieces)))
        factor_of = factor_of * jnp.repeat(heights, extent[axis_at] // parts).reshape([-1 if axis == axis_at else 1 for axis in range(len(extent))])
    return factor_of


def scatter_about(own_key, extent, scale, reach, shards=(), kind=jnp.bfloat16):
    drawn = jax.random.normal(own_key, extent, jnp.float32) * scale
    if len(shards) > 0:
        drawn = levels(own_key, extent, shards, -0.22, 0.18) * drawn
    return jnp.clip(drawn, min=-reach, max=reach).astype(kind)


def setup_inputs(seed: int = 0) -> dict:
    streams_of = jax.random.split(jax.random.key(seed), 19)
    return {
        "inputs": scatter_about(streams_of[0], (ROWS, ROW_LEN, D), 1.0, 6.0, ((0, 8), (1, 4))),
        "segment_ids": draw_segment_ids(jax.random.fold_in(streams_of[18], 71), 0),
        "doc_times": place_ends(jax.random.randint(streams_of[2], (ROWS, SEGS), 0, TSTEPS), jax.random.fold_in(streams_of[2], 1), 0, TSTEPS - 1).astype(jnp.int32),
        "time_weight": scatter_about(streams_of[3], (TEMB, D), TEMB ** -0.5, 0.375),
        "time_bias": scatter_about(streams_of[4], (D,), 0.5, 3.0),
        "norm1_gain": jnp.clip(1.0 + 0.18 * jax.random.normal(streams_of[5], (D,), jnp.float32), 0.099609375, 1.8984375).astype(jnp.bfloat16),
        "norm1_bias": scatter_about(streams_of[6], (D,), 0.5, 3.0),
        "qkv_weight": scatter_about(streams_of[7], (D, 3 * D), D ** -0.5, 0.1875),
        "qkv_bias": scatter_about(streams_of[8], (3 * D,), 0.5, 3.0),
        "out_weight": scatter_about(streams_of[9], (D, D), (max(D // 64, 1)) ** -0.5, 1.5),
        "out_bias": scatter_about(streams_of[10], (D,), 0.5, 3.0),
        "norm2_gain": jnp.clip(1.0 + 0.18 * jax.random.normal(streams_of[11], (D,), jnp.float32), 0.099609375, 1.8984375).astype(jnp.bfloat16),
        "norm2_bias": scatter_about(streams_of[12], (D,), 0.5, 3.0),
        "up_weight": scatter_about(streams_of[13], (D, FF), D ** -0.5, 0.1875),
        "up_bias": scatter_about(streams_of[14], (FF,), 0.5, 3.0),
        "down_weight": scatter_about(streams_of[15], (FF, D), FF ** -0.5, 0.09375),
        "down_bias": scatter_about(streams_of[16], (D,), 0.5, 3.0),
        "cotangent": scatter_about(streams_of[17], (ROWS, ROW_LEN, D), 1.0, 6.0, ((0, 8), (1, 4))),
    }


EPSILON = 1e-05

@jax.custom_vjp
def low(v):
    return lax.optimization_barrier(v.astype(jnp.bfloat16)).astype(jnp.float32)

@jax.custom_vjp
def low_back(v):
    return v

def low_keep(v):
    return (low(v), None)

def low_pass(kept, grad):
    return (grad,)

def back_keep(v):
    return (v, None)

def back_low(kept, grad):
    return (low(grad),)
low.defvjp(low_keep, low_pass)
low_back.defvjp(back_keep, back_low)

def layer_norm(values, gain_vec, shift_vec):
    centred = values - lax.optimization_barrier(jnp.mean(values, axis=-1, keepdims=True))
    spread = lax.optimization_barrier(jnp.mean(centred * centred, axis=-1, keepdims=True))
    return centred * lax.rsqrt(spread + EPSILON) * gain_vec + shift_vec

def rotate(values, cos_tab, sin_tab):
    half_size = values.shape[-1] // 2
    part_one = values[..., :half_size]
    part_two = values[..., half_size:]
    return jnp.concatenate([part_one * cos_tab - part_two * sin_tab, part_two * cos_tab + part_one * sin_tab], axis=-1)

def time_features(doc_times, feat_width):
    half_size = feat_width // 2
    frequency = jnp.exp(-math.log(10000.0) * jnp.arange(half_size, dtype=jnp.float32) / half_size)
    angles = doc_times.astype(jnp.float32)[..., None] * frequency
    return jnp.concatenate([jnp.sin(angles), jnp.cos(angles)], axis=-1)

def rotary_tables(positions, head_size):
    half_size = head_size // 2
    frequency = jnp.exp(-math.log(10000.0) * 2.0 * jnp.arange(half_size, dtype=jnp.float32) / head_size)
    angles = positions.astype(jnp.float32)[..., None] * frequency
    return (jnp.cos(angles)[..., None, :], jnp.sin(angles)[..., None, :])

def row_attention(item):
    queries, keys_rot, values_row, segments = item
    raw_scores = jnp.einsum('qhd,khd->hqk', queries, keys_rot, precision=lax.Precision.HIGHEST)
    scores = low_back(raw_scores * HEAD_DIM ** (-0.5))
    same_doc = (segments[:, None] == segments[None, :])[None]
    masked = jnp.where(same_doc, scores, -1e+30)
    row_max = lax.optimization_barrier(jnp.max(masked, axis=-1, keepdims=True))
    weights = jnp.where(same_doc, jnp.exp(masked - row_max), 0.0)
    attn_probs = weights / lax.optimization_barrier(jnp.sum(weights, axis=-1, keepdims=True))
    return jnp.einsum('hqk,khd->qhd', low(attn_probs), values_row, precision=lax.Precision.HIGHEST)

def forward(start_in, weights_all, features, onehot, cos_tab, sin_tab, segments):
    time_weight, time_bias, norm1_gain, norm1_bias, qkv_weight, qkv_bias, out_weight, out_bias, norm2_gain, norm2_bias, up_weight, up_bias, down_weight, down_bias = weights_all
    highest = lax.Precision.HIGHEST
    row_count, row_len = (start_in.shape[0], start_in.shape[1])
    time_shift = jnp.einsum('rgt,td->rgd', features, time_weight, precision=highest) + time_bias
    stream = start_in + jnp.einsum('rsg,rgd->rsd', onehot, time_shift, precision=highest)
    normed1 = low(layer_norm(stream, norm1_gain, norm1_bias))
    qkv_all = low_back(jnp.einsum('rsd,de->rse', normed1, qkv_weight, precision=highest) + qkv_bias)
    head_shape = (row_count, row_len, HEADS, HEAD_DIM)
    queries = low(rotate(qkv_all[..., :D].reshape(head_shape), cos_tab, sin_tab))
    keys_rot = low(rotate(qkv_all[..., D:2 * D].reshape(head_shape), cos_tab, sin_tab))
    values_low = low(qkv_all[..., 2 * D:].reshape(head_shape))
    attended = lax.map(jax.checkpoint(row_attention), (queries, keys_rot, values_low, segments))
    attended = low(low_back(attended.reshape(row_count, row_len, D)))
    branch = low_back(jnp.einsum('rsd,de->rse', attended, out_weight, precision=highest) + out_bias)
    middle = stream + branch
    normed2 = low(layer_norm(middle, norm2_gain, norm2_bias))
    hidden = low_back(jnp.einsum('rsd,df->rsf', normed2, up_weight, precision=highest) + up_bias)
    active = low(jax.nn.gelu(hidden, approximate=True))
    feed = low_back(jnp.einsum('rsf,fd->rsd', active, down_weight, precision=highest) + down_bias)
    return middle + feed

def reference(inputs, segment_ids, doc_times, time_weight, time_bias, norm1_gain, norm1_bias, qkv_weight, qkv_bias, out_weight, out_bias, norm2_gain, norm2_bias, up_weight, up_bias, down_weight, down_bias, cotangent):
    parameters = tuple((item.astype(jnp.float32) for item in (time_weight, time_bias, norm1_gain, norm1_bias, qkv_weight, qkv_bias, out_weight, out_bias, norm2_gain, norm2_bias, up_weight, up_bias, down_weight, down_bias)))
    features = low(time_features(doc_times, TEMB))
    onehot = (segment_ids[..., None] == jnp.arange(SEGS, dtype=jnp.int32)).astype(jnp.float32)
    positions = jnp.broadcast_to(jnp.arange(ROW_LEN, dtype=jnp.int32)[None, :], segment_ids.shape)
    cos_tab, sin_tab = rotary_tables(positions, HEAD_DIM)
    groups = ROWS // 4

    def regroup(array):
        return array.reshape((groups, 4) + array.shape[1:])

    def step_group(carried, item):
        group_in, group_cot, group_feat, group_hot, group_cos, group_sin, group_seg = item

        def apply_layer(start_in, *weights_all):
            return forward(start_in, weights_all, group_feat, group_hot, group_cos, group_sin, group_seg)
        result, pullback = jax.vjp(apply_layer, group_in.astype(jnp.float32), *parameters)
        cotangents = pullback(group_cot.astype(jnp.float32))
        summed = jax.tree.map(jnp.add, carried, tuple(cotangents[1:]))
        return (summed, (result.astype(jnp.bfloat16), cotangents[0].astype(jnp.bfloat16)))
    initial = jax.tree.map(jnp.zeros_like, parameters)
    totals, (outputs, input_grads) = lax.scan(step_group, initial, (regroup(inputs), regroup(cotangent), regroup(features), regroup(onehot), regroup(cos_tab), regroup(sin_tab), regroup(segment_ids)))
    return (outputs.reshape(ROWS, ROW_LEN, D), input_grads.reshape(ROWS, ROW_LEN, D), totals[0], totals[1], totals[2], totals[3], totals[4], totals[5], totals[6], totals[7], totals[8], totals[9], totals[10], totals[11], totals[12], totals[13])
```

```python
import functools
import math

import jax
import jax.numpy as jnp
from jax import lax
from jax.experimental import pallas as pl
from jax.experimental.pallas import tpu as pltpu
from jax.sharding import Mesh, PartitionSpec as P

HEADS = 16
HEAD_DIM = 64
TEMB = 256
SEGS = 8
EPSILON = 1e-05
F32 = jnp.float32
BF16 = jnp.bfloat16
NEG = -1e30
VMEM = 60 * 1024 * 1024


def swap(value, axis):
    return lax.ppermute(value, axis, [(0, 1), (1, 0)])


def layer_norm(values, gain_vec, shift_vec):
    centred = values - jnp.mean(values, axis=-1, keepdims=True)
    spread = jnp.mean(centred * centred, axis=-1, keepdims=True)
    return centred * lax.rsqrt(spread + EPSILON) * gain_vec + shift_vec


def time_features(doc_times, feat_width):
    half_size = feat_width // 2
    frequency = jnp.exp(-math.log(10000.0) * jnp.arange(half_size, dtype=F32) / half_size)
    angles = doc_times.astype(F32)[..., None] * frequency
    return jnp.concatenate([jnp.sin(angles), jnp.cos(angles)], axis=-1)


def rotary_tables(positions, head_size):
    half_size = head_size // 2
    frequency = jnp.exp(-math.log(10000.0) * 2.0 * jnp.arange(half_size, dtype=F32) / head_size)
    angles = positions.astype(F32)[..., None] * frequency
    cos_tab, sin_tab = jnp.cos(angles), jnp.sin(angles)
    return (
        jnp.concatenate([cos_tab] * 4, axis=-1),
        jnp.concatenate([-sin_tab, sin_tab, -sin_tab, sin_tab], axis=-1),
    )


def dot(left_op, right_op, left_dim=1, right_dim=0):
    return lax.dot_general(
        left_op, right_op, (((left_dim,), (right_dim,)), ((), ())), preferred_element_type=F32
    )


def turn(values, cos_tab, sin_tab):
    slabs = []
    lane = lax.broadcasted_iota(jnp.int32, (values.shape[0], 128), 1)
    first = lane % HEAD_DIM < HEAD_DIM // 2
    for start in range(0, values.shape[1], 128):
        slab = values[:, start : start + 128]
        partner = jnp.where(
            first, pltpu.roll(slab, 128 - HEAD_DIM // 2, 1), pltpu.roll(slab, HEAD_DIM // 2, 1)
        )
        slabs.append(slab * cos_tab + partner * sin_tab)
    return jnp.concatenate(slabs, axis=1)


def qkv_body(x_ref, w_ref, b_ref, cos_ref, sin_ref, *refs):
    q_ref, k_ref, v_ref = refs[-3:]
    width = q_ref.shape[-1]
    full = dot(x_ref[0, 0], w_ref[...]) + b_ref[...]
    cos_tab, sin_tab = cos_ref[0], sin_ref[0]
    q_ref[0, 0] = (turn(full[:, :width], cos_tab, sin_tab) * HEAD_DIM**-0.5).astype(BF16)
    k_ref[0, 0] = turn(full[:, width : 2 * width], cos_tab, sin_tab).astype(BF16)
    v_ref[0, 0] = full[:, 2 * width :].astype(BF16)


def project_qkv(x, weight, bias, cos_tab, sin_tab, offset, pieces, held=()):
    count, rows, shard, model = x.shape
    width = weight.shape[1] // 3
    out = jax.ShapeDtypeStruct((pieces, rows, shard, width), BF16)
    place = pl.BlockSpec((1, 1, shard, width), lambda p, r: (p + offset, r, 0, 0))
    table = pl.BlockSpec((1, shard, 128), lambda p, r: (p + offset, 0, 0))
    return pl.pallas_call(
        qkv_body,
        grid=(count, rows),
        in_specs=[
            pl.BlockSpec((1, 1, shard, model), lambda p, r: (p, r, 0, 0)),
            pl.BlockSpec((model, 3 * width), lambda p, r: (0, 0)),
            pl.BlockSpec((1, 3 * width), lambda p, r: (0, 0)),
            table,
            table,
        ]
        + [pl.BlockSpec(memory_space=pl.ANY)] * len(held),
        out_specs=[place] * 3,
        out_shape=[out] * 3,
        input_output_aliases={5 + n: n for n in range(len(held))},
        compiler_params=pltpu.CompilerParams(vmem_limit_bytes=VMEM),
        cost_estimate=pl.CostEstimate(
            flops=2 * count * rows * shard * model * 3 * width,
            bytes_accessed=2 * (count * rows * shard * (model + 3 * width) + model * 3 * width),
            transcendentals=0,
        ),
        name="qkv",
    )(x, weight, bias, cos_tab, sin_tab, *held)


def head_masks(shape, heads):
    lane = lax.broadcasted_iota(jnp.int32, shape, 1)
    return [(lane // HEAD_DIM == h) for h in range(heads)]


def attend_body(act_ref, q_ref, k_ref, v_ref, segq_ref, segk_ref, o_ref, lse_ref, vt, acc, top, tot, qm):
    row, piece = pl.program_id(0), pl.program_id(1)
    pieces, _, shard, width = k_ref.shape
    heads = width // HEAD_DIM

    @pl.when(piece == 0)
    def _():
        for j in range(pieces):
            vt[:, j * shard : (j + 1) * shard] = v_ref[j, 0].T

    q = q_ref[0, 0]
    for h, mask in enumerate(head_masks(q.shape, heads)):
        qm[h] = jnp.where(mask, q, jnp.zeros_like(q))
    acc[...] = jnp.zeros_like(acc)
    top[...] = jnp.full_like(top, NEG)
    tot[...] = jnp.zeros_like(tot)
    seg_q = segq_ref[0, 0]
    for j in range(pieces):

        @pl.when(act_ref[(row * pieces + piece) * pieces + j] != 0)
        def _():
            k = k_ref[j, 0]
            same = segk_ref[0][:, j : j + 1] == seg_q
            for h in range(heads):
                at = slice(h * HEAD_DIM, (h + 1) * HEAD_DIM)
                s = jnp.where(same, dot(k, qm[h], 1, 1), NEG)
                m_old = top[h : h + 1]
                m_new = jnp.maximum(m_old, jnp.max(s, axis=0, keepdims=True))
                fade = jnp.exp(m_old - m_new)
                p = jnp.exp(s - m_new)
                tot[h : h + 1] = tot[h : h + 1] * fade + jnp.sum(p, axis=0, keepdims=True)
                top[h : h + 1] = m_new
                acc[at] = acc[at] * fade + dot(
                    vt[at, j * shard : (j + 1) * shard], p.astype(BF16)
                )

    for h in range(heads):
        at = slice(h * HEAD_DIM, (h + 1) * HEAD_DIM)
        acc[at] = acc[at] / tot[h : h + 1]
    o_ref[0, 0] = acc[...].T.astype(BF16)
    lse_ref[0, 0] = top[...] + jnp.log(jnp.maximum(tot[...], 1e-30))


def attend(act, q, k, v, seg_row, seg_col):
    pieces, rows, shard, width = q.shape
    heads = width // HEAD_DIM
    one = pl.BlockSpec((1, 1, shard, width), lambda r, i, a: (i, r, 0, 0))
    whole = pl.BlockSpec((pieces, 1, shard, width), lambda r, i, a: (0, r, 0, 0))
    return pl.pallas_call(
        attend_body,
        grid_spec=pltpu.PrefetchScalarGridSpec(
            num_scalar_prefetch=1,
            grid=(rows, pieces),
            in_specs=[
                one,
                whole,
                whole,
                pl.BlockSpec((1, 1, 1, shard), lambda r, i, a: (r, i, 0, 0)),
                pl.BlockSpec((1, shard, pieces), lambda r, i, a: (r, 0, 0)),
            ],
            out_specs=[one, pl.BlockSpec((1, 1, 8, shard), lambda r, i, a: (r, i, 0, 0))],
            scratch_shapes=[
                pltpu.VMEM((width, pieces * shard), BF16),
                pltpu.VMEM((width, shard), F32),
                pltpu.VMEM((8, shard), F32),
                pltpu.VMEM((8, shard), F32),
                pltpu.VMEM((heads, shard, width), BF16),
            ],
        ),
        out_shape=[
            jax.ShapeDtypeStruct(q.shape, BF16),
            jax.ShapeDtypeStruct((rows, pieces, 8, shard), F32),
        ],
        compiler_params=pltpu.CompilerParams(vmem_limit_bytes=VMEM),
        cost_estimate=pl.CostEstimate(
            flops=4 * rows * (pieces * shard) ** 2 * width * 2,
            bytes_accessed=8 * rows * pieces * shard * width,
            transcendentals=rows * (pieces * shard) ** 2 * heads,
        ),
        name="attend",
    )(act, q, k, v, seg_row, seg_col)


def attend_back_body(
    act_ref, q_ref, k_ref, v_ref, o_ref, do_ref, lse_ref, segq_ref, segk_ref, cos_ref, sin_ref,
    g_ref, kt, dk, dv, dqt, qm, gm,
):
    row, piece = pl.program_id(0), pl.program_id(1)
    pieces, _, shard, width = k_ref.shape
    heads = width // HEAD_DIM

    @pl.when(piece == 0)
    def _():
        for j in range(pieces):
            kt[:, j * shard : (j + 1) * shard] = k_ref[j, 0].T
        dk[...] = jnp.zeros_like(dk)
        dv[...] = jnp.zeros_like(dv)

    q, do = q_ref[0, 0], do_ref[0, 0]
    for h, mask in enumerate(head_masks(q.shape, heads)):
        qm[h] = jnp.where(mask, q, jnp.zeros_like(q))
        gm[h] = jnp.where(mask, do, jnp.zeros_like(do))
    dqt[...] = jnp.zeros_like(dqt)
    prod = do.astype(F32) * o_ref[0, 0].astype(F32)
    prod_hi = prod.astype(BF16)
    prod_lo = (prod - prod_hi.astype(F32)).astype(BF16)
    pick = (
        lax.broadcasted_iota(jnp.int32, (8, width), 1) // HEAD_DIM
        == lax.broadcasted_iota(jnp.int32, (8, width), 0)
    ).astype(BF16)
    delta = dot(pick, prod_hi, 1, 1) + dot(pick, prod_lo, 1, 1)
    lse = lse_ref[0, 0]
    seg_q = segq_ref[0, 0]
    for j in range(pieces):

        @pl.when(act_ref[(row * pieces + piece) * pieces + j] != 0)
        def _():
            k, v = k_ref[j, 0], v_ref[j, 0]
            same = segk_ref[0][:, j : j + 1] == seg_q
            dk_sum = dk[j]
            dv_sum = dv[j]
            for h in range(heads):
                at = slice(h * HEAD_DIM, (h + 1) * HEAD_DIM)
                s = dot(k, qm[h], 1, 1)
                p = jnp.exp(jnp.where(same, s - lse[h : h + 1], NEG))
                dp = dot(v, gm[h], 1, 1)
                ds = (p * (dp - delta[h : h + 1])).astype(BF16)
                dv_sum = dv_sum + dot(p.astype(BF16), gm[h])
                dk_sum = dk_sum + dot(ds, qm[h])
                dqt[at] = dqt[at] + dot(kt[at, j * shard : (j + 1) * shard], ds)
            dk[j] = dk_sum
            dv[j] = dv_sum

    g_ref[piece, 0, :, 0:width] = turn(
        dqt[...].T * HEAD_DIM**-0.5, cos_ref[piece], -sin_ref[piece]
    ).astype(BF16)

    @pl.when(piece == pieces - 1)
    def _():
        for j in range(pieces):
            g_ref[j, 0, :, width : 2 * width] = turn(dk[j], cos_ref[j], -sin_ref[j]).astype(BF16)
            g_ref[j, 0, :, 2 * width :] = dv[j].astype(BF16)


def attend_back(act, q, k, v, o, do, lse, seg_row, seg_col, cos_tab, sin_tab):
    pieces, rows, shard, width = q.shape
    heads = width // HEAD_DIM
    one = pl.BlockSpec((1, 1, shard, width), lambda r, i, a: (i, r, 0, 0))
    whole = pl.BlockSpec((pieces, 1, shard, width), lambda r, i, a: (0, r, 0, 0))
    table = pl.BlockSpec((pieces, shard, 128), lambda r, i, a: (0, 0, 0))
    return pl.pallas_call(
        attend_back_body,
        grid_spec=pltpu.PrefetchScalarGridSpec(
            num_scalar_prefetch=1,
            grid=(rows, pieces),
            in_specs=[
                one,
                whole,
                whole,
                one,
                one,
                pl.BlockSpec((1, 1, 8, shard), lambda r, i, a: (r, i, 0, 0)),
                pl.BlockSpec((1, 1, 1, shard), lambda r, i, a: (r, i, 0, 0)),
                pl.BlockSpec((1, shard, pieces), lambda r, i, a: (r, 0, 0)),
                table,
                table,
            ],
            out_specs=pl.BlockSpec((pieces, 1, shard, 3 * width), lambda r, i, a: (0, r, 0, 0)),
            scratch_shapes=[
                pltpu.VMEM((width, pieces * shard), BF16),
                pltpu.VMEM((pieces, shard, width), F32),
                pltpu.VMEM((pieces, shard, width), F32),
                pltpu.VMEM((width, shard), F32),
                pltpu.VMEM((heads, shard, width), BF16),
                pltpu.VMEM((heads, shard, width), BF16),
            ],
        ),
        out_shape=jax.ShapeDtypeStruct((pieces, rows, shard, 3 * width), BF16),
        compiler_params=pltpu.CompilerParams(vmem_limit_bytes=VMEM),
        cost_estimate=pl.CostEstimate(
            flops=10 * rows * (pieces * shard) ** 2 * width * 2,
            bytes_accessed=16 * rows * pieces * shard * width,
            transcendentals=rows * (pieces * shard) ** 2 * heads,
        ),
        name="attend_back",
    )(act, q, k, v, o, do, lse, seg_row, seg_col, cos_tab, sin_tab)


def spread(own):
    one = swap(own, "c")
    two = swap(own, "y")
    three = swap(two, "c")
    return own, one, two, three


def exchange(parts):
    far = swap(parts[2:4], "y")
    return parts[0], swap(parts[1], "c"), far[0], swap(far[1], "c")


def pick(values, index, axis):
    return lax.dynamic_index_in_dim(values, index, axis, keepdims=False)


def local(
    inputs, segment_ids, doc_times, time_weight, time_bias, norm1_gain, norm1_bias, qkv_weight, qkv_bias,
    out_weight, out_bias, norm2_gain, norm2_bias, up_weight, up_bias, down_weight, down_bias, cotangent,
    *, dp,
):
    rows, shard, model = inputs.shape
    parts = 4
    tokens = rows * shard
    hidden_width = up_weight.shape[1]
    width = model // parts
    highest = lax.Precision.HIGHEST
    x_at, y_at, c_at = lax.axis_index("x"), lax.axis_index("y"), lax.axis_index("c")
    me = 2 * y_at + c_at
    order = [me ^ i for i in range(parts)]

    segs = jnp.stack(spread(segment_ids), axis=1)
    seg_row = segs[:, :, None, :]
    seg_col = segs.transpose(0, 2, 1)
    low_id, high_id = segs.min(axis=2), segs.max(axis=2)
    act = (low_id[:, :, None] <= high_id[:, None, :]) & (low_id[:, None, :] <= high_id[:, :, None])
    act = act.astype(jnp.int32).reshape(-1)
    positions = jnp.stack([o * shard + jnp.arange(shard, dtype=jnp.int32) for o in order])
    cos_tab, sin_tab = rotary_tables(positions, HEAD_DIM)

    doc_slots = jnp.arange(SEGS, dtype=jnp.int32)
    onehot = (segment_ids[..., None] == doc_slots).astype(F32)
    features = time_features(doc_times, TEMB).astype(BF16)
    time_shift = jnp.dot(features.reshape(rows * SEGS, TEMB), time_weight, preferred_element_type=F32)
    time_shift = time_shift.reshape(rows, SEGS, model) + time_bias.astype(F32)
    stream = inputs.astype(F32) + jnp.einsum("rsg,rgd->rsd", onehot, time_shift, precision=highest)
    normed1, norm1_back = jax.vjp(layer_norm, stream, norm1_gain.astype(F32), norm1_bias.astype(F32))
    own1, one1, two1, three1 = spread(normed1.astype(BF16))
    near1, far1 = jnp.stack([own1, one1]), jnp.stack([two1, three1])

    qkv_own = pick(qkv_weight.reshape(model, 3, parts, width), me, 2).reshape(model, 3 * width)
    qkv_bias_own = pick(qkv_bias.reshape(3, parts, width), me, 1).reshape(1, 3 * width).astype(F32)
    held = project_qkv(near1, qkv_own, qkv_bias_own, cos_tab, sin_tab, 0, parts)
    q, k, v = project_qkv(far1, qkv_own, qkv_bias_own, cos_tab, sin_tab, 2, parts, held)
    o, lse = attend(act, q, k, v, seg_row, seg_col)
    attended = jnp.concatenate([p.reshape(tokens, width) for p in exchange(o)], axis=1)
    out_blocks = out_weight.reshape(parts, width, model)
    out_own = jnp.concatenate([pick(out_blocks, o_at, 0) for o_at in order], axis=0)
    branch = dot(attended, out_own) + out_bias.astype(F32)
    middle = stream + branch.reshape(rows, shard, model)
    normed2, norm2_back = jax.vjp(layer_norm, middle, norm2_gain.astype(F32), norm2_bias.astype(F32))
    normed2 = normed2.astype(BF16).reshape(tokens, model)

    piece = hidden_width // (2 * dp)
    half = hidden_width // 2
    up_own = pick(up_weight.reshape(model, dp, 2, piece), c_at, 2).reshape(model, half)
    up_bias_own = pick(up_bias.reshape(dp, 2, piece), c_at, 1).reshape(half).astype(F32)
    down_own = pick(down_weight.reshape(dp, 2, piece, model), c_at, 1).reshape(half, model)
    cot = cotangent.reshape(tokens, model)
    cot_both = jnp.concatenate([cot, swap(cot, "c")], axis=0)
    normed2_both = jnp.concatenate([normed2, swap(normed2, "c")], axis=0)
    hidden = dot(normed2_both, up_own) + up_bias_own
    active, gate_back = jax.vjp(functools.partial(jax.nn.gelu, approximate=True), hidden)
    active = active.astype(BF16)
    feed = dot(active, down_own)
    feed = feed[:tokens] + swap(feed[tokens:].astype(BF16), "c").astype(F32)
    output = (middle + (feed + down_bias.astype(F32)).reshape(rows, shard, model)).astype(BF16)
    down_grad = dot(active, cot_both, 0, 0).astype(BF16)
    grad_hidden = gate_back(dot(cot_both, down_own, 1, 1))[0].astype(BF16)
    grad_normed2 = dot(grad_hidden, up_own, 1, 1)
    up_grad = dot(normed2_both, grad_hidden, 0, 0).astype(BF16)
    grad_normed2 = grad_normed2[:tokens] + swap(grad_normed2[tokens:].astype(BF16), "c").astype(F32)
    grad_mid_norm, gain2_grad, shift2_grad = norm2_back(grad_normed2.reshape(rows, shard, model))
    grad_middle = cotangent.astype(F32) + grad_mid_norm
    grad_middle_low = grad_middle.astype(BF16).reshape(tokens, model)

    grad_att = dot(grad_middle_low, out_own, 1, 1).astype(BF16)
    grad_att = jnp.stack(
        [grad_att[:, i * width : (i + 1) * width].reshape(rows, shard, width) for i in range(parts)]
    )
    grad_o = jnp.stack(exchange(grad_att))
    out_grad = dot(attended, grad_middle_low, 0, 0).reshape(parts, width, model)
    out_grad = jnp.concatenate([pick(out_grad, o_at, 0) for o_at in order], axis=0).astype(BF16)
    grad_qkv = attend_back(act, q, k, v, o, grad_o, lse, seg_row, seg_col, cos_tab, sin_tab)
    grad_near = grad_qkv[:2].reshape(2 * tokens, 3 * width)
    grad_far = grad_qkv[2:].reshape(2 * tokens, 3 * width)
    qkv_grad = (
        dot(near1.reshape(2 * tokens, model), grad_near, 0, 0)
        + dot(far1.reshape(2 * tokens, model), grad_far, 0, 0)
    ).astype(BF16)
    part1 = dot(grad_qkv.reshape(4 * tokens, 3 * width), qkv_own, 1, 1).astype(BF16)
    part1 = part1.reshape(4, tokens, model)
    here = part1[0].astype(F32) + swap(part1[1], "c").astype(F32)
    there = part1[2].astype(F32) + swap(part1[3], "c").astype(F32)
    grad_normed1 = here + swap(there.astype(BF16), "y").astype(F32)
    grad_norm, gain1_grad, shift1_grad = norm1_back(grad_normed1.reshape(rows, shard, model))
    grad_stream = grad_middle + grad_norm
    input_grad = grad_stream.astype(BF16)
    grad_shift = jnp.einsum("rsg,rsd->rgd", onehot, grad_stream, precision=highest)
    time_b_grad = jnp.sum(grad_shift, axis=(0, 1))
    time_w_grad = jnp.einsum("rgt,rgd->td", features.astype(F32), grad_shift, precision=highest)

    depth = dp // 2

    def halve(values, axis_name, at, dim):
        shape = values.shape
        split = values.reshape(shape[:dim] + (2, shape[dim] // 2) + shape[dim + 1 :])
        sent = swap(pick(split, 1 - at, dim), axis_name)
        return (pick(split, at, dim).astype(F32) + sent.astype(F32)).astype(BF16)

    def over_x(values):
        split = values.reshape(depth, 2, values.shape[0] // dp, values.shape[1])
        sent = swap(pick(split, 1 - x_at, 1), "x")
        return (pick(split, x_at, 1).astype(F32) + sent.astype(F32)).astype(BF16)

    def over_z(values):
        return lax.psum_scatter(values, "z", scatter_dimension=0, tiled=False)

    def join(values, axis_name, at):
        other = swap(values, axis_name)
        return jnp.where(at == 0, jnp.stack([values, other]), jnp.stack([other, values]))

    down_sum = over_z(halve(over_x(down_grad), "y", y_at, 2))
    up_sum = over_z(over_x(halve(up_grad, "y", y_at, 1)))
    out_sum = over_z(over_x(halve(halve(out_grad, "c", c_at, 1), "y", y_at, 1)))
    qkv_sum = over_z(over_x(qkv_grad))
    down_done = join(jnp.concatenate(list(join(down_sum, "y", y_at)), axis=1), "c", c_at)
    down_done = down_done.reshape(hidden_width // dp, model).astype(F32)
    up_done = join(jnp.concatenate(list(join(up_sum, "y", y_at)), axis=1), "c", c_at)
    up_done = up_done.reshape(2, model // dp, dp, piece).transpose(1, 2, 0, 3)
    up_done = up_done.reshape(model // dp, hidden_width).astype(F32)
    out_done = join(jnp.concatenate(list(join(out_sum, "y", y_at)), axis=1), "c", c_at)
    out_done = jnp.concatenate(list(out_done), axis=1).astype(F32)
    qkv_done = join(join(qkv_sum, "c", c_at), "y", y_at).reshape(parts, model // dp, 3, width)
    qkv_done = qkv_done.transpose(1, 2, 0, 3).reshape(model // dp, 3 * model).astype(F32)

    def total(values):
        return jnp.sum(values.astype(F32), axis=0)

    up_b = total(grad_hidden).reshape(dp, 1, piece)
    up_b = jnp.where(jnp.arange(2)[:, None] == c_at, up_b, 0.0).reshape(hidden_width)
    qkv_b = total(grad_qkv.reshape(4 * tokens, 3 * width)).reshape(3, 1, width)
    qkv_b = jnp.where(jnp.arange(parts)[:, None] == me, qkv_b, 0.0).reshape(3 * model)
    vectors = [
        time_b_grad, gain1_grad, shift1_grad, qkv_b, total(grad_middle_low), gain2_grad, shift2_grad, up_b, total(cot),
    ]
    small = [time_w_grad] + vectors
    small = jnp.concatenate([s.reshape(dp, -1) for s in small], axis=1).astype(BF16)
    small = small.astype(F32) + swap(small, "c").astype(F32)
    small = small + swap(small.astype(BF16), "y").astype(F32)
    small = over_z(over_x(small.astype(BF16)))[0].astype(F32)
    done = []
    start = 0
    for s in [time_w_grad] + vectors:
        done.append(small[start : start + s.size // dp])
        start += s.size // dp
    time_w_done = done[0].reshape(TEMB // dp, model)
    return (
        output, input_grad, time_w_done, done[1], done[2], done[3], qkv_done, done[4], out_done, done[5],
        done[6], done[7], up_done, done[8], down_done, done[9],
    )


def solution(mesh):
    dp, seq = mesh.shape["dp"], mesh.shape["seq"]
    fine = Mesh(mesh.devices.reshape(dp // 2, 2, seq // 2, 2), ("z", "x", "y", "c"))
    rows, seqs = ("z", "x"), ("y", "c")
    placed = (P(rows, seqs, None), P(rows, seqs), P(rows, None)) + (P(),) * 14 + (P(rows, seqs, None),)
    vec, mat = P(rows), P(rows, None)
    return jax.shard_map(
        functools.partial(local, dp=dp),
        mesh=fine,
        in_specs=placed,
        out_specs=(
            P(rows, seqs, None), P(rows, seqs, None), mat, vec, vec, vec, mat, vec, mat, vec, vec, vec, mat, vec, mat, vec,
        ),
        check_vma=False,
    )
```

```python
import functools
import math

import jax
import jax.numpy as jnp
from jax import lax
from jax.experimental import pallas as pl
from jax.experimental.pallas import tpu as pltpu
from jax.sharding import Mesh, PartitionSpec as P

HEADS = 16
HEAD_DIM = 64
TEMB = 256
SEGS = 8
EPSILON = 1e-05
F32 = jnp.float32
BF16 = jnp.bfloat16
NEG = -1e30
LOG2E = math.log2(math.e)
GELU_A = math.sqrt(2.0 / math.pi)
GELU_B = GELU_A * 0.044715
BLOCK = 256
VMEM = 60 * 1024 * 1024


def swap(value, axis):
    return lax.ppermute(value, axis, [(0, 1), (1, 0)])


def time_features(doc_times, column, half_size):
    frequency = jnp.exp(-math.log(10000.0) * (column % half_size).astype(F32) / half_size)
    angles = doc_times.astype(F32)[..., None] * frequency
    return jnp.where(column < half_size, jnp.sin(angles), jnp.cos(angles)).astype(BF16)


def rotary_tables(positions, head_size):
    half_size = head_size // 2
    frequency = jnp.exp(-math.log(10000.0) * 2.0 * jnp.arange(half_size, dtype=F32) / head_size)
    angles = positions.astype(F32)[..., None] * frequency
    cos_tab, sin_tab = jnp.cos(angles), jnp.sin(angles)
    return (
        jnp.concatenate([cos_tab] * 4, axis=-1),
        jnp.concatenate([-sin_tab, sin_tab, -sin_tab, sin_tab], axis=-1),
    )


def dot(left_op, right_op, left_dim=1, right_dim=0):
    return lax.dot_general(
        left_op, right_op, (((left_dim,), (right_dim,)), ((), ())), preferred_element_type=F32
    )


def turn(values, cos_tab, sin_tab):
    slabs = []
    lane = lax.broadcasted_iota(jnp.int32, (values.shape[0], 128), 1)
    first = lane % HEAD_DIM < HEAD_DIM // 2
    for start in range(0, values.shape[1], 128):
        slab = values[:, start : start + 128]
        partner = jnp.where(
            first, pltpu.roll(slab, 128 - HEAD_DIM // 2, 1), pltpu.roll(slab, HEAD_DIM // 2, 1)
        )
        slabs.append(slab * cos_tab + partner * sin_tab)
    return jnp.concatenate(slabs, axis=1)


def split_low(values):
    high = values.astype(BF16)
    return jnp.concatenate([high, (values - high.astype(F32)).astype(BF16)], axis=0)


def centre(values):
    scale = 1.0 / values.shape[-1]
    centred = values - jnp.sum(values, axis=-1, keepdims=True) * scale
    spread = jnp.sum(centred * centred, axis=-1, keepdims=True) * scale
    inverse = lax.rsqrt(spread + EPSILON)
    return centred * inverse, inverse


def norm_back(grad, gain, hat, inverse):
    scale = 1.0 / grad.shape[-1]
    scaled = grad * gain
    mean = jnp.sum(scaled, axis=-1, keepdims=True) * scale
    along = jnp.sum(scaled * hat, axis=-1, keepdims=True) * scale
    return inverse * (scaled - mean - hat * along)


def call(body, name, prefetch, grid, ins, outs, scratch=(), deps=(), flops=0, moved=0, trans=0):
    count, held = len(prefetch) + len(ins), len(deps)

    def kernel(*refs):
        body(*refs[:count], *refs[count + held :])

    return pl.pallas_call(
        kernel,
        grid_spec=pltpu.PrefetchScalarGridSpec(
            num_scalar_prefetch=len(prefetch),
            grid=grid,
            in_specs=[spec for _, spec in ins] + [pl.BlockSpec(memory_space=pl.ANY)] * held,
            out_specs=[spec for _, _, spec in outs],
            scratch_shapes=list(scratch),
        ),
        out_shape=[jax.ShapeDtypeStruct(shape, kind) for shape, kind, _ in outs],
        compiler_params=pltpu.CompilerParams(vmem_limit_bytes=VMEM),
        cost_estimate=pl.CostEstimate(flops=flops, bytes_accessed=moved, transcendentals=trans),
        name=name,
    )(*prefetch, *[array for array, _ in ins], *deps)


def fixed(shape):
    return pl.BlockSpec(shape, lambda *_: (0,) * len(shape))


def along(shape, axis=0):
    return pl.BlockSpec(shape, lambda g, *_: tuple(g if n == axis else 0 for n in range(len(shape))))


def norm1_body(x_ref, seg_ref, shift_ref, gain_ref, bias_ref, stream_ref, low_ref):
    slots = lax.broadcasted_iota(jnp.int32, (SEGS, seg_ref.shape[-1]), 0) == seg_ref[0]
    onehot = slots.astype(F32).astype(BF16)
    added = dot(jnp.concatenate([onehot, onehot], axis=0), split_low(shift_ref[0]), 0, 0)
    stream = x_ref[0].astype(F32) + added
    hat, _ = centre(stream)
    stream_ref[0] = stream
    low_ref[0] = (hat * gain_ref[...] + bias_ref[...]).astype(BF16)


def norm1(x, seg, shift, gain, bias):
    rows, shard, model = x.shape
    block = along((1, shard, model))
    return call(
        norm1_body, "norm1", (), (rows,),
        [(x, block), (seg, along((1, 1, shard))), (shift, along((1, SEGS, model))), (gain, fixed((1, model))), (bias, fixed((1, model)))],
        [(x.shape, F32, block), (x.shape, BF16, block)],
        moved=8 * x.size,
    )


def qkv_body(me_ref, a_ref, b_ref, wq_ref, wk_ref, wv_ref, bq_ref, bk_ref, bv_ref, cos_ref, sin_ref, *refs):
    q_ref, k_ref, v_ref, w_ref = refs[-4:]
    rows, shard, model = a_ref.shape
    width = wq_ref.shape[1]

    def run(x_ref):
        x = x_ref[...].reshape(rows * shard, model)
        cos_tab = jnp.concatenate([cos_ref[0]] * rows, axis=0)
        sin_tab = jnp.concatenate([sin_ref[0]] * rows, axis=0)
        q = turn(dot(x, wq_ref[...]) + bq_ref[...].astype(F32), cos_tab, sin_tab)
        q_ref[0] = (q * (LOG2E * HEAD_DIM**-0.5)).astype(BF16).reshape(rows, shard, width)
        k = turn(dot(x, wk_ref[...]) + bk_ref[...].astype(F32), cos_tab, sin_tab)
        k_ref[0] = k.astype(BF16).reshape(rows, shard, width)
        v = dot(x, wv_ref[...]) + bv_ref[...].astype(F32)
        v_ref[0] = v.astype(BF16).reshape(rows, shard, width)

    @pl.when(pl.program_id(0) == 0)
    def _():
        w_ref[:, 0:width] = wq_ref[...]
        w_ref[:, width : 2 * width] = wk_ref[...]
        w_ref[:, 2 * width :] = wv_ref[...]
        run(a_ref)

    @pl.when(pl.program_id(0) == 1)
    def _():
        run(b_ref)


def project_qkv(me, first, second, weight, bias, cos_tab, sin_tab, offset, parts, held=(), deps=()):
    rows, shard, model = first.shape
    width = model // parts
    out = jax.ShapeDtypeStruct((parts, rows, shard, width), BF16)
    place = pl.BlockSpec((1, rows, shard, width), lambda p, m: (p + offset, 0, 0, 0))
    table = pl.BlockSpec((1, shard, 128), lambda p, m: (p + offset, 0, 0))

    def column(part, height):
        return pl.BlockSpec((height, width), lambda p, m: (0, part * parts + m[0]))

    extra = list(held) + list(deps)
    return pl.pallas_call(
        qkv_body,
        grid_spec=pltpu.PrefetchScalarGridSpec(
            num_scalar_prefetch=1,
            grid=(2,),
            in_specs=[fixed(first.shape), fixed(first.shape)]
            + [column(n, model) for n in range(3)]
            + [column(n, 1) for n in range(3)]
            + [table, table]
            + [pl.BlockSpec(memory_space=pl.ANY)] * len(extra),
            out_specs=[place] * 3 + [fixed((model, 3 * width))],
        ),
        out_shape=[out] * 3 + [jax.ShapeDtypeStruct((model, 3 * width), BF16)],
        input_output_aliases={11 + n: n for n in range(len(held))},
        compiler_params=pltpu.CompilerParams(vmem_limit_bytes=VMEM),
        cost_estimate=pl.CostEstimate(
            flops=12 * rows * shard * model * width, bytes_accessed=12 * rows * shard * model, transcendentals=0
        ),
        name="qkv",
    )(me, first, second, weight, weight, weight, bias, bias, bias, cos_tab, sin_tab, *extra)


PLACED = (2, 0, 3, 1)


def seg_columns(segq_all, segk):
    pieces, shard, _ = segk.shape
    for j in range(pieces):
        row = jnp.broadcast_to(segq_all[j:j+1].astype(F32), (128, shard))
        segk[j] = row.T

def attend_body(cnt_ref, idx_ref, q_ref, k_ref, v_ref, seg_ref, o_ref, lse_ref, vt, segk, qmt, acc):
    row = pl.program_id(0)
    pieces, _, shard, width = k_ref.shape
    heads = width // HEAD_DIM

    @pl.when(row == 0)
    def _():
        qmt[...] = jnp.zeros_like(qmt)

    for j in range(pieces):
        vt[j] = v_ref[j, 0].T
    seg_columns(seg_ref[0], segk)

    @pl.loop(0, pieces)
    def _(piece):
        attend_piece(row, piece, cnt_ref, idx_ref, q_ref, k_ref, v_ref, seg_ref, o_ref, lse_ref, vt, segk, qmt, acc)

def attend_piece(row, piece, cnt_ref, idx_ref, q_ref, k_ref, v_ref, seg_ref, o_ref, lse_ref, vt, segk, qmt, acc):
    pieces, _, shard, width = k_ref.shape
    heads = width // HEAD_DIM
    qt = q_ref[piece, 0].T
    for h in range(heads):
        at = slice(h * HEAD_DIM, (h + 1) * HEAD_DIM)
        qmt[at, h * shard : (h + 1) * shard] = qt[at]
    at_q = row * pieces + piece
    seg_q = seg_ref[0, pl.ds(piece, 1)].astype(F32)

    def run(count):
        @pl.when(cnt_ref[at_q] == count)
        def _():
            qm = qmt[...]
            places = [idx_ref[at_q * pieces + t] for t in range(count)]
            top, tot, out = [None] * heads, [None] * heads, [None] * heads
            later = dot(k_ref[places[0], 0], qm)
            for t in range(count):
                s = later
                if t + 1 < count:
                    later = dot(k_ref[places[t + 1], 0], qm)
                col = segk[places[t]]
                same = jnp.concatenate([col] * (shard // 128), axis=1) == seg_q
                for h in range(heads):
                    at = slice(h * HEAD_DIM, (h + 1) * HEAD_DIM)
                    sh = jnp.where(same, s[:, h * shard : (h + 1) * shard], NEG)
                    best = jnp.max(sh, axis=0, keepdims=True)
                    if t:
                        best = jnp.maximum(top[h], best)
                        fade = jnp.exp2(top[h] - best)
                    p = jnp.exp2(sh - best)
                    total = jnp.sum(p, axis=0, keepdims=True)
                    part = dot(vt[places[t], at], p.astype(BF16))
                    if t:
                        total = tot[h] * fade + total
                        part = out[h] * fade + part
                    top[h], tot[h], out[h] = best, total, part
            for h in range(heads):
                acc[h * HEAD_DIM : (h + 1) * HEAD_DIM] = out[h] / tot[h]
                lse_ref[0, piece, h : h + 1] = top[h] + jnp.log2(tot[h])

    for count in range(1, pieces + 1):
        run(count)
    o_ref[piece, 0] = acc[...].T.astype(BF16)

def row_blocks(pieces, shard, width, axis=1):
    return along((pieces, 1, shard, width), axis)


def attend(cnt, idx, q, k, v, seg):
    pieces, rows, shard, width = q.shape
    heads = width // HEAD_DIM
    whole = row_blocks(pieces, shard, width)
    pairs = rows * (pieces * shard) ** 2
    return call(
        attend_body, "attend", (cnt, idx), (rows,),
        [(q, whole), (k, whole), (v, whole), (seg, along((1, pieces, shard)))],
        [(q.shape, BF16, whole), ((rows, pieces, 8, shard), F32, along((1, pieces, 8, shard)))],
        [
            pltpu.VMEM((pieces, width, shard), BF16),
            pltpu.VMEM((pieces, shard, 128), F32),
            pltpu.VMEM((width, heads * shard), BF16),
            pltpu.VMEM((width, shard), F32),
        ],
        flops=16 * pairs * width, moved=8 * q.size, trans=pairs * heads,
    )


def attend_back_body(cnt_ref, idx_ref, q_ref, k_ref, v_ref, o_ref, do_ref, lse_ref, seg_ref, cos_ref, sin_ref,
    g_ref, kt, segk, dk, dv, dqt, qmt, gmt, qst, gst):
    row = pl.program_id(0)
    pieces, _, shard, width = k_ref.shape

    @pl.when(row == 0)
    def _():
        qmt[...] = jnp.zeros_like(qmt)
        gmt[...] = jnp.zeros_like(gmt)

    for j in range(pieces):
        kt[j] = k_ref[j, 0].T
    seg_columns(seg_ref[0], segk)
    dk[...] = jnp.zeros_like(dk)
    dv[...] = jnp.zeros_like(dv)

    @pl.loop(0, pieces)
    def _(piece):
        back_piece(row, piece, cnt_ref, idx_ref, q_ref, k_ref, v_ref, o_ref, do_ref, lse_ref, seg_ref, cos_ref, sin_ref,
            g_ref, kt, segk, dk, dv, dqt, qmt, gmt, qst, gst)

    for j in range(pieces):
        at = PLACED[j]
        g_ref[at, 0, :, width : 2 * width] = turn(dk[j] * (1 / LOG2E), cos_ref[j], -sin_ref[j]).astype(BF16)
        g_ref[at, 0, :, 2 * width :] = dv[j].astype(BF16)

def back_piece(row, piece, cnt_ref, idx_ref, q_ref, k_ref, v_ref, o_ref, do_ref, lse_ref, seg_ref, cos_ref, sin_ref,
            g_ref, kt, segk, dk, dv, dqt, qmt, gmt, qst, gst):
    pieces, _, shard, width = k_ref.shape
    heads = width // HEAD_DIM
    q, do = q_ref[piece, 0], do_ref[piece, 0]
    qt, gt = q.T, do.T
    lane = lax.broadcasted_iota(jnp.int32, q.shape, 1) // HEAD_DIM
    for h in range(heads):
        at = slice(h * HEAD_DIM, (h + 1) * HEAD_DIM)
        qa = slice(h * shard, (h + 1) * shard)
        qmt[at, qa] = qt[at]
        gmt[at, qa] = gt[at]
        qst[qa] = jnp.where(lane == h, q, jnp.zeros_like(q))
        gst[qa] = jnp.where(lane == h, do, jnp.zeros_like(do))
    prod = do.astype(F32) * o_ref[piece, 0].astype(F32)
    prod_hi = prod.astype(BF16)
    prod_lo = (prod - prod_hi.astype(F32)).astype(BF16)
    pick = (lax.broadcasted_iota(jnp.int32, (8, width), 1) // HEAD_DIM == lax.broadcasted_iota(jnp.int32, (8, width), 0)).astype(BF16)
    delta = dot(pick, prod_hi, 1, 1) + dot(pick, prod_lo, 1, 1)
    lse = lse_ref[0, piece]
    at_q = row * pieces + piece
    seg_q = seg_ref[0, pl.ds(piece, 1)].astype(F32)

    def run(count):
        @pl.when(cnt_ref[at_q] == count)
        def _():
            places = [idx_ref[at_q * pieces + t] for t in range(count)]
            qm, gm = qmt[...], gmt[...]
            later = dot(k_ref[places[0], 0], qm), dot(v_ref[places[0], 0], gm)
            out = [None] * heads
            for t in range(count):
                s, dp = later
                j = places[t]
                if t + 1 < count:
                    later = dot(k_ref[places[t + 1], 0], qm), dot(v_ref[places[t + 1], 0], gm)
                col = segk[j]
                same = jnp.concatenate([col] * (shard // 128), axis=1) == seg_q
                ps, dss = [], []
                for h in range(heads):
                    at = slice(h * HEAD_DIM, (h + 1) * HEAD_DIM)
                    qa = slice(h * shard, (h + 1) * shard)
                    p = jnp.exp2(jnp.where(same, s[:, qa] - lse[h : h + 1], NEG))
                    ds = (p * (dp[:, qa] - delta[h : h + 1])).astype(BF16)
                    ps.append(p.astype(BF16))
                    dss.append(ds)
                    part = dot(kt[j, at], ds)
                    out[h] = part if t == 0 else out[h] + part
                dv[j] += dot(jnp.concatenate(ps, axis=1), gst[...])
                dk[j] += dot(jnp.concatenate(dss, axis=1), qst[...])
            for h in range(heads):
                dqt[h * HEAD_DIM : (h + 1) * HEAD_DIM] = out[h]

    for count in range(1, pieces + 1):
        run(count)
    place = jnp.where(piece % 2 == 1, piece // 2, 2 + piece // 2)
    g_ref[place, 0, :, 0:width] = turn(dqt[...].T * HEAD_DIM**-0.5, cos_ref[piece], -sin_ref[piece]).astype(BF16)

def attend_back(cnt, idx, q, k, v, o, do, lse, seg, cos_tab, sin_tab, deps=()):
    pieces, rows, shard, width = q.shape
    heads = width // HEAD_DIM
    whole, table = row_blocks(pieces, shard, width), fixed((pieces, shard, 128))
    pairs = rows * (pieces * shard) ** 2
    return call(
        attend_back_body, "attend_back", (cnt, idx), (rows,),
        [(q, whole), (k, whole), (v, whole), (o, whole), (do, whole), (lse, along((1, pieces, 8, shard)))]
        + [(seg, along((1, pieces, shard))), (cos_tab, table), (sin_tab, table)],
        [((pieces, rows, shard, 3 * width), BF16, row_blocks(pieces, shard, 3 * width))],
        [
            pltpu.VMEM((pieces, width, shard), BF16),
            pltpu.VMEM((pieces, shard, 128), F32),
            pltpu.VMEM((pieces, shard, width), F32),
            pltpu.VMEM((pieces, shard, width), F32),
            pltpu.VMEM((width, shard), F32),
            pltpu.VMEM((width, heads * shard), BF16),
            pltpu.VMEM((width, heads * shard), BF16),
            pltpu.VMEM((heads * shard, width), BF16),
            pltpu.VMEM((heads * shard, width), BF16),
        ],
        deps=deps, flops=40 * pairs * width, moved=16 * q.size, trans=pairs * heads,
    )[0]


def middle_body(order_ref, a0, a1, a2, a3, w0, w1, w2, w3, stream_ref, bias_ref, gain_ref, shift_ref, mid_ref, low_ref):
    total = dot(a0[0], w0[...]) + dot(a1[0], w1[...])
    total = total + (dot(a2[0], w2[...]) + dot(a3[0], w3[...]))
    mid = stream_ref[0] + (total + bias_ref[...])
    hat, _ = centre(mid)
    mid_ref[0] = mid
    low_ref[0] = (hat * gain_ref[...] + shift_ref[...]).astype(BF16)


def out_blocks(weight, parts):
    width = weight.shape[0] // parts

    def block(i):
        return pl.BlockSpec((width, weight.shape[1]), lambda g, o: (o[i], 0))

    return [(weight, block(i)) for i in range(parts)]


def middle_norm(order, attended, weight, stream, bias, gain, shift):
    rows, shard, model = stream.shape
    parts = len(attended)
    width = model // parts
    block, line = along((1, shard, model)), fixed((1, model))
    return call(
        middle_body, "middle", (order,), (rows,),
        [(a, along((1, shard, width))) for a in attended] + out_blocks(weight, parts)
        + [(stream, block), (bias, line), (gain, line), (shift, line)],
        [(stream.shape, F32, block), (stream.shape, BF16, block)],
        flops=2 * rows * shard * model * model, moved=14 * stream.size,
    )


def cot_body(blk_ref, a_ref, b_ref, up_ref, down_ref, g_ref, up_out, down_out):
    tokens = a_ref.shape[0]
    down = down_ref[...]
    g_ref[0:tokens] = dot(a_ref[...], down, 1, 1).astype(BF16)
    g_ref[tokens:] = dot(b_ref[...], down, 1, 1).astype(BF16)
    up_out[...] = up_ref[...]
    down_out[...] = down


def cot_down(blk, own, other, up, down, picked, half):
    tokens, model = own.shape
    steps = half // BLOCK
    column = along((2 * tokens, BLOCK), 1)
    if picked:
        up_at, down_at = along((model, BLOCK), 1), along((BLOCK, model))
    else:
        up_at = pl.BlockSpec((model, BLOCK), lambda g, b: (0, b[g]))
        down_at = pl.BlockSpec((BLOCK, model), lambda g, b: (b[g], 0))
    return call(
        cot_body, "cot_down", (blk,), (steps,),
        [(own, fixed(own.shape)), (other, fixed(own.shape)), (up, up_at), (down, down_at)],
        [
            ((2 * tokens, half), BF16, column),
            ((model, half), BF16, along((model, BLOCK), 1)),
            ((half, model), BF16, along((BLOCK, model))),
        ],
        flops=4 * tokens * model * half, moved=2 * (2 * tokens * (model + half) + 4 * model * half),
    )


def hidden_body(a_ref, b_ref, g_ref, up_ref, bias_ref, act_ref, grad_ref, sum_ref):
    tokens = a_ref.shape[0]
    up, bias = up_ref[...], bias_ref[...]
    chunk = 256 if tokens % 256 == 0 else tokens
    places = [(ref, start, n * tokens + start) for n, ref in enumerate((a_ref, b_ref)) for start in range(0, tokens, chunk)]
    total = 0.0
    later = dot(a_ref[0:chunk], up)
    for n, (ref, start, at) in enumerate(places):
        v = later + bias
        if n + 1 < len(places):
            ref, start, _ = places[n + 1]
            later = dot(ref[start : start + chunk], up)
        square = v * v
        tanh = jnp.tanh(v * (GELU_A + GELU_B * square))
        gate = 0.5 + 0.5 * tanh
        act = v * gate
        slope = gate + act * ((1.0 - tanh) * (GELU_A + 3.0 * GELU_B * square))
        grad = (slope * g_ref[at : at + chunk].astype(F32)).astype(BF16)
        act_ref[at : at + chunk] = act.astype(BF16)
        grad_ref[at : at + chunk] = grad
        total = total + jnp.sum(grad.astype(F32), axis=0, keepdims=True)
    sum_ref[...] = total


def hidden_units(own, other, grads, up, bias):
    tokens, model = own.shape
    half = up.shape[1]
    column, line = along((2 * tokens, BLOCK), 1), along((1, BLOCK), 1)
    return call(
        hidden_body, "hidden", (), (half // BLOCK,),
        [(own, fixed(own.shape)), (other, fixed(own.shape)), (grads, column), (up, along((model, BLOCK), 1)), (bias, line)],
        [(grads.shape, BF16, column), (grads.shape, BF16, column), ((1, half), F32, line)],
        flops=4 * tokens * model * half, moved=2 * (2 * tokens * (model + 3 * half) + model * half), trans=2 * tokens * half,
    )


def middle_back_body(
    order_ref, part_ref, sent_ref, mid_ref, cot_ref, gain_ref, w0, w1, w2, w3, grad_ref, low_ref, att_ref, sums_ref,
):
    grad = part_ref[0].astype(F32) + sent_ref[0].astype(F32)
    hat, inverse = centre(mid_ref[0])
    cot = cot_ref[0].astype(F32)
    total = cot + norm_back(grad, gain_ref[...], hat, inverse)
    low = total.astype(BF16)
    grad_ref[0] = total
    low_ref[0] = low
    for n, w in enumerate((w0, w1, w2, w3)):
        att_ref[n, 0] = dot(low, w[...], 1, 1).astype(BF16)

    @pl.when(pl.program_id(0) == 0)
    def _():
        sums_ref[...] = jnp.zeros_like(sums_ref)

    sums_ref[0:1] += jnp.sum(grad * hat, axis=0, keepdims=True)
    sums_ref[1:2] += jnp.sum(grad, axis=0, keepdims=True)
    sums_ref[2:3] += jnp.sum(low.astype(F32), axis=0, keepdims=True)
    sums_ref[3:4] += jnp.sum(cot, axis=0, keepdims=True)


def middle_back(order, part, sent, mid, cot, gain, weight, parts, deps=()):
    rows, shard, model = mid.shape
    width = model // parts
    block = along((1, shard, model))
    return call(
        middle_back_body, "middle_back", (order,), (rows,),
        [(part, block), (sent, block), (mid, block), (cot, block), (gain, fixed((1, model)))] + out_blocks(weight, parts),
        [
            (mid.shape, F32, block),
            (mid.shape, BF16, block),
            ((parts, rows, shard, width), BF16, along((parts, 1, shard, width), 1)),
            ((8, model), F32, fixed((8, model))),
        ],
        deps=deps, flops=2 * rows * shard * model * model, moved=18 * mid.size,
    )


def norm1_back_body(part_ref, near_ref, far_ref, stream_ref, mid_ref, gain_ref, seg_ref, in_ref, shift_ref, sums_ref):
    grad = part_ref[0].astype(F32) + near_ref[0].astype(F32) + far_ref[0].astype(F32)
    hat, inverse = centre(stream_ref[0])
    total = mid_ref[0] + norm_back(grad, gain_ref[...], hat, inverse)
    in_ref[0] = total.astype(BF16)
    slots = lax.broadcasted_iota(jnp.int32, (SEGS, seg_ref.shape[-1]), 0) == seg_ref[0]
    onehot = slots.astype(F32).astype(BF16)
    shift_ref[0] = dot(jnp.concatenate([onehot, onehot], axis=1), split_low(total))

    @pl.when(pl.program_id(0) == 0)
    def _():
        sums_ref[...] = jnp.zeros_like(sums_ref)

    sums_ref[0:1] += jnp.sum(grad * hat, axis=0, keepdims=True)
    sums_ref[1:2] += jnp.sum(grad, axis=0, keepdims=True)


def norm1_back(part, near, far, stream, mid, gain, seg):
    rows, shard, model = stream.shape
    block = along((1, shard, model))
    return call(
        norm1_back_body, "norm1_back", (), (rows,),
        [(part, block), (near, block), (far, block), (stream, block), (mid, block), (gain, fixed((1, model))), (seg, along((1, 1, shard)))],
        [
            (stream.shape, BF16, block),
            ((rows, SEGS, model), F32, along((1, SEGS, model))),
            ((8, model), F32, fixed((8, model))),
        ],
        moved=16 * stream.size,
    )


def exchange(parts):
    far = swap(parts[2:4], "y")
    return [parts[0], swap(parts[1], "c"), far[0], swap(far[1], "c")]


def cut(values, index, size, axis):
    return lax.dynamic_slice_in_dim(values, index * size, size, axis)


def add_low(kept, sent):
    return (kept.astype(F32) + sent.astype(F32)).astype(BF16)


def ordered(at, own, other, axis):
    return jnp.where(at == 0, jnp.concatenate([own, other], axis), jnp.concatenate([other, own], axis))


def local(
    inputs, segment_ids, doc_times, time_weight, time_bias, norm1_gain, norm1_bias, qkv_weight, qkv_bias,
    out_weight, out_bias, norm2_gain, norm2_bias, up_weight, up_bias, down_weight, down_bias, cotangent,
    *, dp,
):
    rows, shard, model = inputs.shape
    parts = 4
    tokens = rows * shard
    hidden_width = up_weight.shape[1]
    width = model // parts
    depth = dp // 2
    half = hidden_width // 2
    piece = half // dp
    z_at, x_at, y_at, c_at = (lax.axis_index(name) for name in ("z", "x", "y", "c"))
    me = 2 * y_at + c_at
    order = [me ^ i for i in range(parts)]
    order_list = jnp.stack(order).astype(jnp.int32)
    me_list = order_list[:1]

    def line(vector):
        return vector.astype(F32)[None]

    seg = segment_ids[:, None, :]
    features = time_features(doc_times.reshape(rows * SEGS), jnp.arange(TEMB), TEMB // 2)
    time_shift = dot(features, time_weight).reshape(rows, SEGS, model) + time_bias.astype(F32)
    stream, own1 = norm1(inputs, seg, time_shift, line(norm1_gain), line(norm1_bias))
    one1 = swap(own1, "c")
    two1 = swap(own1, "y")

    seg_two = swap(segment_ids, "y")
    segs = jnp.stack([segment_ids, swap(segment_ids, "c"), seg_two, swap(seg_two, "c")], axis=1)
    low_id, high_id = segs.min(axis=2), segs.max(axis=2)
    act = (low_id[:, :, None] <= high_id[:, None, :]) & (low_id[:, None, :] <= high_id[:, :, None])
    places = jnp.arange(parts, dtype=jnp.int32)
    rank = jnp.cumsum(act.astype(jnp.int32), axis=2) - 1
    chosen = act[..., None] & (rank[..., None] == places)
    idx = jnp.sum(jnp.where(chosen, places[:, None], 0), axis=2).astype(jnp.int32).reshape(-1)
    cnt = jnp.sum(act.astype(jnp.int32), axis=2).reshape(-1)
    positions = jnp.stack([o * shard + jnp.arange(shard, dtype=jnp.int32) for o in order])
    cos_tab, sin_tab = rotary_tables(positions, HEAD_DIM)
    all_times = lax.all_gather(doc_times.reshape(rows * SEGS), ("z", "x"))

    cot = cotangent.reshape(tokens, model)
    cot_other = swap(cot, "c")
    turned = jnp.stack([1 - x_at, x_at])
    if piece % BLOCK == 0:
        blk = ((jnp.arange(depth)[None, :] * 2 + turned[:, None]) * 2 + c_at) * (piece // BLOCK)
        blk = (blk[..., None] + jnp.arange(piece // BLOCK)).reshape(-1).astype(jnp.int32)
        up_from, down_from = up_weight, down_weight
    else:
        blk = jnp.zeros((half // BLOCK,), jnp.int32)
        up_from = up_weight.reshape(model, depth, 2, 2, piece)
        up_from = lax.dynamic_index_in_dim(up_from, c_at, 3, keepdims=False)
        up_from = jnp.where(x_at == 1, up_from, up_from[:, :, ::-1]).transpose(0, 2, 1, 3).reshape(model, half)
        down_from = down_weight.reshape(depth, 2, 2, piece, model)
        down_from = lax.dynamic_index_in_dim(down_from, c_at, 2, keepdims=False)
        down_from = jnp.where(x_at == 1, down_from, down_from[:, ::-1]).transpose(1, 0, 2, 3).reshape(half, model)
    grad_act, up_own, down_own = cot_down(blk, cot, cot_other, up_from, down_from, piece % BLOCK != 0, half)
    up_bias_own = lax.dynamic_index_in_dim(up_bias.reshape(depth, 2, 2, piece), c_at, 2, keepdims=False)
    up_bias_own = jnp.where(x_at == 1, up_bias_own, up_bias_own[:, ::-1]).transpose(1, 0, 2).reshape(half)

    bias_line = qkv_bias.reshape(1, 3 * model)
    *held, _ = project_qkv(me_list, own1, one1, qkv_weight, bias_line, cos_tab, sin_tab, 0, parts, (), (grad_act,))
    three1 = swap(two1, "c")
    q, k, v, qkv_own = project_qkv(me_list, two1, three1, qkv_weight, bias_line, cos_tab, sin_tab, 2, parts, held)
    o, lse = attend(cnt, idx, q, k, v, segs)
    attended = exchange(o)
    middle, normed2 = middle_norm(
        order_list, attended, out_weight, stream, line(out_bias), line(norm2_gain), line(norm2_bias)
    )

    normed2 = normed2.reshape(tokens, model)
    normed2_other = swap(normed2, "c")
    active, grad_hidden, up_b = hidden_units(normed2, normed2_other, grad_act, up_own, line(up_bias_own))
    part2_sent = swap(dot(grad_hidden[tokens:], up_own, 1, 1).astype(BF16), "c").reshape(rows, shard, model)
    part2 = dot(grad_hidden[:tokens], up_own, 1, 1).astype(BF16).reshape(rows, shard, model)
    grad_middle, grad_middle_low, grad_att, sums2 = middle_back(
        order_list, part2, part2_sent, middle, cotangent, line(norm2_gain), out_weight, parts
    )
    grad_o = jnp.stack(exchange(grad_att))

    cot_both = jnp.concatenate([cot, cot_other], axis=0)
    normed2_both = jnp.concatenate([normed2, normed2_other], axis=0)
    down_sent = swap(dot(active[:, : half // 2], cot_both, 0, 0).astype(BF16), "x")
    up_grad = dot(normed2_both, grad_hidden, 0, 0).astype(BF16)
    up_z = lax.psum_scatter(up_grad, "z", scatter_dimension=0, tiled=True)
    down_kept = dot(active[:, half // 2 :], cot_both, 0, 0).astype(BF16)
    feed_sent = swap(dot(active[tokens:], down_own).astype(BF16), "c")
    feed = dot(active[:tokens], down_own) + feed_sent.astype(F32) + line(down_bias)
    output = (middle + feed.reshape(rows, shard, model)).astype(BF16)
    attended_all = jnp.concatenate([a.reshape(tokens, width) for a in attended], axis=1)
    out_grad = dot(attended_all, grad_middle_low.reshape(tokens, model), 0, 0).astype(BF16)

    grad_qkv = attend_back(cnt, idx, q, k, v, o, grad_o, lse, segs, cos_tab, sin_tab, (down_kept, up_grad, down_sent))
    part1_out = dot(grad_qkv[:2].reshape(2 * tokens, 3 * width), qkv_own, 1, 1).astype(BF16)
    part1_out = part1_out.reshape(2, rows, shard, model)
    part1 = dot(grad_qkv[2:].reshape(2 * tokens, 3 * width), qkv_own, 1, 1).astype(BF16)
    part1 = part1.reshape(2, rows, shard, model)
    near = swap(part1_out[0], "c")
    there = add_low(part1[1], swap(part1_out[1], "c"))
    far = swap(there, "y")
    normed1_all = jnp.stack([one1, three1, own1, two1]).reshape(parts * tokens, model)
    grad_qkv = grad_qkv.reshape(parts * tokens, 3 * width)
    qkv_grad = dot(normed1_all, grad_qkv, 0, 0).astype(BF16)
    qkv_b = jnp.sum(grad_qkv.astype(F32), axis=0)
    input_grad, grad_shift, sums1 = norm1_back(part1[0], near, far, stream, grad_middle, line(norm1_gain), seg)

    down_x = add_low(down_kept, down_sent)
    down_y = add_low(cut(down_x, y_at, model // 2, 1), swap(cut(down_x, 1 - y_at, model // 2, 1), "y"))
    down_z = lax.psum_scatter(down_y, "z", scatter_dimension=0, tiled=True)
    up_rows = model // dp
    up_sent = swap(cut(up_z, 1 - x_at, up_rows, 0), "x")
    up_sent = jnp.concatenate([up_sent[:, half // 2 :], up_sent[:, : half // 2]], axis=1)
    up_x = add_low(cut(up_z, x_at, up_rows, 0), up_sent)
    up_y = add_low(cut(up_x, y_at, half // 2, 1), swap(cut(up_x, 1 - y_at, half // 2, 1), "y"))
    out_grad = jnp.concatenate([cut(out_grad, o_at, width, 0) for o_at in order], axis=0)
    out_c = add_low(cut(out_grad, c_at, model // 2, 1), swap(cut(out_grad, 1 - c_at, model // 2, 1), "c"))
    out_y = add_low(cut(out_c, y_at, width, 1), swap(cut(out_c, 1 - y_at, width, 1), "y"))
    late = jnp.concatenate([qkv_grad, out_y], axis=1).reshape(depth, 2 * up_rows, model)
    late_x = add_low(cut(late, x_at, up_rows, 1), swap(cut(late, 1 - x_at, up_rows, 1), "x"))
    late_z = lax.psum_scatter(late_x, "z", scatter_dimension=0, tiled=False)

    down_done = ordered(y_at, down_z, swap(down_z, "y"), 1)
    down_done = ordered(c_at, down_done, swap(down_done, "c"), 0).astype(F32)
    up_done = ordered(y_at, up_y, swap(up_y, "y"), 1)
    up_done = ordered(c_at, up_done[None], swap(up_done, "c")[None], 0).reshape(2, up_rows, 2, depth, piece)
    up_done = jnp.where(x_at == 1, up_done, up_done[:, :, ::-1]).transpose(1, 3, 2, 0, 4)
    up_done = up_done.reshape(up_rows, hidden_width).astype(F32)
    late_done = ordered(c_at, late_z[None], swap(late_z, "c")[None], 0)
    late_done = ordered(y_at, late_done[None], swap(late_done, "y")[None], 0).reshape(parts, up_rows, model)
    qkv_done = late_done[:, :, : 3 * width].reshape(parts, up_rows, 3, width).transpose(1, 2, 0, 3)
    qkv_done = qkv_done.reshape(up_rows, 3 * model).astype(F32)
    out_done = late_done[:, :, 3 * width :].reshape(2, 2, up_rows, width).transpose(2, 1, 0, 3)
    out_done = out_done.reshape(up_rows, model).astype(F32)

    up_b = up_b.reshape(2, depth, 1, piece)
    up_b = jnp.where(x_at == 1, up_b, up_b[::-1]).transpose(1, 0, 2, 3)
    up_b = jnp.where(jnp.arange(2)[:, None] == c_at, up_b, 0.0).reshape(-1, model)
    qkv_b = jnp.where(jnp.arange(parts)[:, None] == me, qkv_b.reshape(3, 1, width), 0.0).reshape(3, model)
    small = jnp.concatenate(
        [grad_shift.reshape(rows * SEGS, model), sums1[:2], sums2[:4], qkv_b, up_b], axis=0
    )
    small = add_low(small, swap(small.astype(BF16), "c"))
    small = add_low(small, swap(small, "y"))
    small = lax.all_gather(small, ("z", "x"))
    shifts = small[:, : rows * SEGS].reshape(dp * rows * SEGS, model)
    columns = (2 * z_at + x_at) * (TEMB // dp) + jnp.arange(TEMB // dp)
    wanted = time_features(all_times.reshape(-1), columns, TEMB // 2)
    time_w_done = dot(wanted, shifts, 0, 0)
    sums = jnp.sum(small[:, rows * SEGS :].astype(F32), axis=0)
    dp_at = 2 * z_at + x_at

    def share(vector):
        return cut(vector.reshape(-1), dp_at, vector.size // dp, 0)

    time_b_done = jnp.sum(cut(shifts, dp_at, up_rows, 1).astype(F32), axis=0)
    return (
        output, input_grad, time_w_done, time_b_done, share(sums[0]), share(sums[1]), qkv_done, share(sums[6:9]),
        out_done, share(sums[4]), share(sums[2]), share(sums[3]), up_done, share(sums[9:]), down_done, share(sums[5]),
    )


def solution(mesh):
    dp, seq = mesh.shape["dp"], mesh.shape["seq"]
    fine = Mesh(mesh.devices.reshape(dp // 2, 2, seq // 2, 2), ("z", "x", "y", "c"))
    rows, seqs = ("z", "x"), ("y", "c")
    placed = (P(rows, seqs, None), P(rows, seqs), P(rows, None)) + (P(),) * 14 + (P(rows, seqs, None),)
    vec, mat = P(rows), P(rows, None)
    return jax.shard_map(
        functools.partial(local, dp=dp),
        mesh=fine,
        in_specs=placed,
        out_specs=(
            P(rows, seqs, None), P(rows, seqs, None), mat, vec, vec, vec, mat, vec, mat, vec, vec, vec, mat, vec, mat, vec,
        ),
        check_vma=False,
    )
```

```python
import functools
import math

import jax
import jax.numpy as jnp
from jax import lax
from jax.experimental import pallas as pl
from jax.experimental.pallas import tpu as pltpu
from jax.sharding import Mesh, PartitionSpec as P

HEADS = 16
HEAD_DIM = 64
TEMB = 256
SEGS = 8
EPSILON = 1e-05
F32 = jnp.float32
BF16 = jnp.bfloat16
NEG = -1e30
LOG2E = math.log2(math.e)
GELU_A = math.sqrt(2.0 / math.pi)
GELU_B = GELU_A * 0.044715
BLOCK = 256
VMEM = 60 * 1024 * 1024


def swap(value, axis):
    return lax.ppermute(value, axis, [(0, 1), (1, 0)])


def time_features(doc_times, column, half_size):
    frequency = jnp.exp(-math.log(10000.0) * (column % half_size).astype(F32) / half_size)
    angles = doc_times.astype(F32)[..., None] * frequency
    return jnp.where(column < half_size, jnp.sin(angles), jnp.cos(angles)).astype(BF16)


def rotary_tables(positions, head_size):
    half_size = head_size // 2
    frequency = jnp.exp(-math.log(10000.0) * 2.0 * jnp.arange(half_size, dtype=F32) / head_size)
    angles = positions.astype(F32)[..., None] * frequency
    cos_tab, sin_tab = jnp.cos(angles), jnp.sin(angles)
    return (
        jnp.concatenate([cos_tab] * 4, axis=-1),
        jnp.concatenate([-sin_tab, sin_tab, -sin_tab, sin_tab], axis=-1),
    )


def dot(left_op, right_op, left_dim=1, right_dim=0):
    return lax.dot_general(
        left_op, right_op, (((left_dim,), (right_dim,)), ((), ())), preferred_element_type=F32
    )


def turn(values, cos_tab, sin_tab):
    slabs = []
    lane = lax.broadcasted_iota(jnp.int32, (values.shape[0], 128), 1)
    first = lane % HEAD_DIM < HEAD_DIM // 2
    for start in range(0, values.shape[1], 128):
        slab = values[:, start : start + 128]
        partner = jnp.where(
            first, pltpu.roll(slab, 128 - HEAD_DIM // 2, 1), pltpu.roll(slab, HEAD_DIM // 2, 1)
        )
        slabs.append(slab * cos_tab + partner * sin_tab)
    return jnp.concatenate(slabs, axis=1)


def split_low(values):
    high = values.astype(BF16)
    return jnp.concatenate([high, (values - high.astype(F32)).astype(BF16)], axis=0)


def centre(values):
    scale = 1.0 / values.shape[-1]
    centred = values - jnp.sum(values, axis=-1, keepdims=True) * scale
    spread = jnp.sum(centred * centred, axis=-1, keepdims=True) * scale
    inverse = lax.rsqrt(spread + EPSILON)
    return centred * inverse, inverse


def norm_back(grad, gain, hat, inverse):
    scale = 1.0 / grad.shape[-1]
    scaled = grad * gain
    mean = jnp.sum(scaled, axis=-1, keepdims=True) * scale
    along = jnp.sum(scaled * hat, axis=-1, keepdims=True) * scale
    return inverse * (scaled - mean - hat * along)


def call(body, name, prefetch, grid, ins, outs, scratch=(), deps=(), held=(), flops=0, moved=0, trans=0):
    count = len(prefetch) + len(ins)
    extra = [array for array, _ in held] + list(deps)

    def kernel(*refs):
        body(*refs[:count], *refs[count + len(extra) :])

    return pl.pallas_call(
        kernel,
        grid_spec=pltpu.PrefetchScalarGridSpec(
            num_scalar_prefetch=len(prefetch),
            grid=grid,
            in_specs=[spec for _, spec in ins] + [pl.BlockSpec(memory_space=pl.ANY)] * len(extra),
            out_specs=[spec for _, _, spec in outs],
            scratch_shapes=list(scratch),
        ),
        out_shape=[jax.ShapeDtypeStruct(shape, kind) for shape, kind, _ in outs],
        input_output_aliases={count + n: out for n, (_, out) in enumerate(held)},
        compiler_params=pltpu.CompilerParams(vmem_limit_bytes=VMEM),
        cost_estimate=pl.CostEstimate(flops=flops, bytes_accessed=moved, transcendentals=trans),
        name=name,
    )(*prefetch, *[array for array, _ in ins], *extra)


def fixed(shape):
    return pl.BlockSpec(shape, lambda *_: (0,) * len(shape))


def part(shape, row):
    return pl.BlockSpec(shape, lambda *_: (row,) + (0,) * (len(shape) - 1))


def along(shape, axis=0):
    return pl.BlockSpec(shape, lambda g, *_: tuple(g if n == axis else 0 for n in range(len(shape))))


def norm1_body(x_ref, seg_ref, shift_ref, gain_ref, bias_ref, stream_ref, low_ref):
    slots = lax.broadcasted_iota(jnp.int32, (SEGS, seg_ref.shape[-1]), 0) == seg_ref[0]
    onehot = slots.astype(F32).astype(BF16)
    added = dot(jnp.concatenate([onehot, onehot], axis=0), split_low(shift_ref[0]), 0, 0)
    stream = x_ref[0].astype(F32) + added
    hat, _ = centre(stream)
    stream_ref[...] = stream
    low_ref[...] = (hat * gain_ref[...] + bias_ref[...]).astype(BF16)


def norm1(row, x, seg, shift, gain, bias):
    _, shard, model = x.shape
    whole = fixed((shard, model))
    return call(
        norm1_body, "norm1", (), (1,),
        [(x, part((1, shard, model), row)), (seg, part((1, 1, shard), row)), (shift, part((1, SEGS, model), row))]
        + [(gain, fixed((1, model))), (bias, fixed((1, model)))],
        [((shard, model), F32, whole), ((shard, model), BF16, whole)],
        moved=8 * shard * model,
    )


def qkv_body(me_ref, x0, x1, x2, x3, w_ref, b_ref, cos_ref, sin_ref, out_ref, all_ref, own_ref):
    pieces, shard, _ = cos_ref.shape
    refs = (x0, x1, x2, x3)
    step = pl.program_id(0)

    @pl.when(step == 0)
    def _():
        for n, x_ref in enumerate(refs):
            all_ref[0, n] = x_ref[...]

    def run(turned):
        w = w_ref[...]
        later = dot(x0[...], w)
        for n in range(pieces):
            full = later + b_ref[...].astype(F32)
            if n + 1 < pieces:
                later = dot(refs[n + 1][...], w)
            if turned:
                full = turn(full, cos_ref[n], sin_ref[n]) * jnp.where(step == 0, LOG2E * HEAD_DIM**-0.5, 1.0)
            out_ref[0, n] = full.astype(BF16)

    own_ref[...] = w_ref[...].T

    @pl.when(step < 2)
    def _():
        run(True)

    @pl.when(step == 2)
    def _():
        run(False)


def project_qkv(row, rows, me, pieces, weight, bias, cos_tab, sin_tab, held=(), deps=()):
    shard, model = pieces[0].shape
    parts = len(pieces)
    width = model // parts
    return call(
        qkv_body, "qkv", (me,), (3,),
        [(x, fixed((shard, model))) for x in pieces]
        + [
            (weight, pl.BlockSpec((model, width), lambda g, m: (0, g * parts + m[0]))),
            (bias, pl.BlockSpec((1, width), lambda g, m: (0, g * parts + m[0]))),
            (cos_tab, fixed(cos_tab.shape)),
            (sin_tab, fixed(cos_tab.shape)),
        ],
        [
            ((3, parts, shard, width), BF16, along((1, parts, shard, width))),
            ((rows, parts, shard, model), BF16, part((1, parts, shard, model), row)),
            ((3 * width, model), BF16, along((width, model))),
        ],
        held=[(array, 1) for array in held], deps=deps,
        flops=6 * parts * shard * model * width, moved=2 * (3 * model * width + 2 * parts * shard * model),
    )


def seg_columns(segq_all, segk):
    pieces, shard, _ = segk.shape
    for j in range(pieces):
        row = jnp.broadcast_to(segq_all[j:j+1].astype(F32), (128, shard))
        segk[j] = row.T

def attend_body(cnt_ref, idx_ref, qkv_ref, seg_ref, o_ref, one_ref, far_ref, lse_ref, vt, segk, qmt, acc):
    _, pieces, shard, width = qkv_ref.shape
    q_ref, k_ref, v_ref = (qkv_ref.at[n] for n in range(3))
    qmt[...] = jnp.zeros_like(qmt)
    for j in range(pieces):
        vt[j] = v_ref[j].T
    seg_columns(seg_ref[0], segk)

    @pl.loop(0, pieces)
    def _(piece):
        attend_piece(piece, cnt_ref, idx_ref, q_ref, k_ref, seg_ref, o_ref, lse_ref, vt, segk, qmt, acc)

    one_ref[...] = o_ref[1]
    far_ref[...] = o_ref[2:]


def attend_piece(piece, cnt_ref, idx_ref, q_ref, k_ref, seg_ref, o_ref, lse_ref, vt, segk, qmt, acc):
    pieces, shard, width = k_ref.shape
    heads = width // HEAD_DIM
    qt = q_ref[piece].T
    for h in range(heads):
        at = slice(h * HEAD_DIM, (h + 1) * HEAD_DIM)
        qmt[at, h * shard : (h + 1) * shard] = qt[at]
    seg_q = seg_ref[0, pl.ds(piece, 1)].astype(F32)

    def run(count):
        @pl.when(cnt_ref[piece] == count)
        def _():
            qm = qmt[...]
            places = [idx_ref[piece * pieces + t] for t in range(count)]
            top, tot, out = [None] * heads, [None] * heads, [None] * heads
            later = dot(k_ref[places[0]], qm)
            for t in range(count):
                s = later
                if t + 1 < count:
                    later = dot(k_ref[places[t + 1]], qm)
                col = segk[places[t]]
                same = jnp.concatenate([col] * (shard // 128), axis=1) == seg_q
                for h in range(heads):
                    at = slice(h * HEAD_DIM, (h + 1) * HEAD_DIM)
                    sh = jnp.where(same, s[:, h * shard : (h + 1) * shard], NEG)
                    best = jnp.max(sh, axis=0, keepdims=True)
                    if t:
                        best = jnp.maximum(top[h], best)
                        fade = jnp.exp2(top[h] - best)
                    p = jnp.exp2(sh - best)
                    total = jnp.sum(p, axis=0, keepdims=True)
                    part = dot(vt[places[t], at], p.astype(BF16))
                    if t:
                        total = tot[h] * fade + total
                        part = out[h] * fade + part
                    top[h], tot[h], out[h] = best, total, part
            for h in range(heads):
                acc[h * HEAD_DIM : (h + 1) * HEAD_DIM] = out[h] / tot[h]
                lse_ref[piece, h : h + 1] = top[h] + jnp.log2(tot[h])

    for count in range(1, pieces + 1):
        run(count)
    o_ref[piece] = acc[...].T.astype(BF16)

def attend(row, cnt, idx, qkv, seg):
    _, pieces, shard, width = qkv.shape
    heads = width // HEAD_DIM
    pairs = (pieces * shard) ** 2
    shape, shape_lse = (pieces, shard, width), (pieces, 8, shard)
    return call(
        attend_body, "attend", (cnt, idx), (1,),
        [(qkv, fixed(qkv.shape)), (seg, part((1, pieces, shard), row))],
        [
            (shape, BF16, fixed(shape)),
            (shape[1:], BF16, fixed(shape[1:])),
            ((2,) + shape[1:], BF16, fixed((2,) + shape[1:])),
            (shape_lse, F32, fixed(shape_lse)),
        ],
        [
            pltpu.VMEM((pieces, width, shard), BF16),
            pltpu.VMEM((pieces, shard, 128), F32),
            pltpu.VMEM((width, heads * shard), BF16),
            pltpu.VMEM((width, shard), F32),
        ],
        flops=16 * pairs * width, moved=2 * qkv.size, trans=pairs * heads,
    )


def attend_back_body(
    cnt_ref, idx_ref, qkv_ref, o_ref, do0, do1, do2, do3, lse_ref, seg_ref, cos_ref, sin_ref, w_ref,
    g_ref, p0_ref, p1_ref, p2_ref, p3_ref, kt, segk, dk, dv, dq, dqt, qmt, gmt, qst, gst, do_ref,
):
    _, pieces, shard, width = qkv_ref.shape
    q_ref, k_ref, v_ref = (qkv_ref.at[n] for n in range(3))
    qmt[...] = jnp.zeros_like(qmt)
    gmt[...] = jnp.zeros_like(gmt)
    for j, ref in enumerate((do0, do1, do2, do3)):
        kt[j] = k_ref[j].T
        do_ref[j] = ref[...].reshape(shard, width)
    seg_columns(seg_ref[0], segk)
    dk[...] = jnp.zeros_like(dk)
    dv[...] = jnp.zeros_like(dv)

    @pl.loop(0, pieces)
    def _(piece):
        back_piece(
            piece, cnt_ref, idx_ref, q_ref, k_ref, v_ref, o_ref, do_ref, lse_ref, seg_ref, cos_ref, sin_ref,
            kt, segk, dk, dv, dq, dqt, qmt, gmt, qst, gst,
        )

    for j, ref in ((1, p1_ref), (3, p3_ref), (0, p0_ref), (2, p2_ref)):
        grad_k = turn(dk[j] * (1 / LOG2E), cos_ref[j], -sin_ref[j]).astype(BF16)
        grad = jnp.concatenate([dq[j], grad_k, dv[j].astype(BF16)], axis=1)
        g_ref[0, j] = grad
        ref[...] = dot(grad, w_ref[...]).astype(BF16)


def back_piece(
    piece, cnt_ref, idx_ref, q_ref, k_ref, v_ref, o_ref, do_ref, lse_ref, seg_ref, cos_ref, sin_ref,
    kt, segk, dk, dv, dq, dqt, qmt, gmt, qst, gst,
):
    pieces, shard, width = k_ref.shape
    heads = width // HEAD_DIM
    q, do = q_ref[piece], do_ref[piece]
    qt, gt = q.T, do.T
    lane = lax.broadcasted_iota(jnp.int32, q.shape, 1) // HEAD_DIM
    for h in range(heads):
        at = slice(h * HEAD_DIM, (h + 1) * HEAD_DIM)
        qa = slice(h * shard, (h + 1) * shard)
        qmt[at, qa] = qt[at]
        gmt[at, qa] = gt[at]
        qst[qa] = jnp.where(lane == h, q, jnp.zeros_like(q))
        gst[qa] = jnp.where(lane == h, do, jnp.zeros_like(do))
    prod = do.astype(F32) * o_ref[piece].astype(F32)
    prod_hi = prod.astype(BF16)
    prod_lo = (prod - prod_hi.astype(F32)).astype(BF16)
    pick = (lax.broadcasted_iota(jnp.int32, (8, width), 1) // HEAD_DIM == lax.broadcasted_iota(jnp.int32, (8, width), 0)).astype(BF16)
    delta = dot(pick, prod_hi, 1, 1) + dot(pick, prod_lo, 1, 1)
    lse = lse_ref[piece]
    seg_q = seg_ref[0, pl.ds(piece, 1)].astype(F32)

    def run(count):
        @pl.when(cnt_ref[piece] == count)
        def _():
            places = [idx_ref[piece * pieces + t] for t in range(count)]
            qm, gm = qmt[...], gmt[...]
            later = dot(k_ref[places[0]], qm), dot(v_ref[places[0]], gm)
            out = [None] * heads
            for t in range(count):
                s, dp = later
                j = places[t]
                if t + 1 < count:
                    later = dot(k_ref[places[t + 1]], qm), dot(v_ref[places[t + 1]], gm)
                col = segk[j]
                same = jnp.concatenate([col] * (shard // 128), axis=1) == seg_q
                ps, dss = [], []
                for h in range(heads):
                    at = slice(h * HEAD_DIM, (h + 1) * HEAD_DIM)
                    qa = slice(h * shard, (h + 1) * shard)
                    p = jnp.exp2(jnp.where(same, s[:, qa] - lse[h : h + 1], NEG))
                    ds = (p * (dp[:, qa] - delta[h : h + 1])).astype(BF16)
                    ps.append(p.astype(BF16))
                    dss.append(ds)
                    part = dot(kt[j, at], ds)
                    out[h] = part if t == 0 else out[h] + part
                dv[j] += dot(jnp.concatenate(ps, axis=1), gst[...])
                dk[j] += dot(jnp.concatenate(dss, axis=1), qst[...])
            for h in range(heads):
                dqt[h * HEAD_DIM : (h + 1) * HEAD_DIM] = out[h]

    for count in range(1, pieces + 1):
        run(count)
    dq[piece] = turn(dqt[...].T * HEAD_DIM**-0.5, cos_ref[piece], -sin_ref[piece]).astype(BF16)


def attend_back(row, rows, cnt, idx, qkv, o, do, lse, seg, cos_tab, sin_tab, weight, held=(), deps=()):
    _, pieces, shard, width = qkv.shape
    model = weight.shape[1]
    heads = width // HEAD_DIM
    table = fixed((pieces, shard, 128))
    pairs = (pieces * shard) ** 2
    square, wide = (width, heads * shard), (pieces, shard, width)
    far = [part((1, shard, width), n) for n in range(2)]
    return call(
        attend_back_body, "attend_back", (cnt, idx), (1,),
        [(qkv, fixed(qkv.shape)), (o, fixed(o.shape)), (do[0], fixed((shard, width))), (do[1], fixed((shard, width)))]
        + [(do[2], far[0]), (do[3], fixed((shard, width))), (lse, fixed(lse.shape)), (seg, part((1, pieces, shard), row))]
        + [(cos_tab, table), (sin_tab, table), (weight, fixed(weight.shape))],
        [((rows, pieces, shard, 3 * width), BF16, part((1, pieces, shard, 3 * width), row))]
        + [((shard, model), BF16, fixed((shard, model)))] * pieces,
        [
            pltpu.VMEM((pieces, width, shard), BF16),
            pltpu.VMEM((pieces, shard, 128), F32),
            pltpu.VMEM(wide, F32),
            pltpu.VMEM(wide, F32),
            pltpu.VMEM(wide, BF16),
            pltpu.VMEM((width, shard), F32),
            pltpu.VMEM(square, BF16),
            pltpu.VMEM(square, BF16),
            pltpu.VMEM(square[::-1], BF16),
            pltpu.VMEM(square[::-1], BF16),
            pltpu.VMEM(wide, BF16),
        ],
        held=[(array, 0) for array in held], deps=deps,
        flops=40 * pairs * width, moved=16 * qkv.size, trans=pairs * heads,
    )


def middle_body(
    order_ref, a0, a1, a2, a3, w0, w1, w2, w3, stream_ref, bias_ref, gain_ref, shift_ref, mid_ref, low_ref, all_ref,
):
    shard, model = stream_ref.shape
    total = 0.0
    for n, (a, w) in enumerate(((a0, w0), (a1, w1), (a2, w2), (a3, w3))):
        values = a[...].reshape(shard, a.shape[-1])
        total = total + dot(values, w[...])
        all_ref[0, :, n * a.shape[-1] : (n + 1) * a.shape[-1]] = values
    mid = stream_ref[...] + (total + bias_ref[...])
    hat, _ = centre(mid)
    mid_ref[...] = mid
    low_ref[...] = (hat * gain_ref[...] + shift_ref[...]).astype(BF16)


def out_blocks(weight, parts):
    width = weight.shape[0] // parts

    def block(i):
        return pl.BlockSpec((width, weight.shape[1]), lambda g, o: (o[i], 0))

    return [(weight, block(i)) for i in range(parts)]


def middle_norm(row, rows, order, attended, weight, stream, bias, gain, shift, held=()):
    shard, model = stream.shape
    parts = len(attended)
    width = model // parts
    block, line = fixed((shard, model)), fixed((1, model))
    first = [part((1, shard, width), 0), fixed((shard, width)), part((1, shard, width), 0), fixed((shard, width))]
    return call(
        middle_body, "middle", (order,), (1,),
        list(zip(attended, first)) + out_blocks(weight, parts) + [(stream, block), (bias, line), (gain, line), (shift, line)],
        [
            (stream.shape, F32, block),
            (stream.shape, BF16, block),
            ((rows, shard, model), BF16, part((1, shard, model), row)),
        ],
        held=[(array, 2) for array in held], flops=2 * shard * model * model, moved=14 * stream.size,
    )


def cot_body(blk_ref, a_ref, b_ref, up_ref, down_ref, g_ref, up_out, down_out, both_ref):
    tokens = a_ref.shape[0]
    down = down_ref[...]

    @pl.when(pl.program_id(0) == 0)
    def _():
        both_ref[0:tokens] = a_ref[...]
        both_ref[tokens:] = b_ref[...]

    g_ref[0:tokens] = dot(a_ref[...], down, 1, 1).astype(BF16)
    g_ref[tokens:] = dot(b_ref[...], down, 1, 1).astype(BF16)
    up_out[...] = up_ref[...]
    down_out[...] = down


def cot_down(blk, own, other, up, down, picked, half):
    tokens, model = own.shape
    steps = half // BLOCK
    column = along((2 * tokens, BLOCK), 1)
    if picked:
        up_at, down_at = along((model, BLOCK), 1), along((BLOCK, model))
    else:
        up_at = pl.BlockSpec((model, BLOCK), lambda g, b: (0, b[g]))
        down_at = pl.BlockSpec((BLOCK, model), lambda g, b: (b[g], 0))
    return call(
        cot_body, "cot_down", (blk,), (steps,),
        [(own, fixed(own.shape)), (other, fixed(own.shape)), (up, up_at), (down, down_at)],
        [
            ((2 * tokens, half), BF16, column),
            ((model, half), BF16, along((model, BLOCK), 1)),
            ((half, model), BF16, along((BLOCK, model))),
            ((2 * tokens, model), BF16, fixed((2 * tokens, model))),
        ],
        flops=4 * tokens * model * half, moved=2 * (2 * tokens * (model + half) + 4 * model * half),
    )


def hidden_body(*refs):
    pieces, (g_ref, up_ref, bias_ref, act_ref, grad_ref, sum_ref, both_ref) = refs[:-7], refs[-7:]
    chunk = pieces[0].shape[0]

    @pl.when(pl.program_id(0) == 0)
    def _():
        for n, ref in enumerate(pieces):
            both_ref[n * chunk : (n + 1) * chunk] = ref[...]

    up, bias = up_ref[...], bias_ref[...]
    total = 0.0
    later = dot(pieces[0][...], up)
    for n in range(len(pieces)):
        at = slice(n * chunk, (n + 1) * chunk)
        v = later + bias
        if n + 1 < len(pieces):
            later = dot(pieces[n + 1][...], up)
        square = v * v
        tanh = jnp.tanh(v * (GELU_A + GELU_B * square))
        gate = 0.5 + 0.5 * tanh
        act = v * gate
        slope = gate + act * ((1.0 - tanh) * (GELU_A + 3.0 * GELU_B * square))
        grad = (slope * g_ref[at].astype(F32)).astype(BF16)
        act_ref[at] = act.astype(BF16)
        grad_ref[at] = grad
        total = total + jnp.sum(grad.astype(F32), axis=0, keepdims=True)
    sum_ref[...] = total


def hidden_units(pieces, grads, up, bias):
    chunk, model = pieces[0].shape
    tokens, half = grads.shape
    column, line = along((tokens, BLOCK), 1), along((1, BLOCK), 1)
    return call(
        hidden_body, "hidden", (), (half // BLOCK,),
        [(piece, fixed((chunk, model))) for piece in pieces]
        + [(grads, column), (up, along((model, BLOCK), 1)), (bias, line)],
        [
            (grads.shape, BF16, column),
            (grads.shape, BF16, column),
            ((1, half), F32, line),
            ((tokens, model), BF16, fixed((tokens, model))),
        ],
        flops=2 * tokens * model * half, moved=2 * (tokens * (2 * model + 3 * half) + model * half), trans=tokens * half,
    )


def middle_back_body(
    order_ref, part_ref, sent_ref, mid_ref, cot_ref, gain_ref, w0, w1, w2, w3,
    grad_ref, low_ref, att0_ref, att1_ref, far_ref, sums_ref,
):
    grad = part_ref[...].astype(F32) + sent_ref[...].astype(F32)
    hat, inverse = centre(mid_ref[...])
    cot = cot_ref[0].astype(F32)
    total = cot + norm_back(grad, gain_ref[...], hat, inverse)
    low = total.astype(BF16)
    grad_ref[...] = total
    low_ref[0] = low
    far_ref[0] = dot(low, w2[...], 1, 1).astype(BF16)
    far_ref[1] = dot(low, w3[...], 1, 1).astype(BF16)
    att1_ref[...] = dot(low, w1[...], 1, 1).astype(BF16)
    att0_ref[...] = dot(low, w0[...], 1, 1).astype(BF16)
    sums_ref[0:1] = jnp.sum(grad * hat, axis=0, keepdims=True)
    sums_ref[1:2] = jnp.sum(grad, axis=0, keepdims=True)
    sums_ref[2:3] = jnp.sum(low.astype(F32), axis=0, keepdims=True)
    sums_ref[3:4] = jnp.sum(cot, axis=0, keepdims=True)


def middle_back(row, rows, order, own, sent, mid, cot, gain, weight, parts, held=(), deps=()):
    shard, model = mid.shape
    width = model // parts
    block, place = fixed((shard, model)), part((1, shard, model), row)
    flat = pl.BlockSpec((shard, model), lambda *_: (row, 0))
    return call(
        middle_back_body, "middle_back", (order,), (1,),
        [(own, flat), (sent, flat), (mid, block), (cot, place), (gain, fixed((1, model)))] + out_blocks(weight, parts),
        [
            (mid.shape, F32, block),
            ((rows, shard, model), BF16, place),
            ((shard, width), BF16, fixed((shard, width))),
            ((shard, width), BF16, fixed((shard, width))),
            ((2, shard, width), BF16, fixed((2, shard, width))),
            ((8, model), F32, fixed((8, model))),
        ],
        held=[(array, 1) for array in held], deps=deps, flops=2 * shard * model * model, moved=18 * mid.size,
    )


def norm1_back_body(part_ref, near_ref, far_ref, stream_ref, mid_ref, gain_ref, seg_ref, in_ref, shift_ref, sums_ref):
    grad = part_ref[...].astype(F32) + near_ref[...].astype(F32) + far_ref[...].astype(F32)
    hat, inverse = centre(stream_ref[...])
    total = mid_ref[...] + norm_back(grad, gain_ref[...], hat, inverse)
    in_ref[0] = total.astype(BF16)
    slots = lax.broadcasted_iota(jnp.int32, (SEGS, seg_ref.shape[-1]), 0) == seg_ref[0]
    onehot = slots.astype(F32).astype(BF16)
    shift_ref[...] = dot(jnp.concatenate([onehot, onehot], axis=1), split_low(total))
    sums_ref[0:1] = jnp.sum(grad * hat, axis=0, keepdims=True)
    sums_ref[1:2] = jnp.sum(grad, axis=0, keepdims=True)


def norm1_back(row, rows, own, near, far, stream, mid, gain, seg, held=(), deps=()):
    shard, model = stream.shape
    block = fixed((shard, model))
    return call(
        norm1_back_body, "norm1_back", (), (1,),
        [(own, block), (near, block), (far, block), (stream, block), (mid, block), (gain, fixed((1, model)))]
        + [(seg, part((1, 1, shard), row))],
        [
            ((rows, shard, model), BF16, part((1, shard, model), row)),
            ((SEGS, model), F32, fixed((SEGS, model))),
            ((8, model), F32, fixed((8, model))),
        ],
        held=[(array, 0) for array in held], deps=deps, moved=16 * stream.size,
    )


def exchange(own, one, far):
    far = swap(far, "y")
    return [own, swap(one, "c"), far, swap(far[1], "c")]


def after(value, *others):
    return lax.optimization_barrier((value,) + others)[0]


def cut(values, index, size, axis):
    return lax.dynamic_slice_in_dim(values, index * size, size, axis)


def add_low(kept, sent):
    return (kept.astype(F32) + sent.astype(F32)).astype(BF16)


def ordered(at, own, other, axis):
    return jnp.where(at == 0, jnp.concatenate([own, other], axis), jnp.concatenate([other, own], axis))


def local(
    inputs, segment_ids, doc_times, time_weight, time_bias, norm1_gain, norm1_bias, qkv_weight, qkv_bias,
    out_weight, out_bias, norm2_gain, norm2_bias, up_weight, up_bias, down_weight, down_bias, cotangent,
    *, dp,
):
    rows, shard, model = inputs.shape
    parts = 4
    tokens = rows * shard
    hidden_width = up_weight.shape[1]
    width = model // parts
    depth = dp // 2
    half = hidden_width // 2
    piece = half // dp
    z_at, x_at, y_at, c_at = (lax.axis_index(name) for name in ("z", "x", "y", "c"))
    me = 2 * y_at + c_at
    order = [me ^ i for i in range(parts)]
    order_list = jnp.stack(order).astype(jnp.int32)
    me_list = order_list[:1]

    def line(vector):
        return vector.astype(F32)[None]

    seg = segment_ids[:, None, :]
    features = time_features(doc_times.reshape(rows * SEGS), jnp.arange(TEMB), TEMB // 2)
    time_shift = dot(features, time_weight).reshape(rows, SEGS, model) + time_bias.astype(F32)
    stream, own1, one1, two1 = [], [], [], []
    for r in range(rows):
        values, low = norm1(r, inputs, seg, time_shift, line(norm1_gain), line(norm1_bias))
        stream.append(values)
        own1.append(low)
        two1.append(swap(low, "y"))
        one1.append(swap(low, "c"))

    seg_two = swap(segment_ids, "y")
    segs = jnp.stack([segment_ids, swap(segment_ids, "c"), seg_two, swap(seg_two, "c")], axis=1)
    low_id, high_id = segs.min(axis=2), segs.max(axis=2)
    act = (low_id[:, :, None] <= high_id[:, None, :]) & (low_id[:, None, :] <= high_id[:, :, None])
    places = jnp.arange(parts, dtype=jnp.int32)
    rank = jnp.cumsum(act.astype(jnp.int32), axis=2) - 1
    chosen = act[..., None] & (rank[..., None] == places)
    idx = jnp.sum(jnp.where(chosen, places[:, None], 0), axis=2).astype(jnp.int32).reshape(rows, -1)
    cnt = jnp.sum(act.astype(jnp.int32), axis=2)
    positions = jnp.stack([o * shard + jnp.arange(shard, dtype=jnp.int32) for o in order])
    cos_tab, sin_tab = rotary_tables(positions, HEAD_DIM)

    cot = cotangent.reshape(tokens, model)
    cot_other = swap(cot, "c")
    turned = jnp.stack([1 - x_at, x_at])
    if piece % BLOCK == 0:
        blk = ((jnp.arange(depth)[None, :] * 2 + turned[:, None]) * 2 + c_at) * (piece // BLOCK)
        blk = (blk[..., None] + jnp.arange(piece // BLOCK)).reshape(-1).astype(jnp.int32)
        up_from, down_from = up_weight, down_weight
    else:
        blk = jnp.zeros((half // BLOCK,), jnp.int32)
        up_from = up_weight.reshape(model, depth, 2, 2, piece)
        up_from = lax.dynamic_index_in_dim(up_from, c_at, 3, keepdims=False)
        up_from = jnp.where(x_at == 1, up_from, up_from[:, :, ::-1]).transpose(0, 2, 1, 3).reshape(model, half)
        down_from = down_weight.reshape(depth, 2, 2, piece, model)
        down_from = lax.dynamic_index_in_dim(down_from, c_at, 2, keepdims=False)
        down_from = jnp.where(x_at == 1, down_from, down_from[:, ::-1]).transpose(1, 0, 2, 3).reshape(half, model)
    grad_act, up_own, down_own, cot_both = cot_down(
        blk, cot, cot_other, up_from, down_from, piece % BLOCK != 0, half
    )
    up_bias_own = lax.dynamic_index_in_dim(up_bias.reshape(depth, 2, 2, piece), c_at, 2, keepdims=False)
    up_bias_own = jnp.where(x_at == 1, up_bias_own, up_bias_own[:, ::-1]).transpose(1, 0, 2).reshape(half)

    bias_line = qkv_bias.reshape(1, 3 * model)
    qkv, o, lse, attended, middle, normed2, normed2_other = [], [], [], [], [], [], []
    normed1_all, attended_all = (), ()
    for r in range(rows):
        deps = (grad_act,) if r == 0 else ()
        taken = (own1[r], one1[r], two1[r], swap(two1[r], "c"))
        found, normed1_all, qkv_own = project_qkv(
            r, rows, me_list, taken, qkv_weight, bias_line, cos_tab, sin_tab, normed1_all, deps
        )
        normed1_all = (normed1_all,)
        qkv.append(found)
        out, out_one, out_far, scale = attend(r, cnt[r], idx[r], found, segs)
        o.append(out)
        lse.append(scale)
        attended.append(exchange(out, out_one, out_far))
    for r in range(rows):
        values, low, attended_all = middle_norm(
            r, rows, order_list, attended[r], out_weight, stream[r], line(out_bias), line(norm2_gain), line(norm2_bias),
            attended_all,
        )
        attended_all = (attended_all,)
        middle.append(values)
        normed2.append(low)
        normed2_other.append(swap(low, "c"))

    active, grad_hidden, up_b, normed2_both = hidden_units(
        normed2 + normed2_other, grad_act, up_own, line(up_bias_own)
    )
    down_out = dot(active[:, : half // 2], cot_both, 0, 0).astype(BF16)
    down_sent = swap(down_out, "x")
    up_grad = dot(normed2_both, grad_hidden, 0, 0).astype(BF16)
    up_z = lax.psum_scatter(up_grad, "z", scatter_dimension=0, tiled=True)
    grad_hidden = after(grad_hidden, down_out, up_grad)
    part2_sent = swap(dot(grad_hidden[tokens:], up_own, 1, 1).astype(BF16), "c")
    part2 = dot(grad_hidden[:tokens], up_own, 1, 1).astype(BF16)
    grad_middle, grad_o, sums2 = [], [], 0.0
    grad_middle_low = ()
    for r in range(rows):
        values, grad_middle_low, att0, att1, far, found = middle_back(
            r, rows, order_list, part2, part2_sent, middle[r], cotangent, line(norm2_gain), out_weight, parts,
            grad_middle_low,
        )
        grad_middle_low = (grad_middle_low,)
        grad_middle.append(values)
        grad_o.append(exchange(att0, att1, far))
        sums2 = sums2 + found[:4]
    (grad_middle_low,) = grad_middle_low

    active_late = after(active, grad_middle_low)
    down_kept = dot(active_late[:, half // 2 :], cot_both, 0, 0).astype(BF16)
    feed_sent = swap(dot(active_late[tokens:], down_own).astype(BF16), "c")
    feed = dot(active_late[:tokens], down_own) + feed_sent.astype(F32) + line(down_bias)
    output = (jnp.stack(middle) + feed.reshape(rows, shard, model)).astype(BF16)
    out_grad = dot(
        attended_all[0].reshape(tokens, model), grad_middle_low.reshape(tokens, model), 0, 0
    ).astype(BF16)

    grad_qkv, back = (), []
    for r in range(rows):
        deps = (down_kept, output, out_grad) if r == 0 else ()
        grad_qkv, own, one, two, three = attend_back(
            r, rows, cnt[r], idx[r], qkv[r], o[r], grad_o[r], lse[r], segs, cos_tab, sin_tab, qkv_own, grad_qkv, deps
        )
        grad_qkv = (grad_qkv,)
        back.append((own, swap(one, "c"), swap(add_low(two, swap(three, "c")), "y")))
    grad_qkv = grad_qkv[0].reshape(parts * tokens, 3 * width)
    qkv_grad = dot(normed1_all[0].reshape(parts * tokens, model), grad_qkv, 0, 0).astype(BF16)
    qkv_b = jnp.sum(grad_qkv.astype(F32), axis=0)
    input_grad, grad_shift, sums1 = (), [], 0.0
    for r in range(rows):
        input_grad, found, sums = norm1_back(
            r, rows, *back[r], stream[r], grad_middle[r], line(norm1_gain), seg, input_grad
        )
        input_grad = (input_grad,)
        grad_shift.append(found)
        sums1 = sums1 + sums[:2]
    (input_grad,) = input_grad

    down_x = add_low(down_kept, down_sent)
    down_y = add_low(cut(down_x, y_at, model // 2, 1), swap(cut(down_x, 1 - y_at, model // 2, 1), "y"))
    down_z = lax.psum_scatter(down_y, "z", scatter_dimension=0, tiled=True)
    up_rows = model // dp
    up_sent = swap(cut(up_z, 1 - x_at, up_rows, 0), "x")
    up_sent = jnp.concatenate([up_sent[:, half // 2 :], up_sent[:, : half // 2]], axis=1)
    up_x = add_low(cut(up_z, x_at, up_rows, 0), up_sent)
    up_y = add_low(cut(up_x, y_at, half // 2, 1), swap(cut(up_x, 1 - y_at, half // 2, 1), "y"))
    out_grad = jnp.concatenate([cut(out_grad, o_at, width, 0) for o_at in order], axis=0)
    out_c = add_low(cut(out_grad, c_at, model // 2, 1), swap(cut(out_grad, 1 - c_at, model // 2, 1), "c"))
    out_y = add_low(cut(out_c, y_at, width, 1), swap(cut(out_c, 1 - y_at, width, 1), "y"))
    late = jnp.concatenate([qkv_grad, out_y], axis=1).reshape(depth, 2 * up_rows, model)
    late_x = add_low(cut(late, x_at, up_rows, 1), swap(cut(late, 1 - x_at, up_rows, 1), "x"))
    late_z = lax.psum_scatter(late_x, "z", scatter_dimension=0, tiled=False)

    down_done = ordered(y_at, down_z, swap(down_z, "y"), 1)
    down_done = ordered(c_at, down_done, swap(down_done, "c"), 0).astype(F32)
    up_done = ordered(y_at, up_y, swap(up_y, "y"), 1)
    up_done = ordered(c_at, up_done[None], swap(up_done, "c")[None], 0).reshape(2, up_rows, 2, depth, piece)
    up_done = jnp.where(x_at == 1, up_done, up_done[:, :, ::-1]).transpose(1, 3, 2, 0, 4)
    up_done = up_done.reshape(up_rows, hidden_width).astype(F32)
    late_done = ordered(c_at, late_z[None], swap(late_z, "c")[None], 0)
    late_done = ordered(y_at, late_done[None], swap(late_done, "y")[None], 0).reshape(parts, up_rows, model)
    qkv_done = late_done[:, :, : 3 * width].reshape(parts, up_rows, 3, width).transpose(1, 2, 0, 3)
    qkv_done = qkv_done.reshape(up_rows, 3 * model).astype(F32)
    out_done = late_done[:, :, 3 * width :].reshape(2, 2, up_rows, width).transpose(2, 1, 0, 3)
    out_done = out_done.reshape(up_rows, model).astype(F32)

    up_b = up_b.reshape(2, depth, 1, piece)
    up_b = jnp.where(x_at == 1, up_b, up_b[::-1]).transpose(1, 0, 2, 3)
    up_b = jnp.where(jnp.arange(2)[:, None] == c_at, up_b, 0.0).reshape(-1, model)
    qkv_b = jnp.where(jnp.arange(parts)[:, None] == me, qkv_b.reshape(3, 1, width), 0.0).reshape(3, model)
    times = doc_times.reshape(1, rows * SEGS)
    times = jnp.concatenate([times // 32, times % 32], axis=1).astype(F32)
    times = jnp.pad(times, ((0, 0), (0, model - times.shape[1])))
    small = jnp.concatenate(grad_shift + [sums1, sums2, qkv_b, up_b, times], axis=0)
    small = add_low(small, swap(small.astype(BF16), "c"))
    small = add_low(small, swap(small, "y"))
    small = ordered(x_at, small[None], swap(small, "x")[None], 0)
    if depth == 4:
        others = [lax.ppermute(small, "z", [(i, i ^ n) for i in range(depth)]) for n in range(1, depth)]
        small = jnp.stack([small] + others)
        small = jnp.stack([lax.dynamic_index_in_dim(small, z_at ^ n, 0, keepdims=False) for n in range(depth)])
    else:
        small = lax.all_gather(small, "z")
    small = small.reshape(dp, small.shape[2], model)
    all_times = small[:, -1, : 2 * rows * SEGS].astype(F32) * 0.25
    all_times = all_times[:, : rows * SEGS] * 32.0 + all_times[:, rows * SEGS :]
    shifts = small[:, : rows * SEGS].reshape(dp * rows * SEGS, model)
    columns = (2 * z_at + x_at) * (TEMB // dp) + jnp.arange(TEMB // dp)
    wanted = time_features(all_times.reshape(-1), columns, TEMB // 2)
    time_w_done = dot(wanted, shifts, 0, 0)
    sums = jnp.sum(small[:, rows * SEGS :].astype(F32), axis=0)
    dp_at = 2 * z_at + x_at

    def share(vector):
        return cut(vector.reshape(-1), dp_at, vector.size // dp, 0)

    time_b_done = jnp.sum(cut(shifts, dp_at, up_rows, 1).astype(F32), axis=0)
    return (
        output, input_grad, time_w_done, time_b_done, share(sums[0]), share(sums[1]), qkv_done, share(sums[6:9]),
        out_done, share(sums[4]), share(sums[2]), share(sums[3]), up_done, share(sums[9:-1]), down_done, share(sums[5]),
    )


def solution(mesh):
    dp, seq = mesh.shape["dp"], mesh.shape["seq"]
    fine = Mesh(mesh.devices.reshape(dp // 2, 2, seq // 2, 2), ("z", "x", "y", "c"))
    rows, seqs = ("z", "x"), ("y", "c")
    placed = (P(rows, seqs, None), P(rows, seqs), P(rows, None)) + (P(),) * 14 + (P(rows, seqs, None),)
    vec, mat = P(rows), P(rows, None)
    return jax.shard_map(
        functools.partial(local, dp=dp),
        mesh=fine,
        in_specs=placed,
        out_specs=(
            P(rows, seqs, None), P(rows, seqs, None), mat, vec, vec, vec, mat, vec, mat, vec, vec, vec, mat, vec, mat, vec,
        ),
        check_vma=False,
    )
```

```python
import functools
import math

import jax
import jax.numpy as jnp
from jax import lax
from jax.experimental import pallas as pl
from jax.experimental.pallas import tpu as pltpu
from jax.sharding import Mesh, PartitionSpec as P

HEADS = 16
HEAD_DIM = 64
TEMB = 256
SEGS = 8
EPSILON = 1e-05
F32 = jnp.float32
BF16 = jnp.bfloat16
NEG = -1e30
LOG2E = math.log2(math.e)
GELU_A = math.sqrt(2.0 / math.pi)
GELU_B = GELU_A * 0.044715
BLOCK = 256
VMEM = 60 * 1024 * 1024


def swap(value, axis):
    return lax.ppermute(value, axis, [(0, 1), (1, 0)])


def time_features(doc_times, column, half_size):
    frequency = jnp.exp(-math.log(10000.0) * (column % half_size).astype(F32) / half_size)
    angles = doc_times.astype(F32)[..., None] * frequency
    return jnp.where(column < half_size, jnp.sin(angles), jnp.cos(angles)).astype(BF16)


def rotary_tables(positions, head_size):
    half_size = head_size // 2
    frequency = jnp.exp(-math.log(10000.0) * 2.0 * jnp.arange(half_size, dtype=F32) / head_size)
    angles = positions.astype(F32)[..., None] * frequency
    cos_tab, sin_tab = jnp.cos(angles), jnp.sin(angles)
    return (
        jnp.concatenate([cos_tab] * 4, axis=-1),
        jnp.concatenate([-sin_tab, sin_tab, -sin_tab, sin_tab], axis=-1),
    )


def dot(left_op, right_op, left_dim=1, right_dim=0):
    return lax.dot_general(
        left_op, right_op, (((left_dim,), (right_dim,)), ((), ())), preferred_element_type=F32
    )


def turn(values, cos_tab, sin_tab):
    slabs = []
    lane = lax.broadcasted_iota(jnp.int32, (values.shape[0], 128), 1)
    first = lane % HEAD_DIM < HEAD_DIM // 2
    for start in range(0, values.shape[1], 128):
        slab = values[:, start : start + 128]
        partner = jnp.where(
            first, pltpu.roll(slab, 128 - HEAD_DIM // 2, 1), pltpu.roll(slab, HEAD_DIM // 2, 1)
        )
        slabs.append(slab * cos_tab + partner * sin_tab)
    return jnp.concatenate(slabs, axis=1)


def split_low(values):
    high = values.astype(BF16)
    return jnp.concatenate([high, (values - high.astype(F32)).astype(BF16)], axis=0)


def centre(values):
    scale = 1.0 / values.shape[-1]
    centred = values - jnp.sum(values, axis=-1, keepdims=True) * scale
    spread = jnp.sum(centred * centred, axis=-1, keepdims=True) * scale
    inverse = lax.rsqrt(spread + EPSILON)
    return centred * inverse, inverse


def norm_back(grad, gain, hat, inverse):
    scale = 1.0 / grad.shape[-1]
    scaled = grad * gain
    mean = jnp.sum(scaled, axis=-1, keepdims=True) * scale
    along = jnp.sum(scaled * hat, axis=-1, keepdims=True) * scale
    return inverse * (scaled - mean - hat * along)


def call(body, name, prefetch, grid, ins, outs, scratch=(), deps=(), held=(), flops=0, moved=0, trans=0):
    count = len(prefetch) + len(ins)
    extra = [array for array, _ in held] + list(deps)

    def kernel(*refs):
        body(*refs[:count], *refs[count + len(extra) :])

    return pl.pallas_call(
        kernel,
        grid_spec=pltpu.PrefetchScalarGridSpec(
            num_scalar_prefetch=len(prefetch),
            grid=grid,
            in_specs=[spec for _, spec in ins] + [pl.BlockSpec(memory_space=pl.ANY)] * len(extra),
            out_specs=[spec for _, _, spec in outs],
            scratch_shapes=list(scratch),
        ),
        out_shape=[jax.ShapeDtypeStruct(shape, kind) for shape, kind, _ in outs],
        input_output_aliases={count + n: out for n, (_, out) in enumerate(held)},
        compiler_params=pltpu.CompilerParams(vmem_limit_bytes=VMEM),
        cost_estimate=pl.CostEstimate(flops=flops, bytes_accessed=moved, transcendentals=trans),
        name=name,
    )(*prefetch, *[array for array, _ in ins], *extra)


def fixed(shape):
    return pl.BlockSpec(shape, lambda *_: (0,) * len(shape))


def along(shape, axis=0, start=0):
    return pl.BlockSpec(shape, lambda g, *_: tuple(start + g if n == axis else 0 for n in range(len(shape))))


def norm1_body(x_ref, seg_ref, shift_ref, gain_ref, bias_ref, stream_ref, low_ref):
    slots = lax.broadcasted_iota(jnp.int32, (SEGS, seg_ref.shape[-1]), 0) == seg_ref[0]
    onehot = slots.astype(F32).astype(BF16)
    added = dot(jnp.concatenate([onehot, onehot], axis=0), split_low(shift_ref[0]), 0, 0)
    stream = x_ref[0].astype(F32) + added
    hat, _ = centre(stream)
    stream_ref[0] = stream
    low_ref[0] = (hat * gain_ref[...] + bias_ref[...]).astype(BF16)


def norm1(x, seg, shift, gain, bias):
    rows, shard, model = x.shape
    block = along((1, shard, model))
    return call(
        norm1_body, "norm1", (), (rows,),
        [(x, block), (seg, along((1, 1, shard))), (shift, along((1, SEGS, model))), (gain, fixed((1, model))), (bias, fixed((1, model)))],
        [(x.shape, F32, block), (x.shape, BF16, block)],
        moved=8 * x.size,
    )


def qkv_body(me_ref, a_ref, b_ref, w_ref, bias_ref, cos_ref, sin_ref, out_ref, all_ref, own_ref):
    rows, shard, model = a_ref.shape
    width = w_ref.shape[1]
    refs = (a_ref, b_ref)
    step = pl.program_id(0)

    @pl.when(step == 0)
    def _():
        for n, x_ref in enumerate(refs):
            all_ref[n] = x_ref[...]

    def run(turned):
        w, bias = w_ref[...], bias_ref[...].astype(F32)
        found = [dot(x_ref[...].reshape(rows * shard, model), w) for x_ref in refs]
        for n, full in enumerate(found):
            for r in range(rows):
                values = full[r * shard : (r + 1) * shard] + bias
                if turned:
                    values = turn(values, cos_ref[n], sin_ref[n]) * jnp.where(step == 0, LOG2E * HEAD_DIM**-0.5, 1.0)
                out_ref[0, n, r] = values.astype(BF16)

    own_ref[...] = w_ref[...].T

    @pl.when(step < 2)
    def _():
        run(True)

    @pl.when(step == 2)
    def _():
        run(False)


def project_qkv(pair, parts, me, first, second, weight, bias, cos_tab, sin_tab, held=(), deps=()):
    rows, shard, model = first.shape
    width = model // parts
    return call(
        qkv_body, "qkv", (me,), (3,),
        [(first, fixed(first.shape)), (second, fixed(first.shape))]
        + [
            (weight, pl.BlockSpec((model, width), lambda g, m: (0, g * parts + m[0]))),
            (bias, pl.BlockSpec((1, width), lambda g, m: (0, g * parts + m[0]))),
            (cos_tab, pl.BlockSpec((2, shard, 128), lambda g, m: (pair, 0, 0))),
            (sin_tab, pl.BlockSpec((2, shard, 128), lambda g, m: (pair, 0, 0))),
        ],
        [
            ((3, parts, rows, shard, width), BF16, pl.BlockSpec((1, 2, rows, shard, width), lambda g, m: (g, pair, 0, 0, 0))),
            ((parts, rows, shard, model), BF16, pl.BlockSpec((2, rows, shard, model), lambda g, m: (pair, 0, 0, 0))),
            ((3 * width, model), BF16, along((width, model))),
        ],
        held=[(array, n) for n, array in enumerate(held)], deps=deps,
        flops=12 * rows * shard * model * width, moved=2 * (3 * model * width + 4 * rows * shard * model),
    )


def seg_columns(segq_all, segk):
    pieces, shard, _ = segk.shape
    for j in range(pieces):
        row = jnp.broadcast_to(segq_all[j:j+1].astype(F32), (128, shard))
        segk[j] = row.T

def attend_body(start, cnt_ref, idx_ref, qkv_ref, seg_ref, o_ref, one_ref, far_ref, lse_ref, vt, segk, qmt, acc):
    row = pl.program_id(0) + start
    _, pieces, _, shard, width = qkv_ref.shape
    heads = width // HEAD_DIM

    @pl.when(pl.program_id(0) == 0)
    def _():
        qmt[...] = jnp.zeros_like(qmt)

    for j in range(pieces):
        vt[j] = qkv_ref[2, j, 0].T
        qt = qkv_ref[0, j, 0].T
        for h in range(heads):
            at = slice(h * HEAD_DIM, (h + 1) * HEAD_DIM)
            qmt[j, at, h * shard : (h + 1) * shard] = qt[at]
    seg_columns(seg_ref[0], segk)

    @pl.loop(0, pieces)
    def _(piece):
        attend_piece(row * pieces + piece, piece, cnt_ref, idx_ref, qkv_ref.at[1], seg_ref, lse_ref, vt, segk, qmt, acc)

    for j in range(pieces):
        o_ref[j, 0] = acc[j].T.astype(BF16)
    one_ref[0] = o_ref[1, 0]
    far_ref[:, 0] = o_ref[2:, 0]


def attend_piece(at_q, piece, cnt_ref, idx_ref, k_ref, seg_ref, lse_ref, vt, segk, qmt, acc):
    pieces, _, shard, width = k_ref.shape
    heads = width // HEAD_DIM
    seg_q = seg_ref[0, pl.ds(piece, 1)].astype(F32)

    def run(count):
        @pl.when(cnt_ref[at_q] == count)
        def _():
            qm = qmt[piece]
            places = [idx_ref[at_q * pieces + t] for t in range(count)]
            top, tot, out = [None] * heads, [None] * heads, [None] * heads
            later = dot(k_ref[places[0], 0], qm)
            for t in range(count):
                s = later
                if t + 1 < count:
                    later = dot(k_ref[places[t + 1], 0], qm)
                col = segk[places[t]]
                same = jnp.concatenate([col] * (shard // 128), axis=1) == seg_q
                for h in range(heads):
                    at = slice(h * HEAD_DIM, (h + 1) * HEAD_DIM)
                    sh = jnp.where(same, s[:, h * shard : (h + 1) * shard], NEG)
                    best = jnp.max(sh, axis=0, keepdims=True)
                    if t:
                        best = jnp.maximum(top[h], best)
                        fade = jnp.exp2(top[h] - best)
                    p = jnp.exp2(sh - best)
                    total = jnp.sum(p, axis=0, keepdims=True)
                    found = dot(vt[places[t], at], p.astype(BF16))
                    if t:
                        total = tot[h] * fade + total
                        found = out[h] * fade + found
                    top[h], tot[h], out[h] = best, total, found
            for h in range(heads):
                acc[piece, h * HEAD_DIM : (h + 1) * HEAD_DIM] = out[h] / tot[h]
                lse_ref[0, piece, h : h + 1] = top[h] + jnp.log2(tot[h])

    for count in range(1, pieces + 1):
        run(count)


def attend(start, count, cnt, idx, qkv, seg, held=()):
    _, pieces, rows, shard, width = qkv.shape
    heads = width // HEAD_DIM
    pairs = count * (pieces * shard) ** 2
    return call(
        functools.partial(attend_body, start), "attend", (cnt, idx), (count,),
        [(qkv, along((3, pieces, 1, shard, width), 2, start)), (seg, along((1, pieces, shard), 0, start))],
        [
            ((pieces, rows, shard, width), BF16, along((pieces, 1, shard, width), 1, start)),
            ((count, shard, width), BF16, along((1, shard, width))),
            ((2, count, shard, width), BF16, along((2, 1, shard, width), 1)),
            ((rows, pieces, 8, shard), F32, along((1, pieces, 8, shard), 0, start)),
        ],
        [
            pltpu.VMEM((pieces, width, shard), BF16),
            pltpu.VMEM((pieces, shard, 128), F32),
            pltpu.VMEM((pieces, width, heads * shard), BF16),
            pltpu.VMEM((pieces, width, shard), F32),
        ],
        held=list(zip(held, (0, 3))), flops=16 * pairs * width, moved=8 * count * pieces * shard * width, trans=pairs * heads,
    )


def attend_back_body(
    start, cnt_ref, idx_ref, qkv_ref, o_ref, do0, do1, do2, do3, lse_ref, seg_ref, cos_ref, sin_ref, w_ref,
    g_ref, p0_ref, p1_ref, p2_ref, p3_ref, kt, segk, dk, dv, dqt, qmt, gmt, qst, gst, low,
):
    row = pl.program_id(0) + start
    _, pieces, _, shard, width = qkv_ref.shape
    heads = width // HEAD_DIM

    @pl.when(pl.program_id(0) == 0)
    def _():
        qmt[...] = jnp.zeros_like(qmt)
        gmt[...] = jnp.zeros_like(gmt)

    seg_columns(seg_ref[0], segk)
    dk[...] = jnp.zeros_like(dk)
    dv[...] = jnp.zeros_like(dv)
    lane = lax.broadcasted_iota(jnp.int32, (shard, width), 1) // HEAD_DIM
    chosen = lax.broadcasted_iota(jnp.int32, (8, width), 1) // HEAD_DIM
    chosen = (chosen == lax.broadcasted_iota(jnp.int32, (8, width), 0)).astype(BF16)
    for j, do_ref in enumerate((do0, do1, do2, do3)):
        kt[j] = qkv_ref[1, j, 0].T
        q, do = qkv_ref[0, j, 0], do_ref[...].reshape(shard, width)
        qt, gt = q.T, do.T
        for h in range(heads):
            at, qa = slice(h * HEAD_DIM, (h + 1) * HEAD_DIM), slice(h * shard, (h + 1) * shard)
            qmt[j, at, qa] = qt[at]
            gmt[j, at, qa] = gt[at]
            qst[j, qa] = jnp.where(lane == h, q, jnp.zeros_like(q))
            gst[j, qa] = jnp.where(lane == h, do, jnp.zeros_like(do))
        prod = do.astype(F32) * o_ref[j, 0].astype(F32)
        high = prod.astype(BF16)
        low[j] = dot(chosen, high, 1, 1) + dot(chosen, (prod - high.astype(F32)).astype(BF16), 1, 1)

    @pl.loop(0, pieces)
    def _(piece):
        back_piece(
            row * pieces + piece, piece, cnt_ref, idx_ref, qkv_ref.at[1], qkv_ref.at[2], lse_ref, seg_ref,
            kt, segk, dk, dv, dqt, qmt, gmt, qst, gst, low,
        )

    for j, ref in ((1, p1_ref), (3, p3_ref), (0, p0_ref), (2, p2_ref)):
        grad_q = turn(dqt[j].T * HEAD_DIM**-0.5, cos_ref[j], -sin_ref[j]).astype(BF16)
        grad_k = turn(dk[j] * (1 / LOG2E), cos_ref[j], -sin_ref[j]).astype(BF16)
        grad = jnp.concatenate([grad_q, grad_k, dv[j].astype(BF16)], axis=1)
        g_ref[j, 0] = grad
        ref[0] = dot(grad, w_ref[...]).astype(BF16)


def back_piece(
    at_q, piece, cnt_ref, idx_ref, k_ref, v_ref, lse_ref, seg_ref, kt, segk, dk, dv, dqt, qmt, gmt, qst, gst, low
):
    pieces, _, shard, width = k_ref.shape
    heads = width // HEAD_DIM
    lse, delta = lse_ref[0, piece], low[piece]
    seg_q = seg_ref[0, pl.ds(piece, 1)].astype(F32)

    def run(count):
        @pl.when(cnt_ref[at_q] == count)
        def _():
            places = [idx_ref[at_q * pieces + t] for t in range(count)]
            qm, gm = qmt[piece], gmt[piece]
            later = dot(k_ref[places[0], 0], qm), dot(v_ref[places[0], 0], gm)
            out = [None] * heads
            for t in range(count):
                s, dp = later
                j = places[t]
                if t + 1 < count:
                    later = dot(k_ref[places[t + 1], 0], qm), dot(v_ref[places[t + 1], 0], gm)
                col = segk[j]
                same = jnp.concatenate([col] * (shard // 128), axis=1) == seg_q
                ps, dss = [], []
                for h in range(heads):
                    at, qa = slice(h * HEAD_DIM, (h + 1) * HEAD_DIM), slice(h * shard, (h + 1) * shard)
                    p = jnp.exp2(jnp.where(same, s[:, qa] - lse[h : h + 1], NEG))
                    ds = (p * (dp[:, qa] - delta[h : h + 1])).astype(BF16)
                    ps.append(p.astype(BF16))
                    dss.append(ds)
                    found = dot(kt[j, at], ds)
                    out[h] = found if t == 0 else out[h] + found
                dv[j] += dot(jnp.concatenate(ps, axis=1), gst[piece])
                dk[j] += dot(jnp.concatenate(dss, axis=1), qst[piece])
            for h in range(heads):
                dqt[piece, h * HEAD_DIM : (h + 1) * HEAD_DIM] = out[h]

    for count in range(1, pieces + 1):
        run(count)


def attend_back(start, count, cnt, idx, qkv, o, do, lse, seg, cos_tab, sin_tab, weight, held=(), deps=()):
    _, pieces, rows, shard, width = qkv.shape
    model = weight.shape[1]
    heads = width // HEAD_DIM
    table = fixed((pieces, shard, 128))
    pairs = count * (pieces * shard) ** 2
    square, wide = (pieces, width, heads * shard), (pieces, shard, width)
    one = along((1, shard, width), 0, start)
    return call(
        functools.partial(attend_back_body, start), "attend_back", (cnt, idx), (count,),
        [(qkv, along((3, pieces, 1, shard, width), 2, start)), (o, along((pieces, 1, shard, width), 1, start))]
        + [(do[0], one), (do[1], one), (do[2], along((1, 1, shard, width), 1, start)), (do[3], one)]
        + [(lse, along((1, pieces, 8, shard), 0, start)), (seg, along((1, pieces, shard), 0, start))]
        + [(cos_tab, table), (sin_tab, table), (weight, fixed(weight.shape))],
        [((pieces, rows, shard, 3 * width), BF16, along((pieces, 1, shard, 3 * width), 1, start))]
        + [((count, shard, model), BF16, along((1, shard, model)))] * pieces,
        [
            pltpu.VMEM((pieces, width, shard), BF16),
            pltpu.VMEM((pieces, shard, 128), F32),
            pltpu.VMEM(wide, F32),
            pltpu.VMEM(wide, F32),
            pltpu.VMEM((pieces, width, shard), F32),
            pltpu.VMEM(square, BF16),
            pltpu.VMEM(square, BF16),
            pltpu.VMEM((pieces, heads * shard, width), BF16),
            pltpu.VMEM((pieces, heads * shard, width), BF16),
            pltpu.VMEM((pieces, 8, shard), F32),
        ],
        held=[(array, 0) for array in held], deps=deps,
        flops=40 * pairs * width, moved=16 * count * pieces * shard * width, trans=pairs * heads,
    )


def middle_body(
    order_ref, a0, a1, a2, a3, w0, w1, w2, w3, stream_ref, bias_ref, gain_ref, shift_ref, mid_ref, low_ref, all_ref,
):
    _, shard, model = stream_ref.shape
    total = 0.0
    for n, (a, w) in enumerate(((a0, w0), (a1, w1), (a2, w2), (a3, w3))):
        values = a[...].reshape(shard, a.shape[-1])
        total = total + dot(values, w[...])
        all_ref[0, :, n * a.shape[-1] : (n + 1) * a.shape[-1]] = values
    mid = stream_ref[0] + (total + bias_ref[...])
    hat, _ = centre(mid)
    mid_ref[0] = mid
    low_ref[0] = (hat * gain_ref[...] + shift_ref[...]).astype(BF16)


def out_blocks(weight, parts):
    width = weight.shape[0] // parts

    def block(i):
        return pl.BlockSpec((width, weight.shape[1]), lambda g, o: (o[i], 0))

    return [(weight, block(i)) for i in range(parts)]


def middle_norm(start, count, order, attended, weight, stream, bias, gain, shift, held=()):
    rows, shard, model = stream.shape
    parts = len(attended)
    width = model // parts
    block, line, one = along((1, shard, model), 0, start), fixed((1, model)), along((1, shard, width))
    first = [along((1, 1, shard, width), 1, start), one, along((1, 1, shard, width), 1), one]
    return call(
        middle_body, "middle", (order,), (count,),
        list(zip(attended, first)) + out_blocks(weight, parts) + [(stream, block), (bias, line), (gain, line), (shift, line)],
        [
            (stream.shape, F32, block),
            ((count, shard, model), BF16, along((1, shard, model))),
            (stream.shape, BF16, block),
        ],
        held=list(zip(held, (0, 2))), flops=2 * count * shard * model * model, moved=14 * count * shard * model,
    )


def cot_body(blk_ref, a_ref, b_ref, up_ref, down_ref, g_ref, up_out, down_out, both_ref):
    tokens = a_ref.shape[0]
    down = down_ref[...]

    @pl.when(pl.program_id(0) == 0)
    def _():
        both_ref[0:tokens] = a_ref[...]
        both_ref[tokens:] = b_ref[...]

    g_ref[0:tokens] = dot(a_ref[...], down, 1, 1).astype(BF16)
    g_ref[tokens:] = dot(b_ref[...], down, 1, 1).astype(BF16)
    up_out[...] = up_ref[...]
    down_out[...] = down


def cot_down(blk, own, other, up, down, picked, half):
    tokens, model = own.shape
    steps = half // BLOCK
    column = along((2 * tokens, BLOCK), 1)
    if picked:
        up_at, down_at = along((model, BLOCK), 1), along((BLOCK, model))
    else:
        up_at = pl.BlockSpec((model, BLOCK), lambda g, b: (0, b[g]))
        down_at = pl.BlockSpec((BLOCK, model), lambda g, b: (b[g], 0))
    return call(
        cot_body, "cot_down", (blk,), (steps,),
        [(own, fixed(own.shape)), (other, fixed(own.shape)), (up, up_at), (down, down_at)],
        [
            ((2 * tokens, half), BF16, column),
            ((model, half), BF16, along((model, BLOCK), 1)),
            ((half, model), BF16, along((BLOCK, model))),
            ((2 * tokens, model), BF16, fixed((2 * tokens, model))),
        ],
        flops=4 * tokens * model * half, moved=2 * (2 * tokens * (model + half) + 4 * model * half),
    )


def hidden_body(blocks, *refs):
    pieces, refs = refs[:-10], refs[-10:]
    g_ref, up_ref, row_ref, bias_ref, act_ref, grad_ref, sum_ref, both_ref, part_ref, held = refs
    sizes = [ref.shape[0] * ref.shape[1] for ref in pieces]
    starts = [sum(sizes[:n]) for n in range(len(sizes))]
    step = pl.program_id(0)

    @pl.when(step == 0)
    def _():
        for ref, at, size in zip(pieces, starts, sizes):
            both_ref[at : at + size] = ref[...].reshape(size, ref.shape[2])

    @pl.when(step < blocks)
    def _():
        up, bias = up_ref[...], bias_ref[...]
        total = 0.0
        later = dot(pieces[0][...].reshape(sizes[0], -1), up)
        for n, (start, size) in enumerate(zip(starts, sizes)):
            at = slice(start, start + size)
            v = later + bias
            if n + 1 < len(pieces):
                later = dot(pieces[n + 1][...].reshape(sizes[n + 1], -1), up)
            square = v * v
            tanh = jnp.tanh(v * (GELU_A + GELU_B * square))
            gate = 0.5 + 0.5 * tanh
            act = v * gate
            slope = gate + act * ((1.0 - tanh) * (GELU_A + 3.0 * GELU_B * square))
            grad = (slope * g_ref[at].astype(F32)).astype(BF16)
            act_ref[at] = act.astype(BF16)
            grad_ref[at] = grad
            held[step, at] = grad
            total = total + jnp.sum(grad.astype(F32), axis=0, keepdims=True)
        sum_ref[...] = total

    @pl.when(step >= blocks)
    def _():
        grad = jnp.concatenate([held[n] for n in range(blocks)], axis=1)
        part_ref[...] = dot(grad, row_ref[...], 1, 1).astype(BF16)


def hidden_units(pieces, grads, up, bias):
    model = pieces[0].shape[2]
    tokens, half = grads.shape
    blocks, more = half // BLOCK, model // BLOCK

    def first(g):
        return jnp.minimum(g, blocks - 1)

    def second(g):
        return jnp.maximum(g - blocks, 0)

    column, line = pl.BlockSpec((tokens, BLOCK), lambda g: (0, first(g))), pl.BlockSpec((1, BLOCK), lambda g: (0, first(g)))
    return call(
        functools.partial(hidden_body, blocks), "hidden", (), (blocks + more,),
        [(piece, fixed(piece.shape)) for piece in pieces]
        + [
            (grads, column),
            (up, pl.BlockSpec((model, BLOCK), lambda g: (0, first(g)))),
            (up, pl.BlockSpec((BLOCK, half), lambda g: (second(g), 0))),
            (bias, line),
        ],
        [
            (grads.shape, BF16, column),
            (grads.shape, BF16, column),
            ((1, half), F32, line),
            ((tokens, model), BF16, fixed((tokens, model))),
            ((tokens, model), BF16, pl.BlockSpec((tokens, BLOCK), lambda g: (0, second(g)))),
        ],
        [pltpu.VMEM((blocks, tokens, BLOCK), BF16)],
        flops=4 * tokens * model * half, moved=2 * (tokens * (3 * model + 3 * half) + 2 * model * half), trans=tokens * half,
    )


def middle_back_body(
    order_ref, part_ref, sent_ref, mid_ref, cot_ref, gain_ref, w0, w1, w2, w3,
    grad_ref, low_ref, att0_ref, att1_ref, far_ref, sums_ref,
):
    grad = part_ref[...].astype(F32) + sent_ref[...].astype(F32)
    hat, inverse = centre(mid_ref[0])
    cot = cot_ref[0].astype(F32)
    total = cot + norm_back(grad, gain_ref[...], hat, inverse)
    low = total.astype(BF16)
    grad_ref[0] = total
    low_ref[0] = low
    far_ref[0, 0] = dot(low, w2[...], 1, 1).astype(BF16)
    far_ref[1, 0] = dot(low, w3[...], 1, 1).astype(BF16)
    att1_ref[0] = dot(low, w1[...], 1, 1).astype(BF16)
    att0_ref[0] = dot(low, w0[...], 1, 1).astype(BF16)

    @pl.when(pl.program_id(0) == 0)
    def _():
        sums_ref[...] = jnp.zeros_like(sums_ref)

    sums_ref[0:1] += jnp.sum(grad * hat, axis=0, keepdims=True)
    sums_ref[1:2] += jnp.sum(grad, axis=0, keepdims=True)
    sums_ref[2:3] += jnp.sum(low.astype(F32), axis=0, keepdims=True)
    sums_ref[3:4] += jnp.sum(cot, axis=0, keepdims=True)


def middle_back(order, both, sent, mid, cot, gain, weight, parts, deps=()):
    rows, shard, model = mid.shape
    width = model // parts
    block, one = along((1, shard, model)), along((1, shard, width))
    flat = pl.BlockSpec((shard, model), lambda g, o: (g, 0))
    return call(
        middle_back_body, "middle_back", (order,), (rows,),
        [(both, flat), (sent, flat), (mid, block), (cot, block), (gain, fixed((1, model)))] + out_blocks(weight, parts),
        [
            (mid.shape, F32, block),
            (mid.shape, BF16, block),
            ((rows, shard, width), BF16, one),
            ((rows, shard, width), BF16, one),
            ((2, rows, shard, width), BF16, along((2, 1, shard, width), 1)),
            ((8, model), F32, fixed((8, model))),
        ],
        deps=deps, flops=2 * rows * shard * model * model, moved=18 * mid.size,
    )


def norm1_back_body(part_ref, near_ref, far_ref, stream_ref, mid_ref, gain_ref, seg_ref, in_ref, shift_ref, sums_ref):
    grad = part_ref[0].astype(F32) + near_ref[0].astype(F32) + far_ref[0].astype(F32)
    hat, inverse = centre(stream_ref[0])
    total = mid_ref[0] + norm_back(grad, gain_ref[...], hat, inverse)
    in_ref[0] = total.astype(BF16)
    slots = lax.broadcasted_iota(jnp.int32, (SEGS, seg_ref.shape[-1]), 0) == seg_ref[0]
    onehot = slots.astype(F32).astype(BF16)
    shift_ref[0] = dot(jnp.concatenate([onehot, onehot], axis=1), split_low(total))

    @pl.when(pl.program_id(0) == 0)
    def _():
        sums_ref[...] = jnp.zeros_like(sums_ref)

    sums_ref[0:1] += jnp.sum(grad * hat, axis=0, keepdims=True)
    sums_ref[1:2] += jnp.sum(grad, axis=0, keepdims=True)


def norm1_back(start, count, own, near, far, stream, mid, gain, seg, held=(), deps=()):
    rows, shard, model = stream.shape
    block, own_block = along((1, shard, model), 0, start), along((1, shard, model))
    return call(
        norm1_back_body, "norm1_back", (), (count,),
        [(own, own_block), (near, own_block), (far, own_block), (stream, block), (mid, block), (gain, fixed((1, model)))]
        + [(seg, along((1, 1, shard), 0, start))],
        [
            (stream.shape, BF16, block),
            ((count, SEGS, model), F32, along((1, SEGS, model))),
            ((8, model), F32, fixed((8, model))),
        ],
        held=[(array, 0) for array in held], deps=deps, moved=16 * count * shard * model,
    )


def exchange(own, one, far):
    far = swap(far, "y")
    return [own, swap(one, "c"), far, swap(far[1], "c")]


def after(value, *others):
    return lax.optimization_barrier((value,) + others)[0]


def cut(values, index, size, axis):
    return lax.dynamic_slice_in_dim(values, index * size, size, axis)


def add_low(kept, sent):
    return (kept.astype(F32) + sent.astype(F32)).astype(BF16)


def ordered(at, own, other, axis):
    return jnp.where(at == 0, jnp.concatenate([own, other], axis), jnp.concatenate([other, own], axis))


def local(
    inputs, segment_ids, doc_times, time_weight, time_bias, norm1_gain, norm1_bias, qkv_weight, qkv_bias,
    out_weight, out_bias, norm2_gain, norm2_bias, up_weight, up_bias, down_weight, down_bias, cotangent,
    *, dp,
):
    rows, shard, model = inputs.shape
    parts = 4
    tokens = rows * shard
    hidden_width = up_weight.shape[1]
    width = model // parts
    depth = dp // 2
    half = hidden_width // 2
    piece = half // dp
    z_at, x_at, y_at, c_at = (lax.axis_index(name) for name in ("z", "x", "y", "c"))
    me = 2 * y_at + c_at
    order = [me ^ i for i in range(parts)]
    order_list = jnp.stack(order).astype(jnp.int32)
    me_list = order_list[:1]

    def line(vector):
        return vector.astype(F32)[None]

    groups = [(0, rows - 1), (rows - 1, 1)] if rows > 1 else [(0, 1)]
    seg = segment_ids[:, None, :]
    features = time_features(doc_times.reshape(rows * SEGS), jnp.arange(TEMB), TEMB // 2)
    time_shift = dot(features, time_weight).reshape(rows, SEGS, model) + time_bias.astype(F32)
    stream, own1 = norm1(inputs, seg, time_shift, line(norm1_gain), line(norm1_bias))
    two1 = swap(own1, "y")
    one1 = swap(own1, "c")

    seg_two = swap(segment_ids, "y")
    segs = jnp.stack([segment_ids, swap(segment_ids, "c"), seg_two, swap(seg_two, "c")], axis=1)
    low_id, high_id = segs.min(axis=2), segs.max(axis=2)
    act = (low_id[:, :, None] <= high_id[:, None, :]) & (low_id[:, None, :] <= high_id[:, :, None])
    places = jnp.arange(parts, dtype=jnp.int32)
    rank = jnp.cumsum(act.astype(jnp.int32), axis=2) - 1
    chosen = act[..., None] & (rank[..., None] == places)
    idx = jnp.sum(jnp.where(chosen, places[:, None], 0), axis=2).astype(jnp.int32).reshape(-1)
    cnt = jnp.sum(act.astype(jnp.int32), axis=2).reshape(-1)
    positions = jnp.stack([o * shard + jnp.arange(shard, dtype=jnp.int32) for o in order])
    cos_tab, sin_tab = rotary_tables(positions, HEAD_DIM)

    cot = cotangent.reshape(tokens, model)
    cot_other = swap(cot, "c")
    turned = jnp.stack([1 - x_at, x_at])
    if piece % BLOCK == 0:
        blk = ((jnp.arange(depth)[None, :] * 2 + turned[:, None]) * 2 + c_at) * (piece // BLOCK)
        blk = (blk[..., None] + jnp.arange(piece // BLOCK)).reshape(-1).astype(jnp.int32)
        up_from, down_from = up_weight, down_weight
    else:
        blk = jnp.zeros((half // BLOCK,), jnp.int32)
        up_from = up_weight.reshape(model, depth, 2, 2, piece)
        up_from = lax.dynamic_index_in_dim(up_from, c_at, 3, keepdims=False)
        up_from = jnp.where(x_at == 1, up_from, up_from[:, :, ::-1]).transpose(0, 2, 1, 3).reshape(model, half)
        down_from = down_weight.reshape(depth, 2, 2, piece, model)
        down_from = lax.dynamic_index_in_dim(down_from, c_at, 2, keepdims=False)
        down_from = jnp.where(x_at == 1, down_from, down_from[:, ::-1]).transpose(1, 0, 2, 3).reshape(half, model)
    grad_act, up_own, down_own, cot_both = cot_down(
        blk, cot, cot_other, up_from, down_from, piece % BLOCK != 0, half
    )
    up_bias_own = lax.dynamic_index_in_dim(up_bias.reshape(depth, 2, 2, piece), c_at, 2, keepdims=False)
    up_bias_own = jnp.where(x_at == 1, up_bias_own, up_bias_own[:, ::-1]).transpose(1, 0, 2).reshape(half)

    bias_line = qkv_bias.reshape(1, 3 * model)
    qkv, normed1_all, qkv_own = project_qkv(
        0, parts, me_list, own1, one1, qkv_weight, bias_line, cos_tab, sin_tab, (), (grad_act,)
    )
    two1 = after(two1, qkv)
    qkv, normed1_all, _ = project_qkv(
        1, parts, me_list, two1, swap(two1, "c"), qkv_weight, bias_line, cos_tab, sin_tab, (qkv, normed1_all)
    )
    o, lse, attended = None, None, []
    for start, count in groups:
        held = () if o is None else (o, lse)
        o, out_one, out_far, lse = attend(start, count, cnt, idx, qkv, segs, held)
        attended.append(exchange(o, out_one, out_far))
    held, normed2, normed2_other = (), [], []
    for (start, count), values in zip(groups, attended):
        values = [o] + values[1:]
        middle, low, attended_all = middle_norm(
            start, count, order_list, values, out_weight, stream, line(out_bias), line(norm2_gain), line(norm2_bias), held
        )
        held = (middle, attended_all)
        normed2.append(low)
        normed2_other.append(swap(low, "c"))

    active, grad_hidden, up_b, normed2_both, part2 = hidden_units(
        normed2 + normed2_other, grad_act, up_own, line(up_bias_own)
    )
    part2_sent = swap(part2[tokens:], "c")
    grad_middle, grad_middle_low, att0, att1, far, sums2 = middle_back(
        order_list, part2, part2_sent, middle, cotangent, line(norm2_gain), out_weight, parts
    )
    grad_o = exchange(att0, att1, far)
    sums2 = sums2[:4]

    active_late, grad_hidden_late = lax.optimization_barrier((active, grad_hidden, far))[:2]
    up_grad = dot(normed2_both, grad_hidden_late, 0, 0).astype(BF16)
    up_z = lax.psum_scatter(up_grad, "z", scatter_dimension=0, tiled=True)
    down_out = dot(active_late[:, : half // 2], cot_both, 0, 0).astype(BF16)
    down_sent = swap(down_out, "x")
    active_late = after(active_late, down_out, up_grad)
    down_kept = dot(active_late[:, half // 2 :], cot_both, 0, 0).astype(BF16)
    feed_sent = swap(dot(active_late[tokens:], down_own).astype(BF16), "c")
    feed = dot(active_late[:tokens], down_own) + feed_sent.astype(F32) + line(down_bias)
    output = (middle + feed.reshape(rows, shard, model)).astype(BF16)
    out_grad = dot(
        attended_all.reshape(tokens, model), grad_middle_low.reshape(tokens, model), 0, 0
    ).astype(BF16)

    grad_qkv, back = (), []
    deps = (down_kept, output, out_grad)
    for start, count in groups:
        grad_qkv, own, one, two, three = attend_back(
            start, count, cnt, idx, qkv, o, grad_o, lse, segs, cos_tab, sin_tab, qkv_own, grad_qkv, deps
        )
        grad_qkv = (grad_qkv,)
        there = add_low(two, swap(three, "c"))
        deps = (there,)
        back.append((own, swap(one, "c"), swap(there, "y")))
    grad_qkv = after(grad_qkv[0], there).reshape(parts * tokens, 3 * width)
    qkv_grad = dot(normed1_all.reshape(parts * tokens, model), grad_qkv, 0, 0).astype(BF16)
    qkv_b = jnp.sum(grad_qkv.astype(F32), axis=0)
    held, grad_shift, sums1 = (), [], 0.0
    for (start, count), values in zip(groups, back):
        input_grad, found, sums = norm1_back(
            start, count, *values, stream, grad_middle, line(norm1_gain), seg, held, (qkv_grad,)
        )
        held = (input_grad,)
        grad_shift.append(found.reshape(count * SEGS, model))
        sums1 = sums1 + sums[:2]

    down_x = add_low(down_kept, down_sent)
    down_y = add_low(cut(down_x, y_at, model // 2, 1), swap(cut(down_x, 1 - y_at, model // 2, 1), "y"))
    down_z = lax.psum_scatter(down_y, "z", scatter_dimension=0, tiled=True)
    up_rows = model // dp
    up_sent = swap(cut(up_z, 1 - x_at, up_rows, 0), "x")
    up_sent = jnp.concatenate([up_sent[:, half // 2 :], up_sent[:, : half // 2]], axis=1)
    up_x = add_low(cut(up_z, x_at, up_rows, 0), up_sent)
    up_y = add_low(cut(up_x, y_at, half // 2, 1), swap(cut(up_x, 1 - y_at, half // 2, 1), "y"))
    out_grad = jnp.concatenate([cut(out_grad, o_at, width, 0) for o_at in order], axis=0)
    out_c = add_low(cut(out_grad, c_at, model // 2, 1), swap(cut(out_grad, 1 - c_at, model // 2, 1), "c"))
    out_y = add_low(cut(out_c, y_at, width, 1), swap(cut(out_c, 1 - y_at, width, 1), "y"))
    late = jnp.concatenate([qkv_grad, out_y], axis=1).reshape(depth, 2 * up_rows, model)
    late_x = add_low(cut(late, x_at, up_rows, 1), swap(cut(late, 1 - x_at, up_rows, 1), "x"))
    late_z = lax.psum_scatter(late_x, "z", scatter_dimension=0, tiled=False)

    down_done = ordered(y_at, down_z, swap(down_z, "y"), 1)
    down_done = ordered(c_at, down_done, swap(down_done, "c"), 0).astype(F32)
    up_done = ordered(y_at, up_y, swap(up_y, "y"), 1)
    up_done = ordered(c_at, up_done[None], swap(up_done, "c")[None], 0).reshape(2, up_rows, 2, depth, piece)
    up_done = jnp.where(x_at == 1, up_done, up_done[:, :, ::-1]).transpose(1, 3, 2, 0, 4)
    up_done = up_done.reshape(up_rows, hidden_width).astype(F32)
    late_done = ordered(c_at, late_z[None], swap(late_z, "c")[None], 0)
    late_done = ordered(y_at, late_done[None], swap(late_done, "y")[None], 0).reshape(parts, up_rows, model)
    qkv_done = late_done[:, :, : 3 * width].reshape(parts, up_rows, 3, width).transpose(1, 2, 0, 3)
    qkv_done = qkv_done.reshape(up_rows, 3 * model).astype(F32)
    out_done = late_done[:, :, 3 * width :].reshape(2, 2, up_rows, width).transpose(2, 1, 0, 3)
    out_done = out_done.reshape(up_rows, model).astype(F32)

    up_b = up_b.reshape(2, depth, 1, piece)
    up_b = jnp.where(x_at == 1, up_b, up_b[::-1]).transpose(1, 0, 2, 3)
    up_b = jnp.where(jnp.arange(2)[:, None] == c_at, up_b, 0.0).reshape(-1, model)
    qkv_b = jnp.where(jnp.arange(parts)[:, None] == me, qkv_b.reshape(3, 1, width), 0.0).reshape(3, model)
    times = doc_times.reshape(1, rows * SEGS)
    times = jnp.concatenate([times // 32, times % 32], axis=1).astype(F32)
    times = jnp.pad(times, ((0, 0), (0, model - times.shape[1])))
    small = jnp.concatenate(grad_shift + [sums1, sums2, qkv_b, up_b, times], axis=0)
    small = add_low(small, swap(small.astype(BF16), "c"))
    small = add_low(small, swap(small, "y"))
    small = ordered(x_at, small[None], swap(small, "x")[None], 0)
    if depth == 4:
        others = [lax.ppermute(small, "z", [(i, i ^ n) for i in range(depth)]) for n in range(1, depth)]
        small = jnp.stack([small] + others)
        small = jnp.stack([lax.dynamic_index_in_dim(small, z_at ^ n, 0, keepdims=False) for n in range(depth)])
    else:
        small = lax.all_gather(small, "z")
    small = small.reshape(dp, small.shape[2], model)
    all_times = small[:, -1, : 2 * rows * SEGS].astype(F32) * 0.25
    all_times = all_times[:, : rows * SEGS] * 32.0 + all_times[:, rows * SEGS :]
    shifts = small[:, : rows * SEGS].reshape(dp * rows * SEGS, model)
    columns = (2 * z_at + x_at) * (TEMB // dp) + jnp.arange(TEMB // dp)
    wanted = time_features(all_times.reshape(-1), columns, TEMB // 2)
    time_w_done = dot(wanted, shifts, 0, 0)
    sums = jnp.sum(small[:, rows * SEGS :].astype(F32), axis=0)
    dp_at = 2 * z_at + x_at

    def share(vector):
        return cut(vector.reshape(-1), dp_at, vector.size // dp, 0)

    time_b_done = jnp.sum(cut(shifts, dp_at, up_rows, 1).astype(F32), axis=0)
    return (
        output, input_grad, time_w_done, time_b_done, share(sums[0]), share(sums[1]), qkv_done, share(sums[6:9]),
        out_done, share(sums[4]), share(sums[2]), share(sums[3]), up_done, share(sums[9:-1]), down_done, share(sums[5]),
    )


def solution(mesh):
    dp, seq = mesh.shape["dp"], mesh.shape["seq"]
    fine = Mesh(mesh.devices.reshape(dp // 2, 2, seq // 2, 2), ("z", "x", "y", "c"))
    rows, seqs = ("z", "x"), ("y", "c")
    placed = (P(rows, seqs, None), P(rows, seqs), P(rows, None)) + (P(),) * 14 + (P(rows, seqs, None),)
    vec, mat = P(rows), P(rows, None)
    return jax.shard_map(
        functools.partial(local, dp=dp),
        mesh=fine,
        in_specs=placed,
        out_specs=(
            P(rows, seqs, None), P(rows, seqs, None), mat, vec, vec, vec, mat, vec, mat, vec, vec, vec, mat, vec, mat, vec,
        ),
        check_vma=False,
    )
```

```python
import functools
import math

import jax
import jax.numpy as jnp
from jax import lax
from jax.experimental import pallas as pl
from jax.experimental.pallas import tpu as pltpu
from jax.sharding import Mesh, PartitionSpec as P

HEADS = 16
HEAD_DIM = 64
TEMB = 256
SEGS = 8
EPSILON = 1e-05
F32 = jnp.float32
BF16 = jnp.bfloat16
NEG = -1e30
LOG2E = math.log2(math.e)
GELU_A = math.sqrt(2.0 / math.pi)
GELU_B = GELU_A * 0.044715
BLOCK = 256
VMEM = 60 * 1024 * 1024


def swap(value, axis):
    return lax.ppermute(value, axis, [(0, 1), (1, 0)])


def time_features(doc_times, column, half_size):
    frequency = jnp.exp(-math.log(10000.0) * (column % half_size).astype(F32) / half_size)
    angles = doc_times.astype(F32)[..., None] * frequency
    return jnp.where(column < half_size, jnp.sin(angles), jnp.cos(angles)).astype(BF16)


def rotary_tables(positions, head_size):
    half_size = head_size // 2
    frequency = jnp.exp(-math.log(10000.0) * 2.0 * jnp.arange(half_size, dtype=F32) / head_size)
    angles = positions.astype(F32)[..., None] * frequency
    cos_tab, sin_tab = jnp.cos(angles), jnp.sin(angles)
    return (
        jnp.concatenate([cos_tab] * 4, axis=-1),
        jnp.concatenate([-sin_tab, sin_tab, -sin_tab, sin_tab], axis=-1),
    )


def dot(left_op, right_op, left_dim=1, right_dim=0):
    return lax.dot_general(
        left_op, right_op, (((left_dim,), (right_dim,)), ((), ())), preferred_element_type=F32
    )


def turn(values, cos_tab, sin_tab):
    slabs = []
    lane = lax.broadcasted_iota(jnp.int32, (values.shape[0], 128), 1)
    first = lane % HEAD_DIM < HEAD_DIM // 2
    for start in range(0, values.shape[1], 128):
        slab = values[:, start : start + 128]
        partner = jnp.where(
            first, pltpu.roll(slab, 128 - HEAD_DIM // 2, 1), pltpu.roll(slab, HEAD_DIM // 2, 1)
        )
        slabs.append(slab * cos_tab + partner * sin_tab)
    return jnp.concatenate(slabs, axis=1)


def split_low(values):
    high = values.astype(BF16)
    return jnp.concatenate([high, (values - high.astype(F32)).astype(BF16)], axis=0)


def centre(values):
    scale = 1.0 / values.shape[-1]
    centred = values - jnp.sum(values, axis=-1, keepdims=True) * scale
    spread = jnp.sum(centred * centred, axis=-1, keepdims=True) * scale
    inverse = lax.rsqrt(spread + EPSILON)
    return centred * inverse, inverse


def norm_back(grad, gain, hat, inverse):
    scale = 1.0 / grad.shape[-1]
    scaled = grad * gain
    mean = jnp.sum(scaled, axis=-1, keepdims=True) * scale
    along = jnp.sum(scaled * hat, axis=-1, keepdims=True) * scale
    return inverse * (scaled - mean - hat * along)


def call(body, name, prefetch, grid, ins, outs, scratch=(), deps=(), held=()):
    count = len(prefetch) + len(ins)
    extra = [array for array, _ in held] + list(deps)

    def kernel(*refs):
        body(*refs[:count], *refs[count + len(extra) :])

    return pl.pallas_call(
        kernel,
        grid_spec=pltpu.PrefetchScalarGridSpec(
            num_scalar_prefetch=len(prefetch),
            grid=grid,
            in_specs=[spec for _, spec in ins] + [pl.BlockSpec(memory_space=pl.ANY)] * len(extra),
            out_specs=[spec for _, _, spec in outs],
            scratch_shapes=list(scratch),
        ),
        out_shape=[jax.ShapeDtypeStruct(shape, kind) for shape, kind, _ in outs],
        input_output_aliases={count + n: out for n, (_, out) in enumerate(held)},
        compiler_params=pltpu.CompilerParams(vmem_limit_bytes=VMEM),
        name=name,
    )(*prefetch, *[array for array, _ in ins], *extra)


def fixed(shape):
    return pl.BlockSpec(shape, lambda *_: (0,) * len(shape))


def along(shape, axis=0, start=0):
    return pl.BlockSpec(shape, lambda g, *_: tuple(start + g if n == axis else 0 for n in range(len(shape))))


def norm1_body(x_ref, seg_ref, shift_ref, gain_ref, bias_ref, stream_ref, low_ref):
    slots = lax.broadcasted_iota(jnp.int32, (SEGS, seg_ref.shape[-1]), 0) == seg_ref[0]
    onehot = slots.astype(F32).astype(BF16)
    added = dot(jnp.concatenate([onehot, onehot], axis=0), split_low(shift_ref[0]), 0, 0)
    stream = x_ref[0].astype(F32) + added
    hat, _ = centre(stream)
    stream_ref[0] = stream
    low_ref[0] = (hat * gain_ref[...] + bias_ref[...]).astype(BF16)


def norm1(x, seg, shift, gain, bias):
    rows, shard, model = x.shape
    block = along((1, shard, model))
    return call(
        norm1_body, "norm1", (), (rows,),
        [(x, block), (seg, along((1, 1, shard))), (shift, along((1, SEGS, model))), (gain, fixed((1, model))), (bias, fixed((1, model)))],
        [(x.shape, F32, block), (x.shape, BF16, block)],
    )


def qkv_body(me_ref, a_ref, b_ref, w_ref, bias_ref, cos_ref, sin_ref, out_ref, all_ref, own_ref):
    rows, shard, model = a_ref.shape
    width = w_ref.shape[1]
    refs = (a_ref, b_ref)
    step = pl.program_id(0)

    @pl.when(step == 0)
    def _():
        for n, x_ref in enumerate(refs):
            all_ref[n] = x_ref[...]

    def run(turned):
        w, bias = w_ref[...], bias_ref[...].astype(F32)
        found = [dot(x_ref[...].reshape(rows * shard, model), w) for x_ref in refs]
        for n, full in enumerate(found):
            for r in range(rows):
                values = full[r * shard : (r + 1) * shard] + bias
                if turned:
                    values = turn(values, cos_ref[n], sin_ref[n]) * jnp.where(step == 0, LOG2E * HEAD_DIM**-0.5, 1.0)
                out_ref[0, n, r] = values.astype(BF16)

    own_ref[...] = w_ref[...].T

    @pl.when(step < 2)
    def _():
        run(True)

    @pl.when(step == 2)
    def _():
        run(False)


def project_qkv(pair, parts, me, first, second, weight, bias, cos_tab, sin_tab, held=(), deps=()):
    rows, shard, model = first.shape
    width = model // parts
    return call(
        qkv_body, "qkv", (me,), (3,),
        [(first, fixed(first.shape)), (second, fixed(first.shape))]
        + [
            (weight, pl.BlockSpec((model, width), lambda g, m: (0, g * parts + m[0]))),
            (bias, pl.BlockSpec((1, width), lambda g, m: (0, g * parts + m[0]))),
            (cos_tab, pl.BlockSpec((2, shard, 128), lambda g, m: (pair, 0, 0))),
            (sin_tab, pl.BlockSpec((2, shard, 128), lambda g, m: (pair, 0, 0))),
        ],
        [
            ((3, parts, rows, shard, width), BF16, pl.BlockSpec((1, 2, rows, shard, width), lambda g, m: (g, pair, 0, 0, 0))),
            ((parts, rows, shard, model), BF16, pl.BlockSpec((2, rows, shard, model), lambda g, m: (pair, 0, 0, 0))),
            ((3 * width, model), BF16, along((width, model))),
        ],
        held=[(array, n) for n, array in enumerate(held)], deps=deps
    )


def seg_columns(segq_all, segk):
    pieces, shard, _ = segk.shape
    for j in range(pieces):
        row = jnp.broadcast_to(segq_all[j:j+1].astype(F32), (128, shard))
        segk[j] = row.T

def attend_body(start, cnt_ref, idx_ref, qkv_ref, seg_ref, o_ref, one_ref, far_ref, lse_ref, vt, segk, qmt, acc):
    row = pl.program_id(0) + start
    _, pieces, _, shard, width = qkv_ref.shape
    heads = width // HEAD_DIM

    @pl.when(pl.program_id(0) == 0)
    def _():
        qmt[...] = jnp.zeros_like(qmt)

    for j in range(pieces):
        vt[j] = qkv_ref[2, j, 0].T
        qt = qkv_ref[0, j, 0].T
        for h in range(heads):
            at = slice(h * HEAD_DIM, (h + 1) * HEAD_DIM)
            qmt[j, at, h * shard : (h + 1) * shard] = qt[at]
    seg_columns(seg_ref[0], segk)

    @pl.loop(0, pieces)
    def _(piece):
        attend_piece(row * pieces + piece, piece, cnt_ref, idx_ref, qkv_ref.at[1], seg_ref, lse_ref, vt, segk, qmt, acc)

    for j in range(pieces):
        o_ref[j, 0] = acc[j].T.astype(BF16)
    one_ref[0] = o_ref[1, 0]
    far_ref[:, 0] = o_ref[2:, 0]


def attend_piece(at_q, piece, cnt_ref, idx_ref, k_ref, seg_ref, lse_ref, vt, segk, qmt, acc):
    pieces, _, shard, width = k_ref.shape
    heads = width // HEAD_DIM
    seg_q = seg_ref[0, pl.ds(piece, 1)].astype(F32)

    def run(count):
        @pl.when(cnt_ref[at_q] == count)
        def _():
            qm = qmt[piece]
            places = [idx_ref[at_q * pieces + t] for t in range(count)]
            top, tot, out = [None] * heads, [None] * heads, [None] * heads
            later = dot(k_ref[places[0], 0], qm)
            for t in range(count):
                s = later
                if t + 1 < count:
                    later = dot(k_ref[places[t + 1], 0], qm)
                col = segk[places[t]]
                same = jnp.concatenate([col] * (shard // 128), axis=1) == seg_q
                for h in range(heads):
                    at = slice(h * HEAD_DIM, (h + 1) * HEAD_DIM)
                    sh = jnp.where(same, s[:, h * shard : (h + 1) * shard], NEG)
                    best = jnp.max(sh, axis=0, keepdims=True)
                    if t:
                        best = jnp.maximum(top[h], best)
                        fade = jnp.exp2(top[h] - best)
                    p = jnp.exp2(sh - best)
                    total = jnp.sum(p, axis=0, keepdims=True)
                    found = dot(vt[places[t], at], p.astype(BF16))
                    if t:
                        total = tot[h] * fade + total
                        found = out[h] * fade + found
                    top[h], tot[h], out[h] = best, total, found
            for h in range(heads):
                acc[piece, h * HEAD_DIM : (h + 1) * HEAD_DIM] = out[h] / tot[h]
                lse_ref[0, piece, h : h + 1] = top[h] + jnp.log2(tot[h])

    for count in range(1, pieces + 1):
        run(count)


def attend(start, count, cnt, idx, qkv, seg, held=()):
    _, pieces, rows, shard, width = qkv.shape
    heads = width // HEAD_DIM
    pairs = count * (pieces * shard) ** 2
    return call(
        functools.partial(attend_body, start), "attend", (cnt, idx), (count,),
        [(qkv, along((3, pieces, 1, shard, width), 2, start)), (seg, along((1, pieces, shard), 0, start))],
        [
            ((pieces, rows, shard, width), BF16, along((pieces, 1, shard, width), 1, start)),
            ((count, shard, width), BF16, along((1, shard, width))),
            ((2, count, shard, width), BF16, along((2, 1, shard, width), 1)),
            ((rows, pieces, 8, shard), F32, along((1, pieces, 8, shard), 0, start)),
        ],
        [
            pltpu.VMEM((pieces, width, shard), BF16),
            pltpu.VMEM((pieces, shard, 128), F32),
            pltpu.VMEM((pieces, width, heads * shard), BF16),
            pltpu.VMEM((pieces, width, shard), F32),
        ],
        held=list(zip(held, (0, 3)))
    )


def attend_back_body(
    start, cnt_ref, idx_ref, qkv_ref, o_ref, do0, do1, do2, do3, lse_ref, seg_ref, cos_ref, sin_ref, w_ref,
    g_ref, p0_ref, p1_ref, p2_ref, p3_ref, kt, segk, dk, dv, dqt, qmt, gmt, qst, gst, low,
):
    row = pl.program_id(0) + start
    _, pieces, _, shard, width = qkv_ref.shape
    heads = width // HEAD_DIM

    @pl.when(pl.program_id(0) == 0)
    def _():
        qmt[...] = jnp.zeros_like(qmt)
        gmt[...] = jnp.zeros_like(gmt)

    seg_columns(seg_ref[0], segk)
    dk[...] = jnp.zeros_like(dk)
    dv[...] = jnp.zeros_like(dv)
    lane = lax.broadcasted_iota(jnp.int32, (shard, width), 1) // HEAD_DIM
    chosen = lax.broadcasted_iota(jnp.int32, (8, width), 1) // HEAD_DIM
    chosen = (chosen == lax.broadcasted_iota(jnp.int32, (8, width), 0)).astype(BF16)
    for j, do_ref in enumerate((do0, do1, do2, do3)):
        kt[j] = qkv_ref[1, j, 0].T
        q, do = qkv_ref[0, j, 0], do_ref[...].reshape(shard, width)
        qt, gt = q.T, do.T
        for h in range(heads):
            at, qa = slice(h * HEAD_DIM, (h + 1) * HEAD_DIM), slice(h * shard, (h + 1) * shard)
            qmt[j, at, qa] = qt[at]
            gmt[j, at, qa] = gt[at]
            qst[j, qa] = jnp.where(lane == h, q, jnp.zeros_like(q))
            gst[j, qa] = jnp.where(lane == h, do, jnp.zeros_like(do))
        prod = do.astype(F32) * o_ref[j, 0].astype(F32)
        high = prod.astype(BF16)
        low[j] = dot(chosen, high, 1, 1) + dot(chosen, (prod - high.astype(F32)).astype(BF16), 1, 1)

    @pl.loop(0, pieces)
    def _(piece):
        back_piece(
            row * pieces + piece, piece, cnt_ref, idx_ref, qkv_ref.at[1], qkv_ref.at[2], lse_ref, seg_ref,
            kt, segk, dk, dv, dqt, qmt, gmt, qst, gst, low,
        )

    for j, ref in ((1, p1_ref), (3, p3_ref), (0, p0_ref), (2, p2_ref)):
        grad_q = turn(dqt[j].T * HEAD_DIM**-0.5, cos_ref[j], -sin_ref[j]).astype(BF16)
        grad_k = turn(dk[j] * (1 / LOG2E), cos_ref[j], -sin_ref[j]).astype(BF16)
        grad = jnp.concatenate([grad_q, grad_k, dv[j].astype(BF16)], axis=1)
        g_ref[j, 0] = grad
        ref[0] = dot(grad, w_ref[...]).astype(BF16)


def back_piece(
    at_q, piece, cnt_ref, idx_ref, k_ref, v_ref, lse_ref, seg_ref, kt, segk, dk, dv, dqt, qmt, gmt, qst, gst, low
):
    pieces, _, shard, width = k_ref.shape
    heads = width // HEAD_DIM
    lse, delta = lse_ref[0, piece], low[piece]
    seg_q = seg_ref[0, pl.ds(piece, 1)].astype(F32)

    def run(count):
        @pl.when(cnt_ref[at_q] == count)
        def _():
            places = [idx_ref[at_q * pieces + t] for t in range(count)]
            qm, gm = qmt[piece], gmt[piece]
            later = dot(k_ref[places[0], 0], qm), dot(v_ref[places[0], 0], gm)
            out = [None] * heads
            for t in range(count):
                s, dp = later
                j = places[t]
                if t + 1 < count:
                    later = dot(k_ref[places[t + 1], 0], qm), dot(v_ref[places[t + 1], 0], gm)
                col = segk[j]
                same = jnp.concatenate([col] * (shard // 128), axis=1) == seg_q
                ps, dss = [], []
                for h in range(heads):
                    at, qa = slice(h * HEAD_DIM, (h + 1) * HEAD_DIM), slice(h * shard, (h + 1) * shard)
                    p = jnp.exp2(jnp.where(same, s[:, qa] - lse[h : h + 1], NEG))
                    ds = (p * (dp[:, qa] - delta[h : h + 1])).astype(BF16)
                    ps.append(p.astype(BF16))
                    dss.append(ds)
                    found = dot(kt[j, at], ds)
                    out[h] = found if t == 0 else out[h] + found
                dv[j] += dot(jnp.concatenate(ps, axis=1), gst[piece])
                dk[j] += dot(jnp.concatenate(dss, axis=1), qst[piece])
            for h in range(heads):
                dqt[piece, h * HEAD_DIM : (h + 1) * HEAD_DIM] = out[h]

    for count in range(1, pieces + 1):
        run(count)


def attend_back(start, count, cnt, idx, qkv, o, do, lse, seg, cos_tab, sin_tab, weight, held=(), deps=()):
    _, pieces, rows, shard, width = qkv.shape
    model = weight.shape[1]
    heads = width // HEAD_DIM
    table = fixed((pieces, shard, 128))
    pairs = count * (pieces * shard) ** 2
    square, wide = (pieces, width, heads * shard), (pieces, shard, width)
    one = along((1, shard, width), 0, start)
    return call(
        functools.partial(attend_back_body, start), "attend_back", (cnt, idx), (count,),
        [(qkv, along((3, pieces, 1, shard, width), 2, start)), (o, along((pieces, 1, shard, width), 1, start))]
        + [(do[0], one), (do[1], one), (do[2], along((1, 1, shard, width), 1, start)), (do[3], one)]
        + [(lse, along((1, pieces, 8, shard), 0, start)), (seg, along((1, pieces, shard), 0, start))]
        + [(cos_tab, table), (sin_tab, table), (weight, fixed(weight.shape))],
        [((pieces, rows, shard, 3 * width), BF16, along((pieces, 1, shard, 3 * width), 1, start))]
        + [((count, shard, model), BF16, along((1, shard, model)))] * pieces,
        [
            pltpu.VMEM((pieces, width, shard), BF16),
            pltpu.VMEM((pieces, shard, 128), F32),
            pltpu.VMEM(wide, F32),
            pltpu.VMEM(wide, F32),
            pltpu.VMEM((pieces, width, shard), F32),
            pltpu.VMEM(square, BF16),
            pltpu.VMEM(square, BF16),
            pltpu.VMEM((pieces, heads * shard, width), BF16),
            pltpu.VMEM((pieces, heads * shard, width), BF16),
            pltpu.VMEM((pieces, 8, shard), F32),
        ],
        held=[(array, 0) for array in held], deps=deps
    )


def middle_body(
    order_ref, a0, a1, a2, a3, w0, w1, w2, w3, stream_ref, bias_ref, gain_ref, shift_ref, mid_ref, low_ref, all_ref,
):
    _, shard, model = stream_ref.shape
    total = 0.0
    for n, (a, w) in enumerate(((a0, w0), (a1, w1), (a2, w2), (a3, w3))):
        values = a[...].reshape(shard, a.shape[-1])
        total = total + dot(values, w[...])
        all_ref[0, :, n * a.shape[-1] : (n + 1) * a.shape[-1]] = values
    mid = stream_ref[0] + (total + bias_ref[...])
    hat, _ = centre(mid)
    mid_ref[0] = mid
    low_ref[0] = (hat * gain_ref[...] + shift_ref[...]).astype(BF16)


def out_blocks(weight, parts):
    width = weight.shape[0] // parts

    def block(i):
        return pl.BlockSpec((width, weight.shape[1]), lambda g, o: (o[i], 0))

    return [(weight, block(i)) for i in range(parts)]


def middle_norm(start, count, order, attended, weight, stream, bias, gain, shift, held=()):
    rows, shard, model = stream.shape
    parts = len(attended)
    width = model // parts
    block, line, one = along((1, shard, model), 0, start), fixed((1, model)), along((1, shard, width))
    first = [along((1, 1, shard, width), 1, start), one, along((1, 1, shard, width), 1), one]
    return call(
        middle_body, "middle", (order,), (count,),
        list(zip(attended, first)) + out_blocks(weight, parts) + [(stream, block), (bias, line), (gain, line), (shift, line)],
        [
            (stream.shape, F32, block),
            ((count, shard, model), BF16, along((1, shard, model))),
            (stream.shape, BF16, block),
        ],
        held=list(zip(held, (0, 2)))
    )


def cot_body(blk_ref, a_ref, b_ref, up_ref, down_ref, g_ref, up_out, down_out, both_ref):
    tokens = a_ref.shape[0]
    down = down_ref[...]

    @pl.when(pl.program_id(0) == 0)
    def _():
        both_ref[0:tokens] = a_ref[...]
        both_ref[tokens:] = b_ref[...]

    g_ref[0:tokens] = dot(a_ref[...], down, 1, 1).astype(BF16)
    g_ref[tokens:] = dot(b_ref[...], down, 1, 1).astype(BF16)
    up_out[...] = up_ref[...]
    down_out[...] = down


def cot_down(blk, own, other, up, down, picked, half):
    tokens, model = own.shape
    steps = half // BLOCK
    column = along((2 * tokens, BLOCK), 1)
    if picked:
        up_at, down_at = along((model, BLOCK), 1), along((BLOCK, model))
    else:
        up_at = pl.BlockSpec((model, BLOCK), lambda g, b: (0, b[g]))
        down_at = pl.BlockSpec((BLOCK, model), lambda g, b: (b[g], 0))
    return call(
        cot_body, "cot_down", (blk,), (steps,),
        [(own, fixed(own.shape)), (other, fixed(own.shape)), (up, up_at), (down, down_at)],
        [
            ((2 * tokens, half), BF16, column),
            ((model, half), BF16, along((model, BLOCK), 1)),
            ((half, model), BF16, along((BLOCK, model))),
            ((2 * tokens, model), BF16, fixed((2 * tokens, model))),
        ]
    )


def hidden_body(blocks, *refs):
    pieces, refs = refs[:-10], refs[-10:]
    g_ref, up_ref, row_ref, bias_ref, act_ref, grad_ref, sum_ref, both_ref, part_ref, held = refs
    sizes = [ref.shape[0] * ref.shape[1] for ref in pieces]
    starts = [sum(sizes[:n]) for n in range(len(sizes))]
    step = pl.program_id(0)

    @pl.when(step == 0)
    def _():
        for ref, at, size in zip(pieces, starts, sizes):
            both_ref[at : at + size] = ref[...].reshape(size, ref.shape[2])

    @pl.when(step < blocks)
    def _():
        up, bias = up_ref[...], bias_ref[...]
        total = 0.0
        later = dot(pieces[0][...].reshape(sizes[0], -1), up)
        for n, (start, size) in enumerate(zip(starts, sizes)):
            at = slice(start, start + size)
            v = later + bias
            if n + 1 < len(pieces):
                later = dot(pieces[n + 1][...].reshape(sizes[n + 1], -1), up)
            square = v * v
            tanh = jnp.tanh(v * (GELU_A + GELU_B * square))
            gate = 0.5 + 0.5 * tanh
            act = v * gate
            slope = gate + act * ((1.0 - tanh) * (GELU_A + 3.0 * GELU_B * square))
            grad = (slope * g_ref[at].astype(F32)).astype(BF16)
            act_ref[at] = act.astype(BF16)
            grad_ref[at] = grad
            held[step, at] = grad
            total = total + jnp.sum(grad.astype(F32), axis=0, keepdims=True)
        sum_ref[...] = total

    @pl.when(step >= blocks)
    def _():
        grad = jnp.concatenate([held[n] for n in range(blocks)], axis=1)
        part_ref[...] = dot(grad, row_ref[...], 1, 1).astype(BF16)


def hidden_units(pieces, grads, up, bias):
    model = pieces[0].shape[2]
    tokens, half = grads.shape
    blocks, more = half // BLOCK, model // BLOCK

    def first(g):
        return jnp.minimum(g, blocks - 1)

    def second(g):
        return jnp.maximum(g - blocks, 0)

    column, line = pl.BlockSpec((tokens, BLOCK), lambda g: (0, first(g))), pl.BlockSpec((1, BLOCK), lambda g: (0, first(g)))
    return call(
        functools.partial(hidden_body, blocks), "hidden", (), (blocks + more,),
        [(piece, fixed(piece.shape)) for piece in pieces]
        + [
            (grads, column),
            (up, pl.BlockSpec((model, BLOCK), lambda g: (0, first(g)))),
            (up, pl.BlockSpec((BLOCK, half), lambda g: (second(g), 0))),
            (bias, line),
        ],
        [
            (grads.shape, BF16, column),
            (grads.shape, BF16, column),
            ((1, half), F32, line),
            ((tokens, model), BF16, fixed((tokens, model))),
            ((tokens, model), BF16, pl.BlockSpec((tokens, BLOCK), lambda g: (0, second(g)))),
        ],
        [pltpu.VMEM((blocks, tokens, BLOCK), BF16)]
    )


def middle_back_body(
    order_ref, part_ref, sent_ref, mid_ref, cot_ref, gain_ref, w0, w1, w2, w3,
    grad_ref, low_ref, att0_ref, att1_ref, far_ref, sums_ref,
):
    grad = part_ref[...].astype(F32) + sent_ref[...].astype(F32)
    hat, inverse = centre(mid_ref[0])
    cot = cot_ref[0].astype(F32)
    total = cot + norm_back(grad, gain_ref[...], hat, inverse)
    low = total.astype(BF16)
    grad_ref[0] = total
    low_ref[0] = low
    far_ref[0, 0] = dot(low, w2[...], 1, 1).astype(BF16)
    far_ref[1, 0] = dot(low, w3[...], 1, 1).astype(BF16)
    att1_ref[0] = dot(low, w1[...], 1, 1).astype(BF16)
    att0_ref[0] = dot(low, w0[...], 1, 1).astype(BF16)

    @pl.when(pl.program_id(0) == 0)
    def _():
        sums_ref[...] = jnp.zeros_like(sums_ref)

    sums_ref[0:1] += jnp.sum(grad * hat, axis=0, keepdims=True)
    sums_ref[1:2] += jnp.sum(grad, axis=0, keepdims=True)
    sums_ref[2:3] += jnp.sum(low.astype(F32), axis=0, keepdims=True)
    sums_ref[3:4] += jnp.sum(cot, axis=0, keepdims=True)


def middle_back(order, both, sent, mid, cot, gain, weight, parts, deps=()):
    rows, shard, model = mid.shape
    width = model // parts
    block, one = along((1, shard, model)), along((1, shard, width))
    flat = pl.BlockSpec((shard, model), lambda g, o: (g, 0))
    return call(
        middle_back_body, "middle_back", (order,), (rows,),
        [(both, flat), (sent, flat), (mid, block), (cot, block), (gain, fixed((1, model)))] + out_blocks(weight, parts),
        [
            (mid.shape, F32, block),
            (mid.shape, BF16, block),
            ((rows, shard, width), BF16, one),
            ((rows, shard, width), BF16, one),
            ((2, rows, shard, width), BF16, along((2, 1, shard, width), 1)),
            ((8, model), F32, fixed((8, model))),
        ],
        deps=deps
    )


def norm1_back_body(part_ref, near_ref, far_ref, stream_ref, mid_ref, gain_ref, seg_ref, in_ref, shift_ref, sums_ref):
    grad = part_ref[0].astype(F32) + near_ref[0].astype(F32) + far_ref[0].astype(F32)
    hat, inverse = centre(stream_ref[0])
    total = mid_ref[0] + norm_back(grad, gain_ref[...], hat, inverse)
    in_ref[0] = total.astype(BF16)
    slots = lax.broadcasted_iota(jnp.int32, (SEGS, seg_ref.shape[-1]), 0) == seg_ref[0]
    onehot = slots.astype(F32).astype(BF16)
    shift_ref[0] = dot(jnp.concatenate([onehot, onehot], axis=1), split_low(total))

    @pl.when(pl.program_id(0) == 0)
    def _():
        sums_ref[...] = jnp.zeros_like(sums_ref)

    sums_ref[0:1] += jnp.sum(grad * hat, axis=0, keepdims=True)
    sums_ref[1:2] += jnp.sum(grad, axis=0, keepdims=True)


def norm1_back(start, count, own, near, far, stream, mid, gain, seg, held=(), deps=()):
    rows, shard, model = stream.shape
    block, own_block = along((1, shard, model), 0, start), along((1, shard, model))
    return call(
        norm1_back_body, "norm1_back", (), (count,),
        [(own, own_block), (near, own_block), (far, own_block), (stream, block), (mid, block), (gain, fixed((1, model)))]
        + [(seg, along((1, 1, shard), 0, start))],
        [
            (stream.shape, BF16, block),
            ((count, SEGS, model), F32, along((1, SEGS, model))),
            ((8, model), F32, fixed((8, model))),
        ],
        held=[(array, 0) for array in held], deps=deps
    )


def exchange(own, one, far, *others):
    return [own, swap(one, "c"), far, swap(after(far[1], *others), "c")]


def after(value, *others):
    return lax.optimization_barrier((value,) + others)[0]


def cut(values, index, size, axis):
    return lax.dynamic_slice_in_dim(values, index * size, size, axis)


def add_low(kept, sent):
    return (kept.astype(F32) + sent.astype(F32)).astype(BF16)


def over_z(values, at, depth):
    if depth != 4:
        return lax.psum_scatter(values, "z", scatter_dimension=0, tiled=False)
    total = lax.dynamic_index_in_dim(values, at, 0, keepdims=False).astype(F32)
    for n in range(1, depth):
        sent = lax.dynamic_index_in_dim(values, at ^ n, 0, keepdims=False)
        total = total + lax.ppermute(sent, "z", [(i, i ^ n) for i in range(depth)]).astype(F32)
    return total.astype(BF16)


def ordered(at, own, other, axis):
    return jnp.where(at == 0, jnp.concatenate([own, other], axis), jnp.concatenate([other, own], axis))


def finish_body(blocks, at_ref, d0, d1, u0, u1, l0, l1, down_ref, up_ref, qkv_ref, out_ref):
    c_at = at_ref[0]
    width = u0.shape[1] // (2 * blocks)
    depth = d0.shape[0]
    for c in range(2):
        mine = c_at == c
        down_ref[c * depth : (c + 1) * depth] = jnp.where(mine, d0[...], d1[...]).astype(F32)
        up = jnp.where(mine, u0[...], u1[...]).astype(F32)
        for x in range(2):
            for z in range(blocks):
                at, place = ((2 * z + x) * 2 + c) * width, (x * blocks + z) * width
                up_ref[:, at : at + width] = up[:, place : place + width]
        late = jnp.where(mine, l0[...], l1[...]).astype(F32)
        half = out_ref.shape[1] // 2
        size = half // 2
        out_ref[:, c * half : (c + 1) * half] = late[:, 6 * size :]
        for y in range(2):
            for n in range(3):
                at = n * 4 * size + (2 * y + c) * size
                qkv_ref[:, at : at + size] = late[:, (3 * y + n) * size : (3 * y + n + 1) * size]


def finish(c_at, dp, piece, down, up, late, parts):
    rows, model = up[0].shape[0], down[0].shape[1]
    depth = dp // 2
    if piece % 128 == 0:
        at = c_at.astype(jnp.int32)[None]
        shapes = [(2 * down[0].shape[0], model), (rows, 2 * up[0].shape[1]), (rows, 3 * model), (rows, model)]
        arrays = list(down) + list(up) + list(late)
        return call(
            functools.partial(finish_body, depth), "finish", (at,), (1,),
            [(array, fixed(array.shape)) for array in arrays], [(shape, F32, fixed(shape)) for shape in shapes],
        )
    down_done = ordered(c_at, *down, 0).astype(F32)
    up_done = ordered(c_at, up[0][None], up[1][None], 0).reshape(2, rows, 2, depth, piece)
    up_done = up_done.transpose(1, 3, 2, 0, 4).reshape(rows, -1).astype(F32)
    both = ordered(c_at, late[0][None], late[1][None], 0)
    width = model // parts
    qkv_done = both[:, :, : 6 * width].reshape(2, rows, 2, 3, width).transpose(1, 3, 2, 0, 4)
    qkv_done = qkv_done.reshape(rows, 3 * model).astype(F32)
    out_done = jnp.concatenate([both[0, :, 6 * width :], both[1, :, 6 * width :]], axis=1).astype(F32)
    return down_done, up_done, qkv_done, out_done


def local(
    inputs, segment_ids, doc_times, time_weight, time_bias, norm1_gain, norm1_bias, qkv_weight, qkv_bias,
    out_weight, out_bias, norm2_gain, norm2_bias, up_weight, up_bias, down_weight, down_bias, cotangent,
    *, dp,
):
    rows, shard, model = inputs.shape
    parts = 4
    tokens = rows * shard
    hidden_width = up_weight.shape[1]
    width = model // parts
    depth = dp // 2
    half = hidden_width // 2
    piece = half // dp
    z_at, x_at, y_at, c_at = (lax.axis_index(name) for name in ("z", "x", "y", "c"))
    me = 2 * y_at + c_at

    def line(vector):
        return vector.astype(F32)[None]

    seg_two = swap(segment_ids, "y")
    segs = jnp.stack([segment_ids, swap(segment_ids, "c"), seg_two, swap(seg_two, "c")], axis=1)

    groups = [(0, rows - 1), (rows - 1, 1)] if rows > 1 else [(0, 1)]
    seg = segment_ids[:, None, :]
    features = time_features(doc_times.reshape(rows * SEGS), jnp.arange(TEMB), TEMB // 2)
    time_shift = dot(features, time_weight).reshape(rows, SEGS, model) + time_bias.astype(F32)
    stream, own1 = norm1(inputs, seg, time_shift, line(norm1_gain), line(norm1_bias))
    own1, segs = lax.optimization_barrier((own1, segs))
    two1 = swap(own1, "y")
    one1 = swap(own1, "c")

    me, x_at, z_at, c_at, y_at, _ = lax.optimization_barrier((me, x_at, z_at, c_at, y_at, own1))
    order = [me ^ i for i in range(parts)]
    order_list = jnp.stack(order).astype(jnp.int32)
    me_list = order_list[:1]
    low_id, high_id = segs.min(axis=2), segs.max(axis=2)
    act = (low_id[:, :, None] <= high_id[:, None, :]) & (low_id[:, None, :] <= high_id[:, :, None])
    places = jnp.arange(parts, dtype=jnp.int32)
    rank = jnp.cumsum(act.astype(jnp.int32), axis=2) - 1
    chosen = act[..., None] & (rank[..., None] == places)
    idx = jnp.sum(jnp.where(chosen, places[:, None], 0), axis=2).astype(jnp.int32).reshape(-1)
    cnt = jnp.sum(act.astype(jnp.int32), axis=2).reshape(-1)
    positions = jnp.stack([o * shard + jnp.arange(shard, dtype=jnp.int32) for o in order])
    cos_tab, sin_tab = rotary_tables(positions, HEAD_DIM)

    cot = cotangent.reshape(tokens, model)
    cot_other = swap(cot, "c")
    turned = jnp.stack([1 - x_at, x_at])
    if piece % BLOCK == 0:
        blk = ((jnp.arange(depth)[None, :] * 2 + turned[:, None]) * 2 + c_at) * (piece // BLOCK)
        blk = (blk[..., None] + jnp.arange(piece // BLOCK)).reshape(-1).astype(jnp.int32)
        up_from, down_from = up_weight, down_weight
    else:
        blk = jnp.zeros((half // BLOCK,), jnp.int32)
        up_from = up_weight.reshape(model, depth, 2, 2, piece)
        up_from = lax.dynamic_index_in_dim(up_from, c_at, 3, keepdims=False)
        up_from = jnp.where(x_at == 1, up_from, up_from[:, :, ::-1]).transpose(0, 2, 1, 3).reshape(model, half)
        down_from = down_weight.reshape(depth, 2, 2, piece, model)
        down_from = lax.dynamic_index_in_dim(down_from, c_at, 2, keepdims=False)
        down_from = jnp.where(x_at == 1, down_from, down_from[:, ::-1]).transpose(1, 0, 2, 3).reshape(half, model)
    grad_act, up_own, down_own, cot_both = cot_down(
        blk, cot, cot_other, up_from, down_from, piece % BLOCK != 0, half
    )
    up_bias_own = lax.dynamic_index_in_dim(up_bias.reshape(depth, 2, 2, piece), c_at, 2, keepdims=False)
    up_bias_own = jnp.where(x_at == 1, up_bias_own, up_bias_own[:, ::-1]).transpose(1, 0, 2).reshape(half)

    bias_line = qkv_bias.reshape(1, 3 * model)
    qkv, normed1_all, qkv_own = project_qkv(
        0, parts, me_list, own1, one1, qkv_weight, bias_line, cos_tab, sin_tab, (), (grad_act,)
    )
    two1 = after(two1, qkv)
    qkv, normed1_all, _ = project_qkv(
        1, parts, me_list, two1, swap(two1, "c"), qkv_weight, bias_line, cos_tab, sin_tab, (qkv, normed1_all)
    )
    o, lse, attended = None, None, []
    for start, count in groups:
        held = () if o is None else (o, lse)
        o, out_one, out_far, lse = attend(start, count, cnt, idx, qkv, segs, held)
        attended.append((out_one, swap(out_far, "y")))
    held, normed2, normed2_other = (), [], []
    for (start, count), values in zip(groups, attended):
        values = exchange(o, *values, o)
        middle, low, attended_all = middle_norm(
            start, count, order_list, values, out_weight, stream, line(out_bias), line(norm2_gain), line(norm2_bias), held
        )
        held = (middle, attended_all)
        normed2.append(low)
        normed2_other.append(swap(low, "c"))

    active, grad_hidden, up_b, normed2_both, part2 = hidden_units(
        normed2 + normed2_other, grad_act, up_own, line(up_bias_own)
    )
    part2_sent = swap(part2[tokens:], "c")
    grad_middle, grad_middle_low, att0, att1, far, sums2 = middle_back(
        order_list, part2, part2_sent, middle, cotangent, line(norm2_gain), out_weight, parts
    )
    far = swap(far, "y")
    sums2 = sums2[:4]

    active_late, grad_hidden_late = lax.optimization_barrier((active, grad_hidden, att0))[:2]
    up_grad = dot(normed2_both, grad_hidden_late, 0, 0).astype(BF16)
    up_half = (x_at == y_at).astype(jnp.int32)
    up_sent = swap(cut(up_grad, 1 - up_half, half // 2, 1), "y")
    down_out = dot(active_late[:, : half // 2], cot_both, 0, 0).astype(BF16)
    down_sent = swap(down_out, "x")
    active_late = after(active_late, down_out, up_grad, far)
    down_kept = dot(active_late[:, half // 2 :], cot_both, 0, 0).astype(BF16)
    feed_sent = swap(dot(active_late[tokens:], down_own).astype(BF16), "c")
    feed = dot(active_late[:tokens], down_own) + feed_sent.astype(F32) + line(down_bias)
    output = (middle + feed.reshape(rows, shard, model)).astype(BF16)
    out_grad = dot(
        attended_all.reshape(tokens, model), grad_middle_low.reshape(tokens, model), 0, 0
    ).astype(BF16)

    grad_o = exchange(att0, att1, far, down_kept, output, out_grad)
    grad_qkv, back = (), []
    deps = (down_kept, output, out_grad)
    for start, count in groups:
        grad_qkv, own, one, two, three = attend_back(
            start, count, cnt, idx, qkv, o, grad_o, lse, segs, cos_tab, sin_tab, qkv_own, grad_qkv, deps
        )
        grad_qkv = (grad_qkv,)
        there = add_low(two, swap(three, "c"))
        if back:
            there = after(there, back[-1][2])
        else:
            down_x = add_low(down_kept, down_sent)
            down_z = lax.psum_scatter(down_x, "z", scatter_dimension=0, tiled=True)
        deps = (there, down_x)
        back.append((own, swap(one, "c"), swap(there, "y")))
    up_rows = model // dp
    up_y = add_low(cut(after(up_grad, there), up_half, half // 2, 1), up_sent).reshape(depth, 2 * up_rows, half // 2)
    up_sent = swap(cut(up_y, 1 - x_at, up_rows, 1), "x")
    out_grad = jnp.concatenate([cut(out_grad, o_at, width, 0) for o_at in order], axis=0)
    out_c = add_low(cut(out_grad, c_at, model // 2, 1), swap(cut(out_grad, 1 - c_at, model // 2, 1), "c"))
    out_c = out_c.reshape(depth, 2 * up_rows, model // 2)
    out_x = add_low(cut(out_c, x_at, up_rows, 1), swap(cut(out_c, 1 - x_at, up_rows, 1), "x"))
    grad_qkv = after(grad_qkv[0], there, up_y).reshape(parts * tokens, 3 * width)
    qkv_grad = dot(normed1_all.reshape(parts * tokens, model), grad_qkv, 0, 0).astype(BF16)
    qkv_b = jnp.sum(grad_qkv.astype(F32), axis=0)
    qkv_grad = qkv_grad.reshape(depth, 2 * up_rows, 3 * width)
    qkv_sent = swap(cut(qkv_grad, 1 - x_at, up_rows, 1), "x")
    up_x = add_low(cut(up_y, x_at, up_rows, 1), up_sent)
    up_z = lax.psum_scatter(up_x, "z", scatter_dimension=0, tiled=False)
    held, grad_shift, sums1 = (), [], 0.0
    deps = (qkv_grad,)
    for (start, count), values in zip(groups, back):
        input_grad, found, sums = norm1_back(
            start, count, *values, stream, grad_middle, line(norm1_gain), seg, held, deps
        )
        deps = (up_x,)
        held = (input_grad,)
        grad_shift.append(found.reshape(count * SEGS, model))
        sums1 = sums1 + sums[:2]

    qkv_x = add_low(cut(qkv_grad, x_at, up_rows, 1), qkv_sent)
    late = over_z(jnp.concatenate([qkv_x, out_x], axis=2), z_at, depth)
    late_sent = swap(late, "y")
    qkv_y = ordered(y_at, late[None, :, : 3 * width], late_sent[None, :, : 3 * width], 0)
    out_y = add_low(late[:, 3 * width :], late_sent[:, 3 * width :])
    late = jnp.concatenate([qkv_y[0], qkv_y[1], out_y], axis=1)
    late_other = swap(late, "c")
    down_y = add_low(down_z, swap(down_z, "y"))
    down_other = swap(down_y, "c")
    up_done = ordered(y_at, up_z, swap(up_z, "y"), 1)
    up_other = swap(up_done, "c")

    down_done, up_done, qkv_done, out_done = finish(
        c_at, dp, piece, (down_y, down_other), (up_done, up_other), (late, late_other), parts
    )

    up_b = up_b.reshape(2, depth, 1, piece)
    up_b = jnp.where(x_at == 1, up_b, up_b[::-1]).transpose(1, 0, 2, 3)
    up_b = jnp.where(jnp.arange(2)[:, None] == c_at, up_b, 0.0).reshape(-1, model)
    qkv_b = jnp.where(jnp.arange(parts)[:, None] == me, qkv_b.reshape(3, 1, width), 0.0).reshape(3, model)
    times = doc_times.reshape(1, rows * SEGS)
    times = jnp.concatenate([times // 32, times % 32], axis=1).astype(F32)
    times = jnp.pad(times, ((0, 0), (0, model - times.shape[1])))
    small = jnp.concatenate(grad_shift + [sums1, sums2, qkv_b, up_b, times], axis=0)
    small = add_low(small, swap(small.astype(BF16), "c"))
    small = add_low(small, swap(small, "y"))
    small = ordered(x_at, small[None], swap(small, "x")[None], 0)
    if depth == 4:
        others = [lax.ppermute(small, "z", [(i, i ^ n) for i in range(depth)]) for n in range(1, depth)]
        small = jnp.stack([small] + others)
        small = jnp.stack([lax.dynamic_index_in_dim(small, z_at ^ n, 0, keepdims=False) for n in range(depth)])
    else:
        small = lax.all_gather(small, "z")
    small = small.reshape(dp, small.shape[2], model)
    all_times = small[:, -1, : 2 * rows * SEGS].astype(F32) * 0.25
    all_times = all_times[:, : rows * SEGS] * 32.0 + all_times[:, rows * SEGS :]
    shifts = small[:, : rows * SEGS].reshape(dp * rows * SEGS, model)
    columns = (2 * z_at + x_at) * (TEMB // dp) + jnp.arange(TEMB // dp)
    wanted = time_features(all_times.reshape(-1), columns, TEMB // 2)
    time_w_done = dot(wanted, shifts, 0, 0)
    sums = jnp.sum(small[:, rows * SEGS :].astype(F32), axis=0)
    dp_at = 2 * z_at + x_at

    def share(vector):
        return cut(vector.reshape(-1), dp_at, vector.size // dp, 0)

    time_b_done = jnp.sum(cut(shifts, dp_at, up_rows, 1).astype(F32), axis=0)
    return (
        output, input_grad, time_w_done, time_b_done, share(sums[0]), share(sums[1]), qkv_done, share(sums[6:9]),
        out_done, share(sums[4]), share(sums[2]), share(sums[3]), up_done, share(sums[9:-1]), down_done, share(sums[5]),
    )


def solution(mesh):
    dp, seq = mesh.shape["dp"], mesh.shape["seq"]
    fine = Mesh(mesh.devices.reshape(dp // 2, 2, seq // 2, 2), ("z", "x", "y", "c"))
    rows, seqs = ("z", "x"), ("y", "c")
    placed = (P(rows, seqs, None), P(rows, seqs), P(rows, None)) + (P(),) * 14 + (P(rows, seqs, None),)
    vec, mat = P(rows), P(rows, None)
    return jax.shard_map(
        functools.partial(local, dp=dp),
        mesh=fine,
        in_specs=placed,
        out_specs=(
            P(rows, seqs, None), P(rows, seqs, None), mat, vec, vec, vec, mat, vec, mat, vec, vec, vec, mat, vec, mat, vec,
        ),
        check_vma=False,
    )
```

```python
import functools
import math

import jax
import jax.numpy as jnp
from jax import lax
from jax.experimental import pallas as pl
from jax.experimental.pallas import tpu as pltpu
from jax.sharding import Mesh, PartitionSpec as P

HEADS = 16
HEAD_DIM = 64
TEMB = 256
SEGS = 8
EPSILON = 1e-05
F32 = jnp.float32
BF16 = jnp.bfloat16
NEG = -1e30
LOG2E = math.log2(math.e)
GELU_A = math.sqrt(2.0 / math.pi)
GELU_B = GELU_A * 0.044715
BLOCK = 256
VMEM = 60 * 1024 * 1024


def swap(value, axis):
    return lax.ppermute(value, axis, [(0, 1), (1, 0)])


def time_features(doc_times, column, half_size):
    frequency = jnp.exp(-math.log(10000.0) * (column % half_size).astype(F32) / half_size)
    angles = doc_times.astype(F32)[..., None] * frequency
    return jnp.where(column < half_size, jnp.sin(angles), jnp.cos(angles)).astype(BF16)


def rotary_tables(positions, head_size):
    half_size = head_size // 2
    frequency = jnp.exp(-math.log(10000.0) * 2.0 * jnp.arange(half_size, dtype=F32) / head_size)
    angles = positions.astype(F32)[..., None] * frequency
    cos_tab, sin_tab = jnp.cos(angles), jnp.sin(angles)
    return (
        jnp.concatenate([cos_tab] * 4, axis=-1),
        jnp.concatenate([-sin_tab, sin_tab, -sin_tab, sin_tab], axis=-1),
    )


def dot(left_op, right_op, left_dim=1, right_dim=0):
    return lax.dot_general(
        left_op, right_op, (((left_dim,), (right_dim,)), ((), ())), preferred_element_type=F32
    )


def turn(values, cos_tab, sin_tab):
    slabs = []
    lane = lax.broadcasted_iota(jnp.int32, (values.shape[0], 128), 1)
    first = lane % HEAD_DIM < HEAD_DIM // 2
    for start in range(0, values.shape[1], 128):
        slab = values[:, start : start + 128]
        partner = jnp.where(
            first, pltpu.roll(slab, 128 - HEAD_DIM // 2, 1), pltpu.roll(slab, HEAD_DIM // 2, 1)
        )
        slabs.append(slab * cos_tab + partner * sin_tab)
    return jnp.concatenate(slabs, axis=1)


def split_low(values):
    high = values.astype(BF16)
    return jnp.concatenate([high, (values - high.astype(F32)).astype(BF16)], axis=0)


def centre(values):
    scale = 1.0 / values.shape[-1]
    centred = values - jnp.sum(values, axis=-1, keepdims=True) * scale
    spread = jnp.sum(centred * centred, axis=-1, keepdims=True) * scale
    inverse = lax.rsqrt(spread + EPSILON)
    return centred * inverse, inverse


def norm_back(grad, gain, hat, inverse):
    scale = 1.0 / grad.shape[-1]
    scaled = grad * gain
    mean = jnp.sum(scaled, axis=-1, keepdims=True) * scale
    along = jnp.sum(scaled * hat, axis=-1, keepdims=True) * scale
    return inverse * (scaled - mean - hat * along)


def call(body, name, prefetch, grid, ins, outs, scratch=(), deps=(), held=()):
    count = len(prefetch) + len(ins)
    extra = [array for array, _ in held] + list(deps)

    def kernel(*refs):
        body(*refs[:count], *refs[count + len(extra) :])

    return pl.pallas_call(
        kernel,
        grid_spec=pltpu.PrefetchScalarGridSpec(
            num_scalar_prefetch=len(prefetch),
            grid=grid,
            in_specs=[spec for _, spec in ins] + [pl.BlockSpec(memory_space=pl.ANY)] * len(extra),
            out_specs=[spec for _, _, spec in outs],
            scratch_shapes=list(scratch),
        ),
        out_shape=[jax.ShapeDtypeStruct(shape, kind) for shape, kind, _ in outs],
        input_output_aliases={count + n: out for n, (_, out) in enumerate(held)},
        compiler_params=pltpu.CompilerParams(vmem_limit_bytes=VMEM),
        name=name,
    )(*prefetch, *[array for array, _ in ins], *extra)


def fixed(shape):
    return pl.BlockSpec(shape, lambda *_: (0,) * len(shape))


def along(shape, axis=0, start=0):
    return pl.BlockSpec(shape, lambda g, *_: tuple(start + g if n == axis else 0 for n in range(len(shape))))


def norm1_body(x_ref, seg_ref, shift_ref, gain_ref, bias_ref, stream_ref, low_ref):
    slots = lax.broadcasted_iota(jnp.int32, (SEGS, seg_ref.shape[-1]), 0) == seg_ref[0]
    onehot = slots.astype(F32).astype(BF16)
    added = dot(jnp.concatenate([onehot, onehot], axis=0), split_low(shift_ref[0]), 0, 0)
    stream = x_ref[0].astype(F32) + added
    hat, _ = centre(stream)
    stream_ref[0] = stream
    low_ref[0] = (hat * gain_ref[...] + bias_ref[...]).astype(BF16)


def norm1(x, seg, shift, gain, bias):
    rows, shard, model = x.shape
    block = along((1, shard, model))
    return call(
        norm1_body, "norm1", (), (rows,),
        [(x, block), (seg, along((1, 1, shard))), (shift, along((1, SEGS, model))), (gain, fixed((1, model))), (bias, fixed((1, model)))],
        [(x.shape, F32, block), (x.shape, BF16, block)],
    )


def qkv_body(me_ref, a_ref, b_ref, w_ref, bias_ref, cos_ref, sin_ref, out_ref, all_ref, own_ref):
    rows, shard, model = a_ref.shape
    width = w_ref.shape[1]
    refs = (a_ref, b_ref)
    step = pl.program_id(0)

    @pl.when(step == 0)
    def _():
        for n, x_ref in enumerate(refs):
            all_ref[n] = x_ref[...]

    def run(turned):
        w, bias = w_ref[...], bias_ref[...].astype(F32)
        found = [dot(x_ref[...].reshape(rows * shard, model), w) for x_ref in refs]
        for n, full in enumerate(found):
            for r in range(rows):
                values = full[r * shard : (r + 1) * shard] + bias
                if turned:
                    values = turn(values, cos_ref[n], sin_ref[n]) * jnp.where(step == 0, LOG2E * HEAD_DIM**-0.5, 1.0)
                out_ref[0, n, r] = values.astype(BF16)

    own_ref[...] = w_ref[...].T

    @pl.when(step < 2)
    def _():
        run(True)

    @pl.when(step == 2)
    def _():
        run(False)


def project_qkv(pair, parts, me, first, second, weight, bias, cos_tab, sin_tab, held=(), deps=()):
    rows, shard, model = first.shape
    width = model // parts
    return call(
        qkv_body, "qkv", (me,), (3,),
        [(first, fixed(first.shape)), (second, fixed(first.shape))]
        + [
            (weight, pl.BlockSpec((model, width), lambda g, m: (0, g * parts + m[0]))),
            (bias, pl.BlockSpec((1, width), lambda g, m: (0, g * parts + m[0]))),
            (cos_tab, pl.BlockSpec((2, shard, 128), lambda g, m: (pair, 0, 0))),
            (sin_tab, pl.BlockSpec((2, shard, 128), lambda g, m: (pair, 0, 0))),
        ],
        [
            ((3, parts, rows, shard, width), BF16, pl.BlockSpec((1, 2, rows, shard, width), lambda g, m: (g, pair, 0, 0, 0))),
            ((parts, rows, shard, model), BF16, pl.BlockSpec((2, rows, shard, model), lambda g, m: (pair, 0, 0, 0))),
            ((3 * width, model), BF16, along((width, model))),
        ],
        held=[(array, n) for n, array in enumerate(held)], deps=deps
    )


def seg_columns(segq_all, segk):
    pieces, shard, _ = segk.shape
    for j in range(pieces):
        row = jnp.broadcast_to(segq_all[j:j+1].astype(F32), (128, shard))
        segk[j] = row.T

def attend_body(start, cnt_ref, idx_ref, qkv_ref, seg_ref, o_ref, one_ref, far_ref, lse_ref, vt, segk, qmt, acc):
    row = pl.program_id(0) + start
    _, pieces, _, shard, width = qkv_ref.shape
    heads = width // HEAD_DIM

    @pl.when(pl.program_id(0) == 0)
    def _():
        qmt[...] = jnp.zeros_like(qmt)

    for j in range(pieces):
        vt[j] = qkv_ref[2, j, 0].T
        qt = qkv_ref[0, j, 0].T
        for h in range(heads):
            at = slice(h * HEAD_DIM, (h + 1) * HEAD_DIM)
            qmt[j, at, h * shard : (h + 1) * shard] = qt[at]
    seg_columns(seg_ref[0], segk)

    @pl.loop(0, pieces)
    def _(piece):
        attend_piece(row * pieces + piece, piece, cnt_ref, idx_ref, qkv_ref.at[1], seg_ref, lse_ref, vt, segk, qmt, acc)

    for j in range(pieces):
        o_ref[j, 0] = acc[j].T.astype(BF16)
    one_ref[0] = o_ref[1, 0]
    far_ref[:, 0] = o_ref[2:, 0]


def attend_piece(at_q, piece, cnt_ref, idx_ref, k_ref, seg_ref, lse_ref, vt, segk, qmt, acc):
    pieces, _, shard, width = k_ref.shape
    heads = width // HEAD_DIM
    seg_q = seg_ref[0, pl.ds(piece, 1)].astype(F32)

    def run(count):
        @pl.when(cnt_ref[at_q] == count)
        def _():
            qm = qmt[piece]
            places = [idx_ref[at_q * pieces + t] for t in range(count)]
            top, tot, out = [None] * heads, [None] * heads, [None] * heads
            later = dot(k_ref[places[0], 0], qm)
            for t in range(count):
                s = later
                if t + 1 < count:
                    later = dot(k_ref[places[t + 1], 0], qm)
                col = segk[places[t]]
                same = jnp.concatenate([col] * (shard // 128), axis=1) == seg_q
                for h in range(heads):
                    at = slice(h * HEAD_DIM, (h + 1) * HEAD_DIM)
                    sh = jnp.where(same, s[:, h * shard : (h + 1) * shard], NEG)
                    best = jnp.max(sh, axis=0, keepdims=True)
                    if t:
                        best = jnp.maximum(top[h], best)
                        fade = jnp.exp2(top[h] - best)
                    p = jnp.exp2(sh - best)
                    total = jnp.sum(p, axis=0, keepdims=True)
                    found = dot(vt[places[t], at], p.astype(BF16))
                    if t:
                        total = tot[h] * fade + total
                        found = out[h] * fade + found
                    top[h], tot[h], out[h] = best, total, found
            for h in range(heads):
                acc[piece, h * HEAD_DIM : (h + 1) * HEAD_DIM] = out[h] / tot[h]
                lse_ref[0, piece, h : h + 1] = top[h] + jnp.log2(tot[h])

    for count in range(1, pieces + 1):
        run(count)


def attend(start, count, cnt, idx, qkv, seg, held=()):
    _, pieces, rows, shard, width = qkv.shape
    heads = width // HEAD_DIM
    pairs = count * (pieces * shard) ** 2
    return call(
        functools.partial(attend_body, start), "attend", (cnt, idx), (count,),
        [(qkv, along((3, pieces, 1, shard, width), 2, start)), (seg, along((1, pieces, shard), 0, start))],
        [
            ((pieces, rows, shard, width), BF16, along((pieces, 1, shard, width), 1, start)),
            ((count, shard, width), BF16, along((1, shard, width))),
            ((2, count, shard, width), BF16, along((2, 1, shard, width), 1)),
            ((rows, pieces, 8, shard), F32, along((1, pieces, 8, shard), 0, start)),
        ],
        [
            pltpu.VMEM((pieces, width, shard), BF16),
            pltpu.VMEM((pieces, shard, 128), F32),
            pltpu.VMEM((pieces, width, heads * shard), BF16),
            pltpu.VMEM((pieces, width, shard), F32),
        ],
        held=list(zip(held, (0, 3)))
    )


def attend_back_body(
    start, cnt_ref, idx_ref, qkv_ref, o_ref, do0, do1, do2, do3, lse_ref, seg_ref, cos_ref, sin_ref, w_ref,
    g_ref, p0_ref, p1_ref, p2_ref, p3_ref, kt, segk, dk, dv, dqt, qmt, gmt, qst, gst, low,
):
    row = pl.program_id(0) + start
    _, pieces, _, shard, width = qkv_ref.shape
    heads = width // HEAD_DIM

    @pl.when(pl.program_id(0) == 0)
    def _():
        qmt[...] = jnp.zeros_like(qmt)
        gmt[...] = jnp.zeros_like(gmt)

    seg_columns(seg_ref[0], segk)
    dk[...] = jnp.zeros_like(dk)
    dv[...] = jnp.zeros_like(dv)
    lane = lax.broadcasted_iota(jnp.int32, (shard, width), 1) // HEAD_DIM
    chosen = lax.broadcasted_iota(jnp.int32, (8, width), 1) // HEAD_DIM
    chosen = (chosen == lax.broadcasted_iota(jnp.int32, (8, width), 0)).astype(BF16)
    for j, do_ref in enumerate((do0, do1, do2, do3)):
        kt[j] = qkv_ref[1, j, 0].T
        q, do = qkv_ref[0, j, 0], do_ref[...].reshape(shard, width)
        qt, gt = q.T, do.T
        for h in range(heads):
            at, qa = slice(h * HEAD_DIM, (h + 1) * HEAD_DIM), slice(h * shard, (h + 1) * shard)
            qmt[j, at, qa] = qt[at]
            gmt[j, at, qa] = gt[at]
            qst[j, qa] = jnp.where(lane == h, q, jnp.zeros_like(q))
            gst[j, qa] = jnp.where(lane == h, do, jnp.zeros_like(do))
        prod = do.astype(F32) * o_ref[j, 0].astype(F32)
        high = prod.astype(BF16)
        low[j] = dot(chosen, high, 1, 1) + dot(chosen, (prod - high.astype(F32)).astype(BF16), 1, 1)

    @pl.loop(0, pieces)
    def _(piece):
        back_piece(
            row * pieces + piece, piece, cnt_ref, idx_ref, qkv_ref.at[1], qkv_ref.at[2], lse_ref, seg_ref,
            kt, segk, dk, dv, dqt, qmt, gmt, qst, gst, low,
        )

    for j, ref in ((1, p1_ref), (3, p3_ref), (0, p0_ref), (2, p2_ref)):
        grad_q = turn(dqt[j].T * HEAD_DIM**-0.5, cos_ref[j], -sin_ref[j]).astype(BF16)
        grad_k = turn(dk[j] * (1 / LOG2E), cos_ref[j], -sin_ref[j]).astype(BF16)
        grad = jnp.concatenate([grad_q, grad_k, dv[j].astype(BF16)], axis=1)
        g_ref[j, 0] = grad
        ref[0] = dot(grad, w_ref[...]).astype(BF16)


def back_piece(
    at_q, piece, cnt_ref, idx_ref, k_ref, v_ref, lse_ref, seg_ref, kt, segk, dk, dv, dqt, qmt, gmt, qst, gst, low
):
    pieces, _, shard, width = k_ref.shape
    heads = width // HEAD_DIM
    lse, delta = lse_ref[0, piece], low[piece]
    seg_q = seg_ref[0, pl.ds(piece, 1)].astype(F32)

    def run(count):
        @pl.when(cnt_ref[at_q] == count)
        def _():
            places = [idx_ref[at_q * pieces + t] for t in range(count)]
            qm, gm = qmt[piece], gmt[piece]
            later = dot(k_ref[places[0], 0], qm), dot(v_ref[places[0], 0], gm)
            out = [None] * heads
            for t in range(count):
                s, dp = later
                j = places[t]
                if t + 1 < count:
                    later = dot(k_ref[places[t + 1], 0], qm), dot(v_ref[places[t + 1], 0], gm)
                col = segk[j]
                same = jnp.concatenate([col] * (shard // 128), axis=1) == seg_q
                ps, dss = [], []
                for h in range(heads):
                    at, qa = slice(h * HEAD_DIM, (h + 1) * HEAD_DIM), slice(h * shard, (h + 1) * shard)
                    p = jnp.exp2(jnp.where(same, s[:, qa] - lse[h : h + 1], NEG))
                    ds = (p * (dp[:, qa] - delta[h : h + 1])).astype(BF16)
                    ps.append(p.astype(BF16))
                    dss.append(ds)
                    found = dot(kt[j, at], ds)
                    out[h] = found if t == 0 else out[h] + found
                dv[j] += dot(jnp.concatenate(ps, axis=1), gst[piece])
                dk[j] += dot(jnp.concatenate(dss, axis=1), qst[piece])
            for h in range(heads):
                dqt[piece, h * HEAD_DIM : (h + 1) * HEAD_DIM] = out[h]

    for count in range(1, pieces + 1):
        run(count)


def attend_back(start, count, cnt, idx, qkv, o, do, lse, seg, cos_tab, sin_tab, weight, held=(), deps=()):
    _, pieces, rows, shard, width = qkv.shape
    model = weight.shape[1]
    heads = width // HEAD_DIM
    table = fixed((pieces, shard, 128))
    pairs = count * (pieces * shard) ** 2
    square, wide = (pieces, width, heads * shard), (pieces, shard, width)
    one = along((1, shard, width), 0, start)
    return call(
        functools.partial(attend_back_body, start), "attend_back", (cnt, idx), (count,),
        [(qkv, along((3, pieces, 1, shard, width), 2, start)), (o, along((pieces, 1, shard, width), 1, start))]
        + [(do[0], one), (do[1], one), (do[2], along((1, 1, shard, width), 1, start)), (do[3], one)]
        + [(lse, along((1, pieces, 8, shard), 0, start)), (seg, along((1, pieces, shard), 0, start))]
        + [(cos_tab, table), (sin_tab, table), (weight, fixed(weight.shape))],
        [((pieces, rows, shard, 3 * width), BF16, along((pieces, 1, shard, 3 * width), 1, start))]
        + [((count, shard, model), BF16, along((1, shard, model)))] * pieces,
        [
            pltpu.VMEM((pieces, width, shard), BF16),
            pltpu.VMEM((pieces, shard, 128), F32),
            pltpu.VMEM(wide, F32),
            pltpu.VMEM(wide, F32),
            pltpu.VMEM((pieces, width, shard), F32),
            pltpu.VMEM(square, BF16),
            pltpu.VMEM(square, BF16),
            pltpu.VMEM((pieces, heads * shard, width), BF16),
            pltpu.VMEM((pieces, heads * shard, width), BF16),
            pltpu.VMEM((pieces, 8, shard), F32),
        ],
        held=[(array, 0) for array in held], deps=deps
    )


def middle_body(
    order_ref, a0, a1, a2, a3, w0, w1, w2, w3, stream_ref, bias_ref, gain_ref, shift_ref, mid_ref, low_ref, all_ref,
):
    _, shard, model = stream_ref.shape
    total = 0.0
    for n, (a, w) in enumerate(((a0, w0), (a1, w1), (a2, w2), (a3, w3))):
        values = a[...].reshape(shard, a.shape[-1])
        total = total + dot(values, w[...])
        all_ref[0, :, n * a.shape[-1] : (n + 1) * a.shape[-1]] = values
    mid = stream_ref[0] + (total + bias_ref[...])
    hat, _ = centre(mid)
    mid_ref[0] = mid
    low_ref[0] = (hat * gain_ref[...] + shift_ref[...]).astype(BF16)


def out_blocks(weight, parts):
    width = weight.shape[0] // parts

    def block(i):
        return pl.BlockSpec((width, weight.shape[1]), lambda g, o: (o[i], 0))

    return [(weight, block(i)) for i in range(parts)]


def middle_norm(start, count, order, attended, weight, stream, bias, gain, shift, held=()):
    rows, shard, model = stream.shape
    parts = len(attended)
    width = model // parts
    block, line, one = along((1, shard, model), 0, start), fixed((1, model)), along((1, shard, width))
    first = [along((1, 1, shard, width), 1, start), one, along((1, 1, shard, width), 1), one]
    return call(
        middle_body, "middle", (order,), (count,),
        list(zip(attended, first)) + out_blocks(weight, parts) + [(stream, block), (bias, line), (gain, line), (shift, line)],
        [
            (stream.shape, F32, block),
            ((count, shard, model), BF16, along((1, shard, model))),
            (stream.shape, BF16, block),
        ],
        held=list(zip(held, (0, 2)))
    )


def cot_body(blk_ref, a_ref, b_ref, up_ref, down_ref, g_ref, up_out, down_out, both_ref):
    tokens = a_ref.shape[0]
    down = down_ref[...]

    @pl.when(pl.program_id(0) == 0)
    def _():
        both_ref[0:tokens] = a_ref[...]
        both_ref[tokens:] = b_ref[...]

    g_ref[0:tokens] = dot(a_ref[...], down, 1, 1).astype(BF16)
    g_ref[tokens:] = dot(b_ref[...], down, 1, 1).astype(BF16)
    up_out[...] = up_ref[...]
    down_out[...] = down


def cot_down(blk, own, other, up, down, picked, half):
    tokens, model = own.shape
    steps = half // BLOCK
    column = along((2 * tokens, BLOCK), 1)
    if picked:
        up_at, down_at = along((model, BLOCK), 1), along((BLOCK, model))
    else:
        up_at = pl.BlockSpec((model, BLOCK), lambda g, b: (0, b[g]))
        down_at = pl.BlockSpec((BLOCK, model), lambda g, b: (b[g], 0))
    return call(
        cot_body, "cot_down", (blk,), (steps,),
        [(own, fixed(own.shape)), (other, fixed(own.shape)), (up, up_at), (down, down_at)],
        [
            ((2 * tokens, half), BF16, column),
            ((model, half), BF16, along((model, BLOCK), 1)),
            ((half, model), BF16, along((BLOCK, model))),
            ((2 * tokens, model), BF16, fixed((2 * tokens, model))),
        ]
    )


def hidden_body(blocks, *refs):
    pieces, refs = refs[:-10], refs[-10:]
    g_ref, up_ref, row_ref, bias_ref, act_ref, grad_ref, sum_ref, both_ref, part_ref, held = refs
    sizes = [ref.shape[0] * ref.shape[1] for ref in pieces]
    starts = [sum(sizes[:n]) for n in range(len(sizes))]
    step = pl.program_id(0)

    @pl.when(step == 0)
    def _():
        for ref, at, size in zip(pieces, starts, sizes):
            both_ref[at : at + size] = ref[...].reshape(size, ref.shape[2])

    @pl.when(step < blocks)
    def _():
        up, bias = up_ref[...], bias_ref[...]
        total = 0.0
        later = dot(pieces[0][...].reshape(sizes[0], -1), up)
        for n, (start, size) in enumerate(zip(starts, sizes)):
            at = slice(start, start + size)
            v = later + bias
            if n + 1 < len(pieces):
                later = dot(pieces[n + 1][...].reshape(sizes[n + 1], -1), up)
            square = v * v
            tanh = jnp.tanh(v * (GELU_A + GELU_B * square))
            gate = 0.5 + 0.5 * tanh
            act = v * gate
            slope = gate + act * ((1.0 - tanh) * (GELU_A + 3.0 * GELU_B * square))
            grad = (slope * g_ref[at].astype(F32)).astype(BF16)
            act_ref[at] = act.astype(BF16)
            grad_ref[at] = grad
            held[step, at] = grad
            total = total + jnp.sum(grad.astype(F32), axis=0, keepdims=True)
        sum_ref[...] = total

    @pl.when(step >= blocks)
    def _():
        grad = jnp.concatenate([held[n] for n in range(blocks)], axis=1)
        part_ref[...] = dot(grad, row_ref[...], 1, 1).astype(BF16)


def hidden_units(pieces, grads, up, bias):
    model = pieces[0].shape[2]
    tokens, half = grads.shape
    blocks, more = half // BLOCK, model // BLOCK

    def first(g):
        return jnp.minimum(g, blocks - 1)

    def second(g):
        return jnp.maximum(g - blocks, 0)

    column, line = pl.BlockSpec((tokens, BLOCK), lambda g: (0, first(g))), pl.BlockSpec((1, BLOCK), lambda g: (0, first(g)))
    return call(
        functools.partial(hidden_body, blocks), "hidden", (), (blocks + more,),
        [(piece, fixed(piece.shape)) for piece in pieces]
        + [
            (grads, column),
            (up, pl.BlockSpec((model, BLOCK), lambda g: (0, first(g)))),
            (up, pl.BlockSpec((BLOCK, half), lambda g: (second(g), 0))),
            (bias, line),
        ],
        [
            (grads.shape, BF16, column),
            (grads.shape, BF16, column),
            ((1, half), F32, line),
            ((tokens, model), BF16, fixed((tokens, model))),
            ((tokens, model), BF16, pl.BlockSpec((tokens, BLOCK), lambda g: (0, second(g)))),
        ],
        [pltpu.VMEM((blocks, tokens, BLOCK), BF16)]
    )


def sent_body(half_ref, both_ref, cot_ref, out_ref, keep_ref, act_ref, up_out, up_keep, down_out):
    both = both_ref[...]
    down_out[...] = dot(act_ref[...], cot_ref[...], 0, 0).astype(BF16)
    up_out[...] = dot(both, out_ref[...], 0, 0).astype(BF16)
    up_keep[...] = dot(both, keep_ref[...], 0, 0).astype(BF16)


def sent_grads(kept, both, cot, grad, act):
    tokens, model = both.shape
    half = grad.shape[1] // 2
    steps = half // BLOCK
    column = along((model, BLOCK), 1)
    return call(
        sent_body, "sent_grads", (kept,), (steps,),
        [
            (both, fixed(both.shape)),
            (cot, fixed(cot.shape)),
            (grad, pl.BlockSpec((tokens, BLOCK), lambda g, k: (0, (1 - k[0]) * steps + g))),
            (grad, pl.BlockSpec((tokens, BLOCK), lambda g, k: (0, k[0] * steps + g))),
            (act, along((tokens, BLOCK), 1)),
        ],
        [((model, half), BF16, column), ((model, half), BF16, column), ((half, model), BF16, along((BLOCK, model)))],
    )


def kept_body(order_ref, act_ref, half_ref, cot_ref, down_ref, att_ref, low_ref, kept_ref, feed_ref, out_ref, keep_ref):
    parts = order_ref.shape[0]
    width = att_ref.shape[1] // parts
    kept_ref[...] = dot(half_ref[...], cot_ref[...], 0, 0).astype(BF16)
    feed_ref[...] = dot(act_ref[...], down_ref[...]).astype(BF16)
    grad = dot(att_ref[...], low_ref[...], 0, 0).astype(BF16)
    step, steps = pl.program_id(0), pl.num_programs(0)

    def write(ref):
        for n in range(parts):
            at = pl.multiple_of(order_ref[n] * width, width)
            ref[pl.ds(at, width)] = grad[n * width : (n + 1) * width]

    @pl.when(2 * step < steps)
    def _():
        write(out_ref)

    @pl.when(2 * step >= steps)
    def _():
        write(keep_ref)


def kept_grads(order, act, cot, down, attended, low, c_at, deps=()):
    tokens, half = act.shape
    model = cot.shape[1]
    steps = model // BLOCK
    rows = half // (2 * steps)
    own = attended.shape[0]
    place = jnp.concatenate([order, c_at.astype(jnp.int32)[None]])

    def body(place_ref, *refs):
        kept_body(place_ref.at[0 : order.shape[0]], *refs)

    def low_at(g, p):
        c = p[order.shape[0]]
        mine = 2 * g >= steps
        return 0, jnp.where(mine, c * (steps // 2) + g - steps // 2, (1 - c) * (steps // 2) + g)

    return call(
        body, "kept_grads", (place,), (steps,),
        [
            (act, fixed(act.shape)),
            (act, along((tokens, rows), 1, steps)),
            (cot, fixed(cot.shape)),
            (down, along((half, BLOCK), 1)),
            (attended, fixed(attended.shape)),
            (low, pl.BlockSpec((own, BLOCK), low_at)),
        ],
        [
            ((half // 2, model), BF16, along((rows, model))),
            ((tokens, model), BF16, along((tokens, BLOCK), 1)),
            ((model, model // 2), BF16, pl.BlockSpec((model, BLOCK), lambda g, p: (0, jnp.minimum(g, steps // 2 - 1)))),
            ((model, model // 2), BF16, pl.BlockSpec((model, BLOCK), lambda g, p: (0, jnp.maximum(g - steps // 2, 0)))),
        ],
        deps=deps,
    )


def middle_back_body(
    order_ref, part_ref, sent_ref, mid_ref, cot_ref, gain_ref, w0, w1, w2, w3,
    grad_ref, low_ref, att0_ref, att1_ref, far_ref, sums_ref,
):
    grad = part_ref[...].astype(F32) + sent_ref[...].astype(F32)
    hat, inverse = centre(mid_ref[0])
    cot = cot_ref[0].astype(F32)
    total = cot + norm_back(grad, gain_ref[...], hat, inverse)
    low = total.astype(BF16)
    grad_ref[0] = total
    low_ref[0] = low
    far_ref[0, 0] = dot(low, w2[...], 1, 1).astype(BF16)
    far_ref[1, 0] = dot(low, w3[...], 1, 1).astype(BF16)
    att1_ref[0] = dot(low, w1[...], 1, 1).astype(BF16)
    att0_ref[0] = dot(low, w0[...], 1, 1).astype(BF16)

    @pl.when(pl.program_id(0) == 0)
    def _():
        sums_ref[...] = jnp.zeros_like(sums_ref)

    sums_ref[0:1] += jnp.sum(grad * hat, axis=0, keepdims=True)
    sums_ref[1:2] += jnp.sum(grad, axis=0, keepdims=True)
    sums_ref[2:3] += jnp.sum(low.astype(F32), axis=0, keepdims=True)
    sums_ref[3:4] += jnp.sum(cot, axis=0, keepdims=True)


def middle_back(order, both, sent, mid, cot, gain, weight, parts, deps=()):
    rows, shard, model = mid.shape
    width = model // parts
    block, one = along((1, shard, model)), along((1, shard, width))
    flat = pl.BlockSpec((shard, model), lambda g, o: (g, 0))
    return call(
        middle_back_body, "middle_back", (order,), (rows,),
        [(both, flat), (sent, flat), (mid, block), (cot, block), (gain, fixed((1, model)))] + out_blocks(weight, parts),
        [
            (mid.shape, F32, block),
            (mid.shape, BF16, block),
            ((rows, shard, width), BF16, one),
            ((rows, shard, width), BF16, one),
            ((2, rows, shard, width), BF16, along((2, 1, shard, width), 1)),
            ((8, model), F32, fixed((8, model))),
        ],
        deps=deps
    )


def norm1_back_body(part_ref, near_ref, far_ref, stream_ref, mid_ref, gain_ref, seg_ref, in_ref, shift_ref, sums_ref):
    grad = part_ref[0].astype(F32) + near_ref[0].astype(F32) + far_ref[0].astype(F32)
    hat, inverse = centre(stream_ref[0])
    total = mid_ref[0] + norm_back(grad, gain_ref[...], hat, inverse)
    in_ref[0] = total.astype(BF16)
    slots = lax.broadcasted_iota(jnp.int32, (SEGS, seg_ref.shape[-1]), 0) == seg_ref[0]
    onehot = slots.astype(F32).astype(BF16)
    shift_ref[0] = dot(jnp.concatenate([onehot, onehot], axis=1), split_low(total))

    @pl.when(pl.program_id(0) == 0)
    def _():
        sums_ref[...] = jnp.zeros_like(sums_ref)

    sums_ref[0:1] += jnp.sum(grad * hat, axis=0, keepdims=True)
    sums_ref[1:2] += jnp.sum(grad, axis=0, keepdims=True)


def norm1_back(start, count, own, near, far, stream, mid, gain, seg, held=(), deps=()):
    rows, shard, model = stream.shape
    block, own_block = along((1, shard, model), 0, start), along((1, shard, model))
    return call(
        norm1_back_body, "norm1_back", (), (count,),
        [(own, own_block), (near, own_block), (far, own_block), (stream, block), (mid, block), (gain, fixed((1, model)))]
        + [(seg, along((1, 1, shard), 0, start))],
        [
            (stream.shape, BF16, block),
            ((count, SEGS, model), F32, along((1, SEGS, model))),
            ((8, model), F32, fixed((8, model))),
        ],
        held=[(array, 0) for array in held], deps=deps
    )


def exchange(own, one, far):
    return [own, swap(one, "c"), far, swap(far[1], "c")]


def tie(*values):
    return lax.optimization_barrier(values)


def cut(values, index, size, axis):
    return lax.dynamic_slice_in_dim(values, index * size, size, axis)


def add_low(kept, sent):
    return (kept.astype(F32) + sent.astype(F32)).astype(BF16)


def over_z(values, at, depth):
    if depth != 4:
        return lax.psum_scatter(values, "z", scatter_dimension=0, tiled=False)
    parts = [lax.dynamic_index_in_dim(values, at ^ n, 0, keepdims=False) for n in range(depth)]
    own = parts[0].astype(F32)
    sent = [lax.ppermute(parts[n], "z", [(i, i ^ n) for i in range(depth)]) for n in range(1, depth)]
    return (own + sent[0].astype(F32) + sent[1].astype(F32) + sent[2].astype(F32)).astype(BF16)


def ordered(at, own, other, axis):
    return jnp.where(at == 0, jnp.concatenate([own, other], axis), jnp.concatenate([other, own], axis))


def finish_body(blocks, at_ref, d0, d1, u0, u1, l0, l1, down_ref, up_ref, qkv_ref, out_ref):
    c_at = at_ref[0]
    width = u0.shape[1] // (2 * blocks)
    depth = d0.shape[0]
    for c in range(2):
        mine = c_at == c
        down_ref[c * depth : (c + 1) * depth] = jnp.where(mine, d0[...], d1[...]).astype(F32)
        up = jnp.where(mine, u0[...], u1[...]).astype(F32)
        for x in range(2):
            for z in range(blocks):
                at, place = ((2 * z + x) * 2 + c) * width, (x * blocks + z) * width
                up_ref[:, at : at + width] = up[:, place : place + width]
        late = jnp.where(mine, l0[...], l1[...]).astype(F32)
        half = out_ref.shape[1] // 2
        size = half // 2
        out_ref[:, c * half : (c + 1) * half] = late[:, 6 * size :]
        for y in range(2):
            for n in range(3):
                at = n * 4 * size + (2 * y + c) * size
                qkv_ref[:, at : at + size] = late[:, (3 * y + n) * size : (3 * y + n + 1) * size]


def finish(c_at, dp, piece, down, up, late, parts):
    rows, model = up[0].shape[0], down[0].shape[1]
    depth = dp // 2
    if piece % 128 == 0:
        at = c_at.astype(jnp.int32)[None]
        shapes = [(2 * down[0].shape[0], model), (rows, 2 * up[0].shape[1]), (rows, 3 * model), (rows, model)]
        arrays = list(down) + list(up) + list(late)
        return call(
            functools.partial(finish_body, depth), "finish", (at,), (1,),
            [(array, fixed(array.shape)) for array in arrays], [(shape, F32, fixed(shape)) for shape in shapes],
        )
    down_done = ordered(c_at, *down, 0).astype(F32)
    up_done = ordered(c_at, up[0][None], up[1][None], 0).reshape(2, rows, 2, depth, piece)
    up_done = up_done.transpose(1, 3, 2, 0, 4).reshape(rows, -1).astype(F32)
    both = ordered(c_at, late[0][None], late[1][None], 0)
    width = model // parts
    qkv_done = both[:, :, : 6 * width].reshape(2, rows, 2, 3, width).transpose(1, 3, 2, 0, 4)
    qkv_done = qkv_done.reshape(rows, 3 * model).astype(F32)
    out_done = jnp.concatenate([both[0, :, 6 * width :], both[1, :, 6 * width :]], axis=1).astype(F32)
    return down_done, up_done, qkv_done, out_done


def local(
    inputs, segment_ids, doc_times, time_weight, time_bias, norm1_gain, norm1_bias, qkv_weight, qkv_bias,
    out_weight, out_bias, norm2_gain, norm2_bias, up_weight, up_bias, down_weight, down_bias, cotangent,
    *, dp,
):
    rows, shard, model = inputs.shape
    parts = 4
    tokens = rows * shard
    hidden_width = up_weight.shape[1]
    width = model // parts
    depth = dp // 2
    half = hidden_width // 2
    piece = half // dp
    z_at, x_at, y_at, c_at = (lax.axis_index(name) for name in ("z", "x", "y", "c"))
    me = 2 * y_at + c_at

    def line(vector):
        return vector.astype(F32)[None]

    seg_two = swap(segment_ids, "y")
    segs = jnp.stack([segment_ids, swap(segment_ids, "c"), seg_two, swap(seg_two, "c")], axis=1)

    groups = [(0, rows - 1), (rows - 1, 1)] if rows > 1 else [(0, 1)]
    seg = segment_ids[:, None, :]
    features = time_features(doc_times.reshape(rows * SEGS), jnp.arange(TEMB), TEMB // 2)
    time_shift = dot(features, time_weight).reshape(rows, SEGS, model) + time_bias.astype(F32)
    stream, own1 = norm1(inputs, seg, time_shift, line(norm1_gain), line(norm1_bias))
    own1, segs = tie(own1, segs)
    two1 = swap(own1, "y")
    one1 = swap(own1, "c")

    me, x_at, z_at, c_at, y_at, own1 = tie(me, x_at, z_at, c_at, y_at, own1)
    order = [me ^ i for i in range(parts)]
    order_list = jnp.stack(order).astype(jnp.int32)
    me_list = order_list[:1]
    low_id, high_id = segs.min(axis=2), segs.max(axis=2)
    act = (low_id[:, :, None] <= high_id[:, None, :]) & (low_id[:, None, :] <= high_id[:, :, None])
    places = jnp.arange(parts, dtype=jnp.int32)
    rank = jnp.cumsum(act.astype(jnp.int32), axis=2) - 1
    chosen = act[..., None] & (rank[..., None] == places)
    idx = jnp.sum(jnp.where(chosen, places[:, None], 0), axis=2).astype(jnp.int32).reshape(-1)
    cnt = jnp.sum(act.astype(jnp.int32), axis=2).reshape(-1)
    positions = jnp.stack([o * shard + jnp.arange(shard, dtype=jnp.int32) for o in order])
    cos_tab, sin_tab = rotary_tables(positions, HEAD_DIM)

    cot = cotangent.reshape(tokens, model)
    cot_other = swap(cot, "c")
    turned = jnp.stack([1 - x_at, x_at])
    if piece % BLOCK == 0:
        blk = ((jnp.arange(depth)[None, :] * 2 + turned[:, None]) * 2 + c_at) * (piece // BLOCK)
        blk = (blk[..., None] + jnp.arange(piece // BLOCK)).reshape(-1).astype(jnp.int32)
        up_from, down_from = up_weight, down_weight
    else:
        blk = jnp.zeros((half // BLOCK,), jnp.int32)
        up_from = up_weight.reshape(model, depth, 2, 2, piece)
        up_from = lax.dynamic_index_in_dim(up_from, c_at, 3, keepdims=False)
        up_from = jnp.where(x_at == 1, up_from, up_from[:, :, ::-1]).transpose(0, 2, 1, 3).reshape(model, half)
        down_from = down_weight.reshape(depth, 2, 2, piece, model)
        down_from = lax.dynamic_index_in_dim(down_from, c_at, 2, keepdims=False)
        down_from = jnp.where(x_at == 1, down_from, down_from[:, ::-1]).transpose(1, 0, 2, 3).reshape(half, model)
    grad_act, up_own, down_own, cot_both = cot_down(
        blk, cot, cot_other, up_from, down_from, piece % BLOCK != 0, half
    )
    up_bias_own = lax.dynamic_index_in_dim(up_bias.reshape(depth, 2, 2, piece), c_at, 2, keepdims=False)
    up_bias_own = jnp.where(x_at == 1, up_bias_own, up_bias_own[:, ::-1]).transpose(1, 0, 2).reshape(half)

    bias_line = qkv_bias.reshape(1, 3 * model)
    qkv, normed1_all, qkv_own = project_qkv(
        0, parts, me_list, own1, one1, qkv_weight, bias_line, cos_tab, sin_tab, (), (grad_act,)
    )
    two1, qkv = tie(two1, qkv)
    qkv, normed1_all, _ = project_qkv(
        1, parts, me_list, two1, swap(two1, "c"), qkv_weight, bias_line, cos_tab, sin_tab, (qkv, normed1_all)
    )
    o, lse, attended = None, None, []
    for start, count in groups:
        held = () if o is None else (o, lse)
        o, out_one, out_far, lse = attend(start, count, cnt, idx, qkv, segs, held)
        attended.append((out_one, swap(out_far, "y")))
    held, normed2, normed2_other = (), [], []
    for (start, count), values in zip(groups, attended):
        far, o = tie(values[1], o)
        values = exchange(o, values[0], far)
        middle, low, attended_all = middle_norm(
            start, count, order_list, values, out_weight, stream, line(out_bias), line(norm2_gain), line(norm2_bias), held
        )
        held = (middle, attended_all)
        normed2.append(low)
        normed2_other.append(swap(low, "c"))

    active, grad_hidden, up_b, normed2_both, part2 = hidden_units(
        normed2 + normed2_other, grad_act, up_own, line(up_bias_own)
    )
    part2_sent = swap(part2[tokens:], "c")
    grad_middle, grad_middle_low, att0, att1, far, sums2 = middle_back(
        order_list, part2, part2_sent, middle, cotangent, line(norm2_gain), out_weight, parts
    )
    far = swap(far, "y")
    sums2 = sums2[:4]

    active, grad_hidden, att0 = tie(active, grad_hidden, att0)
    up_half = (x_at == y_at).astype(jnp.int32)
    up_out, up_grad, down_out = sent_grads(up_half[None], normed2_both, cot_both, grad_hidden, active)
    up_sent, down_sent = swap(up_out, "y"), swap(down_out, "x")
    down_kept, feed, out_sent, out_grad = kept_grads(
        order_list, active, cot_both, down_own, attended_all.reshape(tokens, model),
        grad_middle_low.reshape(tokens, model), c_at, (down_out, far),
    )
    out_sent = swap(out_sent, "c")
    feed = feed[:tokens].astype(F32) + swap(feed[tokens:], "c").astype(F32) + line(down_bias)
    output = (middle + feed.reshape(rows, shard, model)).astype(BF16)

    up_rows = model // dp
    down_kept, output, out_grad, far = tie(down_kept, output, out_grad, far)
    grad_o = exchange(att0, att1, far)
    grad_qkv, back = (), []
    for start, count in groups:
        grad_qkv, own, one, two, three = attend_back(
            start, count, cnt, idx, qkv, o, grad_o, lse, segs, cos_tab, sin_tab, qkv_own, grad_qkv,
            (there, down_x, up_out) if back else (),
        )
        grad_qkv = (grad_qkv,)
        if not back:
            own, up_grad, down_kept, out_grad = tie(own, up_grad, down_kept, out_grad)
            down_x = add_low(down_kept, down_sent)
            down_z = lax.psum_scatter(down_x, "z", scatter_dimension=0, tiled=True)
            up_y = add_low(up_grad, up_sent).reshape(depth, 2 * up_rows, half // 2)
            up_out = cut(up_y, 1 - x_at, up_rows, 1)
            up_sent = swap(up_out, "x")
        there = add_low(two, swap(three, "c"))
        if not back:
            there, up_out = tie(there, up_out)
        back.append((own, swap(one, "c"), swap(there, "y")))
    out_c = add_low(out_grad, out_sent)
    out_c = out_c.reshape(depth, 2 * up_rows, model // 2)
    out_x = add_low(cut(out_c, x_at, up_rows, 1), swap(cut(out_c, 1 - x_at, up_rows, 1), "x"))
    grad_qkv, there, far = tie(grad_qkv[0], there, back[0][2])
    back[0] = back[0][:2] + (far,)
    back[-1] = back[-1][:2] + (swap(there, "y"),)
    grad_qkv = grad_qkv.reshape(parts * tokens, 3 * width)
    qkv_grad = dot(normed1_all.reshape(parts * tokens, model), grad_qkv, 0, 0).astype(BF16)
    qkv_b = jnp.sum(grad_qkv.astype(F32), axis=0)
    qkv_grad, up_y = tie(qkv_grad.reshape(depth, 2 * up_rows, 3 * width), up_y)
    qkv_sent = swap(cut(qkv_grad, 1 - x_at, up_rows, 1), "x")
    held, grad_shift, sums1 = (), [], 0.0
    deps = (qkv_grad,)
    for (start, count), values in zip(groups, back):
        input_grad, found, sums = norm1_back(
            start, count, *values, stream, grad_middle, line(norm1_gain), seg, held, deps
        )
        if not held:
            input_grad, up_y = tie(input_grad, up_y)
            up_x = add_low(cut(up_y, x_at, up_rows, 1), up_sent)
            up_z = lax.psum_scatter(up_x, "z", scatter_dimension=0, tiled=False)
            deps = (up_x,)
        held = (input_grad,)
        grad_shift.append(found.reshape(count * SEGS, model))
        sums1 = sums1 + sums[:2]
    qkv_x = add_low(cut(qkv_grad, x_at, up_rows, 1), qkv_sent)

    up_b = up_b.reshape(2, depth, 1, piece)
    up_b = jnp.where(x_at == 1, up_b, up_b[::-1]).transpose(1, 0, 2, 3)
    up_b = jnp.where(jnp.arange(2)[:, None] == c_at, up_b, 0.0).reshape(-1, model)
    qkv_b = jnp.where(jnp.arange(parts)[:, None] == me, qkv_b.reshape(3, 1, width), 0.0).reshape(3, model)
    times = doc_times.reshape(1, rows * SEGS)
    times = jnp.concatenate([times // 32, times % 32], axis=1).astype(F32)
    times = jnp.pad(times, ((0, 0), (0, model - times.shape[1])))
    small = jnp.concatenate(grad_shift + [sums1, sums2, qkv_b, up_b, times], axis=0)
    small, qkv_x, out_x = tie(add_low(small, swap(small.astype(BF16), "c")), qkv_x, out_x)
    late = jnp.concatenate([qkv_x, out_x], axis=2)
    small = add_low(small, swap(small, "y"))
    small = ordered(x_at, small[None], swap(small, "x")[None], 0)
    if depth == 4:
        others = [lax.ppermute(small, "z", [(i, i ^ n) for i in range(depth)]) for n in range(1, depth)]
        small = jnp.stack([small] + others)
        small = jnp.stack([lax.dynamic_index_in_dim(small, z_at ^ n, 0, keepdims=False) for n in range(depth)])
    else:
        small = lax.all_gather(small, "z")
    small = small.reshape(dp, small.shape[2], model)

    small, down_z, up_z = tie(small, down_z, up_z)
    late = over_z(late, z_at, depth)
    late_sent = swap(late, "y")
    qkv_y = ordered(y_at, late[None, :, : 3 * width], late_sent[None, :, : 3 * width], 0)
    out_y = add_low(late[:, 3 * width :], late_sent[:, 3 * width :])
    late = jnp.concatenate([qkv_y[0], qkv_y[1], out_y], axis=1)
    late_other = swap(late, "c")
    down_y = add_low(down_z, swap(down_z, "y"))
    down_other = swap(down_y, "c")
    up_done = ordered(y_at, up_z, swap(up_z, "y"), 1)
    up_other = swap(up_done, "c")

    down_done, up_done, qkv_done, out_done = finish(
        c_at, dp, piece, (down_y, down_other), (up_done, up_other), (late, late_other), parts
    )

    all_times = small[:, -1, : 2 * rows * SEGS].astype(F32) * 0.25
    all_times = all_times[:, : rows * SEGS] * 32.0 + all_times[:, rows * SEGS :]
    shifts = small[:, : rows * SEGS].reshape(dp * rows * SEGS, model)
    columns = (2 * z_at + x_at) * (TEMB // dp) + jnp.arange(TEMB // dp)
    wanted = time_features(all_times.reshape(-1), columns, TEMB // 2)
    time_w_done = dot(wanted, shifts, 0, 0)
    sums = jnp.sum(small[:, rows * SEGS :].astype(F32), axis=0)
    dp_at = 2 * z_at + x_at

    def share(vector):
        return cut(vector.reshape(-1), dp_at, vector.size // dp, 0)

    time_b_done = jnp.sum(cut(shifts, dp_at, up_rows, 1).astype(F32), axis=0)
    return (
        output, input_grad, time_w_done, time_b_done, share(sums[0]), share(sums[1]), qkv_done, share(sums[6:9]),
        out_done, share(sums[4]), share(sums[2]), share(sums[3]), up_done, share(sums[9:-1]), down_done, share(sums[5]),
    )


def solution(mesh):
    dp, seq = mesh.shape["dp"], mesh.shape["seq"]
    fine = Mesh(mesh.devices.reshape(dp // 2, 2, seq // 2, 2), ("z", "x", "y", "c"))
    rows, seqs = ("z", "x"), ("y", "c")
    placed = (P(rows, seqs, None), P(rows, seqs), P(rows, None)) + (P(),) * 14 + (P(rows, seqs, None),)
    vec, mat = P(rows), P(rows, None)
    return jax.shard_map(
        functools.partial(local, dp=dp),
        mesh=fine,
        in_specs=placed,
        out_specs=(
            P(rows, seqs, None), P(rows, seqs, None), mat, vec, vec, vec, mat, vec, mat, vec, vec, vec, mat, vec, mat, vec,
        ),
        check_vma=False,
    )
```

```python
import functools
import math

import jax
import jax.numpy as jnp
from jax import lax
from jax.experimental import pallas as pl
from jax.experimental.pallas import tpu as pltpu
from jax.sharding import Mesh, PartitionSpec as P

HEADS = 16
HEAD_DIM = 64
TEMB = 256
SEGS = 8
EPSILON = 1e-05
F32 = jnp.float32
BF16 = jnp.bfloat16
NEG = -1e30
LOG2E = math.log2(math.e)
GELU_A = math.sqrt(2.0 / math.pi)
GELU_B = GELU_A * 0.044715
BLOCK = 256
VMEM = 60 * 1024 * 1024
TIME_BIAS, GAIN1, BIAS1, OUT_BIAS, GAIN2, BIAS2, DOWN_BIAS, QKV_BIAS, UP_BIAS = (slice(n, n + 1) for n in (0, 1, 2, 3, 4, 5, 6, 7, 10))


def swap(value, axis):
    return lax.ppermute(value, axis, [(0, 1), (1, 0)])


def time_features(doc_times, column, half_size):
    frequency = jnp.exp(-math.log(10000.0) * (column % half_size).astype(F32) / half_size)
    angles = doc_times.astype(F32)[..., None] * frequency
    return jnp.where(column < half_size, jnp.sin(angles), jnp.cos(angles)).astype(BF16)


def rotary_tables(positions, head_size):
    half_size = head_size // 2
    frequency = jnp.exp(-math.log(10000.0) * 2.0 * jnp.arange(half_size, dtype=F32) / head_size)
    angles = positions.astype(F32)[..., None] * frequency
    cos_tab, sin_tab = jnp.cos(angles), jnp.sin(angles)
    return (
        jnp.concatenate([cos_tab] * 4, axis=-1),
        jnp.concatenate([-sin_tab, sin_tab, -sin_tab, sin_tab], axis=-1),
    )


def dot(left_op, right_op, left_dim=1, right_dim=0):
    return lax.dot_general(
        left_op, right_op, (((left_dim,), (right_dim,)), ((), ())), preferred_element_type=F32
    )


def turn(values, cos_tab, sin_tab):
    slabs = []
    lane = lax.broadcasted_iota(jnp.int32, (values.shape[0], 128), 1)
    first = lane % HEAD_DIM < HEAD_DIM // 2
    for start in range(0, values.shape[1], 128):
        slab = values[:, start : start + 128]
        partner = jnp.where(
            first, pltpu.roll(slab, 128 - HEAD_DIM // 2, 1), pltpu.roll(slab, HEAD_DIM // 2, 1)
        )
        slabs.append(slab * cos_tab + partner * sin_tab)
    return jnp.concatenate(slabs, axis=1)


def split_low(values):
    high = values.astype(BF16)
    return jnp.concatenate([high, (values - high.astype(F32)).astype(BF16)], axis=0)


def centre(values):
    scale = 1.0 / values.shape[-1]
    centred = values - jnp.sum(values, axis=-1, keepdims=True) * scale
    spread = jnp.sum(centred * centred, axis=-1, keepdims=True) * scale
    inverse = lax.rsqrt(spread + EPSILON)
    return centred * inverse, inverse


def norm_back(grad, gain, hat, inverse):
    scale = 1.0 / grad.shape[-1]
    scaled = grad * gain
    mean = jnp.sum(scaled, axis=-1, keepdims=True) * scale
    along = jnp.sum(scaled * hat, axis=-1, keepdims=True) * scale
    return inverse * (scaled - mean - hat * along)


def call(body, name, prefetch, grid, ins, outs, scratch=(), deps=(), held=()):
    count = len(prefetch) + len(ins)
    extra = [array for array, _ in held] + list(deps)

    def kernel(*refs):
        body(*refs[:count], *refs[count + len(extra) :])

    return pl.pallas_call(
        kernel,
        grid_spec=pltpu.PrefetchScalarGridSpec(
            num_scalar_prefetch=len(prefetch),
            grid=grid,
            in_specs=[spec for _, spec in ins] + [pl.BlockSpec(memory_space=pl.ANY)] * len(extra),
            out_specs=[spec for _, _, spec in outs],
            scratch_shapes=list(scratch),
        ),
        out_shape=[jax.ShapeDtypeStruct(shape, kind) for shape, kind, _ in outs],
        input_output_aliases={count + n: out for n, (_, out) in enumerate(held)},
        compiler_params=pltpu.CompilerParams(vmem_limit_bytes=VMEM),
        name=name,
    )(*prefetch, *[array for array, _ in ins], *extra)


def fixed(shape):
    return pl.BlockSpec(shape, lambda *_: (0,) * len(shape))


def along(shape, axis=0, start=0):
    return pl.BlockSpec(shape, lambda g, *_: tuple(start + g if n == axis else 0 for n in range(len(shape))))


def norm1_body(x_ref, seg_ref, shift_ref, vec_ref, stream_ref, low_ref):
    seg = seg_ref[pl.ds(pl.program_id(0), 1)]
    slots = lax.broadcasted_iota(jnp.int32, (SEGS, seg.shape[-1]), 0) == seg
    onehot = slots.astype(F32).astype(BF16)
    shift = shift_ref[0] + vec_ref[TIME_BIAS]
    added = dot(jnp.concatenate([onehot, onehot], axis=0), split_low(shift), 0, 0)
    stream = x_ref[0].astype(F32) + added
    hat, _ = centre(stream)
    stream_ref[0] = stream
    low_ref[0] = (hat * vec_ref[GAIN1] + vec_ref[BIAS1]).astype(BF16)


def norm1(x, seg, shift, vecs):
    rows, shard, model = x.shape
    block = along((1, shard, model))
    return call(
        norm1_body, "norm1", (), (rows,),
        [(x, block), (seg, fixed(seg.shape)), (shift, along((1, SEGS, model))), (vecs, fixed(vecs.shape))],
        [(x.shape, F32, block), (x.shape, BF16, block)],
    )


def qkv_body(me_ref, a_ref, b_ref, w_ref, vec_ref, cos_ref, sin_ref, out_ref, own_ref):
    rows, shard, model = a_ref.shape
    width = w_ref.shape[1]
    places = [(n, r) for n in range(2) for r in range(rows)]
    step = pl.program_id(0)

    def run(turned):
        w = w_ref[...]
        bias = vec_ref[pl.ds(QKV_BIAS.start + step, 1), pl.ds(pl.multiple_of(me_ref[0] * width, width), width)]
        later = dot(a_ref[0], w)
        for at, (n, r) in enumerate(places):
            values = later + bias
            if at + 1 < len(places):
                x_ref = (a_ref, b_ref)[places[at + 1][0]]
                later = dot(x_ref[places[at + 1][1]], w)
            if turned:
                values = turn(values, cos_ref[n], sin_ref[n]) * jnp.where(step == 0, LOG2E * HEAD_DIM**-0.5, 1.0)
            out_ref[0, n, r] = values.astype(BF16)

    own_ref[...] = w_ref[...].T

    @pl.when(step < 2)
    def _():
        run(True)

    @pl.when(step == 2)
    def _():
        run(False)


def project_qkv(pair, parts, me, first, second, weight, vecs, cos_tab, sin_tab, held=(), deps=()):
    rows, shard, model = first.shape
    width = model // parts
    return call(
        qkv_body, "qkv", (me,), (3,),
        [(first, fixed(first.shape)), (second, fixed(first.shape))]
        + [
            (weight, pl.BlockSpec((model, width), lambda g, m: (0, g * parts + m[0]))),
            (vecs, fixed(vecs.shape)),
            (cos_tab, pl.BlockSpec((2, shard, 128), lambda g, m: (pair, 0, 0))),
            (sin_tab, pl.BlockSpec((2, shard, 128), lambda g, m: (pair, 0, 0))),
        ],
        [
            ((3, parts, rows, shard, width), BF16, pl.BlockSpec((1, 2, rows, shard, width), lambda g, m: (g, pair, 0, 0, 0))),
            ((3 * width, model), BF16, along((width, model))),
        ],
        held=[(array, n) for n, array in enumerate(held)], deps=deps,
    )


def qkv_grads(x_at, pieces, grad, blocks):
    rows, shard, model = pieces[0].shape
    tokens = rows * shard
    parts, columns = len(pieces), grad.shape[3]
    size = model // (2 * blocks)

    def body(at_ref, x0, x1, x2, x3, g_ref, out_ref, keep_ref, sum_ref):
        total, sums = 0.0, 0.0
        for n, x_ref in enumerate((x0, x1, x2, x3)):
            g = g_ref[n].reshape(tokens, g_ref.shape[3])
            total = total + dot(x_ref[...].reshape(tokens, model), g, 0, 0)
            sums = sums + jnp.sum(g.astype(F32), axis=0, keepdims=True)
        low = total.astype(BF16)
        for x in range(2):
            for b in range(blocks):
                values = low[(2 * b + x) * size : (2 * b + x + 1) * size]

                @pl.when(at_ref[0] == x)
                def _():
                    keep_ref[b] = values

                @pl.when(at_ref[0] != x)
                def _():
                    out_ref[b] = values

        sum_ref[...] = sums

    block = along((blocks, size, BLOCK), 2)
    shape = (blocks, size, columns)
    return call(
        body, "qkv_grads", (x_at.astype(jnp.int32)[None],), (columns // BLOCK,),
        [(x, fixed(x.shape)) for x in pieces] + [(grad, along((parts, rows, shard, BLOCK), 3))],
        [(shape, BF16, block), (shape, BF16, block), ((1, columns), F32, along((1, BLOCK), 1))],
    )


def seg_columns(segq_all, segk):
    pieces, shard, _ = segk.shape
    for j in range(pieces):
        row = jnp.broadcast_to(segq_all[j:j+1].astype(F32), (128, shard))
        segk[j] = row.T

def attend_body(start, cnt_ref, idx_ref, qkv_ref, seg_ref, o_ref, one_ref, far_ref, lse_ref, vt, segk, qmt, acc):
    row = pl.program_id(0) + start
    _, pieces, _, shard, width = qkv_ref.shape
    heads = width // HEAD_DIM

    @pl.when(pl.program_id(0) == 0)
    def _():
        qmt[...] = jnp.zeros_like(qmt)

    for j in range(pieces):
        vt[j] = qkv_ref[2, j, 0].T
        qt = qkv_ref[0, j, 0].T
        for h in range(heads):
            at = slice(h * HEAD_DIM, (h + 1) * HEAD_DIM)
            qmt[j, at, h * shard : (h + 1) * shard] = qt[at]
    seg_columns(seg_ref[0], segk)

    @pl.loop(0, pieces)
    def _(piece):
        attend_piece(row * pieces + piece, piece, cnt_ref, idx_ref, qkv_ref.at[1], seg_ref, lse_ref, vt, segk, qmt, acc)

    for j in range(pieces):
        o_ref[j, 0] = acc[j].T.astype(BF16)
    one_ref[0] = o_ref[1, 0]
    far_ref[:, 0] = o_ref[2:, 0]


def attend_piece(at_q, piece, cnt_ref, idx_ref, k_ref, seg_ref, lse_ref, vt, segk, qmt, acc):
    pieces, _, shard, width = k_ref.shape
    heads = width // HEAD_DIM
    seg_q = seg_ref[0, pl.ds(piece, 1)].astype(F32)

    def run(count):
        @pl.when(cnt_ref[at_q] == count)
        def _():
            qm = qmt[piece]
            places = [idx_ref[at_q * pieces + t] for t in range(count)]
            top, tot, out = [None] * heads, [None] * heads, [None] * heads
            later = dot(k_ref[places[0], 0], qm)
            for t in range(count):
                s = later
                if t + 1 < count:
                    later = dot(k_ref[places[t + 1], 0], qm)
                col = segk[places[t]]
                same = jnp.concatenate([col] * (shard // 128), axis=1) == seg_q
                for h in range(heads):
                    at = slice(h * HEAD_DIM, (h + 1) * HEAD_DIM)
                    sh = jnp.where(same, s[:, h * shard : (h + 1) * shard], NEG)
                    best = jnp.max(sh, axis=0, keepdims=True)
                    if t:
                        best = jnp.maximum(top[h], best)
                        fade = jnp.exp2(top[h] - best)
                    p = jnp.exp2(sh - best)
                    total = jnp.sum(p, axis=0, keepdims=True)
                    found = dot(vt[places[t], at], p.astype(BF16))
                    if t:
                        total = tot[h] * fade + total
                        found = out[h] * fade + found
                    top[h], tot[h], out[h] = best, total, found
            for h in range(heads):
                acc[piece, h * HEAD_DIM : (h + 1) * HEAD_DIM] = out[h] / tot[h]
                lse_ref[0, piece, h : h + 1] = top[h] + jnp.log2(tot[h])

    for count in range(1, pieces + 1):
        run(count)


def attend(start, count, cnt, idx, qkv, seg, held=()):
    _, pieces, rows, shard, width = qkv.shape
    heads = width // HEAD_DIM
    pairs = count * (pieces * shard) ** 2
    return call(
        functools.partial(attend_body, start), "attend", (cnt, idx), (count,),
        [(qkv, along((3, pieces, 1, shard, width), 2, start)), (seg, along((1, pieces, shard), 0, start))],
        [
            ((pieces, rows, shard, width), BF16, along((pieces, 1, shard, width), 1, start)),
            ((count, shard, width), BF16, along((1, shard, width))),
            ((2, count, shard, width), BF16, along((2, 1, shard, width), 1)),
            ((rows, pieces, 8, shard), F32, along((1, pieces, 8, shard), 0, start)),
        ],
        [
            pltpu.VMEM((pieces, width, shard), BF16),
            pltpu.VMEM((pieces, shard, 128), F32),
            pltpu.VMEM((pieces, width, heads * shard), BF16),
            pltpu.VMEM((pieces, width, shard), F32),
        ],
        held=list(zip(held, (0, 3)))
    )


def attend_back_body(
    start, cnt_ref, idx_ref, qkv_ref, o_ref, do0, do1, do2, do3, lse_ref, seg_ref, cos_ref, sin_ref, w_ref,
    g_ref, p0_ref, p1_ref, p2_ref, p3_ref, kt, segk, dk, dv, dqt, qmt, gmt, qst, gst, low,
):
    row = pl.program_id(0) + start
    _, pieces, _, shard, width = qkv_ref.shape
    heads = width // HEAD_DIM

    @pl.when(pl.program_id(0) == 0)
    def _():
        qmt[...] = jnp.zeros_like(qmt)
        gmt[...] = jnp.zeros_like(gmt)

    seg_columns(seg_ref[0], segk)
    dk[...] = jnp.zeros_like(dk)
    dv[...] = jnp.zeros_like(dv)
    lane = lax.broadcasted_iota(jnp.int32, (shard, width), 1) // HEAD_DIM
    chosen = lax.broadcasted_iota(jnp.int32, (8, width), 1) // HEAD_DIM
    chosen = (chosen == lax.broadcasted_iota(jnp.int32, (8, width), 0)).astype(BF16)
    for j, do_ref in enumerate((do0, do1, do2, do3)):
        kt[j] = qkv_ref[1, j, 0].T
        q, do = qkv_ref[0, j, 0], do_ref[...].reshape(shard, width)
        qt, gt = q.T, do.T
        for h in range(heads):
            at, qa = slice(h * HEAD_DIM, (h + 1) * HEAD_DIM), slice(h * shard, (h + 1) * shard)
            qmt[j, at, qa] = qt[at]
            gmt[j, at, qa] = gt[at]
            qst[j, qa] = jnp.where(lane == h, q, jnp.zeros_like(q))
            gst[j, qa] = jnp.where(lane == h, do, jnp.zeros_like(do))
        prod = do.astype(F32) * o_ref[j, 0].astype(F32)
        high = prod.astype(BF16)
        low[j] = dot(chosen, high, 1, 1) + dot(chosen, (prod - high.astype(F32)).astype(BF16), 1, 1)

    @pl.loop(0, pieces)
    def _(piece):
        back_piece(
            row * pieces + piece, piece, cnt_ref, idx_ref, qkv_ref.at[1], qkv_ref.at[2], lse_ref, seg_ref,
            kt, segk, dk, dv, dqt, qmt, gmt, qst, gst, low,
        )

    for j, ref in ((1, p1_ref), (3, p3_ref), (0, p0_ref), (2, p2_ref)):
        grad_q = turn(dqt[j].T * HEAD_DIM**-0.5, cos_ref[j], -sin_ref[j]).astype(BF16)
        grad_k = turn(dk[j] * (1 / LOG2E), cos_ref[j], -sin_ref[j]).astype(BF16)
        grad = jnp.concatenate([grad_q, grad_k, dv[j].astype(BF16)], axis=1)
        g_ref[j, 0] = grad
        ref[0] = dot(grad, w_ref[...]).astype(BF16)


def back_piece(
    at_q, piece, cnt_ref, idx_ref, k_ref, v_ref, lse_ref, seg_ref, kt, segk, dk, dv, dqt, qmt, gmt, qst, gst, low
):
    pieces, _, shard, width = k_ref.shape
    heads = width // HEAD_DIM
    lse, delta = lse_ref[0, piece], low[piece]
    seg_q = seg_ref[0, pl.ds(piece, 1)].astype(F32)

    def run(count):
        @pl.when(cnt_ref[at_q] == count)
        def _():
            places = [idx_ref[at_q * pieces + t] for t in range(count)]
            qm, gm = qmt[piece], gmt[piece]
            later = dot(k_ref[places[0], 0], qm), dot(v_ref[places[0], 0], gm)
            out = [None] * heads
            for t in range(count):
                s, dp = later
                j = places[t]
                if t + 1 < count:
                    later = dot(k_ref[places[t + 1], 0], qm), dot(v_ref[places[t + 1], 0], gm)
                col = segk[j]
                same = jnp.concatenate([col] * (shard // 128), axis=1) == seg_q
                ps, dss = [], []
                for h in range(heads):
                    at, qa = slice(h * HEAD_DIM, (h + 1) * HEAD_DIM), slice(h * shard, (h + 1) * shard)
                    p = jnp.exp2(jnp.where(same, s[:, qa] - lse[h : h + 1], NEG))
                    ds = (p * (dp[:, qa] - delta[h : h + 1])).astype(BF16)
                    ps.append(p.astype(BF16))
                    dss.append(ds)
                    found = dot(kt[j, at], ds)
                    out[h] = found if t == 0 else out[h] + found
                dv[j] += dot(jnp.concatenate(ps, axis=1), gst[piece])
                dk[j] += dot(jnp.concatenate(dss, axis=1), qst[piece])
            for h in range(heads):
                dqt[piece, h * HEAD_DIM : (h + 1) * HEAD_DIM] = out[h]

    for count in range(1, pieces + 1):
        run(count)


def attend_back(start, count, cnt, idx, qkv, o, do, lse, seg, cos_tab, sin_tab, weight, held=(), deps=()):
    _, pieces, rows, shard, width = qkv.shape
    model = weight.shape[1]
    heads = width // HEAD_DIM
    table = fixed((pieces, shard, 128))
    pairs = count * (pieces * shard) ** 2
    square, wide = (pieces, width, heads * shard), (pieces, shard, width)
    one = along((1, shard, width), 0, start)
    return call(
        functools.partial(attend_back_body, start), "attend_back", (cnt, idx), (count,),
        [(qkv, along((3, pieces, 1, shard, width), 2, start)), (o, along((pieces, 1, shard, width), 1, start))]
        + [(do[0], one), (do[1], one), (do[2], along((1, 1, shard, width), 1, start)), (do[3], one)]
        + [(lse, along((1, pieces, 8, shard), 0, start)), (seg, along((1, pieces, shard), 0, start))]
        + [(cos_tab, table), (sin_tab, table), (weight, fixed(weight.shape))],
        [((pieces, rows, shard, 3 * width), BF16, along((pieces, 1, shard, 3 * width), 1, start))]
        + [((count, shard, model), BF16, along((1, shard, model)))] * pieces,
        [
            pltpu.VMEM((pieces, width, shard), BF16),
            pltpu.VMEM((pieces, shard, 128), F32),
            pltpu.VMEM(wide, F32),
            pltpu.VMEM(wide, F32),
            pltpu.VMEM((pieces, width, shard), F32),
            pltpu.VMEM(square, BF16),
            pltpu.VMEM(square, BF16),
            pltpu.VMEM((pieces, heads * shard, width), BF16),
            pltpu.VMEM((pieces, heads * shard, width), BF16),
            pltpu.VMEM((pieces, 8, shard), F32),
        ],
        held=[(array, 0) for array in held], deps=deps
    )


def middle_body(
    order_ref, a0, a1, a2, a3, w0, w1, w2, w3, stream_ref, vec_ref, mid_ref, low_ref, all_ref,
):
    _, shard, model = stream_ref.shape
    total = 0.0
    for n, (a, w) in enumerate(((a0, w0), (a1, w1), (a2, w2), (a3, w3))):
        values = a[...].reshape(shard, a.shape[-1])
        total = total + dot(values, w[...])
        all_ref[0, :, n * a.shape[-1] : (n + 1) * a.shape[-1]] = values
    mid = stream_ref[0] + (total + vec_ref[OUT_BIAS])
    hat, _ = centre(mid)
    mid_ref[0] = mid
    low_ref[0] = (hat * vec_ref[GAIN2] + vec_ref[BIAS2]).astype(BF16)


def out_blocks(weight, parts):
    width = weight.shape[0] // parts

    def block(i):
        return pl.BlockSpec((width, weight.shape[1]), lambda g, o: (o[i], 0))

    return [(weight, block(i)) for i in range(parts)]


def middle_norm(start, count, order, attended, weight, stream, vecs, held=()):
    rows, shard, model = stream.shape
    parts = len(attended)
    width = model // parts
    block, one = along((1, shard, model), 0, start), along((1, shard, width))
    first = [along((1, 1, shard, width), 1, start), one, along((1, 1, shard, width), 1), one]
    return call(
        middle_body, "middle", (order,), (count,),
        list(zip(attended, first)) + out_blocks(weight, parts) + [(stream, block), (vecs, fixed(vecs.shape))],
        [
            (stream.shape, F32, block),
            ((count, shard, model), BF16, along((1, shard, model))),
            (stream.shape, BF16, block),
        ],
        held=list(zip(held, (0, 2)))
    )


def cot_body(blk_ref, a_ref, b_ref, up_ref, down_ref, g_ref, up_out, down_out, both_ref):
    tokens = a_ref.shape[0]
    down = down_ref[...]

    @pl.when(pl.program_id(0) == 0)
    def _():
        both_ref[0:tokens] = a_ref[...]
        both_ref[tokens:] = b_ref[...]

    g_ref[0:tokens] = dot(a_ref[...], down, 1, 1).astype(BF16)
    g_ref[tokens:] = dot(b_ref[...], down, 1, 1).astype(BF16)
    up_out[...] = up_ref[...]
    down_out[...] = down


def cot_down(blk, own, other, up, down, picked, half):
    tokens, model = own.shape
    steps = half // BLOCK
    column = along((2 * tokens, BLOCK), 1)
    if picked:
        up_at, down_at = along((model, BLOCK), 1), along((BLOCK, model))
    else:
        up_at = pl.BlockSpec((model, BLOCK), lambda g, b: (0, b[g]))
        down_at = pl.BlockSpec((BLOCK, model), lambda g, b: (b[g], 0))
    return call(
        cot_body, "cot_down", (blk,), (steps,),
        [(own, fixed(own.shape)), (other, fixed(own.shape)), (up, up_at), (down, down_at)],
        [
            ((2 * tokens, half), BF16, column),
            ((model, half), BF16, along((model, BLOCK), 1)),
            ((half, model), BF16, along((BLOCK, model))),
            ((2 * tokens, model), BF16, fixed((2 * tokens, model))),
        ]
    )


def hidden_body(blocks, blk_ref, *refs):
    pieces, refs = refs[:-10], refs[-10:]
    g_ref, up_ref, row_ref, bias_ref, act_ref, grad_ref, sum_ref, both_ref, part_ref, held = refs
    sizes = [ref.shape[0] * ref.shape[1] for ref in pieces]
    starts = [sum(sizes[:n]) for n in range(len(sizes))]
    step = pl.program_id(0)

    @pl.when(step == 0)
    def _():
        for ref, at, size in zip(pieces, starts, sizes):
            both_ref[at : at + size] = ref[...].reshape(size, ref.shape[2])

    @pl.when(step < blocks)
    def _():
        up = up_ref[...]
        if bias_ref.shape[1] == BLOCK:
            bias = bias_ref[...]
        else:
            per = bias_ref.shape[1] // BLOCK
            at = pl.multiple_of(blk_ref[step] % per * BLOCK, BLOCK)
            bias = bias_ref[pl.ds(UP_BIAS.start + blk_ref[step] // per, 1), pl.ds(at, BLOCK)]
        total = 0.0
        later = dot(pieces[0][...].reshape(sizes[0], -1), up)
        for n, (start, size) in enumerate(zip(starts, sizes)):
            at = slice(start, start + size)
            v = later + bias
            if n + 1 < len(pieces):
                later = dot(pieces[n + 1][...].reshape(sizes[n + 1], -1), up)
            square = v * v
            tanh = jnp.tanh(v * (GELU_A + GELU_B * square))
            gate = 0.5 + 0.5 * tanh
            act = v * gate
            slope = gate + act * ((1.0 - tanh) * (GELU_A + 3.0 * GELU_B * square))
            grad = (slope * g_ref[at].astype(F32)).astype(BF16)
            act_ref[at] = act.astype(BF16)
            grad_ref[at] = grad
            held[step, at] = grad
            total = total + jnp.sum(grad.astype(F32), axis=0, keepdims=True)
        sum_ref[...] = total

    @pl.when(step >= blocks)
    def _():
        grad = jnp.concatenate([held[n] for n in range(blocks)], axis=1)
        part_ref[...] = dot(grad, row_ref[...], 1, 1).astype(BF16)


def hidden_units(blk, pieces, grads, up, bias):
    model = pieces[0].shape[2]
    tokens, half = grads.shape
    blocks, more = half // BLOCK, model // BLOCK

    def first(g):
        return jnp.minimum(g, blocks - 1)

    def second(g):
        return jnp.maximum(g - blocks, 0)

    column = pl.BlockSpec((tokens, BLOCK), lambda g, b: (0, first(g)))
    line = pl.BlockSpec((1, BLOCK), lambda g, b: (0, first(g)))
    return call(
        functools.partial(hidden_body, blocks), "hidden", (blk,), (blocks + more,),
        [(piece, fixed(piece.shape)) for piece in pieces]
        + [
            (grads, column),
            (up, pl.BlockSpec((model, BLOCK), lambda g, b: (0, first(g)))),
            (up, pl.BlockSpec((BLOCK, half), lambda g, b: (second(g), 0))),
            (bias, line if bias.shape[0] == 1 else fixed(bias.shape)),
        ],
        [
            (grads.shape, BF16, column),
            (grads.shape, BF16, column),
            ((1, half), F32, line),
            ((tokens, model), BF16, fixed((tokens, model))),
            ((tokens, model), BF16, pl.BlockSpec((tokens, BLOCK), lambda g, b: (0, second(g)))),
        ],
        [pltpu.VMEM((blocks, tokens, BLOCK), BF16)]
    )


def sent_body(half_ref, both_ref, cot_ref, out_ref, keep_ref, act_ref, up0, up1, up_keep, down0, down1):
    both = both_ref[...]
    down = dot(act_ref[...], cot_ref[...], 0, 0).astype(BF16)
    up = dot(both, out_ref[...], 0, 0).astype(BF16)

    @pl.when(2 * pl.program_id(0) < pl.num_programs(0))
    def _():
        down0[...] = down
        up0[...] = up

    @pl.when(2 * pl.program_id(0) >= pl.num_programs(0))
    def _():
        down1[...] = down
        up1[...] = up

    up_keep[...] = dot(both, keep_ref[...], 0, 0).astype(BF16)


def sent_grads(kept, both, cot, grad, act):
    tokens, model = both.shape
    half = grad.shape[1] // 2
    steps = half // BLOCK
    cut = steps // 2

    def first(g):
        return jnp.minimum(g, cut - 1)

    def second(g):
        return jnp.maximum(g - cut, 0)

    return call(
        sent_body, "sent_grads", (kept,), (steps,),
        [
            (both, fixed(both.shape)),
            (cot, fixed(cot.shape)),
            (grad, pl.BlockSpec((tokens, BLOCK), lambda g, k: (0, (1 - k[0]) * steps + g))),
            (grad, pl.BlockSpec((tokens, BLOCK), lambda g, k: (0, k[0] * steps + g))),
            (act, along((tokens, BLOCK), 1)),
        ],
        [
            ((model, half // 2), BF16, pl.BlockSpec((model, BLOCK), lambda g, k: (0, first(g)))),
            ((model, half // 2), BF16, pl.BlockSpec((model, BLOCK), lambda g, k: (0, second(g)))),
            ((model, half), BF16, along((model, BLOCK), 1)),
            ((half // 2, model), BF16, pl.BlockSpec((BLOCK, model), lambda g, k: (first(g), 0))),
            ((half // 2, model), BF16, pl.BlockSpec((BLOCK, model), lambda g, k: (second(g), 0))),
        ],
    )


def kept_body(order_ref, act_ref, half_ref, cot_ref, down_ref, att_ref, low_ref, kept_ref, feed_ref, out_ref, keep_ref):
    parts = order_ref.shape[0]
    width = att_ref.shape[1] // parts
    kept_ref[...] = dot(half_ref[...], cot_ref[...], 0, 0).astype(BF16)
    feed_ref[...] = dot(act_ref[...], down_ref[...]).astype(BF16)
    grad = dot(att_ref[...], low_ref[...], 0, 0).astype(BF16)
    step, steps = pl.program_id(0), pl.num_programs(0)

    def write(ref):
        for n in range(parts):
            at = pl.multiple_of(order_ref[n] * width, width)
            ref[pl.ds(at, width)] = grad[n * width : (n + 1) * width]

    @pl.when(2 * step < steps)
    def _():
        write(out_ref)

    @pl.when(2 * step >= steps)
    def _():
        write(keep_ref)


def kept_grads(order, act, cot, down, attended, low, c_at, deps=()):
    tokens, half = act.shape
    model = cot.shape[1]
    steps = model // BLOCK
    rows = half // (2 * steps)
    own = attended.shape[0]
    place = jnp.concatenate([order, c_at.astype(jnp.int32)[None]])

    def body(place_ref, *refs):
        kept_body(place_ref.at[0 : order.shape[0]], *refs)

    def low_at(g, p):
        c = p[order.shape[0]]
        mine = 2 * g >= steps
        return 0, jnp.where(mine, c * (steps // 2) + g - steps // 2, (1 - c) * (steps // 2) + g)

    return call(
        body, "kept_grads", (place,), (steps,),
        [
            (act, fixed(act.shape)),
            (act, along((tokens, rows), 1, steps)),
            (cot, fixed(cot.shape)),
            (down, along((half, BLOCK), 1)),
            (attended, fixed(attended.shape)),
            (low, pl.BlockSpec((own, BLOCK), low_at)),
        ],
        [
            ((half // 2, model), BF16, along((rows, model))),
            ((tokens, model), BF16, along((tokens, BLOCK), 1)),
            ((model, model // 2), BF16, pl.BlockSpec((model, BLOCK), lambda g, p: (0, jnp.minimum(g, steps // 2 - 1)))),
            ((model, model // 2), BF16, pl.BlockSpec((model, BLOCK), lambda g, p: (0, jnp.maximum(g - steps // 2, 0)))),
        ],
        deps=deps,
    )


def middle_back_body(
    order_ref, part_ref, sent_ref, mid_ref, cot_ref, vec_ref, w0, w1, w2, w3,
    grad_ref, low_ref, att0_ref, att1_ref, far_ref, sums_ref,
):
    grad = part_ref[...].astype(F32) + sent_ref[...].astype(F32)
    hat, inverse = centre(mid_ref[0])
    cot = cot_ref[0].astype(F32)
    total = cot + norm_back(grad, vec_ref[GAIN2], hat, inverse)
    low = total.astype(BF16)
    grad_ref[0] = total
    low_ref[0] = low
    far_ref[0, 0] = dot(low, w2[...], 1, 1).astype(BF16)
    far_ref[1, 0] = dot(low, w3[...], 1, 1).astype(BF16)
    att1_ref[0] = dot(low, w1[...], 1, 1).astype(BF16)
    att0_ref[0] = dot(low, w0[...], 1, 1).astype(BF16)

    @pl.when(pl.program_id(0) == 0)
    def _():
        sums_ref[...] = jnp.zeros_like(sums_ref)

    sums_ref[0:1] += jnp.sum(grad * hat, axis=0, keepdims=True)
    sums_ref[1:2] += jnp.sum(grad, axis=0, keepdims=True)
    sums_ref[2:3] += jnp.sum(low.astype(F32), axis=0, keepdims=True)
    sums_ref[3:4] += jnp.sum(cot, axis=0, keepdims=True)


def middle_back(order, both, sent, mid, cot, vecs, weight, parts, deps=()):
    rows, shard, model = mid.shape
    width = model // parts
    block, one = along((1, shard, model)), along((1, shard, width))
    flat = pl.BlockSpec((shard, model), lambda g, o: (g, 0))
    return call(
        middle_back_body, "middle_back", (order,), (rows,),
        [(both, flat), (sent, flat), (mid, block), (cot, block), (vecs, fixed(vecs.shape))] + out_blocks(weight, parts),
        [
            (mid.shape, F32, block),
            (mid.shape, BF16, block),
            ((rows, shard, width), BF16, one),
            ((rows, shard, width), BF16, one),
            ((2, rows, shard, width), BF16, along((2, 1, shard, width), 1)),
            ((8, model), F32, fixed((8, model))),
        ],
        deps=deps
    )


def norm1_back_body(start, part_ref, near_ref, far_ref, stream_ref, mid_ref, vec_ref, seg_ref, in_ref, shift_ref, sums_ref):
    grad = part_ref[0].astype(F32) + near_ref[0].astype(F32) + far_ref[0].astype(F32)
    hat, inverse = centre(stream_ref[0])
    total = mid_ref[0] + norm_back(grad, vec_ref[GAIN1], hat, inverse)
    in_ref[0] = total.astype(BF16)
    seg = seg_ref[pl.ds(pl.program_id(0) + start, 1)]
    slots = lax.broadcasted_iota(jnp.int32, (SEGS, seg.shape[-1]), 0) == seg
    onehot = slots.astype(F32).astype(BF16)
    shift_ref[0] = dot(jnp.concatenate([onehot, onehot], axis=1), split_low(total))

    @pl.when(pl.program_id(0) == 0)
    def _():
        sums_ref[...] = jnp.zeros_like(sums_ref)

    sums_ref[0:1] += jnp.sum(grad * hat, axis=0, keepdims=True)
    sums_ref[1:2] += jnp.sum(grad, axis=0, keepdims=True)


def norm1_back(start, count, own, near, far, stream, mid, vecs, seg, held=(), deps=()):
    rows, shard, model = stream.shape
    block, own_block = along((1, shard, model), 0, start), along((1, shard, model))
    return call(
        functools.partial(norm1_back_body, start), "norm1_back", (), (count,),
        [(own, own_block), (near, own_block), (far, own_block), (stream, block), (mid, block), (vecs, fixed(vecs.shape))]
        + [(seg, fixed(seg.shape))],
        [
            (stream.shape, BF16, block),
            ((count, SEGS, model), F32, along((1, SEGS, model))),
            ((8, model), F32, fixed((8, model))),
        ],
        held=[(array, 0) for array in held], deps=deps
    )


def exchange(own, one, far):
    return [own, swap(one, "c"), far, swap(far[1], "c")]


def tie(*values):
    return lax.optimization_barrier(values)


def cut(values, index, size, axis):
    return lax.dynamic_slice_in_dim(values, index * size, size, axis)


def add_low(kept, sent):
    return (kept.astype(F32) + sent.astype(F32)).astype(BF16)


def over_z(values, at, depth):
    if depth != 4:
        return lax.psum_scatter(values, "z", scatter_dimension=0, tiled=False)
    parts = [lax.dynamic_index_in_dim(values, at ^ n, 0, keepdims=False) for n in range(depth)]
    own = parts[0].astype(F32)
    sent = [lax.ppermute(parts[n], "z", [(i, i ^ n) for i in range(depth)]) for n in range(1, depth)]
    return (own + sent[0].astype(F32) + sent[1].astype(F32) + sent[2].astype(F32)).astype(BF16)


def ordered(at, own, other, axis):
    return jnp.where(at == 0, jnp.concatenate([own, other], axis), jnp.concatenate([other, own], axis))


def finish_body(blocks, at_ref, d0, d1, u0, u1, l0, l1, down_ref, up_ref, qkv_ref, out_ref):
    c_at = at_ref[0]
    width = u0.shape[1] // (2 * blocks)
    depth = d0.shape[0]
    for c in range(2):
        mine = c_at == c
        down_ref[c * depth : (c + 1) * depth] = jnp.where(mine, d0[...], d1[...]).astype(F32)
        up = jnp.where(mine, u0[...], u1[...]).astype(F32)
        for x in range(2):
            for z in range(blocks):
                at, place = ((2 * z + x) * 2 + c) * width, (x * blocks + z) * width
                up_ref[:, at : at + width] = up[:, place : place + width]
        late = jnp.where(mine, l0[...], l1[...]).astype(F32)
        half = out_ref.shape[1] // 2
        size = half // 2
        out_ref[:, c * half : (c + 1) * half] = late[:, 6 * size :]
        for y in range(2):
            for n in range(3):
                at = n * 4 * size + (2 * y + c) * size
                qkv_ref[:, at : at + size] = late[:, (3 * y + n) * size : (3 * y + n + 1) * size]


def finish(c_at, dp, piece, down, up, late, parts):
    rows, model = up[0].shape[0], down[0].shape[1]
    depth = dp // 2
    if piece % 128 == 0:
        at = c_at.astype(jnp.int32)[None]
        shapes = [(2 * down[0].shape[0], model), (rows, 2 * up[0].shape[1]), (rows, 3 * model), (rows, model)]
        arrays = list(down) + list(up) + list(late)
        return call(
            functools.partial(finish_body, depth), "finish", (at,), (1,),
            [(array, fixed(array.shape)) for array in arrays], [(shape, F32, fixed(shape)) for shape in shapes],
        )
    down_done = ordered(c_at, *down, 0).astype(F32)
    up_done = ordered(c_at, up[0][None], up[1][None], 0).reshape(2, rows, 2, depth, piece)
    up_done = up_done.transpose(1, 3, 2, 0, 4).reshape(rows, -1).astype(F32)
    both = ordered(c_at, late[0][None], late[1][None], 0)
    width = model // parts
    qkv_done = both[:, :, : 6 * width].reshape(2, rows, 2, 3, width).transpose(1, 3, 2, 0, 4)
    qkv_done = qkv_done.reshape(rows, 3 * model).astype(F32)
    out_done = jnp.concatenate([both[0, :, 6 * width :], both[1, :, 6 * width :]], axis=1).astype(F32)
    return down_done, up_done, qkv_done, out_done


def local(
    inputs, segment_ids, doc_times, time_weight, time_bias, norm1_gain, norm1_bias, qkv_weight, qkv_bias,
    out_weight, out_bias, norm2_gain, norm2_bias, up_weight, up_bias, down_weight, down_bias, cotangent,
    *, dp,
):
    rows, shard, model = inputs.shape
    parts = 4
    tokens = rows * shard
    hidden_width = up_weight.shape[1]
    width = model // parts
    depth = dp // 2
    half = hidden_width // 2
    piece = half // dp
    z_at, x_at, y_at, c_at = (lax.axis_index(name) for name in ("z", "x", "y", "c"))
    me = 2 * y_at + c_at

    vecs = [time_bias, norm1_gain, norm1_bias, out_bias, norm2_gain, norm2_bias, down_bias, qkv_bias, up_bias]
    vecs = jnp.concatenate(vecs).astype(F32).reshape(-1, model)

    seg_two = swap(segment_ids, "y")
    segs = jnp.stack([segment_ids, swap(segment_ids, "c"), seg_two, swap(seg_two, "c")], axis=1)

    groups = [(0, rows - 1), (rows - 1, 1)] if rows > 1 else [(0, 1)]
    features = time_features(doc_times.reshape(rows * SEGS), jnp.arange(TEMB), TEMB // 2)
    time_shift = dot(features, time_weight).reshape(rows, SEGS, model)
    stream, own1 = norm1(inputs, segment_ids, time_shift, vecs)
    own1, segs = tie(own1, segs)
    two1 = swap(own1, "y")
    one1 = swap(own1, "c")

    me, x_at, z_at, c_at, y_at, own1 = tie(me, x_at, z_at, c_at, y_at, own1)
    order = [me ^ i for i in range(parts)]
    order_list = jnp.stack(order).astype(jnp.int32)
    me_list = order_list[:1]
    low_id, high_id = segs.min(axis=2), segs.max(axis=2)
    act = (low_id[:, :, None] <= high_id[:, None, :]) & (low_id[:, None, :] <= high_id[:, :, None])
    places = jnp.arange(parts, dtype=jnp.int32)
    rank = jnp.cumsum(act.astype(jnp.int32), axis=2) - 1
    chosen = act[..., None] & (rank[..., None] == places)
    idx = jnp.sum(jnp.where(chosen, places[:, None], 0), axis=2).astype(jnp.int32).reshape(-1)
    cnt = jnp.sum(act.astype(jnp.int32), axis=2).reshape(-1)
    positions = jnp.stack([o * shard + jnp.arange(shard, dtype=jnp.int32) for o in order])
    cos_tab, sin_tab = rotary_tables(positions, HEAD_DIM)

    cot = cotangent.reshape(tokens, model)
    cot_other = swap(cot, "c")
    turned = jnp.stack([1 - x_at, x_at])
    if piece % BLOCK == 0:
        blk = ((jnp.arange(depth)[None, :] * 2 + turned[:, None]) * 2 + c_at) * (piece // BLOCK)
        blk = (blk[..., None] + jnp.arange(piece // BLOCK)).reshape(-1).astype(jnp.int32)
        up_from, down_from = up_weight, down_weight
    else:
        blk = jnp.zeros((half // BLOCK,), jnp.int32)
        up_from = up_weight.reshape(model, depth, 2, 2, piece)
        up_from = lax.dynamic_index_in_dim(up_from, c_at, 3, keepdims=False)
        up_from = jnp.where(x_at == 1, up_from, up_from[:, :, ::-1]).transpose(0, 2, 1, 3).reshape(model, half)
        down_from = down_weight.reshape(depth, 2, 2, piece, model)
        down_from = lax.dynamic_index_in_dim(down_from, c_at, 2, keepdims=False)
        down_from = jnp.where(x_at == 1, down_from, down_from[:, ::-1]).transpose(1, 0, 2, 3).reshape(half, model)
    grad_act, up_own, down_own, cot_both = cot_down(
        blk, cot, cot_other, up_from, down_from, piece % BLOCK != 0, half
    )
    up_bias_own = vecs
    if piece % BLOCK:
        up_bias_own = lax.dynamic_index_in_dim(up_bias.reshape(depth, 2, 2, piece), c_at, 2, keepdims=False)
        up_bias_own = jnp.where(x_at == 1, up_bias_own, up_bias_own[:, ::-1]).transpose(1, 0, 2)
        up_bias_own = up_bias_own.reshape(1, half).astype(F32)

    qkv, qkv_own = project_qkv(0, parts, me_list, own1, one1, qkv_weight, vecs, cos_tab, sin_tab, (), (grad_act,))
    two1, qkv = tie(two1, qkv)
    three1 = swap(two1, "c")
    qkv, _ = project_qkv(1, parts, me_list, two1, three1, qkv_weight, vecs, cos_tab, sin_tab, (qkv,))
    o, lse, attended = None, None, []
    for start, count in groups:
        held = () if o is None else (o, lse)
        o, out_one, out_far, lse = attend(start, count, cnt, idx, qkv, segs, held)
        attended.append((out_one, swap(out_far, "y")))
    held, normed2, normed2_other = (), [], []
    for (start, count), values in zip(groups, attended):
        far, o = tie(values[1], o)
        values = exchange(o, values[0], far)
        middle, low, attended_all = middle_norm(
            start, count, order_list, values, out_weight, stream, vecs, held
        )
        held = (middle, attended_all)
        normed2.append(low)
        normed2_other.append(swap(low, "c"))

    active, grad_hidden, up_b, normed2_both, part2 = hidden_units(
        blk, normed2 + normed2_other, grad_act, up_own, up_bias_own
    )
    part2_sent = swap(part2[tokens:], "c")
    grad_middle, grad_middle_low, att0, att1, far, sums2 = middle_back(
        order_list, part2, part2_sent, middle, cotangent, vecs, out_weight, parts
    )
    far = swap(far, "y")
    sums2 = sums2[:4]

    active, grad_hidden, att0 = tie(active, grad_hidden, att0)
    up_half = (x_at == y_at).astype(jnp.int32)
    up_out, up_late, up_grad, down_out, down_late = sent_grads(
        up_half[None], normed2_both, cot_both, grad_hidden, active
    )
    up_out, down_out, far = tie(up_out, down_out, far)
    up_sent, down_sent = swap(up_out, "y"), swap(down_out, "x")
    down_kept, feed, out_sent, out_grad = kept_grads(
        order_list, active, cot_both, down_own, attended_all.reshape(tokens, model),
        grad_middle_low.reshape(tokens, model), c_at, (down_out, far),
    )
    out_sent = swap(out_sent, "c")
    down_kept, feed, up_sent, down_sent, up_late, down_late = tie(
        down_kept, feed, up_sent, down_sent, up_late, down_late
    )
    up_sent = [up_sent, swap(up_late, "y")]
    down_sent = [down_sent, swap(down_late, "x")]
    feed = feed[:tokens].astype(F32) + swap(feed[tokens:], "c").astype(F32) + down_bias.astype(F32)
    output = (middle + feed.reshape(rows, shard, model)).astype(BF16)
    up_rows = model // dp
    out_c = add_low(out_grad, out_sent)

    down_kept, output, out_c, far = tie(down_kept, output, out_c, far)
    out_z = lax.psum_scatter(out_c, "z", scatter_dimension=0, tiled=True)
    grad_o = exchange(att0, att1, far)
    grad_qkv, back = (), []
    for start, count in groups:
        grad_qkv, own, one, two, three = attend_back(
            start, count, cnt, idx, qkv, o, grad_o, lse, segs, cos_tab, sin_tab, qkv_own, grad_qkv,
            (there, down_x, up_out) if back else (),
        )
        grad_qkv = (grad_qkv,)
        if not back:
            own, up_grad, down_kept = tie(own, up_grad, down_kept)
            down_x = add_low(down_kept, jnp.concatenate(down_sent, axis=0))
            down_z = lax.psum_scatter(down_x, "z", scatter_dimension=0, tiled=True)
            up_y = add_low(up_grad, jnp.concatenate(up_sent, axis=1)).reshape(depth, 2 * up_rows, half // 2)
            up_out = cut(up_y, 1 - x_at, up_rows, 1)
            up_sent = swap(up_out, "x")
        there = add_low(two, swap(three, "c"))
        if not back:
            there, up_out = tie(there, up_out)
        back.append((own, swap(one, "c"), swap(there, "y")))
    grad_qkv, there, far, up_sent, up_y = tie(grad_qkv[0], there, back[0][2], up_sent, up_y)
    back[0] = back[0][:2] + (far,)
    back[-1] = back[-1][:2] + (swap(there, "y"),)
    qkv_out, qkv_kept, qkv_b = qkv_grads(x_at, [own1, one1, two1, three1], grad_qkv, depth)
    qkv_sent = swap(qkv_out, "x")
    qkv_kept, up_y, up_sent, out_z = tie(qkv_kept, up_y, up_sent, out_z)
    up_x = add_low(cut(up_y, x_at, up_rows, 1), up_sent)
    up_z = lax.psum_scatter(up_x, "z", scatter_dimension=0, tiled=False)
    out_x = add_low(cut(out_z, x_at, up_rows, 0), swap(cut(out_z, 1 - x_at, up_rows, 0), "x"))
    held, grad_shift, sums1 = (), [], 0.0
    for (start, count), values in zip(groups, back):
        input_grad, found, sums = norm1_back(
            start, count, *values, stream, grad_middle, vecs, segment_ids, held, (up_x if held else qkv_kept,)
        )
        held = (input_grad,)
        grad_shift.append(found.reshape(count * SEGS, model))
        sums1 = sums1 + sums[:2]
    qkv_x = add_low(qkv_kept, qkv_sent)

    up_b = up_b.reshape(2, depth, 1, piece)
    up_b = jnp.where(x_at == 1, up_b, up_b[::-1]).transpose(1, 0, 2, 3)
    up_b = jnp.where(jnp.arange(2)[:, None] == c_at, up_b, 0.0).reshape(-1, model)
    qkv_b = jnp.where(jnp.arange(parts)[:, None] == me, qkv_b.reshape(3, 1, width), 0.0).reshape(3, model)
    times = doc_times.reshape(1, rows * SEGS)
    times = jnp.concatenate([times // 32, times % 32], axis=1).astype(F32)
    times = jnp.pad(times, ((0, 0), (0, model - times.shape[1])))
    small = jnp.concatenate(grad_shift + [sums1, sums2, qkv_b, up_b, times], axis=0)
    small, qkv_x = tie(add_low(small, swap(small.astype(BF16), "c")), qkv_x)
    small = add_low(small, swap(small, "y"))
    small, down_z = tie(small, down_z)
    down_y = add_low(down_z, swap(down_z, "y"))
    small, down_y = tie(ordered(x_at, small[None], swap(small, "x")[None], 0), down_y)
    down_other = swap(down_y, "c")
    if depth == 4:
        others = [lax.ppermute(small, "z", [(i, i ^ n) for i in range(depth)]) for n in range(1, depth)]
        small = jnp.stack([small] + others)
        small = jnp.stack([lax.dynamic_index_in_dim(small, z_at ^ n, 0, keepdims=False) for n in range(depth)])
    else:
        small = lax.all_gather(small, "z")
    small = small.reshape(dp, small.shape[2], model)

    small, up_z = tie(small, up_z)
    up_done = ordered(y_at, up_z, swap(up_z, "y"), 1)
    up_other = swap(up_done, "c")
    late = jnp.concatenate([over_z(qkv_x, z_at, depth), out_x], axis=1)
    late_sent = swap(late, "y")
    qkv_y = ordered(y_at, late[None, :, : 3 * width], late_sent[None, :, : 3 * width], 0)
    out_y = add_low(late[:, 3 * width :], late_sent[:, 3 * width :])
    late = jnp.concatenate([qkv_y[0], qkv_y[1], out_y], axis=1)
    late_other = swap(late, "c")

    down_done, up_done, qkv_done, out_done = finish(
        c_at, dp, piece, (down_y, down_other), (up_done, up_other), (late, late_other), parts
    )

    all_times = small[:, -1, : 2 * rows * SEGS].astype(F32) * 0.25
    all_times = all_times[:, : rows * SEGS] * 32.0 + all_times[:, rows * SEGS :]
    shifts = small[:, : rows * SEGS].reshape(dp * rows * SEGS, model)
    columns = (2 * z_at + x_at) * (TEMB // dp) + jnp.arange(TEMB // dp)
    wanted = time_features(all_times.reshape(-1), columns, TEMB // 2)
    time_w_done = dot(wanted, shifts, 0, 0)
    sums = jnp.sum(small[:, rows * SEGS :].astype(F32), axis=0)
    dp_at = 2 * z_at + x_at

    def share(vector):
        return cut(vector.reshape(-1), dp_at, vector.size // dp, 0)

    time_b_done = jnp.sum(cut(shifts, dp_at, up_rows, 1).astype(F32), axis=0)
    return (
        output, input_grad, time_w_done, time_b_done, share(sums[0]), share(sums[1]), qkv_done, share(sums[6:9]),
        out_done, share(sums[4]), share(sums[2]), share(sums[3]), up_done, share(sums[9:-1]), down_done, share(sums[5]),
    )


def solution(mesh):
    dp, seq = mesh.shape["dp"], mesh.shape["seq"]
    fine = Mesh(mesh.devices.reshape(dp // 2, 2, seq // 2, 2), ("z", "x", "y", "c"))
    rows, seqs = ("z", "x"), ("y", "c")
    placed = (P(rows, seqs, None), P(rows, seqs), P(rows, None)) + (P(),) * 14 + (P(rows, seqs, None),)
    vec, mat = P(rows), P(rows, None)
    return jax.shard_map(
        functools.partial(local, dp=dp),
        mesh=fine,
        in_specs=placed,
        out_specs=(
            P(rows, seqs, None), P(rows, seqs, None), mat, vec, vec, vec, mat, vec, mat, vec, vec, vec, mat, vec, mat, vec,
        ),
        check_vma=False,
    )
```

```python
import functools
import math

import jax
import jax.numpy as jnp
from jax import lax
from jax.experimental import pallas as pl
from jax.experimental.pallas import tpu as pltpu
from jax.sharding import Mesh, PartitionSpec as P

HEADS = 16
HEAD_DIM = 64
TEMB = 256
SEGS = 8
EPSILON = 1e-05
F32 = jnp.float32
BF16 = jnp.bfloat16
NEG = -1e30
LOG2E = math.log2(math.e)
GELU_A = math.sqrt(2.0 / math.pi)
GELU_B = GELU_A * 0.044715
BLOCK = 256
VMEM = 60 * 1024 * 1024


def swap(value, axis):
    return lax.ppermute(value, axis, [(0, 1), (1, 0)])


def time_features(doc_times, column, half_size):
    frequency = jnp.exp(-math.log(10000.0) * (column % half_size).astype(F32) / half_size)
    angles = doc_times.astype(F32)[..., None] * frequency
    return jnp.where(column < half_size, jnp.sin(angles), jnp.cos(angles)).astype(BF16)


def rotary_tables(positions, head_size):
    half_size = head_size // 2
    frequency = jnp.exp(-math.log(10000.0) * 2.0 * jnp.arange(half_size, dtype=F32) / head_size)
    angles = positions.astype(F32)[..., None] * frequency
    cos_tab, sin_tab = jnp.cos(angles), jnp.sin(angles)
    return (
        jnp.concatenate([cos_tab] * 4, axis=-1),
        jnp.concatenate([-sin_tab, sin_tab, -sin_tab, sin_tab], axis=-1),
    )


def dot(left_op, right_op, left_dim=1, right_dim=0):
    return lax.dot_general(
        left_op, right_op, (((left_dim,), (right_dim,)), ((), ())), preferred_element_type=F32
    )


def turn(values, cos_tab, sin_tab):
    slabs = []
    lane = lax.broadcasted_iota(jnp.int32, (values.shape[0], 128), 1)
    first = lane % HEAD_DIM < HEAD_DIM // 2
    for start in range(0, values.shape[1], 128):
        slab = values[:, start : start + 128]
        partner = jnp.where(
            first, pltpu.roll(slab, 128 - HEAD_DIM // 2, 1), pltpu.roll(slab, HEAD_DIM // 2, 1)
        )
        slabs.append(slab * cos_tab + partner * sin_tab)
    return jnp.concatenate(slabs, axis=1)


def split_low(values):
    high = values.astype(BF16)
    return jnp.concatenate([high, (values - high.astype(F32)).astype(BF16)], axis=0)


def centre(values):
    scale = 1.0 / values.shape[-1]
    centred = values - jnp.sum(values, axis=-1, keepdims=True) * scale
    spread = jnp.sum(centred * centred, axis=-1, keepdims=True) * scale
    inverse = lax.rsqrt(spread + EPSILON)
    return centred * inverse, inverse


def norm_back(grad, gain, hat, inverse):
    scale = 1.0 / grad.shape[-1]
    scaled = grad * gain
    mean = jnp.sum(scaled, axis=-1, keepdims=True) * scale
    along = jnp.sum(scaled * hat, axis=-1, keepdims=True) * scale
    return inverse * (scaled - mean - hat * along)


def call(body, name, prefetch, grid, ins, outs, scratch=(), deps=(), held=()):
    count = len(prefetch) + len(ins)
    extra = [array for array, _ in held] + list(deps)

    def kernel(*refs):
        body(*refs[:count], *refs[count + len(extra) :])

    return pl.pallas_call(
        kernel,
        grid_spec=pltpu.PrefetchScalarGridSpec(
            num_scalar_prefetch=len(prefetch),
            grid=grid,
            in_specs=[spec for _, spec in ins] + [pl.BlockSpec(memory_space=pl.ANY)] * len(extra),
            out_specs=[spec for _, _, spec in outs],
            scratch_shapes=list(scratch),
        ),
        out_shape=[jax.ShapeDtypeStruct(shape, kind) for shape, kind, _ in outs],
        input_output_aliases={count + n: out for n, (_, out) in enumerate(held)},
        compiler_params=pltpu.CompilerParams(vmem_limit_bytes=VMEM),
        name=name,
    )(*prefetch, *[array for array, _ in ins], *extra)


def line(ref):
    return ref[...].astype(F32).reshape(1, -1)


def fixed(shape):
    return pl.BlockSpec(shape, lambda *_: (0,) * len(shape))


def along(shape, axis=0, start=0):
    return pl.BlockSpec(shape, lambda g, *_: tuple(start + g if n == axis else 0 for n in range(len(shape))))


def norm1_body(x_ref, seg_ref, shift_ref, time_ref, gain_ref, bias_ref, stream_ref, low_ref):
    seg = seg_ref[pl.ds(pl.program_id(0), 1)]
    slots = lax.broadcasted_iota(jnp.int32, (SEGS, seg.shape[-1]), 0) == seg
    onehot = slots.astype(F32).astype(BF16)
    shift = shift_ref[0] + line(time_ref)
    added = dot(jnp.concatenate([onehot, onehot], axis=0), split_low(shift), 0, 0)
    stream = x_ref[0].astype(F32) + added
    hat, _ = centre(stream)
    stream_ref[0] = stream
    low_ref[0] = (hat * line(gain_ref) + line(bias_ref)).astype(BF16)


def norm1(x, seg, shift, vecs):
    rows, shard, model = x.shape
    block = along((1, shard, model))
    return call(
        norm1_body, "norm1", (), (rows,),
        [(x, block), (seg, fixed(seg.shape)), (shift, along((1, SEGS, model)))]
        + [(vec, fixed(vec.shape)) for vec in vecs],
        [(x.shape, F32, block), (x.shape, BF16, block)],
    )


def qkv_body(me_ref, a_ref, b_ref, w_ref, bias_ref, cos_ref, sin_ref, out_ref, own_ref):
    rows, shard, model = a_ref.shape
    width = w_ref.shape[1]
    places = [(n, r) for n in range(2) for r in range(rows)]
    step = pl.program_id(0)

    def run(turned):
        w = w_ref[...]
        bias = bias_ref[...].astype(F32)
        later = dot(a_ref[0], w)
        for at, (n, r) in enumerate(places):
            values = later + bias
            if at + 1 < len(places):
                x_ref = (a_ref, b_ref)[places[at + 1][0]]
                later = dot(x_ref[places[at + 1][1]], w)
            if turned:
                values = turn(values, cos_ref[n], sin_ref[n]) * jnp.where(step == 0, LOG2E * HEAD_DIM**-0.5, 1.0)
            out_ref[0, n, r] = values.astype(BF16)

    own_ref[...] = w_ref[...].T

    @pl.when(step < 2)
    def _():
        run(True)

    @pl.when(step == 2)
    def _():
        run(False)


def project_qkv(pair, parts, me, first, second, weight, bias, cos_tab, sin_tab, held=(), deps=()):
    rows, shard, model = first.shape
    width = model // parts
    return call(
        qkv_body, "qkv", (me,), (3,),
        [(first, fixed(first.shape)), (second, fixed(first.shape))]
        + [
            (weight, pl.BlockSpec((model, width), lambda g, m: (0, g * parts + m[0]))),
            (bias, pl.BlockSpec((1, width), lambda g, m: (0, g * parts + m[0]))),
            (cos_tab, pl.BlockSpec((2, shard, 128), lambda g, m: (pair, 0, 0))),
            (sin_tab, pl.BlockSpec((2, shard, 128), lambda g, m: (pair, 0, 0))),
        ],
        [
            ((3, parts, rows, shard, width), BF16, pl.BlockSpec((1, 2, rows, shard, width), lambda g, m: (g, pair, 0, 0, 0))),
            ((3 * width, model), BF16, along((width, model))),
        ],
        held=[(array, n) for n, array in enumerate(held)], deps=deps,
    )


def qkv_grads(x_at, pieces, grad, blocks):
    rows, shard, model = pieces[0].shape
    tokens = rows * shard
    parts, columns = len(pieces), grad.shape[3]
    size = model // (2 * blocks)

    def body(at_ref, x0, x1, x2, x3, g_ref, out_ref, keep_ref, sum_ref):
        total, sums = 0.0, 0.0
        for n, x_ref in enumerate((x0, x1, x2, x3)):
            g = g_ref[n].reshape(tokens, g_ref.shape[3])
            total = total + dot(x_ref[...].reshape(tokens, model), g, 0, 0)
            sums = sums + jnp.sum(g.astype(F32), axis=0, keepdims=True)
        low = total.astype(BF16)
        for x in range(2):
            for b in range(blocks):
                values = low[(2 * b + x) * size : (2 * b + x + 1) * size]

                @pl.when(at_ref[0] == x)
                def _():
                    keep_ref[b] = values

                @pl.when(at_ref[0] != x)
                def _():
                    out_ref[b] = values

        sum_ref[...] = sums

    block = along((blocks, size, BLOCK), 2)
    shape = (blocks, size, columns)
    return call(
        body, "qkv_grads", (x_at.astype(jnp.int32)[None],), (columns // BLOCK,),
        [(x, fixed(x.shape)) for x in pieces] + [(grad, along((parts, rows, shard, BLOCK), 3))],
        [(shape, BF16, block), (shape, BF16, block), ((1, columns), F32, along((1, BLOCK), 1))],
    )


def seg_columns(segq_all, segk):
    pieces, shard, _ = segk.shape
    for j in range(pieces):
        row = jnp.broadcast_to(segq_all[j:j+1].astype(F32), (128, shard))
        segk[j] = row.T

def attend_body(start, cnt_ref, idx_ref, qkv_ref, seg_ref, o_ref, one_ref, far_ref, lse_ref, vt, segk, qmt, acc):
    row = pl.program_id(0) + start
    _, pieces, _, shard, width = qkv_ref.shape
    heads = width // HEAD_DIM

    @pl.when(pl.program_id(0) == 0)
    def _():
        qmt[...] = jnp.zeros_like(qmt)

    for j in range(pieces):
        vt[j] = qkv_ref[2, j, 0].T
        qt = qkv_ref[0, j, 0].T
        for h in range(heads):
            at = slice(h * HEAD_DIM, (h + 1) * HEAD_DIM)
            qmt[j, at, h * shard : (h + 1) * shard] = qt[at]
    seg_columns(seg_ref[0], segk)

    @pl.loop(0, pieces)
    def _(piece):
        attend_piece(row * pieces + piece, piece, cnt_ref, idx_ref, qkv_ref.at[1], seg_ref, lse_ref, vt, segk, qmt, acc)

    for j in range(pieces):
        o_ref[j, 0] = acc[j].T.astype(BF16)
    one_ref[0] = o_ref[1, 0]
    far_ref[:, 0] = o_ref[2:, 0]


def attend_piece(at_q, piece, cnt_ref, idx_ref, k_ref, seg_ref, lse_ref, vt, segk, qmt, acc):
    pieces, _, shard, width = k_ref.shape
    heads = width // HEAD_DIM
    seg_q = seg_ref[0, pl.ds(piece, 1)].astype(F32)

    def run(count):
        @pl.when(cnt_ref[at_q] == count)
        def _():
            qm = qmt[piece]
            places = [idx_ref[at_q * pieces + t] for t in range(count)]
            top, tot, out = [None] * heads, [None] * heads, [None] * heads
            later = dot(k_ref[places[0], 0], qm)
            for t in range(count):
                s = later
                if t + 1 < count:
                    later = dot(k_ref[places[t + 1], 0], qm)
                col = segk[places[t]]
                same = jnp.concatenate([col] * (shard // 128), axis=1) == seg_q
                for h in range(heads):
                    at = slice(h * HEAD_DIM, (h + 1) * HEAD_DIM)
                    sh = jnp.where(same, s[:, h * shard : (h + 1) * shard], NEG)
                    best = jnp.max(sh, axis=0, keepdims=True)
                    if t:
                        best = jnp.maximum(top[h], best)
                        fade = jnp.exp2(top[h] - best)
                    p = jnp.exp2(sh - best)
                    total = jnp.sum(p, axis=0, keepdims=True)
                    found = dot(vt[places[t], at], p.astype(BF16))
                    if t:
                        total = tot[h] * fade + total
                        found = out[h] * fade + found
                    top[h], tot[h], out[h] = best, total, found
            for h in range(heads):
                acc[piece, h * HEAD_DIM : (h + 1) * HEAD_DIM] = out[h] / tot[h]
                lse_ref[0, piece, h : h + 1] = top[h] + jnp.log2(tot[h])

    for count in range(1, pieces + 1):
        run(count)


def attend(start, count, cnt, idx, qkv, seg, held=()):
    _, pieces, rows, shard, width = qkv.shape
    heads = width // HEAD_DIM
    pairs = count * (pieces * shard) ** 2
    return call(
        functools.partial(attend_body, start), "attend", (cnt, idx), (count,),
        [(qkv, along((3, pieces, 1, shard, width), 2, start)), (seg, along((1, pieces, shard), 0, start))],
        [
            ((pieces, rows, shard, width), BF16, along((pieces, 1, shard, width), 1, start)),
            ((count, shard, width), BF16, along((1, shard, width))),
            ((2, count, shard, width), BF16, along((2, 1, shard, width), 1)),
            ((rows, pieces, 8, shard), F32, along((1, pieces, 8, shard), 0, start)),
        ],
        [
            pltpu.VMEM((pieces, width, shard), BF16),
            pltpu.VMEM((pieces, shard, 128), F32),
            pltpu.VMEM((pieces, width, heads * shard), BF16),
            pltpu.VMEM((pieces, width, shard), F32),
        ],
        held=list(zip(held, (0, 3)))
    )


def attend_back_body(
    start, cnt_ref, idx_ref, qkv_ref, o_ref, do0, do1, do2, do3, lse_ref, seg_ref, cos_ref, sin_ref, w_ref,
    g_ref, p0_ref, p1_ref, p2_ref, p3_ref, kt, segk, dk, dv, dqt, qmt, gmt, qst, gst, low,
):
    row = pl.program_id(0) + start
    _, pieces, _, shard, width = qkv_ref.shape
    heads = width // HEAD_DIM

    @pl.when(pl.program_id(0) == 0)
    def _():
        qmt[...] = jnp.zeros_like(qmt)
        gmt[...] = jnp.zeros_like(gmt)

    seg_columns(seg_ref[0], segk)
    dk[...] = jnp.zeros_like(dk)
    dv[...] = jnp.zeros_like(dv)
    lane = lax.broadcasted_iota(jnp.int32, (shard, width), 1) // HEAD_DIM
    chosen = lax.broadcasted_iota(jnp.int32, (8, width), 1) // HEAD_DIM
    chosen = (chosen == lax.broadcasted_iota(jnp.int32, (8, width), 0)).astype(BF16)
    for j, do_ref in enumerate((do0, do1, do2, do3)):
        kt[j] = qkv_ref[1, j, 0].T
        q, do = qkv_ref[0, j, 0], do_ref[...].reshape(shard, width)
        qt, gt = q.T, do.T
        for h in range(heads):
            at, qa = slice(h * HEAD_DIM, (h + 1) * HEAD_DIM), slice(h * shard, (h + 1) * shard)
            qmt[j, at, qa] = qt[at]
            gmt[j, at, qa] = gt[at]
            qst[j, qa] = jnp.where(lane == h, q, jnp.zeros_like(q))
            gst[j, qa] = jnp.where(lane == h, do, jnp.zeros_like(do))
        prod = do.astype(F32) * o_ref[j, 0].astype(F32)
        high = prod.astype(BF16)
        low[j] = dot(chosen, high, 1, 1) + dot(chosen, (prod - high.astype(F32)).astype(BF16), 1, 1)

    @pl.loop(0, pieces)
    def _(piece):
        back_piece(
            row * pieces + piece, piece, cnt_ref, idx_ref, qkv_ref.at[1], qkv_ref.at[2], lse_ref, seg_ref,
            kt, segk, dk, dv, dqt, qmt, gmt, qst, gst, low,
        )

    for j, ref in ((1, p1_ref), (3, p3_ref), (0, p0_ref), (2, p2_ref)):
        grad_q = turn(dqt[j].T * HEAD_DIM**-0.5, cos_ref[j], -sin_ref[j]).astype(BF16)
        grad_k = turn(dk[j] * (1 / LOG2E), cos_ref[j], -sin_ref[j]).astype(BF16)
        grad = jnp.concatenate([grad_q, grad_k, dv[j].astype(BF16)], axis=1)
        g_ref[j, 0] = grad
        ref[0] = dot(grad, w_ref[...]).astype(BF16)


def back_piece(
    at_q, piece, cnt_ref, idx_ref, k_ref, v_ref, lse_ref, seg_ref, kt, segk, dk, dv, dqt, qmt, gmt, qst, gst, low
):
    pieces, _, shard, width = k_ref.shape
    heads = width // HEAD_DIM
    lse, delta = lse_ref[0, piece], low[piece]
    seg_q = seg_ref[0, pl.ds(piece, 1)].astype(F32)

    def run(count):
        @pl.when(cnt_ref[at_q] == count)
        def _():
            places = [idx_ref[at_q * pieces + t] for t in range(count)]
            qm, gm = qmt[piece], gmt[piece]
            later = dot(k_ref[places[0], 0], qm), dot(v_ref[places[0], 0], gm)
            out = [None] * heads
            for t in range(count):
                s, dp = later
                j = places[t]
                if t + 1 < count:
                    later = dot(k_ref[places[t + 1], 0], qm), dot(v_ref[places[t + 1], 0], gm)
                col = segk[j]
                same = jnp.concatenate([col] * (shard // 128), axis=1) == seg_q
                ps, dss = [], []
                for h in range(heads):
                    at, qa = slice(h * HEAD_DIM, (h + 1) * HEAD_DIM), slice(h * shard, (h + 1) * shard)
                    p = jnp.exp2(jnp.where(same, s[:, qa] - lse[h : h + 1], NEG))
                    ds = (p * (dp[:, qa] - delta[h : h + 1])).astype(BF16)
                    ps.append(p.astype(BF16))
                    dss.append(ds)
                    found = dot(kt[j, at], ds)
                    out[h] = found if t == 0 else out[h] + found
                dv[j] += dot(jnp.concatenate(ps, axis=1), gst[piece])
                dk[j] += dot(jnp.concatenate(dss, axis=1), qst[piece])
            for h in range(heads):
                dqt[piece, h * HEAD_DIM : (h + 1) * HEAD_DIM] = out[h]

    for count in range(1, pieces + 1):
        run(count)


def attend_back(start, count, cnt, idx, qkv, o, do, lse, seg, cos_tab, sin_tab, weight, held=(), deps=()):
    _, pieces, rows, shard, width = qkv.shape
    model = weight.shape[1]
    heads = width // HEAD_DIM
    table = fixed((pieces, shard, 128))
    pairs = count * (pieces * shard) ** 2
    square, wide = (pieces, width, heads * shard), (pieces, shard, width)
    one = along((1, shard, width), 0, start)
    return call(
        functools.partial(attend_back_body, start), "attend_back", (cnt, idx), (count,),
        [(qkv, along((3, pieces, 1, shard, width), 2, start)), (o, along((pieces, 1, shard, width), 1, start))]
        + [(do[0], one), (do[1], one), (do[2], along((1, 1, shard, width), 1, start)), (do[3], one)]
        + [(lse, along((1, pieces, 8, shard), 0, start)), (seg, along((1, pieces, shard), 0, start))]
        + [(cos_tab, table), (sin_tab, table), (weight, fixed(weight.shape))],
        [((pieces, rows, shard, 3 * width), BF16, along((pieces, 1, shard, 3 * width), 1, start))]
        + [((count, shard, model), BF16, along((1, shard, model)))] * pieces,
        [
            pltpu.VMEM((pieces, width, shard), BF16),
            pltpu.VMEM((pieces, shard, 128), F32),
            pltpu.VMEM(wide, F32),
            pltpu.VMEM(wide, F32),
            pltpu.VMEM((pieces, width, shard), F32),
            pltpu.VMEM(square, BF16),
            pltpu.VMEM(square, BF16),
            pltpu.VMEM((pieces, heads * shard, width), BF16),
            pltpu.VMEM((pieces, heads * shard, width), BF16),
            pltpu.VMEM((pieces, 8, shard), F32),
        ],
        held=[(array, 0) for array in held], deps=deps
    )


def middle_body(
    order_ref, a0, a1, a2, a3, w0, w1, w2, w3, stream_ref, bias_ref, gain_ref, shift_ref, mid_ref, low_ref, all_ref,
):
    _, shard, model = stream_ref.shape
    total = 0.0
    for n, (a, w) in enumerate(((a0, w0), (a1, w1), (a2, w2), (a3, w3))):
        values = a[...].reshape(shard, a.shape[-1])
        total = total + dot(values, w[...])
        all_ref[0, :, n * a.shape[-1] : (n + 1) * a.shape[-1]] = values
    mid = stream_ref[0] + (total + line(bias_ref))
    hat, _ = centre(mid)
    mid_ref[0] = mid
    low_ref[0] = (hat * line(gain_ref) + line(shift_ref)).astype(BF16)


def out_blocks(weight, parts):
    width = weight.shape[0] // parts

    def block(i):
        return pl.BlockSpec((width, weight.shape[1]), lambda g, o: (o[i], 0))

    return [(weight, block(i)) for i in range(parts)]


def middle_norm(start, count, order, attended, weight, stream, vecs, held=()):
    rows, shard, model = stream.shape
    parts = len(attended)
    width = model // parts
    block, one = along((1, shard, model), 0, start), along((1, shard, width))
    first = [along((1, 1, shard, width), 1, start), one, along((1, 1, shard, width), 1), one]
    return call(
        middle_body, "middle", (order,), (count,),
        list(zip(attended, first)) + out_blocks(weight, parts) + [(stream, block)]
        + [(vec, fixed(vec.shape)) for vec in vecs],
        [
            (stream.shape, F32, block),
            ((count, shard, model), BF16, along((1, shard, model))),
            (stream.shape, BF16, block),
        ],
        held=list(zip(held, (0, 2)))
    )


def cot_body(blk_ref, a_ref, b_ref, up_ref, down_ref, g_ref, up_out, down_out, both_ref):
    tokens = a_ref.shape[0]
    down = down_ref[...]

    @pl.when(pl.program_id(0) == 0)
    def _():
        both_ref[0:tokens] = a_ref[...]
        both_ref[tokens:] = b_ref[...]

    g_ref[0:tokens] = dot(a_ref[...], down, 1, 1).astype(BF16)
    g_ref[tokens:] = dot(b_ref[...], down, 1, 1).astype(BF16)
    up_out[...] = up_ref[...]
    down_out[...] = down


def cot_down(blk, own, other, up, down, picked, half):
    tokens, model = own.shape
    steps = half // BLOCK
    column = along((2 * tokens, BLOCK), 1)
    if picked:
        up_at, down_at = along((model, BLOCK), 1), along((BLOCK, model))
    else:
        up_at = pl.BlockSpec((model, BLOCK), lambda g, b: (0, b[g]))
        down_at = pl.BlockSpec((BLOCK, model), lambda g, b: (b[g], 0))
    return call(
        cot_body, "cot_down", (blk,), (steps,),
        [(own, fixed(own.shape)), (other, fixed(own.shape)), (up, up_at), (down, down_at)],
        [
            ((2 * tokens, half), BF16, column),
            ((model, half), BF16, along((model, BLOCK), 1)),
            ((half, model), BF16, along((BLOCK, model))),
            ((2 * tokens, model), BF16, fixed((2 * tokens, model))),
        ]
    )


def hidden_body(blocks, blk_ref, *refs):
    pieces, refs = refs[:-10], refs[-10:]
    g_ref, up_ref, row_ref, bias_ref, act_ref, grad_ref, sum_ref, both_ref, part_ref, held = refs
    sizes = [ref.shape[0] * ref.shape[1] for ref in pieces]
    starts = [sum(sizes[:n]) for n in range(len(sizes))]
    step = pl.program_id(0)

    @pl.when(step == 0)
    def _():
        for ref, at, size in zip(pieces, starts, sizes):
            both_ref[at : at + size] = ref[...].reshape(size, ref.shape[2])

    @pl.when(step < blocks)
    def _():
        up = up_ref[...]
        bias = bias_ref[...].astype(F32)
        total = 0.0
        later = dot(pieces[0][...].reshape(sizes[0], -1), up)
        for n, (start, size) in enumerate(zip(starts, sizes)):
            at = slice(start, start + size)
            v = later + bias
            if n + 1 < len(pieces):
                later = dot(pieces[n + 1][...].reshape(sizes[n + 1], -1), up)
            square = v * v
            tanh = jnp.tanh(v * (GELU_A + GELU_B * square))
            gate = 0.5 + 0.5 * tanh
            act = v * gate
            slope = gate + act * ((1.0 - tanh) * (GELU_A + 3.0 * GELU_B * square))
            grad = (slope * g_ref[at].astype(F32)).astype(BF16)
            act_ref[at] = act.astype(BF16)
            grad_ref[at] = grad
            held[step, at] = grad
            total = total + jnp.sum(grad.astype(F32), axis=0, keepdims=True)
        sum_ref[...] = total

    @pl.when(step >= blocks)
    def _():
        grad = jnp.concatenate([held[n] for n in range(blocks)], axis=1)
        part_ref[...] = dot(grad, row_ref[...], 1, 1).astype(BF16)


def hidden_units(blk, pieces, grads, up, bias):
    model = pieces[0].shape[2]
    tokens, half = grads.shape
    blocks, more = half // BLOCK, model // BLOCK

    def first(g):
        return jnp.minimum(g, blocks - 1)

    def second(g):
        return jnp.maximum(g - blocks, 0)

    column = pl.BlockSpec((tokens, BLOCK), lambda g, b: (0, first(g)))
    line = pl.BlockSpec((1, BLOCK), lambda g, b: (0, first(g)))
    return call(
        functools.partial(hidden_body, blocks), "hidden", (blk,), (blocks + more,),
        [(piece, fixed(piece.shape)) for piece in pieces]
        + [
            (grads, column),
            (up, pl.BlockSpec((model, BLOCK), lambda g, b: (0, first(g)))),
            (up, pl.BlockSpec((BLOCK, half), lambda g, b: (second(g), 0))),
            (bias, pl.BlockSpec((1, BLOCK), lambda g, b: (0, b[first(g)]))),
        ],
        [
            (grads.shape, BF16, column),
            (grads.shape, BF16, column),
            ((1, half), F32, line),
            ((tokens, model), BF16, fixed((tokens, model))),
            ((tokens, model), BF16, pl.BlockSpec((tokens, BLOCK), lambda g, b: (0, second(g)))),
        ],
        [pltpu.VMEM((blocks, tokens, BLOCK), BF16)]
    )


def both_body(cot_ref, grad_ref, act_ref, tok_ref, out_ref):
    half, rows, model = out_ref.shape[1], out_ref.shape[3], out_ref.shape[4]
    size = act_ref.shape[1] // (2 * half)
    rest = tok_ref.shape[1] // (2 * half)
    down = dot(act_ref[...], cot_ref[...], 0, 0).astype(BF16)
    up = dot(tok_ref[...], grad_ref[...], 0, 0).astype(BF16)
    for x in range(2):
        for y in range(half):
            n = half * x + y
            out_ref[x, y, 0, 0:size] = down[n * size : (n + 1) * size]
            for s in range(2):
                at = size + s * rest
                out_ref[x, y, 0, at : at + rest] = up[n * rest : (n + 1) * rest, s * model : (s + 1) * model]


def both_grads(act, cot, tokens, grad, depth):
    count, half = act.shape
    model = cot.shape[1]
    size, rest = half // (4 * depth), model // (4 * depth)
    shape = (2, 2, depth, size + 2 * rest, model)
    if rest % 16 or size % 16:
        down = dot(act, cot, 0, 0).astype(BF16).reshape(depth, 2, 2, size, model)
        up = dot(tokens, grad, 0, 0).astype(BF16).reshape(depth, 2, 2, rest, 2, model)
        up = up.transpose(0, 1, 2, 4, 3, 5).reshape(depth, 2, 2, 2 * rest, model)
        return jnp.concatenate([down, up], axis=3).transpose(1, 2, 0, 3, 4)
    return call(
        both_body, "both_grads", (), (depth,),
        [
            (cot, fixed(cot.shape)),
            (grad, fixed(grad.shape)),
            (act, along((count, half // depth), 1)),
            (tokens, along((count, model // depth), 1)),
        ],
        [(shape, BF16, along((2, 2, 1) + shape[3:], 2))],
    )[0]


def feed_body(order_ref, act_ref, down_ref, att_ref, low_ref, feed_ref, out_ref, keep_ref):
    parts = order_ref.shape[0]
    width = att_ref.shape[1] // parts
    feed_ref[...] = dot(act_ref[...], down_ref[...]).astype(BF16)
    grad = dot(att_ref[...], low_ref[...], 0, 0).astype(BF16)
    step, steps = pl.program_id(0), pl.num_programs(0)

    def write(ref):
        for n in range(parts):
            at = pl.multiple_of(order_ref[n] * width, width)
            ref[pl.ds(at, width)] = grad[n * width : (n + 1) * width]

    @pl.when(2 * step < steps)
    def _():
        write(out_ref)

    @pl.when(2 * step >= steps)
    def _():
        write(keep_ref)


def feed_grads(order, act, down, attended, low, c_at, deps=()):
    tokens, half = act.shape
    own, model = attended.shape
    steps = model // BLOCK
    place = jnp.concatenate([order, c_at.astype(jnp.int32)[None]])

    def body(place_ref, *refs):
        feed_body(place_ref.at[0 : order.shape[0]], *refs)

    def low_at(g, p):
        c = p[order.shape[0]]
        mine = 2 * g >= steps
        return 0, jnp.where(mine, c * (steps // 2) + g - steps // 2, (1 - c) * (steps // 2) + g)

    return call(
        body, "feed_grads", (place,), (steps,),
        [
            (act, fixed(act.shape)),
            (down, along((half, BLOCK), 1)),
            (attended, fixed(attended.shape)),
            (low, pl.BlockSpec((own, BLOCK), low_at)),
        ],
        [
            ((tokens, model), BF16, along((tokens, BLOCK), 1)),
            ((model, model // 2), BF16, pl.BlockSpec((model, BLOCK), lambda g, p: (0, jnp.minimum(g, steps // 2 - 1)))),
            ((model, model // 2), BF16, pl.BlockSpec((model, BLOCK), lambda g, p: (0, jnp.maximum(g - steps // 2, 0)))),
        ],
        deps=deps,
    )


def middle_back_body(
    order_ref, part_ref, sent_ref, mid_ref, cot_ref, gain_ref, w0, w1, w2, w3,
    grad_ref, low_ref, att0_ref, att1_ref, far_ref, sums_ref,
):
    grad = part_ref[...].astype(F32) + sent_ref[...].astype(F32)
    hat, inverse = centre(mid_ref[0])
    cot = cot_ref[0].astype(F32)
    total = cot + norm_back(grad, line(gain_ref), hat, inverse)
    low = total.astype(BF16)
    grad_ref[0] = total
    low_ref[0] = low
    far_ref[0, 0] = dot(low, w2[...], 1, 1).astype(BF16)
    far_ref[1, 0] = dot(low, w3[...], 1, 1).astype(BF16)
    att1_ref[0] = dot(low, w1[...], 1, 1).astype(BF16)
    att0_ref[0] = dot(low, w0[...], 1, 1).astype(BF16)

    @pl.when(pl.program_id(0) == 0)
    def _():
        sums_ref[...] = jnp.zeros_like(sums_ref)

    sums_ref[0:1] += jnp.sum(grad * hat, axis=0, keepdims=True)
    sums_ref[1:2] += jnp.sum(grad, axis=0, keepdims=True)
    sums_ref[2:3] += jnp.sum(low.astype(F32), axis=0, keepdims=True)
    sums_ref[3:4] += jnp.sum(cot, axis=0, keepdims=True)


def middle_back(order, both, sent, mid, cot, gain, weight, parts, deps=()):
    rows, shard, model = mid.shape
    width = model // parts
    block, one = along((1, shard, model)), along((1, shard, width))
    flat = pl.BlockSpec((shard, model), lambda g, o: (g, 0))
    return call(
        middle_back_body, "middle_back", (order,), (rows,),
        [(both, flat), (sent, flat), (mid, block), (cot, block), (gain, fixed(gain.shape))] + out_blocks(weight, parts),
        [
            (mid.shape, F32, block),
            (mid.shape, BF16, block),
            ((rows, shard, width), BF16, one),
            ((rows, shard, width), BF16, one),
            ((2, rows, shard, width), BF16, along((2, 1, shard, width), 1)),
            ((8, model), F32, fixed((8, model))),
        ],
        deps=deps
    )


def norm1_back_body(start, part_ref, near_ref, far_ref, stream_ref, mid_ref, gain_ref, seg_ref, in_ref, shift_ref, sums_ref):
    grad = part_ref[0].astype(F32) + near_ref[0].astype(F32) + far_ref[0].astype(F32)
    hat, inverse = centre(stream_ref[0])
    total = mid_ref[0] + norm_back(grad, line(gain_ref), hat, inverse)
    in_ref[0] = total.astype(BF16)
    seg = seg_ref[pl.ds(pl.program_id(0) + start, 1)]
    slots = lax.broadcasted_iota(jnp.int32, (SEGS, seg.shape[-1]), 0) == seg
    onehot = slots.astype(F32).astype(BF16)
    shift_ref[0] = dot(jnp.concatenate([onehot, onehot], axis=1), split_low(total))

    @pl.when(pl.program_id(0) == 0)
    def _():
        sums_ref[...] = jnp.zeros_like(sums_ref)

    sums_ref[0:1] += jnp.sum(grad * hat, axis=0, keepdims=True)
    sums_ref[1:2] += jnp.sum(grad, axis=0, keepdims=True)


def norm1_back(start, count, own, near, far, stream, mid, gain, seg, held=(), deps=()):
    rows, shard, model = stream.shape
    block, own_block = along((1, shard, model), 0, start), along((1, shard, model))
    return call(
        functools.partial(norm1_back_body, start), "norm1_back", (), (count,),
        [(own, own_block), (near, own_block), (far, own_block), (stream, block), (mid, block), (gain, fixed(gain.shape))]
        + [(seg, fixed(seg.shape))],
        [
            (stream.shape, BF16, block),
            ((count, SEGS, model), F32, along((1, SEGS, model))),
            ((8, model), F32, fixed((8, model))),
        ],
        held=[(array, 0) for array in held], deps=deps
    )


def exchange(own, one, far):
    return [own, swap(one, "c"), far, swap(far[1], "c")]


def tie(*values):
    return lax.optimization_barrier(values)


def cut(values, index, size, axis):
    return lax.dynamic_slice_in_dim(values, index * size, size, axis)


def add_low(kept, sent):
    return (kept.astype(F32) + sent.astype(F32)).astype(BF16)


def over_z(values, at, depth):
    if depth != 4:
        return lax.psum_scatter(values, "z", scatter_dimension=0, tiled=False), []
    parts = [lax.dynamic_index_in_dim(values, at ^ n, 0, keepdims=False) for n in range(depth)]
    sent = [lax.ppermute(parts[n], "z", [(i, i ^ n) for i in range(depth)]) for n in range(1, depth)]
    return parts[0].astype(F32), sent


def ordered(at, own, other, axis):
    return jnp.where(at == 0, jnp.concatenate([own, other], axis), jnp.concatenate([other, own], axis))


def finish_body(blocks, at_ref, g0, g1, l0, l1, down_ref, up_ref, qkv_ref, out_ref):
    c_at = at_ref[0]
    width = up_ref.shape[1] // (4 * blocks)
    rest = up_ref.shape[0] // 2
    size = g0.shape[1] - 2 * rest
    for c in range(2):
        mine = c_at == c
        for y in range(2):
            grads = jnp.where(mine, g0[y], g1[y]).astype(F32)
            at = (2 * c + y) * size
            down_ref[at : at + size] = grads[0:size]
            for b in range(2 * blocks):
                s, at = b // blocks, b % blocks * width
                up_ref[y * rest : (y + 1) * rest, (2 * b + c) * width : (2 * b + c + 1) * width] = grads[
                    size + s * rest : size + (s + 1) * rest, at : at + width
                ]
        late = jnp.where(mine, l0[...], l1[...]).astype(F32)
        half = out_ref.shape[1] // 2
        wide = half // 2
        out_ref[:, c * half : (c + 1) * half] = late[:, 6 * wide :]
        for y in range(2):
            for n in range(3):
                at = n * 4 * wide + (2 * y + c) * wide
                qkv_ref[:, at : at + wide] = late[:, (3 * y + n) * wide : (3 * y + n + 1) * wide]


def finish(c_at, dp, piece, grads, late, parts):
    rows, model = late[0].shape[0], grads[0].shape[2]
    depth, rest = dp // 2, rows // 2
    size = grads[0].shape[1] - 2 * rest
    if piece % 128 == 0:
        at = c_at.astype(jnp.int32)[None]
        shapes = [(4 * size, model), (rows, 2 * dp * piece), (rows, 3 * model), (rows, model)]
        arrays = list(grads) + list(late)
        return call(
            functools.partial(finish_body, depth), "finish", (at,), (1,),
            [(array, fixed(array.shape)) for array in arrays], [(shape, F32, fixed(shape)) for shape in shapes],
        )
    both = ordered(c_at, grads[0][None], grads[1][None], 0)
    down_done = both[:, :, :size].reshape(4 * size, model).astype(F32)
    up_done = both[:, :, size:].reshape(2, 2, 2, rest, depth, piece).transpose(1, 3, 2, 4, 0, 5)
    up_done = up_done.reshape(rows, 2 * dp * piece).astype(F32)
    both = ordered(c_at, late[0][None], late[1][None], 0)
    width = model // parts
    qkv_done = both[:, :, : 6 * width].reshape(2, rows, 2, 3, width).transpose(1, 3, 2, 0, 4)
    qkv_done = qkv_done.reshape(rows, 3 * model).astype(F32)
    out_done = jnp.concatenate([both[0, :, 6 * width :], both[1, :, 6 * width :]], axis=1).astype(F32)
    return down_done, up_done, qkv_done, out_done


def local(
    inputs, segment_ids, doc_times, time_weight, time_bias, norm1_gain, norm1_bias, qkv_weight, qkv_bias,
    out_weight, out_bias, norm2_gain, norm2_bias, up_weight, up_bias, down_weight, down_bias, cotangent,
    *, dp,
):
    rows, shard, model = inputs.shape
    parts = 4
    tokens = rows * shard
    hidden_width = up_weight.shape[1]
    width = model // parts
    depth = dp // 2
    half = hidden_width // 2
    piece = half // dp
    z_at, x_at, y_at, c_at = (lax.axis_index(name) for name in ("z", "x", "y", "c"))
    me = 2 * y_at + c_at

    seg_two = swap(segment_ids, "y")
    segs = jnp.stack([segment_ids, swap(segment_ids, "c"), seg_two, swap(seg_two, "c")], axis=1)

    groups = [(0, rows - 1), (rows - 1, 1)] if rows > 1 else [(0, 1)]
    features = time_features(doc_times.reshape(rows * SEGS), jnp.arange(TEMB), TEMB // 2)
    time_shift = dot(features, time_weight).reshape(rows, SEGS, model)
    stream, own1 = norm1(inputs, segment_ids, time_shift, (time_bias, norm1_gain, norm1_bias))
    own1, segs = tie(own1, segs)
    two1 = swap(own1, "y")
    one1 = swap(own1, "c")

    me, x_at, z_at, c_at, y_at, own1 = tie(me, x_at, z_at, c_at, y_at, own1)
    order = [me ^ i for i in range(parts)]
    order_list = jnp.stack(order).astype(jnp.int32)
    me_list = order_list[:1]
    low_id, high_id = segs.min(axis=2), segs.max(axis=2)
    act = (low_id[:, :, None] <= high_id[:, None, :]) & (low_id[:, None, :] <= high_id[:, :, None])
    places = jnp.arange(parts, dtype=jnp.int32)
    rank = jnp.cumsum(act.astype(jnp.int32), axis=2) - 1
    chosen = act[..., None] & (rank[..., None] == places)
    idx = jnp.sum(jnp.where(chosen, places[:, None], 0), axis=2).astype(jnp.int32).reshape(-1)
    cnt = jnp.sum(act.astype(jnp.int32), axis=2).reshape(-1)
    positions = jnp.stack([o * shard + jnp.arange(shard, dtype=jnp.int32) for o in order])
    cos_tab, sin_tab = rotary_tables(positions, HEAD_DIM)

    cot = cotangent.reshape(tokens, model)
    cot_other = swap(cot, "c")
    if piece % BLOCK == 0:
        blk = (jnp.arange(dp)[:, None] * 2 + c_at) * (piece // BLOCK) + jnp.arange(piece // BLOCK)
        blk = blk.reshape(-1).astype(jnp.int32)
        up_from, down_from = up_weight, down_weight
    else:
        blk = jnp.zeros((half // BLOCK,), jnp.int32)
        up_from = lax.dynamic_index_in_dim(up_weight.reshape(model, dp, 2, piece), c_at, 2, keepdims=False)
        down_from = lax.dynamic_index_in_dim(down_weight.reshape(dp, 2, piece, model), c_at, 1, keepdims=False)
        up_from, down_from = up_from.reshape(model, half), down_from.reshape(half, model)
    grad_act, up_own, down_own, cot_both = cot_down(
        blk, cot, cot_other, up_from, down_from, piece % BLOCK != 0, half
    )
    up_bias_own, bias_blk = up_bias.reshape(1, hidden_width), blk
    if piece % BLOCK:
        up_bias_own = lax.dynamic_index_in_dim(up_bias.reshape(dp, 2, piece), c_at, 1, keepdims=False)
        up_bias_own, bias_blk = up_bias_own.reshape(1, half), jnp.arange(half // BLOCK, dtype=jnp.int32)

    qkv_line = qkv_bias.reshape(1, 3 * model)
    qkv, qkv_own = project_qkv(0, parts, me_list, own1, one1, qkv_weight, qkv_line, cos_tab, sin_tab, (), (grad_act,))
    two1, qkv = tie(two1, qkv)
    three1 = swap(two1, "c")
    qkv, _ = project_qkv(1, parts, me_list, two1, three1, qkv_weight, qkv_line, cos_tab, sin_tab, (qkv,))
    o, lse, attended = None, None, []
    for start, count in groups:
        held = () if o is None else (o, lse)
        o, out_one, out_far, lse = attend(start, count, cnt, idx, qkv, segs, held)
        attended.append((out_one, swap(out_far, "y")))
    held, normed2, normed2_other = (), [], []
    for (start, count), values in zip(groups, attended):
        far, o = tie(values[1], o)
        values = exchange(o, values[0], far)
        middle, low, attended_all = middle_norm(
            start, count, order_list, values, out_weight, stream, (out_bias, norm2_gain, norm2_bias), held
        )
        held = (middle, attended_all)
        normed2.append(low)
        normed2_other.append(swap(low, "c"))

    active, grad_hidden, up_b, normed2_both, part2 = hidden_units(
        bias_blk, normed2 + normed2_other, grad_act, up_own, up_bias_own
    )
    part2_sent = swap(part2[tokens:], "c")
    grad_middle, grad_middle_low, att0, att1, far, sums2 = middle_back(
        order_list, part2, part2_sent, middle, cotangent, norm2_gain, out_weight, parts
    )
    far = swap(far, "y")
    sums2 = sums2[:4]

    active, grad_hidden, att0 = tie(active, grad_hidden, att0)
    grads = both_grads(active, cot_both, normed2_both, grad_hidden, depth)
    grads = lax.psum_scatter(grads.reshape((4,) + grads.shape[2:]), ("x", "y"), scatter_dimension=0, tiled=False)
    feed, out_sent, out_grad = feed_grads(
        order_list, active, down_own, attended_all.reshape(tokens, model), grad_middle_low.reshape(tokens, model), c_at,
        (far,),
    )
    out_sent = swap(out_sent, "c")
    feed = feed[:tokens].astype(F32) + swap(feed[tokens:], "c").astype(F32) + down_bias.astype(F32)
    output = (middle + feed.reshape(rows, shard, model)).astype(BF16)
    up_rows = model // dp
    out_c = add_low(out_grad, out_sent)

    output, out_c, far = tie(output, out_c, far)
    grad_o = exchange(att0, att1, far)
    grad_qkv, back = (), []
    for start, count in groups:
        grad_qkv, own, one, two, three = attend_back(
            start, count, cnt, idx, qkv, o, grad_o, lse, segs, cos_tab, sin_tab, qkv_own, grad_qkv,
            (there, out_x) if back else (),
        )
        grad_qkv = (grad_qkv,)
        there = add_low(two, swap(three, "c"))
        if not back:
            own, out_c = tie(own, out_c.reshape(depth, 2 * up_rows, model // 2))
            out_x = cut(out_c, 1 - x_at, up_rows, 1)
        back.append((own, swap(one, "c"), swap(there, "y")))
    grad_qkv, there, far = tie(grad_qkv[0], there, back[0][2])
    back[0] = back[0][:2] + (far,)
    back[-1] = back[-1][:2] + (swap(there, "y"),)
    qkv_out, qkv_kept, qkv_b = qkv_grads(x_at, [own1, one1, two1, three1], grad_qkv, depth)
    qkv_sent = swap(qkv_out, "x")
    qkv_kept, out_c, grads, out_x = tie(qkv_kept, out_c, grads, swap(out_x, "x"))
    grads = lax.psum_scatter(grads, "z", scatter_dimension=0, tiled=False)
    out_x = add_low(cut(out_c, x_at, up_rows, 1), out_x)
    held, grad_shift, sums1 = (), [], 0.0
    for (start, count), values in zip(groups, back):
        input_grad, found, sums = norm1_back(
            start, count, *values, stream, grad_middle, norm1_gain, segment_ids, held, (out_x if held else qkv_kept,)
        )
        held = (input_grad,)
        grad_shift.append(found.reshape(count * SEGS, model))
        sums1 = sums1 + sums[:2]
    qkv_x = jnp.concatenate([add_low(qkv_kept, qkv_sent), out_x], axis=2)

    up_b = up_b.reshape(dp, 1, piece)
    up_b = jnp.where(jnp.arange(2)[:, None] == c_at, up_b, 0.0).reshape(-1, model)
    qkv_b = jnp.where(jnp.arange(parts)[:, None] == me, qkv_b.reshape(3, 1, width), 0.0).reshape(3, model)
    times = doc_times.reshape(1, rows * SEGS)
    times = jnp.concatenate([times // 32, times % 32], axis=1).astype(F32)
    times = jnp.pad(times, ((0, 0), (0, model - times.shape[1])))
    small = jnp.concatenate(grad_shift + [sums1, sums2, qkv_b, up_b, times], axis=0)
    small, qkv_x = tie(add_low(small, swap(small.astype(BF16), "c")), qkv_x)
    late, late_parts = over_z(qkv_x, z_at, depth)
    small = add_low(small, swap(small, "y"))
    small = ordered(x_at, small[None], swap(small, "x")[None], 0)
    if depth == 4:
        others = [lax.ppermute(small, "z", [(i, i ^ n) for i in range(depth)]) for n in range(1, depth)]
        small = jnp.stack([small] + others)
        small = jnp.stack([lax.dynamic_index_in_dim(small, z_at ^ n, 0, keepdims=False) for n in range(depth)])
    else:
        small = lax.all_gather(small, "z")
    small = small.reshape(dp, small.shape[2], model)

    small, late = tie(small, late)
    late = (late + sum(part.astype(F32) for part in late_parts)).astype(BF16) if depth == 4 else late
    late_sent = swap(late, "y")
    qkv_y = ordered(y_at, late[None, :, : 3 * width], late_sent[None, :, : 3 * width], 0)
    out_y = add_low(late[:, 3 * width :], late_sent[:, 3 * width :])
    late = jnp.concatenate([qkv_y[0], qkv_y[1], out_y], axis=1)
    late_other = swap(late, "c")
    grads = ordered(y_at, grads[None], swap(grads, "y")[None], 0)
    grads_other = swap(grads, "c")

    down_done, up_done, qkv_done, out_done = finish(
        c_at, dp, piece, (grads, grads_other), (late, late_other), parts
    )

    all_times = small[:, -1, : 2 * rows * SEGS].astype(F32) * 0.25
    all_times = all_times[:, : rows * SEGS] * 32.0 + all_times[:, rows * SEGS :]
    shifts = small[:, : rows * SEGS].reshape(dp * rows * SEGS, model)
    columns = (2 * z_at + x_at) * (TEMB // dp) + jnp.arange(TEMB // dp)
    wanted = time_features(all_times.reshape(-1), columns, TEMB // 2)
    time_w_done = dot(wanted, shifts, 0, 0)
    sums = jnp.sum(small[:, rows * SEGS :].astype(F32), axis=0)
    dp_at = 2 * z_at + x_at

    def share(vector):
        return cut(vector.reshape(-1), dp_at, vector.size // dp, 0)

    time_b_done = jnp.sum(cut(shifts, dp_at, up_rows, 1).astype(F32), axis=0)
    return (
        output, input_grad, time_w_done, time_b_done, share(sums[0]), share(sums[1]), qkv_done, share(sums[6:9]),
        out_done, share(sums[4]), share(sums[2]), share(sums[3]), up_done, share(sums[9:-1]), down_done, share(sums[5]),
    )


def solution(mesh):
    dp, seq = mesh.shape["dp"], mesh.shape["seq"]
    fine = Mesh(mesh.devices.reshape(dp // 2, 2, seq // 2, 2), ("z", "x", "y", "c"))
    rows, seqs = ("z", "x"), ("y", "c")
    placed = (P(rows, seqs, None), P(rows, seqs), P(rows, None)) + (P(),) * 14 + (P(rows, seqs, None),)
    vec, mat = P(rows), P(rows, None)
    return jax.shard_map(
        functools.partial(local, dp=dp),
        mesh=fine,
        in_specs=placed,
        out_specs=(
            P(rows, seqs, None), P(rows, seqs, None), mat, vec, vec, vec, mat, vec, mat, vec, vec, vec, mat, vec, mat, vec,
        ),
        check_vma=False,
    )
```

```python
import functools
import math

import jax
import jax.numpy as jnp
from jax import lax
from jax.experimental import pallas as pl
from jax.experimental.pallas import tpu as pltpu
from jax.sharding import Mesh, PartitionSpec as P

HEADS = 16
HEAD_DIM = 64
TEMB = 256
SEGS = 8
EPSILON = 1e-05
F32 = jnp.float32
BF16 = jnp.bfloat16
NEG = -1e30
LOG2E = math.log2(math.e)
GELU_A = math.sqrt(2.0 / math.pi)
GELU_B = GELU_A * 0.044715
BLOCK = 256
VMEM = 60 * 1024 * 1024


def swap(value, axis):
    return lax.ppermute(value, axis, [(0, 1), (1, 0)])


def time_features(doc_times, column, half_size):
    frequency = jnp.exp(-math.log(10000.0) * (column % half_size).astype(F32) / half_size)
    angles = doc_times.astype(F32)[..., None] * frequency
    return jnp.where(column < half_size, jnp.sin(angles), jnp.cos(angles)).astype(BF16)


def rotary_tables(positions, head_size):
    half_size = head_size // 2
    frequency = jnp.exp(-math.log(10000.0) * 2.0 * jnp.arange(half_size, dtype=F32) / head_size)
    angles = positions.astype(F32)[..., None] * frequency
    cos_tab, sin_tab = jnp.cos(angles), jnp.sin(angles)
    return (
        jnp.concatenate([cos_tab] * 4, axis=-1),
        jnp.concatenate([-sin_tab, sin_tab, -sin_tab, sin_tab], axis=-1),
    )


def dot(left_op, right_op, left_dim=1, right_dim=0):
    return lax.dot_general(
        left_op, right_op, (((left_dim,), (right_dim,)), ((), ())), preferred_element_type=F32
    )


def turn(values, cos_tab, sin_tab):
    slabs = []
    lane = lax.broadcasted_iota(jnp.int32, (values.shape[0], 128), 1)
    first = lane % HEAD_DIM < HEAD_DIM // 2
    for start in range(0, values.shape[1], 128):
        slab = values[:, start : start + 128]
        partner = jnp.where(
            first, pltpu.roll(slab, 128 - HEAD_DIM // 2, 1), pltpu.roll(slab, HEAD_DIM // 2, 1)
        )
        slabs.append(slab * cos_tab + partner * sin_tab)
    return jnp.concatenate(slabs, axis=1)


def split_low(values):
    high = values.astype(BF16)
    return jnp.concatenate([high, (values - high.astype(F32)).astype(BF16)], axis=0)


def centre(values):
    scale = 1.0 / values.shape[-1]
    centred = values - jnp.sum(values, axis=-1, keepdims=True) * scale
    spread = jnp.sum(centred * centred, axis=-1, keepdims=True) * scale
    inverse = lax.rsqrt(spread + EPSILON)
    return centred * inverse, inverse


def norm_back(grad, gain, hat, inverse):
    scale = 1.0 / grad.shape[-1]
    scaled = grad * gain
    mean = jnp.sum(scaled, axis=-1, keepdims=True) * scale
    along = jnp.sum(scaled * hat, axis=-1, keepdims=True) * scale
    return inverse * (scaled - mean - hat * along)


def call(body, name, prefetch, grid, ins, outs, scratch=(), deps=(), held=()):
    count = len(prefetch) + len(ins)
    extra = [array for array, _ in held] + list(deps)

    def kernel(*refs):
        body(*refs[:count], *refs[count + len(extra) :])

    return pl.pallas_call(
        kernel,
        grid_spec=pltpu.PrefetchScalarGridSpec(
            num_scalar_prefetch=len(prefetch),
            grid=grid,
            in_specs=[spec for _, spec in ins] + [pl.BlockSpec(memory_space=pl.ANY)] * len(extra),
            out_specs=[spec for _, _, spec in outs],
            scratch_shapes=list(scratch),
        ),
        out_shape=[jax.ShapeDtypeStruct(shape, kind) for shape, kind, _ in outs],
        input_output_aliases={count + n: out for n, (_, out) in enumerate(held)},
        compiler_params=pltpu.CompilerParams(vmem_limit_bytes=VMEM),
        name=name,
    )(*prefetch, *[array for array, _ in ins], *extra)


def line(ref):
    return ref[...].astype(F32).reshape(1, -1)


def fixed(shape):
    return pl.BlockSpec(shape, lambda *_: (0,) * len(shape))


def along(shape, axis=0, start=0):
    return pl.BlockSpec(shape, lambda g, *_: tuple(start + g if n == axis else 0 for n in range(len(shape))))


def norm1_body(x_ref, seg_ref, shift_ref, time_ref, gain_ref, bias_ref, stream_ref, low_ref):
    seg = seg_ref[pl.ds(pl.program_id(0), 1)]
    slots = lax.broadcasted_iota(jnp.int32, (SEGS, seg.shape[-1]), 0) == seg
    onehot = slots.astype(F32).astype(BF16)
    shift = shift_ref[0] + line(time_ref)
    added = dot(jnp.concatenate([onehot, onehot], axis=0), split_low(shift), 0, 0)
    stream = x_ref[0].astype(F32) + added
    hat, _ = centre(stream)
    stream_ref[0] = stream
    low_ref[0] = (hat * line(gain_ref) + line(bias_ref)).astype(BF16)


def norm1(x, seg, shift, vecs):
    rows, shard, model = x.shape
    block = along((1, shard, model))
    return call(
        norm1_body, "norm1", (), (rows,),
        [(x, block), (seg, fixed(seg.shape)), (shift, along((1, SEGS, model)))]
        + [(vec, fixed(vec.shape)) for vec in vecs],
        [(x.shape, F32, block), (x.shape, BF16, block)],
    )


def qkv_body(me_ref, a_ref, b_ref, w_ref, bias_ref, cos_ref, sin_ref, out_ref, own_ref):
    rows, shard, model = a_ref.shape
    width = w_ref.shape[1]
    places = [(n, r) for n in range(2) for r in range(rows)]
    step = pl.program_id(0)

    def run(turned):
        w = w_ref[...]
        bias = bias_ref[...].astype(F32)
        later = dot(a_ref[0], w)
        for at, (n, r) in enumerate(places):
            values = later + bias
            if at + 1 < len(places):
                x_ref = (a_ref, b_ref)[places[at + 1][0]]
                later = dot(x_ref[places[at + 1][1]], w)
            if turned:
                values = turn(values, cos_ref[n], sin_ref[n]) * jnp.where(step == 0, LOG2E * HEAD_DIM**-0.5, 1.0)
            out_ref[0, n, r] = values.astype(BF16)

    own_ref[...] = w_ref[...].T

    @pl.when(step < 2)
    def _():
        run(True)

    @pl.when(step == 2)
    def _():
        run(False)


def project_qkv(pair, parts, me, first, second, weight, bias, cos_tab, sin_tab, held=(), deps=()):
    rows, shard, model = first.shape
    width = model // parts
    return call(
        qkv_body, "qkv", (me,), (3,),
        [(first, fixed(first.shape)), (second, fixed(first.shape))]
        + [
            (weight, pl.BlockSpec((model, width), lambda g, m: (0, g * parts + m[0]))),
            (bias, pl.BlockSpec((1, width), lambda g, m: (0, g * parts + m[0]))),
            (cos_tab, pl.BlockSpec((2, shard, 128), lambda g, m: (pair, 0, 0))),
            (sin_tab, pl.BlockSpec((2, shard, 128), lambda g, m: (pair, 0, 0))),
        ],
        [
            ((3, parts, rows, shard, width), BF16, pl.BlockSpec((1, 2, rows, shard, width), lambda g, m: (g, pair, 0, 0, 0))),
            ((3 * width, model), BF16, along((width, model))),
        ],
        held=[(array, n) for n, array in enumerate(held)], deps=deps,
    )


def qkv_grads(x_at, pieces, grad, blocks, deps=()):
    rows, shard, model = pieces[0].shape
    tokens = rows * shard
    parts, columns = len(pieces), grad.shape[3]
    size = model // (2 * blocks)

    def body(at_ref, x0, x1, x2, x3, g_ref, out_ref, keep_ref, sum_ref):
        total, sums = 0.0, 0.0
        for n, x_ref in enumerate((x0, x1, x2, x3)):
            g = g_ref[n].reshape(tokens, g_ref.shape[3])
            total = total + dot(x_ref[...].reshape(tokens, model), g, 0, 0)
            sums = sums + jnp.sum(g.astype(F32), axis=0, keepdims=True)
        low = total.astype(BF16)
        for x in range(2):
            for b in range(blocks):
                values = low[(2 * b + x) * size : (2 * b + x + 1) * size]

                @pl.when(at_ref[0] == x)
                def _():
                    keep_ref[b] = values

                @pl.when(at_ref[0] != x)
                def _():
                    out_ref[b] = values

        sum_ref[...] = sums

    block = along((blocks, size, BLOCK), 2)
    shape = (blocks, size, columns)
    return call(
        body, "qkv_grads", (x_at.astype(jnp.int32)[None],), (columns // BLOCK,),
        [(x, fixed(x.shape)) for x in pieces] + [(grad, along((parts, rows, shard, BLOCK), 3))],
        [(shape, BF16, block), (shape, BF16, block), ((1, columns), F32, along((1, BLOCK), 1))],
        deps=deps,
    )


def seg_columns(segq_all, segk):
    pieces, shard, _ = segk.shape
    for j in range(pieces):
        row = jnp.broadcast_to(segq_all[j:j+1].astype(F32), (128, shard))
        segk[j] = row.T

def attend_body(start, cnt_ref, idx_ref, qkv_ref, seg_ref, o_ref, one_ref, far_ref, lse_ref, vt, segk, qmt, acc):
    row = pl.program_id(0) + start
    _, pieces, _, shard, width = qkv_ref.shape
    heads = width // HEAD_DIM

    @pl.when(pl.program_id(0) == 0)
    def _():
        qmt[...] = jnp.zeros_like(qmt)

    for j in range(pieces):
        vt[j] = qkv_ref[2, j, 0].T
        qt = qkv_ref[0, j, 0].T
        for h in range(heads):
            at = slice(h * HEAD_DIM, (h + 1) * HEAD_DIM)
            qmt[j, at, h * shard : (h + 1) * shard] = qt[at]
    seg_columns(seg_ref[0], segk)

    @pl.loop(0, pieces)
    def _(piece):
        attend_piece(row * pieces + piece, piece, cnt_ref, idx_ref, qkv_ref.at[1], seg_ref, lse_ref, vt, segk, qmt, acc)

    for j in range(pieces):
        o_ref[j, 0] = acc[j].T.astype(BF16)
    one_ref[0] = o_ref[1, 0]
    far_ref[:, 0] = o_ref[2:, 0]


def attend_piece(at_q, piece, cnt_ref, idx_ref, k_ref, seg_ref, lse_ref, vt, segk, qmt, acc):
    pieces, _, shard, width = k_ref.shape
    heads = width // HEAD_DIM
    seg_q = seg_ref[0, pl.ds(piece, 1)].astype(F32)

    def run(count):
        @pl.when(cnt_ref[at_q] == count)
        def _():
            qm = qmt[piece]
            places = [idx_ref[at_q * pieces + t] for t in range(count)]
            top, tot, out = [None] * heads, [None] * heads, [None] * heads
            later = dot(k_ref[places[0], 0], qm)
            for t in range(count):
                s = later
                if t + 1 < count:
                    later = dot(k_ref[places[t + 1], 0], qm)
                col = segk[places[t]]
                same = jnp.concatenate([col] * (shard // 128), axis=1) == seg_q
                for h in range(heads):
                    at = slice(h * HEAD_DIM, (h + 1) * HEAD_DIM)
                    sh = jnp.where(same, s[:, h * shard : (h + 1) * shard], NEG)
                    best = jnp.max(sh, axis=0, keepdims=True)
                    if t:
                        best = jnp.maximum(top[h], best)
                        fade = jnp.exp2(top[h] - best)
                    p = jnp.exp2(sh - best)
                    total = jnp.sum(p, axis=0, keepdims=True)
                    found = dot(vt[places[t], at], p.astype(BF16))
                    if t:
                        total = tot[h] * fade + total
                        found = out[h] * fade + found
                    top[h], tot[h], out[h] = best, total, found
            for h in range(heads):
                acc[piece, h * HEAD_DIM : (h + 1) * HEAD_DIM] = out[h] / tot[h]
                lse_ref[0, piece, h : h + 1] = top[h] + jnp.log2(tot[h])

    for count in range(1, pieces + 1):
        run(count)


def attend(start, count, cnt, idx, qkv, seg, held=()):
    _, pieces, rows, shard, width = qkv.shape
    heads = width // HEAD_DIM
    pairs = count * (pieces * shard) ** 2
    return call(
        functools.partial(attend_body, start), "attend", (cnt, idx), (count,),
        [(qkv, along((3, pieces, 1, shard, width), 2, start)), (seg, along((1, pieces, shard), 0, start))],
        [
            ((pieces, rows, shard, width), BF16, along((pieces, 1, shard, width), 1, start)),
            ((count, shard, width), BF16, along((1, shard, width))),
            ((2, count, shard, width), BF16, along((2, 1, shard, width), 1)),
            ((rows, pieces, 8, shard), F32, along((1, pieces, 8, shard), 0, start)),
        ],
        [
            pltpu.VMEM((pieces, width, shard), BF16),
            pltpu.VMEM((pieces, shard, 128), F32),
            pltpu.VMEM((pieces, width, heads * shard), BF16),
            pltpu.VMEM((pieces, width, shard), F32),
        ],
        held=list(zip(held, (0, 3)))
    )


def attend_back_body(
    start, cnt_ref, idx_ref, qkv_ref, o_ref, do0, do1, do2, do3, lse_ref, seg_ref, cos_ref, sin_ref, w_ref,
    g_ref, p0_ref, p1_ref, p2_ref, p3_ref, kt, segk, dk, dv, dqt, qmt, gmt, qst, gst, low,
):
    row = pl.program_id(0) + start
    _, pieces, _, shard, width = qkv_ref.shape
    heads = width // HEAD_DIM

    @pl.when(pl.program_id(0) == 0)
    def _():
        qmt[...] = jnp.zeros_like(qmt)
        gmt[...] = jnp.zeros_like(gmt)

    seg_columns(seg_ref[0], segk)
    dk[...] = jnp.zeros_like(dk)
    dv[...] = jnp.zeros_like(dv)
    lane = lax.broadcasted_iota(jnp.int32, (shard, width), 1) // HEAD_DIM
    chosen = lax.broadcasted_iota(jnp.int32, (8, width), 1) // HEAD_DIM
    chosen = (chosen == lax.broadcasted_iota(jnp.int32, (8, width), 0)).astype(BF16)
    for j, do_ref in enumerate((do0, do1, do2, do3)):
        kt[j] = qkv_ref[1, j, 0].T
        q, do = qkv_ref[0, j, 0], do_ref[...].reshape(shard, width)
        qt, gt = q.T, do.T
        for h in range(heads):
            at, qa = slice(h * HEAD_DIM, (h + 1) * HEAD_DIM), slice(h * shard, (h + 1) * shard)
            qmt[j, at, qa] = qt[at]
            gmt[j, at, qa] = gt[at]
            qst[j, qa] = jnp.where(lane == h, q, jnp.zeros_like(q))
            gst[j, qa] = jnp.where(lane == h, do, jnp.zeros_like(do))
        prod = do.astype(F32) * o_ref[j, 0].astype(F32)
        high = prod.astype(BF16)
        low[j] = dot(chosen, high, 1, 1) + dot(chosen, (prod - high.astype(F32)).astype(BF16), 1, 1)

    @pl.loop(0, pieces)
    def _(piece):
        back_piece(
            row * pieces + piece, piece, cnt_ref, idx_ref, qkv_ref.at[1], qkv_ref.at[2], lse_ref, seg_ref,
            kt, segk, dk, dv, dqt, qmt, gmt, qst, gst, low,
        )

    for j, ref in ((1, p1_ref), (3, p3_ref), (0, p0_ref), (2, p2_ref)):
        grad_q = turn(dqt[j].T * HEAD_DIM**-0.5, cos_ref[j], -sin_ref[j]).astype(BF16)
        grad_k = turn(dk[j] * (1 / LOG2E), cos_ref[j], -sin_ref[j]).astype(BF16)
        grad = jnp.concatenate([grad_q, grad_k, dv[j].astype(BF16)], axis=1)
        g_ref[j, 0] = grad
        ref[0] = dot(grad, w_ref[...]).astype(BF16)


def back_piece(
    at_q, piece, cnt_ref, idx_ref, k_ref, v_ref, lse_ref, seg_ref, kt, segk, dk, dv, dqt, qmt, gmt, qst, gst, low
):
    pieces, _, shard, width = k_ref.shape
    heads = width // HEAD_DIM
    lse, delta = lse_ref[0, piece], low[piece]
    seg_q = seg_ref[0, pl.ds(piece, 1)].astype(F32)

    def run(count):
        @pl.when(cnt_ref[at_q] == count)
        def _():
            places = [idx_ref[at_q * pieces + t] for t in range(count)]
            qm, gm = qmt[piece], gmt[piece]
            later = dot(k_ref[places[0], 0], qm), dot(v_ref[places[0], 0], gm)
            out = [None] * heads
            for t in range(count):
                s, dp = later
                j = places[t]
                if t + 1 < count:
                    later = dot(k_ref[places[t + 1], 0], qm), dot(v_ref[places[t + 1], 0], gm)
                col = segk[j]
                same = jnp.concatenate([col] * (shard // 128), axis=1) == seg_q
                ps, dss = [], []
                for h in range(heads):
                    at, qa = slice(h * HEAD_DIM, (h + 1) * HEAD_DIM), slice(h * shard, (h + 1) * shard)
                    p = jnp.exp2(jnp.where(same, s[:, qa] - lse[h : h + 1], NEG))
                    ds = (p * (dp[:, qa] - delta[h : h + 1])).astype(BF16)
                    ps.append(p.astype(BF16))
                    dss.append(ds)
                    found = dot(kt[j, at], ds)
                    out[h] = found if t == 0 else out[h] + found
                dv[j] += dot(jnp.concatenate(ps, axis=1), gst[piece])
                dk[j] += dot(jnp.concatenate(dss, axis=1), qst[piece])
            for h in range(heads):
                dqt[piece, h * HEAD_DIM : (h + 1) * HEAD_DIM] = out[h]

    for count in range(1, pieces + 1):
        run(count)


def attend_back(start, count, cnt, idx, qkv, o, do, lse, seg, cos_tab, sin_tab, weight, held=(), deps=()):
    _, pieces, rows, shard, width = qkv.shape
    model = weight.shape[1]
    heads = width // HEAD_DIM
    table = fixed((pieces, shard, 128))
    pairs = count * (pieces * shard) ** 2
    square, wide = (pieces, width, heads * shard), (pieces, shard, width)
    one = along((1, shard, width), 0, start)
    return call(
        functools.partial(attend_back_body, start), "attend_back", (cnt, idx), (count,),
        [(qkv, along((3, pieces, 1, shard, width), 2, start)), (o, along((pieces, 1, shard, width), 1, start))]
        + [(do[0], one), (do[1], one), (do[2], along((1, 1, shard, width), 1, start)), (do[3], one)]
        + [(lse, along((1, pieces, 8, shard), 0, start)), (seg, along((1, pieces, shard), 0, start))]
        + [(cos_tab, table), (sin_tab, table), (weight, fixed(weight.shape))],
        [((pieces, rows, shard, 3 * width), BF16, along((pieces, 1, shard, 3 * width), 1, start))]
        + [((count, shard, model), BF16, along((1, shard, model)))] * pieces,
        [
            pltpu.VMEM((pieces, width, shard), BF16),
            pltpu.VMEM((pieces, shard, 128), F32),
            pltpu.VMEM(wide, F32),
            pltpu.VMEM(wide, F32),
            pltpu.VMEM((pieces, width, shard), F32),
            pltpu.VMEM(square, BF16),
            pltpu.VMEM(square, BF16),
            pltpu.VMEM((pieces, heads * shard, width), BF16),
            pltpu.VMEM((pieces, heads * shard, width), BF16),
            pltpu.VMEM((pieces, 8, shard), F32),
        ],
        held=[(array, 0) for array in held], deps=deps
    )


def middle_body(
    order_ref, a0, a1, a2, a3, w0, w1, w2, w3, stream_ref, bias_ref, gain_ref, shift_ref, mid_ref, low_ref, all_ref,
):
    _, shard, model = stream_ref.shape
    total = 0.0
    for n, (a, w) in enumerate(((a0, w0), (a1, w1), (a2, w2), (a3, w3))):
        values = a[...].reshape(shard, a.shape[-1])
        total = total + dot(values, w[...])
        all_ref[0, :, n * a.shape[-1] : (n + 1) * a.shape[-1]] = values
    mid = stream_ref[0] + (total + line(bias_ref))
    hat, _ = centre(mid)
    mid_ref[0] = mid
    low_ref[0] = (hat * line(gain_ref) + line(shift_ref)).astype(BF16)


def out_blocks(weight, parts):
    width = weight.shape[0] // parts

    def block(i):
        return pl.BlockSpec((width, weight.shape[1]), lambda g, o: (o[i], 0))

    return [(weight, block(i)) for i in range(parts)]


def middle_norm(start, count, order, attended, weight, stream, vecs, held=()):
    rows, shard, model = stream.shape
    parts = len(attended)
    width = model // parts
    block, one = along((1, shard, model), 0, start), along((1, shard, width))
    first = [along((1, 1, shard, width), 1, start), one, along((1, 1, shard, width), 1), one]
    return call(
        middle_body, "middle", (order,), (count,),
        list(zip(attended, first)) + out_blocks(weight, parts) + [(stream, block)]
        + [(vec, fixed(vec.shape)) for vec in vecs],
        [
            (stream.shape, F32, block),
            ((count, shard, model), BF16, along((1, shard, model))),
            (stream.shape, BF16, block),
        ],
        held=list(zip(held, (0, 2)))
    )


def cot_body(blk_ref, a_ref, b_ref, up_ref, down_ref, g_ref, up_out, down_out, both_ref):
    tokens = a_ref.shape[0]
    down = down_ref[...]

    @pl.when(pl.program_id(0) == 0)
    def _():
        both_ref[0:tokens] = a_ref[...]
        both_ref[tokens:] = b_ref[...]

    g_ref[0:tokens] = dot(a_ref[...], down, 1, 1).astype(BF16)
    g_ref[tokens:] = dot(b_ref[...], down, 1, 1).astype(BF16)
    up_out[...] = up_ref[...]
    down_out[...] = down


def cot_down(blk, own, other, up, down, picked, half):
    tokens, model = own.shape
    steps = half // BLOCK
    column = along((2 * tokens, BLOCK), 1)
    if picked:
        up_at, down_at = along((model, BLOCK), 1), along((BLOCK, model))
    else:
        up_at = pl.BlockSpec((model, BLOCK), lambda g, b: (0, b[g]))
        down_at = pl.BlockSpec((BLOCK, model), lambda g, b: (b[g], 0))
    return call(
        cot_body, "cot_down", (blk,), (steps,),
        [(own, fixed(own.shape)), (other, fixed(own.shape)), (up, up_at), (down, down_at)],
        [
            ((2 * tokens, half), BF16, column),
            ((model, half), BF16, along((model, BLOCK), 1)),
            ((half, model), BF16, along((BLOCK, model))),
            ((2 * tokens, model), BF16, fixed((2 * tokens, model))),
        ]
    )


def hidden_body(blocks, blk_ref, *refs):
    pieces, refs = refs[:-10], refs[-10:]
    g_ref, up_ref, row_ref, bias_ref, act_ref, grad_ref, sum_ref, both_ref, part_ref, held = refs
    sizes = [ref.shape[0] * ref.shape[1] for ref in pieces]
    starts = [sum(sizes[:n]) for n in range(len(sizes))]
    step = pl.program_id(0)

    @pl.when(step == 0)
    def _():
        for ref, at, size in zip(pieces, starts, sizes):
            both_ref[at : at + size] = ref[...].reshape(size, ref.shape[2])

    @pl.when(step < blocks)
    def _():
        up = up_ref[...]
        bias = bias_ref[...].astype(F32)
        total = 0.0
        later = dot(pieces[0][...].reshape(sizes[0], -1), up)
        for n, (start, size) in enumerate(zip(starts, sizes)):
            at = slice(start, start + size)
            v = later + bias
            if n + 1 < len(pieces):
                later = dot(pieces[n + 1][...].reshape(sizes[n + 1], -1), up)
            square = v * v
            tanh = jnp.tanh(v * (GELU_A + GELU_B * square))
            gate = 0.5 + 0.5 * tanh
            act = v * gate
            slope = gate + act * ((1.0 - tanh) * (GELU_A + 3.0 * GELU_B * square))
            grad = (slope * g_ref[at].astype(F32)).astype(BF16)
            act_ref[at] = act.astype(BF16)
            grad_ref[at] = grad
            held[step, at] = grad
            total = total + jnp.sum(grad.astype(F32), axis=0, keepdims=True)
        sum_ref[...] = total

    @pl.when(step >= blocks)
    def _():
        grad = jnp.concatenate([held[n] for n in range(blocks)], axis=1)
        part_ref[...] = dot(grad, row_ref[...], 1, 1).astype(BF16)


def hidden_units(blk, pieces, grads, up, bias):
    model = pieces[0].shape[2]
    tokens, half = grads.shape
    blocks, more = half // BLOCK, model // BLOCK

    def first(g):
        return jnp.minimum(g, blocks - 1)

    def second(g):
        return jnp.maximum(g - blocks, 0)

    column = pl.BlockSpec((tokens, BLOCK), lambda g, b: (0, first(g)))
    line = pl.BlockSpec((1, BLOCK), lambda g, b: (0, first(g)))
    return call(
        functools.partial(hidden_body, blocks), "hidden", (blk,), (blocks + more,),
        [(piece, fixed(piece.shape)) for piece in pieces]
        + [
            (grads, column),
            (up, pl.BlockSpec((model, BLOCK), lambda g, b: (0, first(g)))),
            (up, pl.BlockSpec((BLOCK, half), lambda g, b: (second(g), 0))),
            (bias, pl.BlockSpec((1, BLOCK), lambda g, b: (0, b[first(g)]))),
        ],
        [
            (grads.shape, BF16, column),
            (grads.shape, BF16, column),
            ((1, half), F32, line),
            ((tokens, model), BF16, fixed((tokens, model))),
            ((tokens, model), BF16, pl.BlockSpec((tokens, BLOCK), lambda g, b: (0, second(g)))),
        ],
        [pltpu.VMEM((blocks, tokens, BLOCK), BF16)]
    )


def sent_body(other_ref, tok_ref, cot_ref, grad_ref, act_ref, up_ref, down_ref):
    up_ref[...] = dot(tok_ref[...], grad_ref[...], 0, 0).astype(BF16)
    down_ref[...] = dot(act_ref[...], cot_ref[...], 0, 0).astype(BF16)


def sent_grads(other, tokens, cot, grad, act, steps):
    count, model = tokens.shape
    half = grad.shape[1]
    size = half // (2 * steps)
    wide = half // steps
    return call(
        sent_body, "sent_grads", (other,), (steps,),
        [
            (tokens, fixed(tokens.shape)),
            (cot, fixed(cot.shape)),
            (grad, along((count, wide), 1)),
            (act, pl.BlockSpec((count, size), lambda g, o: (0, 2 * g + o[0]))),
        ],
        [((model, half), BF16, along((model, wide), 1)), ((half // 2, model), BF16, along((size, model)))],
    )


def feed_body(order_ref, act_ref, down_ref, att_ref, low_ref, half_ref, cot_ref, feed_ref, other_ref, out_ref, keep_ref, kept_ref):
    parts = order_ref.shape[0]
    width = att_ref.shape[1] // parts
    feed = dot(act_ref[...], down_ref[...]).astype(BF16)
    feed_ref[...] = feed[: feed_ref.shape[0]]
    other_ref[...] = feed[feed_ref.shape[0] :]
    kept_ref[...] = dot(half_ref[...], cot_ref[...], 0, 0).astype(BF16)
    grad = dot(att_ref[...], low_ref[...], 0, 0).astype(BF16)
    step, steps = pl.program_id(0), pl.num_programs(0)

    def write(ref):
        for n in range(parts):
            at = pl.multiple_of(order_ref[n] * width, width)
            ref[pl.ds(at, width)] = grad[n * width : (n + 1) * width]

    @pl.when(2 * step < steps)
    def _():
        write(out_ref)

    @pl.when(2 * step >= steps)
    def _():
        write(keep_ref)


def feed_grads(order, act, down, attended, low, cot, c_at, x_at, deps=()):
    tokens, half = act.shape
    own, model = attended.shape
    steps = model // BLOCK
    place = jnp.concatenate([order, jnp.stack([c_at, x_at]).astype(jnp.int32)])
    size = half // (2 * steps)

    def body(place_ref, *refs):
        feed_body(place_ref.at[0 : order.shape[0]], *refs)

    def low_at(g, p):
        c = p[order.shape[0]]
        mine = 2 * g >= steps
        return 0, jnp.where(mine, c * (steps // 2) + g - steps // 2, (1 - c) * (steps // 2) + g)

    return call(
        body, "feed_grads", (place,), (steps,),
        [
            (act, fixed(act.shape)),
            (down, along((half, BLOCK), 1)),
            (attended, fixed(attended.shape)),
            (low, pl.BlockSpec((own, BLOCK), low_at)),
            (act, pl.BlockSpec((tokens, size), lambda g, p: (0, 2 * g + p[order.shape[0] + 1]))),
            (cot, fixed(cot.shape)),
        ],
        [
            ((own, model), BF16, along((own, BLOCK), 1)),
            ((own, model), BF16, along((own, BLOCK), 1)),
            ((model, model // 2), BF16, pl.BlockSpec((model, BLOCK), lambda g, p: (0, jnp.minimum(g, steps // 2 - 1)))),
            ((model, model // 2), BF16, pl.BlockSpec((model, BLOCK), lambda g, p: (0, jnp.maximum(g - steps // 2, 0)))),
            ((half // 2, model), BF16, along((size, model))),
        ],
        deps=deps,
    )


def middle_back_body(
    order_ref, part_ref, sent_ref, mid_ref, cot_ref, gain_ref, w0, w1, w2, w3,
    grad_ref, low_ref, att0_ref, att1_ref, far_ref, sums_ref,
):
    grad = part_ref[...].astype(F32) + sent_ref[...].astype(F32)
    hat, inverse = centre(mid_ref[0])
    cot = cot_ref[0].astype(F32)
    total = cot + norm_back(grad, line(gain_ref), hat, inverse)
    low = total.astype(BF16)
    grad_ref[0] = total
    low_ref[0] = low
    far_ref[0, 0] = dot(low, w2[...], 1, 1).astype(BF16)
    far_ref[1, 0] = dot(low, w3[...], 1, 1).astype(BF16)
    att1_ref[0] = dot(low, w1[...], 1, 1).astype(BF16)
    att0_ref[0] = dot(low, w0[...], 1, 1).astype(BF16)

    @pl.when(pl.program_id(0) == 0)
    def _():
        sums_ref[...] = jnp.zeros_like(sums_ref)

    sums_ref[0:1] += jnp.sum(grad * hat, axis=0, keepdims=True)
    sums_ref[1:2] += jnp.sum(grad, axis=0, keepdims=True)
    sums_ref[2:3] += jnp.sum(low.astype(F32), axis=0, keepdims=True)
    sums_ref[3:4] += jnp.sum(cot, axis=0, keepdims=True)


def middle_back(order, both, sent, mid, cot, gain, weight, parts, deps=()):
    rows, shard, model = mid.shape
    width = model // parts
    block, one = along((1, shard, model)), along((1, shard, width))
    flat = pl.BlockSpec((shard, model), lambda g, o: (g, 0))
    return call(
        middle_back_body, "middle_back", (order,), (rows,),
        [(both, flat), (sent, flat), (mid, block), (cot, block), (gain, fixed(gain.shape))] + out_blocks(weight, parts),
        [
            (mid.shape, F32, block),
            (mid.shape, BF16, block),
            ((rows, shard, width), BF16, one),
            ((rows, shard, width), BF16, one),
            ((2, rows, shard, width), BF16, along((2, 1, shard, width), 1)),
            ((8, model), F32, fixed((8, model))),
        ],
        deps=deps
    )


def norm1_back_body(start, part_ref, near_ref, far_ref, stream_ref, mid_ref, gain_ref, seg_ref, in_ref, shift_ref, sums_ref):
    grad = part_ref[0].astype(F32) + near_ref[0].astype(F32) + far_ref[0].astype(F32)
    hat, inverse = centre(stream_ref[0])
    total = mid_ref[0] + norm_back(grad, line(gain_ref), hat, inverse)
    in_ref[0] = total.astype(BF16)
    seg = seg_ref[pl.ds(pl.program_id(0) + start, 1)]
    slots = lax.broadcasted_iota(jnp.int32, (SEGS, seg.shape[-1]), 0) == seg
    onehot = slots.astype(F32).astype(BF16)
    shift_ref[0] = dot(jnp.concatenate([onehot, onehot], axis=1), split_low(total))

    @pl.when(pl.program_id(0) == 0)
    def _():
        sums_ref[...] = jnp.zeros_like(sums_ref)

    sums_ref[0:1] += jnp.sum(grad * hat, axis=0, keepdims=True)
    sums_ref[1:2] += jnp.sum(grad, axis=0, keepdims=True)


def norm1_back(start, count, own, near, far, stream, mid, gain, seg, held=(), deps=()):
    rows, shard, model = stream.shape
    block, own_block = along((1, shard, model), 0, start), along((1, shard, model))
    return call(
        functools.partial(norm1_back_body, start), "norm1_back", (), (count,),
        [(own, own_block), (near, own_block), (far, own_block), (stream, block), (mid, block), (gain, fixed(gain.shape))]
        + [(seg, fixed(seg.shape))],
        [
            (stream.shape, BF16, block),
            ((count, SEGS, model), F32, along((1, SEGS, model))),
            ((8, model), F32, fixed((8, model))),
        ],
        held=[(array, 0) for array in held], deps=deps
    )


def exchange(own, one, far):
    return [own, swap(one, "c"), far, swap(far[1], "c")]


def tie(*values):
    return lax.optimization_barrier(values)


def cut(values, index, size, axis):
    return lax.dynamic_slice_in_dim(values, index * size, size, axis)


def add_low(kept, sent):
    return (kept.astype(F32) + sent.astype(F32)).astype(BF16)


def over_z(values, at, depth):
    if depth != 4:
        return lax.psum_scatter(values, "z", scatter_dimension=0, tiled=False), []
    parts = [lax.dynamic_index_in_dim(values, at ^ n, 0, keepdims=False) for n in range(depth)]
    sent = [lax.ppermute(parts[n], "z", [(i, i ^ n) for i in range(depth)]) for n in range(1, depth)]
    return parts[0].astype(F32), sent


def ordered(at, own, other, axis):
    return jnp.where(at == 0, jnp.concatenate([own, other], axis), jnp.concatenate([other, own], axis))


def finish_body(blocks, at_ref, d0, d1, u0, u1, l0, l1, down_ref, up_ref, qkv_ref, out_ref):
    c_at = at_ref[0]
    width = up_ref.shape[1] // (4 * blocks)
    size = d0.shape[0]
    for c in range(2):
        mine = c_at == c
        down_ref[c * size : (c + 1) * size] = jnp.where(mine, d0[...], d1[...]).astype(F32)
        up = jnp.where(mine, u0[...], u1[...]).astype(F32)
        for b in range(2 * blocks):
            up_ref[:, (2 * b + c) * width : (2 * b + c + 1) * width] = up[:, b * width : (b + 1) * width]
        late = jnp.where(mine, l0[...], l1[...]).astype(F32)
        half = out_ref.shape[1] // 2
        wide = half // 2
        out_ref[:, c * half : (c + 1) * half] = late[:, 6 * wide :]
        for y in range(2):
            for n in range(3):
                at = n * 4 * wide + (2 * y + c) * wide
                qkv_ref[:, at : at + wide] = late[:, (3 * y + n) * wide : (3 * y + n + 1) * wide]


def finish(c_at, dp, piece, down, up, late, parts):
    rows, model = late[0].shape[0], down[0].shape[1]
    depth, size = dp // 2, down[0].shape[0]
    if piece % 128 == 0:
        at = c_at.astype(jnp.int32)[None]
        shapes = [(2 * size, model), (rows, 2 * dp * piece), (rows, 3 * model), (rows, model)]
        arrays = list(down) + list(up) + list(late)
        return call(
            functools.partial(finish_body, depth), "finish", (at,), (1,),
            [(array, fixed(array.shape)) for array in arrays], [(shape, F32, fixed(shape)) for shape in shapes],
        )
    down_done = ordered(c_at, *down, 0).astype(F32)
    up_done = ordered(c_at, up[0][None], up[1][None], 0).reshape(2, rows, dp, piece).transpose(1, 2, 0, 3)
    up_done = up_done.reshape(rows, 2 * dp * piece).astype(F32)
    both = ordered(c_at, late[0][None], late[1][None], 0)
    width = model // parts
    qkv_done = both[:, :, : 6 * width].reshape(2, rows, 2, 3, width).transpose(1, 3, 2, 0, 4)
    qkv_done = qkv_done.reshape(rows, 3 * model).astype(F32)
    out_done = jnp.concatenate([both[0, :, 6 * width :], both[1, :, 6 * width :]], axis=1).astype(F32)
    return down_done, up_done, qkv_done, out_done


def local(
    inputs, segment_ids, doc_times, time_weight, time_bias, norm1_gain, norm1_bias, qkv_weight, qkv_bias,
    out_weight, out_bias, norm2_gain, norm2_bias, up_weight, up_bias, down_weight, down_bias, cotangent,
    *, dp,
):
    rows, shard, model = inputs.shape
    parts = 4
    tokens = rows * shard
    hidden_width = up_weight.shape[1]
    width = model // parts
    depth = dp // 2
    half = hidden_width // 2
    piece = half // dp
    z_at, x_at, y_at, c_at = (lax.axis_index(name) for name in ("z", "x", "y", "c"))
    me = 2 * y_at + c_at

    seg_two = swap(segment_ids, "y")
    segs = jnp.stack([segment_ids, swap(segment_ids, "c"), seg_two, swap(seg_two, "c")], axis=1)

    groups = [(0, rows - 1), (rows - 1, 1)] if rows > 1 else [(0, 1)]
    features = time_features(doc_times.reshape(rows * SEGS), jnp.arange(TEMB), TEMB // 2)
    time_shift = dot(features, time_weight).reshape(rows, SEGS, model)
    stream, own1 = norm1(inputs, segment_ids, time_shift, (time_bias, norm1_gain, norm1_bias))
    own1, segs = tie(own1, segs)
    two1 = swap(own1, "y")
    one1 = swap(own1, "c")

    me, x_at, z_at, c_at, y_at, own1 = tie(me, x_at, z_at, c_at, y_at, own1)
    order = [me ^ i for i in range(parts)]
    order_list = jnp.stack(order).astype(jnp.int32)
    me_list = order_list[:1]
    low_id, high_id = segs.min(axis=2), segs.max(axis=2)
    act = (low_id[:, :, None] <= high_id[:, None, :]) & (low_id[:, None, :] <= high_id[:, :, None])
    places = jnp.arange(parts, dtype=jnp.int32)
    rank = jnp.cumsum(act.astype(jnp.int32), axis=2) - 1
    chosen = act[..., None] & (rank[..., None] == places)
    idx = jnp.sum(jnp.where(chosen, places[:, None], 0), axis=2).astype(jnp.int32).reshape(-1)
    cnt = jnp.sum(act.astype(jnp.int32), axis=2).reshape(-1)
    positions = jnp.stack([o * shard + jnp.arange(shard, dtype=jnp.int32) for o in order])
    cos_tab, sin_tab = rotary_tables(positions, HEAD_DIM)

    cot = cotangent.reshape(tokens, model)
    cot_other = swap(cot, "c")
    if piece % BLOCK == 0:
        blk = (jnp.arange(dp)[:, None] * 2 + c_at) * (piece // BLOCK) + jnp.arange(piece // BLOCK)
        blk = blk.reshape(-1).astype(jnp.int32)
        up_from, down_from = up_weight, down_weight
    else:
        blk = jnp.zeros((half // BLOCK,), jnp.int32)
        up_from = lax.dynamic_index_in_dim(up_weight.reshape(model, dp, 2, piece), c_at, 2, keepdims=False)
        down_from = lax.dynamic_index_in_dim(down_weight.reshape(dp, 2, piece, model), c_at, 1, keepdims=False)
        up_from, down_from = up_from.reshape(model, half), down_from.reshape(half, model)
    grad_act, up_own, down_own, cot_both = cot_down(
        blk, cot, cot_other, up_from, down_from, piece % BLOCK != 0, half
    )
    up_bias_own, bias_blk = up_bias.reshape(1, hidden_width), blk
    if piece % BLOCK:
        up_bias_own = lax.dynamic_index_in_dim(up_bias.reshape(dp, 2, piece), c_at, 1, keepdims=False)
        up_bias_own, bias_blk = up_bias_own.reshape(1, half), jnp.arange(half // BLOCK, dtype=jnp.int32)

    qkv_line = qkv_bias.reshape(1, 3 * model)
    qkv, qkv_own = project_qkv(0, parts, me_list, own1, one1, qkv_weight, qkv_line, cos_tab, sin_tab, (), (grad_act,))
    two1, qkv = tie(two1, qkv)
    three1 = swap(two1, "c")
    qkv, _ = project_qkv(1, parts, me_list, two1, three1, qkv_weight, qkv_line, cos_tab, sin_tab, (qkv,))
    o, lse, attended = None, None, []
    for start, count in groups:
        held = () if o is None else (o, lse)
        o, out_one, out_far, lse = attend(start, count, cnt, idx, qkv, segs, held)
        attended.append((out_one, swap(out_far, "y")))
    held, normed2, normed2_other = (), [], []
    for (start, count), values in zip(groups, attended):
        far, o = tie(values[1], o)
        values = exchange(o, values[0], far)
        middle, low, attended_all = middle_norm(
            start, count, order_list, values, out_weight, stream, (out_bias, norm2_gain, norm2_bias), held
        )
        held = (middle, attended_all)
        normed2.append(low)
        normed2_other.append(swap(low, "c"))

    active, grad_hidden, up_b, normed2_both, part2 = hidden_units(
        bias_blk, normed2 + normed2_other, grad_act, up_own, up_bias_own
    )
    part2_sent = swap(part2[tokens:], "c")
    grad_middle, grad_middle_low, att0, att1, far, sums2 = middle_back(
        order_list, part2, part2_sent, middle, cotangent, norm2_gain, out_weight, parts
    )
    far = swap(far, "y")
    sums2 = sums2[:4]

    active, grad_hidden, att0 = tie(active, grad_hidden, att0)
    up_rows = model // dp
    small_blocks = piece % BLOCK != 0 or depth != model // BLOCK
    if small_blocks:
        up_grad = dot(normed2_both, grad_hidden, 0, 0).astype(BF16)
        down_out = dot(active, cot_both, 0, 0).astype(BF16).reshape(depth, 2, piece, model)
        down_kept = lax.dynamic_index_in_dim(down_out, x_at, 1, keepdims=False).reshape(half // 2, model)
        down_out = lax.dynamic_index_in_dim(down_out, 1 - x_at, 1, keepdims=False).reshape(half // 2, model)
    else:
        up_grad, down_out = sent_grads(
            1 - x_at[None].astype(jnp.int32), normed2_both, cot_both, grad_hidden, active, depth
        )
    up_grad, down_out, far = tie(up_grad, down_out, far)
    up_z = lax.psum_scatter(up_grad, "z", scatter_dimension=0, tiled=True)
    down_sent = swap(down_out[: half // 4], "x")
    if small_blocks:
        feed = dot(active, down_own).astype(BF16)
        feed, feed_other = feed[:tokens], feed[tokens:]
        out_grad = dot(attended_all.reshape(tokens, model), grad_middle_low.reshape(tokens, model), 0, 0).astype(BF16)
        out_grad = jnp.concatenate([cut(out_grad, o_at, width, 0) for o_at in order], axis=0)
        out_sent, out_grad = (cut(out_grad, at, model // 2, 1) for at in (1 - c_at, c_at))
    else:
        feed, feed_other, out_sent, out_grad, down_kept = feed_grads(
            order_list, active, down_own, attended_all.reshape(tokens, model), grad_middle_low.reshape(tokens, model),
            cot_both, c_at, x_at, (far, down_out),
        )
    feed, feed_other, out_sent, out_grad, down_kept, down_sent, down_out = tie(
        feed, feed_other, out_sent, out_grad, down_kept, down_sent, down_out
    )
    down_late = swap(down_out[half // 4 :], "x")
    out_sent = swap(out_sent, "c")
    feed = feed.astype(F32) + swap(feed_other, "c").astype(F32) + down_bias.astype(F32)
    output = (middle + feed.reshape(rows, shard, model)).astype(BF16)
    out_c = add_low(out_grad, out_sent)

    output, out_c, far, down_kept = tie(output, out_c, far, down_kept)
    out_sent = swap(cut(out_c, 1 - y_at, width, 1), "y")
    grad_o = exchange(att0, att1, far)
    back = []
    (start, count), rest = groups[0], groups[1:]
    found = attend_back(start, count, cnt, idx, qkv, o, grad_o, lse, segs, cos_tab, sin_tab, qkv_own)
    *found, down_late, out_sent = tie(*found, down_late, out_sent)
    grad_qkv, own, one, two, three = found
    there = add_low(two, swap(three, "c"))
    down_x = add_low(down_kept, jnp.concatenate([down_sent, down_late], axis=0))
    down_z = lax.psum_scatter(down_x, "z", scatter_dimension=0, tiled=True)
    out_y = add_low(cut(out_c, y_at, width, 1), out_sent).reshape(depth, 2 * up_rows, width)
    out_sent = cut(out_y, 1 - x_at, up_rows, 1)
    there, down_x, out_sent = tie(there, down_x, out_sent)
    far, near = swap(there, "y"), swap(one, "c")
    out_sent = swap(out_sent, "x")
    if rest:
        (start, count), = rest
        found = attend_back(
            start, count, cnt, idx, qkv, o, grad_o, lse, segs, cos_tab, sin_tab, qkv_own, (grad_qkv,),
            (there, down_x),
        )
        *found, far, up_z, out_sent = tie(*found, far, up_z, out_sent)
        back.append((own, near, far))
        grad_qkv, own, one, two, three = found
        there, far = tie(add_low(two, swap(three, "c")), far)
        far, near = swap(there, "y"), swap(one, "c")
        grad_qkv, there = tie(grad_qkv, there)
    up_out = cut(up_z, 1 - x_at, up_rows, 0)
    up_sent = swap(up_out, "x")
    qkv_out, qkv_kept, qkv_b = qkv_grads(x_at, [own1, one1, two1, three1], grad_qkv, depth, (up_out,))
    qkv_out, qkv_kept, far, up_sent = tie(qkv_out, qkv_kept, far, up_sent)
    back.append((own, near, far))
    qkv_sent = swap(qkv_out, "x")
    up_x = add_low(cut(up_z, x_at, up_rows, 0), up_sent)
    out_x = add_low(cut(out_y, x_at, up_rows, 1), out_sent)
    held, grad_shift, sums1 = (), [], 0.0
    for (start, count), values in zip(groups, back):
        input_grad, found, sums = norm1_back(
            start, count, *values, stream, grad_middle, norm1_gain, segment_ids, held, (out_x, up_x, qkv_kept)
        )
        held = (input_grad,)
        grad_shift.append(found.reshape(count * SEGS, model))
        sums1 = sums1 + sums[:2]
    qkv_x = jnp.concatenate([add_low(qkv_kept, qkv_sent), out_x], axis=2)

    up_b = up_b.reshape(dp, 1, piece)
    up_b = jnp.where(jnp.arange(2)[:, None] == c_at, up_b, 0.0).reshape(-1, model)
    qkv_b = jnp.where(jnp.arange(parts)[:, None] == me, qkv_b.reshape(3, 1, width), 0.0).reshape(3, model)
    times = doc_times.reshape(1, rows * SEGS)
    times = jnp.concatenate([times // 32, times % 32], axis=1).astype(F32)
    times = jnp.pad(times, ((0, 0), (0, model - times.shape[1])))
    small = jnp.concatenate(grad_shift + [sums1, sums2, qkv_b, up_b, times], axis=0)
    small, qkv_x = tie(add_low(small, swap(small.astype(BF16), "c")), qkv_x)
    late, late_parts = over_z(qkv_x, z_at, depth)
    small = add_low(small, swap(small, "y"))
    small = ordered(x_at, small[None], swap(small, "x")[None], 0)
    small, down_z, up_x = tie(small, down_z, up_x)
    down_sent, up_sent = swap(down_z, "y"), swap(up_x, "y")
    if depth == 4:
        others = [lax.ppermute(small, "z", [(i, i ^ n) for i in range(depth)]) for n in range(1, depth)]
        small = jnp.stack([small] + others)
        small = jnp.stack([lax.dynamic_index_in_dim(small, z_at ^ n, 0, keepdims=False) for n in range(depth)])
    else:
        small = lax.all_gather(small, "z")
    small = small.reshape(dp, small.shape[2], model)

    small, late, down_sent, up_sent = tie(small, late, down_sent, up_sent)
    down_done, up_done = add_low(down_z, down_sent), add_low(up_x, up_sent)
    down_other, up_other = swap(down_done, "c"), swap(up_done, "c")
    late = (late + sum(part.astype(F32) for part in late_parts)).astype(BF16) if depth == 4 else late
    late_sent = swap(late, "y")
    both = ordered(y_at, late[None], late_sent[None], 0)
    late = jnp.concatenate([both[0, :, : 3 * width], both[1, :, : 3 * width], both[0, :, 3 * width :], both[1, :, 3 * width :]], axis=1)
    late_other = swap(late, "c")

    down_done, up_done, qkv_done, out_done = finish(
        c_at, dp, piece, (down_done, down_other), (up_done, up_other), (late, late_other), parts
    )

    all_times = small[:, -1, : 2 * rows * SEGS].astype(F32) * 0.25
    all_times = all_times[:, : rows * SEGS] * 32.0 + all_times[:, rows * SEGS :]
    shifts = small[:, : rows * SEGS].reshape(dp * rows * SEGS, model)
    columns = (2 * z_at + x_at) * (TEMB // dp) + jnp.arange(TEMB // dp)
    wanted = time_features(all_times.reshape(-1), columns, TEMB // 2)
    time_w_done = dot(wanted, shifts, 0, 0)
    sums = jnp.sum(small[:, rows * SEGS :].astype(F32), axis=0)
    dp_at = 2 * z_at + x_at

    def share(vector):
        return cut(vector.reshape(-1), dp_at, vector.size // dp, 0)

    time_b_done = jnp.sum(cut(shifts, dp_at, up_rows, 1).astype(F32), axis=0)
    return (
        output, input_grad, time_w_done, time_b_done, share(sums[0]), share(sums[1]), qkv_done, share(sums[6:9]),
        out_done, share(sums[4]), share(sums[2]), share(sums[3]), up_done, share(sums[9:-1]), down_done, share(sums[5]),
    )


def solution(mesh):
    dp, seq = mesh.shape["dp"], mesh.shape["seq"]
    fine = Mesh(mesh.devices.reshape(dp // 2, 2, seq // 2, 2), ("z", "x", "y", "c"))
    rows, seqs = ("z", "x"), ("y", "c")
    placed = (P(rows, seqs, None), P(rows, seqs), P(rows, None)) + (P(),) * 14 + (P(rows, seqs, None),)
    vec, mat = P(rows), P(rows, None)
    return jax.shard_map(
        functools.partial(local, dp=dp),
        mesh=fine,
        in_specs=placed,
        out_specs=(
            P(rows, seqs, None), P(rows, seqs, None), mat, vec, vec, vec, mat, vec, mat, vec, vec, vec, mat, vec, mat, vec,
        ),
        check_vma=False,
    )
```

```python
import functools
import math

import jax
import jax.numpy as jnp
from jax import lax
from jax.experimental import pallas as pl
from jax.experimental.pallas import tpu as pltpu
from jax.sharding import Mesh, PartitionSpec as P

HEADS = 16
HEAD_DIM = 64
TEMB = 256
SEGS = 8
EPSILON = 1e-05
F32 = jnp.float32
BF16 = jnp.bfloat16
NEG = -1e30
LOG2E = math.log2(math.e)
GELU_A = math.sqrt(2.0 / math.pi)
GELU_B = GELU_A * 0.044715
BLOCK = 256
VMEM = 60 * 1024 * 1024


def swap(value, axis):
    return lax.ppermute(value, axis, [(0, 1), (1, 0)])


def time_features(doc_times, column, half_size):
    frequency = jnp.exp(-math.log(10000.0) * (column % half_size).astype(F32) / half_size)
    angles = doc_times.astype(F32)[..., None] * frequency
    return jnp.where(column < half_size, jnp.sin(angles), jnp.cos(angles)).astype(BF16)


def rotary_tables(positions, head_size):
    half_size = head_size // 2
    frequency = jnp.exp(-math.log(10000.0) * 2.0 * jnp.arange(half_size, dtype=F32) / head_size)
    angles = positions.astype(F32)[..., None] * frequency
    cos_tab, sin_tab = jnp.cos(angles), jnp.sin(angles)
    return (
        jnp.concatenate([cos_tab] * 4, axis=-1),
        jnp.concatenate([-sin_tab, sin_tab, -sin_tab, sin_tab], axis=-1),
    )


def dot(left_op, right_op, left_dim=1, right_dim=0):
    return lax.dot_general(
        left_op, right_op, (((left_dim,), (right_dim,)), ((), ())), preferred_element_type=F32
    )


def turn(values, cos_tab, sin_tab):
    slabs = []
    lane = lax.broadcasted_iota(jnp.int32, (values.shape[0], 128), 1)
    first = lane % HEAD_DIM < HEAD_DIM // 2
    for start in range(0, values.shape[1], 128):
        slab = values[:, start : start + 128]
        partner = jnp.where(
            first, pltpu.roll(slab, 128 - HEAD_DIM // 2, 1), pltpu.roll(slab, HEAD_DIM // 2, 1)
        )
        slabs.append(slab * cos_tab + partner * sin_tab)
    return jnp.concatenate(slabs, axis=1)


def split_low(values):
    high = values.astype(BF16)
    return jnp.concatenate([high, (values - high.astype(F32)).astype(BF16)], axis=0)


def centre(values):
    scale = 1.0 / values.shape[-1]
    centred = values - jnp.sum(values, axis=-1, keepdims=True) * scale
    spread = jnp.sum(centred * centred, axis=-1, keepdims=True) * scale
    inverse = lax.rsqrt(spread + EPSILON)
    return centred * inverse, inverse


def norm_back(grad, gain, hat, inverse):
    scale = 1.0 / grad.shape[-1]
    scaled = grad * gain
    mean = jnp.sum(scaled, axis=-1, keepdims=True) * scale
    along = jnp.sum(scaled * hat, axis=-1, keepdims=True) * scale
    return inverse * (scaled - mean - hat * along)


def call(body, name, prefetch, grid, ins, outs, scratch=(), deps=(), held=()):
    count = len(prefetch) + len(ins)
    extra = [array for array, _ in held] + list(deps)

    def kernel(*refs):
        body(*refs[:count], *refs[count + len(extra) :])

    return pl.pallas_call(
        kernel,
        grid_spec=pltpu.PrefetchScalarGridSpec(
            num_scalar_prefetch=len(prefetch),
            grid=grid,
            in_specs=[spec for _, spec in ins] + [pl.BlockSpec(memory_space=pl.ANY)] * len(extra),
            out_specs=[spec for _, _, spec in outs],
            scratch_shapes=list(scratch),
        ),
        out_shape=[jax.ShapeDtypeStruct(shape, kind) for shape, kind, _ in outs],
        input_output_aliases={count + n: out for n, (_, out) in enumerate(held)},
        compiler_params=pltpu.CompilerParams(vmem_limit_bytes=VMEM),
        name=name,
    )(*prefetch, *[array for array, _ in ins], *extra)


def line(ref):
    return ref[...].astype(F32).reshape(1, -1)


def fixed(shape):
    return pl.BlockSpec(shape, lambda *_: (0,) * len(shape))


def along(shape, axis=0, start=0):
    return pl.BlockSpec(shape, lambda g, *_: tuple(start + g if n == axis else 0 for n in range(len(shape))))


def norm1_body(x_ref, seg_ref, shift_ref, time_ref, gain_ref, bias_ref, stream_ref, low_ref):
    seg = seg_ref[pl.ds(pl.program_id(0), 1)]
    slots = lax.broadcasted_iota(jnp.int32, (SEGS, seg.shape[-1]), 0) == seg
    onehot = slots.astype(F32).astype(BF16)
    shift = shift_ref[0] + line(time_ref)
    added = dot(jnp.concatenate([onehot, onehot], axis=0), split_low(shift), 0, 0)
    stream = x_ref[0].astype(F32) + added
    hat, _ = centre(stream)
    stream_ref[0] = stream
    low_ref[0] = (hat * line(gain_ref) + line(bias_ref)).astype(BF16)


def norm1(x, seg, shift, vecs):
    rows, shard, model = x.shape
    block = along((1, shard, model))
    return call(
        norm1_body, "norm1", (), (rows,),
        [(x, block), (seg, fixed(seg.shape)), (shift, along((1, SEGS, model)))]
        + [(vec, fixed(vec.shape)) for vec in vecs],
        [(x.shape, F32, block), (x.shape, BF16, block)],
    )


def qkv_body(me_ref, a_ref, b_ref, w_ref, bias_ref, cos_ref, sin_ref, out_ref, own_ref):
    rows, shard, model = a_ref.shape
    width = w_ref.shape[1]
    places = [(n, r) for n in range(2) for r in range(rows)]
    step = pl.program_id(0)

    def run(turned):
        w = w_ref[...]
        bias = bias_ref[...].astype(F32)
        later = dot(a_ref[0], w)
        for at, (n, r) in enumerate(places):
            values = later + bias
            if at + 1 < len(places):
                x_ref = (a_ref, b_ref)[places[at + 1][0]]
                later = dot(x_ref[places[at + 1][1]], w)
            if turned:
                values = turn(values, cos_ref[n], sin_ref[n]) * jnp.where(step == 0, LOG2E * HEAD_DIM**-0.5, 1.0)
            out_ref[0, n, r] = values.astype(BF16)

    own_ref[...] = w_ref[...].T

    @pl.when(step < 2)
    def _():
        run(True)

    @pl.when(step == 2)
    def _():
        run(False)


def project_qkv(pair, parts, me, first, second, weight, bias, cos_tab, sin_tab, held=(), deps=()):
    rows, shard, model = first.shape
    width = model // parts
    return call(
        qkv_body, "qkv", (me,), (3,),
        [(first, fixed(first.shape)), (second, fixed(first.shape))]
        + [
            (weight, pl.BlockSpec((model, width), lambda g, m: (0, g * parts + m[0]))),
            (bias, pl.BlockSpec((1, width), lambda g, m: (0, g * parts + m[0]))),
            (cos_tab, pl.BlockSpec((2, shard, 128), lambda g, m: (pair, 0, 0))),
            (sin_tab, pl.BlockSpec((2, shard, 128), lambda g, m: (pair, 0, 0))),
        ],
        [
            ((3, parts, rows, shard, width), BF16, pl.BlockSpec((1, 2, rows, shard, width), lambda g, m: (g, pair, 0, 0, 0))),
            ((3 * width, model), BF16, along((width, model))),
        ],
        held=[(array, n) for n, array in enumerate(held)], deps=deps,
    )


def qkv_grads(x_at, pieces, grad, blocks, deps=()):
    rows, shard, model = pieces[0].shape
    tokens = rows * shard
    parts, columns = len(pieces), grad.shape[3]
    size = model // (2 * blocks)

    def body(at_ref, x0, x1, x2, x3, g_ref, out_ref, keep_ref, sum_ref):
        total, sums = 0.0, 0.0
        for n, x_ref in enumerate((x0, x1, x2, x3)):
            g = g_ref[n].reshape(tokens, g_ref.shape[3])
            total = total + dot(x_ref[...].reshape(tokens, model), g, 0, 0)
            sums = sums + jnp.sum(g.astype(F32), axis=0, keepdims=True)
        low = total.astype(BF16)
        for x in range(2):
            for b in range(blocks):
                values = low[(2 * b + x) * size : (2 * b + x + 1) * size]

                @pl.when(at_ref[0] == x)
                def _():
                    keep_ref[b] = values

                @pl.when(at_ref[0] != x)
                def _():
                    out_ref[b] = values

        sum_ref[...] = sums

    block = along((blocks, size, BLOCK), 2)
    shape = (blocks, size, columns)
    return call(
        body, "qkv_grads", (x_at.astype(jnp.int32)[None],), (columns // BLOCK,),
        [(x, fixed(x.shape)) for x in pieces] + [(grad, along((parts, rows, shard, BLOCK), 3))],
        [(shape, BF16, block), (shape, BF16, block), ((1, columns), F32, along((1, BLOCK), 1))],
        deps=deps,
    )


def seg_columns(segq_all, segk):
    pieces, shard, _ = segk.shape
    for j in range(pieces):
        row = jnp.broadcast_to(segq_all[j:j+1].astype(F32), (128, shard))
        segk[j] = row.T

def attend_body(start, cnt_ref, idx_ref, qkv_ref, seg_ref, o_ref, one_ref, far_ref, lse_ref, vt, segk, qmt, acc):
    row = pl.program_id(0) + start
    _, pieces, _, shard, width = qkv_ref.shape
    heads = width // HEAD_DIM

    @pl.when(pl.program_id(0) == 0)
    def _():
        qmt[...] = jnp.zeros_like(qmt)

    for j in range(pieces):
        vt[j] = qkv_ref[2, j, 0].T
        qt = qkv_ref[0, j, 0].T
        for h in range(heads):
            at = slice(h * HEAD_DIM, (h + 1) * HEAD_DIM)
            qmt[j, at, h * shard : (h + 1) * shard] = qt[at]
    seg_columns(seg_ref[0], segk)

    @pl.loop(0, pieces)
    def _(piece):
        attend_piece(row * pieces + piece, piece, cnt_ref, idx_ref, qkv_ref.at[1], seg_ref, lse_ref, vt, segk, qmt, acc)

    for j in range(pieces):
        o_ref[j, 0] = acc[j].T.astype(BF16)
    one_ref[0] = o_ref[1, 0]
    far_ref[:, 0] = o_ref[2:, 0]


def attend_piece(at_q, piece, cnt_ref, idx_ref, k_ref, seg_ref, lse_ref, vt, segk, qmt, acc):
    pieces, _, shard, width = k_ref.shape
    heads = width // HEAD_DIM
    seg_q = seg_ref[0, pl.ds(piece, 1)].astype(F32)

    def run(count):
        @pl.when(cnt_ref[at_q] == count)
        def _():
            qm = qmt[piece]
            places = [idx_ref[at_q * pieces + t] for t in range(count)]
            top, tot, out = [None] * heads, [None] * heads, [None] * heads
            later = dot(k_ref[places[0], 0], qm)
            for t in range(count):
                s = later
                if t + 1 < count:
                    later = dot(k_ref[places[t + 1], 0], qm)
                col = segk[places[t]]
                same = jnp.concatenate([col] * (shard // 128), axis=1) == seg_q
                for h in range(heads):
                    at = slice(h * HEAD_DIM, (h + 1) * HEAD_DIM)
                    sh = jnp.where(same, s[:, h * shard : (h + 1) * shard], NEG)
                    best = jnp.max(sh, axis=0, keepdims=True)
                    if t:
                        best = jnp.maximum(top[h], best)
                        fade = jnp.exp2(top[h] - best)
                    p = jnp.exp2(sh - best)
                    values = jnp.concatenate([vt[places[t], at], jnp.ones((16, shard), BF16)], axis=0)
                    found = dot(values, p.astype(BF16))
                    total, found = found[HEAD_DIM : HEAD_DIM + 1], found[:HEAD_DIM]
                    if t:
                        total = tot[h] * fade + total
                        found = out[h] * fade + found
                    top[h], tot[h], out[h] = best, total, found
            for h in range(heads):
                acc[piece, h * HEAD_DIM : (h + 1) * HEAD_DIM] = out[h] / tot[h]
                lse_ref[0, piece, h : h + 1] = top[h] + jnp.log2(tot[h])

    for count in range(1, pieces + 1):
        run(count)


def attend(start, count, cnt, idx, qkv, seg, held=()):
    _, pieces, rows, shard, width = qkv.shape
    heads = width // HEAD_DIM
    pairs = count * (pieces * shard) ** 2
    return call(
        functools.partial(attend_body, start), "attend", (cnt, idx), (count,),
        [(qkv, along((3, pieces, 1, shard, width), 2, start)), (seg, along((1, pieces, shard), 0, start))],
        [
            ((pieces, rows, shard, width), BF16, along((pieces, 1, shard, width), 1, start)),
            ((count, shard, width), BF16, along((1, shard, width))),
            ((2, count, shard, width), BF16, along((2, 1, shard, width), 1)),
            ((rows, pieces, 8, shard), F32, along((1, pieces, 8, shard), 0, start)),
        ],
        [
            pltpu.VMEM((pieces, width, shard), BF16),
            pltpu.VMEM((pieces, shard, 128), F32),
            pltpu.VMEM((pieces, width, heads * shard), BF16),
            pltpu.VMEM((pieces, width, shard), F32),
        ],
        held=list(zip(held, (0, 3)))
    )


def attend_back_body(
    start, cnt_ref, idx_ref, qkv_ref, o_ref, do0, do1, do2, do3, lse_ref, seg_ref, cos_ref, sin_ref, w_ref,
    g_ref, p0_ref, p1_ref, p2_ref, p3_ref, kt, segk, dk, dv, dqt, qmt, gmt, qst, gst, low,
):
    row = pl.program_id(0) + start
    _, pieces, _, shard, width = qkv_ref.shape
    heads = width // HEAD_DIM

    @pl.when(pl.program_id(0) == 0)
    def _():
        qmt[...] = jnp.zeros_like(qmt)
        gmt[...] = jnp.zeros_like(gmt)

    seg_columns(seg_ref[0], segk)
    dk[...] = jnp.zeros_like(dk)
    dv[...] = jnp.zeros_like(dv)
    lane = lax.broadcasted_iota(jnp.int32, (shard, width), 1) // HEAD_DIM
    chosen = lax.broadcasted_iota(jnp.int32, (8, width), 1) // HEAD_DIM
    chosen = (chosen == lax.broadcasted_iota(jnp.int32, (8, width), 0)).astype(BF16)
    for j, do_ref in enumerate((do0, do1, do2, do3)):
        kt[j] = qkv_ref[1, j, 0].T
        q, do = qkv_ref[0, j, 0], do_ref[...].reshape(shard, width)
        qt, gt = q.T, do.T
        for h in range(heads):
            at, qa = slice(h * HEAD_DIM, (h + 1) * HEAD_DIM), slice(h * shard, (h + 1) * shard)
            qmt[j, at, qa] = qt[at]
            gmt[j, at, qa] = gt[at]
            qst[j, qa] = jnp.where(lane == h, q, jnp.zeros_like(q))
            gst[j, qa] = jnp.where(lane == h, do, jnp.zeros_like(do))
        prod = do.astype(F32) * o_ref[j, 0].astype(F32)
        high = prod.astype(BF16)
        low[j] = dot(chosen, high, 1, 1) + dot(chosen, (prod - high.astype(F32)).astype(BF16), 1, 1)

    @pl.loop(0, pieces)
    def _(piece):
        back_piece(
            row * pieces + piece, piece, cnt_ref, idx_ref, qkv_ref.at[1], qkv_ref.at[2], lse_ref, seg_ref,
            kt, segk, dk, dv, dqt, qmt, gmt, qst, gst, low,
        )

    for j, ref in ((1, p1_ref), (3, p3_ref), (0, p0_ref), (2, p2_ref)):
        grad_q = turn(dqt[j].T * HEAD_DIM**-0.5, cos_ref[j], -sin_ref[j]).astype(BF16)
        grad_k = turn(dk[j] * (1 / LOG2E), cos_ref[j], -sin_ref[j]).astype(BF16)
        grad = jnp.concatenate([grad_q, grad_k, dv[j].astype(BF16)], axis=1)
        g_ref[j, 0] = grad
        ref[0] = dot(grad, w_ref[...]).astype(BF16)


def back_piece(
    at_q, piece, cnt_ref, idx_ref, k_ref, v_ref, lse_ref, seg_ref, kt, segk, dk, dv, dqt, qmt, gmt, qst, gst, low
):
    pieces, _, shard, width = k_ref.shape
    heads = width // HEAD_DIM
    lse, delta = lse_ref[0, piece], low[piece]
    seg_q = seg_ref[0, pl.ds(piece, 1)].astype(F32)

    def run(count):
        @pl.when(cnt_ref[at_q] == count)
        def _():
            places = [idx_ref[at_q * pieces + t] for t in range(count)]
            qm, gm = qmt[piece], gmt[piece]
            later = dot(k_ref[places[0], 0], qm), dot(v_ref[places[0], 0], gm)
            out = [None] * heads
            for t in range(count):
                s, dp = later
                j = places[t]
                if t + 1 < count:
                    later = dot(k_ref[places[t + 1], 0], qm), dot(v_ref[places[t + 1], 0], gm)
                col = segk[j]
                same = jnp.concatenate([col] * (shard // 128), axis=1) == seg_q
                ps, dss = [], []
                for h in range(heads):
                    at, qa = slice(h * HEAD_DIM, (h + 1) * HEAD_DIM), slice(h * shard, (h + 1) * shard)
                    p = jnp.exp2(jnp.where(same, s[:, qa] - lse[h : h + 1], NEG))
                    ds = (p * (dp[:, qa] - delta[h : h + 1])).astype(BF16)
                    ps.append(p.astype(BF16))
                    dss.append(ds)
                    found = dot(kt[j, at], ds)
                    out[h] = found if t == 0 else out[h] + found
                dv[j] += dot(jnp.concatenate(ps, axis=1), gst[piece])
                dk[j] += dot(jnp.concatenate(dss, axis=1), qst[piece])
            for h in range(heads):
                dqt[piece, h * HEAD_DIM : (h + 1) * HEAD_DIM] = out[h]

    for count in range(1, pieces + 1):
        run(count)


def attend_back(start, count, cnt, idx, qkv, o, do, lse, seg, cos_tab, sin_tab, weight, held=(), deps=()):
    _, pieces, rows, shard, width = qkv.shape
    model = weight.shape[1]
    heads = width // HEAD_DIM
    table = fixed((pieces, shard, 128))
    pairs = count * (pieces * shard) ** 2
    square, wide = (pieces, width, heads * shard), (pieces, shard, width)
    one = along((1, shard, width), 0, start)
    return call(
        functools.partial(attend_back_body, start), "attend_back", (cnt, idx), (count,),
        [(qkv, along((3, pieces, 1, shard, width), 2, start)), (o, along((pieces, 1, shard, width), 1, start))]
        + [(do[0], one), (do[1], one), (do[2], along((1, 1, shard, width), 1, start)), (do[3], one)]
        + [(lse, along((1, pieces, 8, shard), 0, start)), (seg, along((1, pieces, shard), 0, start))]
        + [(cos_tab, table), (sin_tab, table), (weight, fixed(weight.shape))],
        [((pieces, rows, shard, 3 * width), BF16, along((pieces, 1, shard, 3 * width), 1, start))]
        + [((count, shard, model), BF16, along((1, shard, model)))] * pieces,
        [
            pltpu.VMEM((pieces, width, shard), BF16),
            pltpu.VMEM((pieces, shard, 128), F32),
            pltpu.VMEM(wide, F32),
            pltpu.VMEM(wide, F32),
            pltpu.VMEM((pieces, width, shard), F32),
            pltpu.VMEM(square, BF16),
            pltpu.VMEM(square, BF16),
            pltpu.VMEM((pieces, heads * shard, width), BF16),
            pltpu.VMEM((pieces, heads * shard, width), BF16),
            pltpu.VMEM((pieces, 8, shard), F32),
        ],
        held=[(array, 0) for array in held], deps=deps
    )


def middle_body(
    order_ref, a0, a1, a2, a3, w0, w1, w2, w3, stream_ref, bias_ref, gain_ref, shift_ref, mid_ref, low_ref, all_ref,
):
    _, shard, model = stream_ref.shape
    total = 0.0
    for n, (a, w) in enumerate(((a0, w0), (a1, w1), (a2, w2), (a3, w3))):
        values = a[...].reshape(shard, a.shape[-1])
        total = total + dot(values, w[...])
        all_ref[0, :, n * a.shape[-1] : (n + 1) * a.shape[-1]] = values
    mid = stream_ref[0] + (total + line(bias_ref))
    hat, _ = centre(mid)
    mid_ref[0] = mid
    low_ref[0] = (hat * line(gain_ref) + line(shift_ref)).astype(BF16)


def out_blocks(weight, parts):
    width = weight.shape[0] // parts

    def block(i):
        return pl.BlockSpec((width, weight.shape[1]), lambda g, o: (o[i], 0))

    return [(weight, block(i)) for i in range(parts)]


def middle_norm(start, count, order, attended, weight, stream, vecs, held=()):
    rows, shard, model = stream.shape
    parts = len(attended)
    width = model // parts
    block, one = along((1, shard, model), 0, start), along((1, shard, width))
    first = [along((1, 1, shard, width), 1, start), one, along((1, 1, shard, width), 1), one]
    return call(
        middle_body, "middle", (order,), (count,),
        list(zip(attended, first)) + out_blocks(weight, parts) + [(stream, block)]
        + [(vec, fixed(vec.shape)) for vec in vecs],
        [
            (stream.shape, F32, block),
            ((count, shard, model), BF16, along((1, shard, model))),
            (stream.shape, BF16, block),
        ],
        held=list(zip(held, (0, 2)))
    )


def cot_body(blk_ref, a_ref, b_ref, up_ref, down_ref, g_ref, up_out, down_out, both_ref):
    tokens = a_ref.shape[0]
    down = down_ref[...]

    @pl.when(pl.program_id(0) == 0)
    def _():
        both_ref[0:tokens] = a_ref[...]
        both_ref[tokens:] = b_ref[...]

    g_ref[0:tokens] = dot(a_ref[...], down, 1, 1).astype(BF16)
    g_ref[tokens:] = dot(b_ref[...], down, 1, 1).astype(BF16)
    up_out[...] = up_ref[...]
    down_out[...] = down


def cot_down(blk, own, other, up, down, picked, half):
    tokens, model = own.shape
    steps = half // BLOCK
    column = along((2 * tokens, BLOCK), 1)
    if picked:
        up_at, down_at = along((model, BLOCK), 1), along((BLOCK, model))
    else:
        up_at = pl.BlockSpec((model, BLOCK), lambda g, b: (0, b[g]))
        down_at = pl.BlockSpec((BLOCK, model), lambda g, b: (b[g], 0))
    return call(
        cot_body, "cot_down", (blk,), (steps,),
        [(own, fixed(own.shape)), (other, fixed(own.shape)), (up, up_at), (down, down_at)],
        [
            ((2 * tokens, half), BF16, column),
            ((model, half), BF16, along((model, BLOCK), 1)),
            ((half, model), BF16, along((BLOCK, model))),
            ((2 * tokens, model), BF16, fixed((2 * tokens, model))),
        ]
    )


def hidden_body(blocks, blk_ref, *refs):
    pieces, refs = refs[:-11], refs[-11:]
    g_ref, up_ref, row_ref, bias_ref, act_ref, grad_ref, sum_ref, both_ref, part_ref, other_ref, held = refs
    sizes = [ref.shape[0] * ref.shape[1] for ref in pieces]
    starts = [sum(sizes[:n]) for n in range(len(sizes))]
    step = pl.program_id(0)

    @pl.when(step == 0)
    def _():
        for ref, at, size in zip(pieces, starts, sizes):
            both_ref[at : at + size] = ref[...].reshape(size, ref.shape[2])

    @pl.when(step < blocks)
    def _():
        up = up_ref[...]
        bias = bias_ref[...].astype(F32)
        total = 0.0
        later = dot(pieces[0][...].reshape(sizes[0], -1), up)
        for n, (start, size) in enumerate(zip(starts, sizes)):
            at = slice(start, start + size)
            v = later + bias
            if n + 1 < len(pieces):
                later = dot(pieces[n + 1][...].reshape(sizes[n + 1], -1), up)
            square = v * v
            tanh = jnp.tanh(v * (GELU_A + GELU_B * square))
            gate = 0.5 + 0.5 * tanh
            act = v * gate
            slope = gate + act * ((1.0 - tanh) * (GELU_A + 3.0 * GELU_B * square))
            grad = (slope * g_ref[at].astype(F32)).astype(BF16)
            act_ref[at] = act.astype(BF16)
            grad_ref[at] = grad
            held[step, at] = grad
            total = total + jnp.sum(grad.astype(F32), axis=0, keepdims=True)
        sum_ref[...] = total

    @pl.when(step >= blocks)
    def _():
        grad = jnp.concatenate([held[n] for n in range(blocks)], axis=1)
        found = dot(grad, row_ref[...], 1, 1).astype(BF16)
        part_ref[...] = found[: part_ref.shape[0]]
        other_ref[...] = found[part_ref.shape[0] :]


def hidden_units(blk, pieces, grads, up, bias):
    model = pieces[0].shape[2]
    tokens, half = grads.shape
    blocks, more = half // BLOCK, model // BLOCK

    def first(g):
        return jnp.minimum(g, blocks - 1)

    def second(g):
        return jnp.maximum(g - blocks, 0)

    column = pl.BlockSpec((tokens, BLOCK), lambda g, b: (0, first(g)))
    line = pl.BlockSpec((1, BLOCK), lambda g, b: (0, first(g)))
    return call(
        functools.partial(hidden_body, blocks), "hidden", (blk,), (blocks + more,),
        [(piece, fixed(piece.shape)) for piece in pieces]
        + [
            (grads, column),
            (up, pl.BlockSpec((model, BLOCK), lambda g, b: (0, first(g)))),
            (up, pl.BlockSpec((BLOCK, half), lambda g, b: (second(g), 0))),
            (bias, pl.BlockSpec((1, BLOCK), lambda g, b: (0, b[first(g)]))),
        ],
        [
            (grads.shape, BF16, column),
            (grads.shape, BF16, column),
            ((1, half), F32, line),
            ((tokens, model), BF16, fixed((tokens, model))),
            ((tokens // 2, model), BF16, pl.BlockSpec((tokens // 2, BLOCK), lambda g, b: (0, second(g)))),
            ((tokens // 2, model), BF16, pl.BlockSpec((tokens // 2, BLOCK), lambda g, b: (0, second(g)))),
        ],
        [pltpu.VMEM((blocks, tokens, BLOCK), BF16)]
    )


def sent_body(other_ref, tok_ref, cot_ref, grad_ref, act_ref, up_ref, down_ref):
    up_ref[...] = dot(tok_ref[...], grad_ref[...], 0, 0).astype(BF16)
    down_ref[...] = dot(act_ref[...], cot_ref[...], 0, 0).astype(BF16)


def sent_grads(other, tokens, cot, grad, act, steps):
    count, model = tokens.shape
    half = grad.shape[1]
    size = half // (2 * steps)
    wide = half // steps
    return call(
        sent_body, "sent_grads", (other,), (steps,),
        [
            (tokens, fixed(tokens.shape)),
            (cot, fixed(cot.shape)),
            (grad, along((count, wide), 1)),
            (act, pl.BlockSpec((count, size), lambda g, o: (0, 2 * g + o[0]))),
        ],
        [((model, half), BF16, along((model, wide), 1)), ((half // 2, model), BF16, along((size, model)))],
    )


def feed_body(order_ref, act_ref, down_ref, att_ref, low_ref, half_ref, cot_ref, feed_ref, other_ref, out_ref, keep_ref, kept_ref):
    parts = order_ref.shape[0]
    width = att_ref.shape[1] // parts
    feed = dot(act_ref[...], down_ref[...]).astype(BF16)
    feed_ref[...] = feed[: feed_ref.shape[0]]
    other_ref[...] = feed[feed_ref.shape[0] :]
    kept_ref[...] = dot(half_ref[...], cot_ref[...], 0, 0).astype(BF16)
    grad = dot(att_ref[...], low_ref[...], 0, 0).astype(BF16)
    step, steps = pl.program_id(0), pl.num_programs(0)

    def write(ref):
        for n in range(parts):
            at = pl.multiple_of(order_ref[n] * width, width)
            ref[pl.ds(at, width)] = grad[n * width : (n + 1) * width]

    @pl.when(2 * step < steps)
    def _():
        write(out_ref)

    @pl.when(2 * step >= steps)
    def _():
        write(keep_ref)


def feed_grads(order, act, down, attended, low, cot, c_at, x_at, deps=()):
    tokens, half = act.shape
    own, model = attended.shape
    steps = model // BLOCK
    place = jnp.concatenate([order, jnp.stack([c_at, x_at]).astype(jnp.int32)])
    size = half // (2 * steps)

    def body(place_ref, *refs):
        feed_body(place_ref.at[0 : order.shape[0]], *refs)

    def low_at(g, p):
        c = p[order.shape[0]]
        mine = 2 * g >= steps
        return 0, jnp.where(mine, c * (steps // 2) + g - steps // 2, (1 - c) * (steps // 2) + g)

    return call(
        body, "feed_grads", (place,), (steps,),
        [
            (act, fixed(act.shape)),
            (down, along((half, BLOCK), 1)),
            (attended, fixed(attended.shape)),
            (low, pl.BlockSpec((own, BLOCK), low_at)),
            (act, pl.BlockSpec((tokens, size), lambda g, p: (0, 2 * g + p[order.shape[0] + 1]))),
            (cot, fixed(cot.shape)),
        ],
        [
            ((own, model), BF16, along((own, BLOCK), 1)),
            ((own, model), BF16, along((own, BLOCK), 1)),
            ((model, model // 2), BF16, pl.BlockSpec((model, BLOCK), lambda g, p: (0, jnp.minimum(g, steps // 2 - 1)))),
            ((model, model // 2), BF16, pl.BlockSpec((model, BLOCK), lambda g, p: (0, jnp.maximum(g - steps // 2, 0)))),
            ((half // 2, model), BF16, along((size, model))),
        ],
        deps=deps,
    )


def middle_back_body(
    order_ref, part_ref, sent_ref, mid_ref, cot_ref, gain_ref, w0, w1, w2, w3,
    grad_ref, low_ref, att0_ref, att1_ref, far_ref, sums_ref,
):
    grad = part_ref[...].astype(F32) + sent_ref[...].astype(F32)
    hat, inverse = centre(mid_ref[0])
    cot = cot_ref[0].astype(F32)
    total = cot + norm_back(grad, line(gain_ref), hat, inverse)
    low = total.astype(BF16)
    grad_ref[0] = total
    low_ref[0] = low
    far_ref[0, 0] = dot(low, w2[...], 1, 1).astype(BF16)
    far_ref[1, 0] = dot(low, w3[...], 1, 1).astype(BF16)
    att1_ref[0] = dot(low, w1[...], 1, 1).astype(BF16)
    att0_ref[0] = dot(low, w0[...], 1, 1).astype(BF16)

    @pl.when(pl.program_id(0) == 0)
    def _():
        sums_ref[...] = jnp.zeros_like(sums_ref)

    sums_ref[0:1] += jnp.sum(grad * hat, axis=0, keepdims=True)
    sums_ref[1:2] += jnp.sum(grad, axis=0, keepdims=True)
    sums_ref[2:3] += jnp.sum(low.astype(F32), axis=0, keepdims=True)
    sums_ref[3:4] += jnp.sum(cot, axis=0, keepdims=True)


def middle_back(order, both, sent, mid, cot, gain, weight, parts, deps=()):
    rows, shard, model = mid.shape
    width = model // parts
    block, one = along((1, shard, model)), along((1, shard, width))
    flat = pl.BlockSpec((shard, model), lambda g, o: (g, 0))
    return call(
        middle_back_body, "middle_back", (order,), (rows,),
        [(both, flat), (sent, flat), (mid, block), (cot, block), (gain, fixed(gain.shape))] + out_blocks(weight, parts),
        [
            (mid.shape, F32, block),
            (mid.shape, BF16, block),
            ((rows, shard, width), BF16, one),
            ((rows, shard, width), BF16, one),
            ((2, rows, shard, width), BF16, along((2, 1, shard, width), 1)),
            ((8, model), F32, fixed((8, model))),
        ],
        deps=deps
    )


def norm1_back_body(start, part_ref, near_ref, far_ref, stream_ref, mid_ref, gain_ref, seg_ref, in_ref, shift_ref, sums_ref):
    grad = part_ref[0].astype(F32) + near_ref[0].astype(F32) + far_ref[0].astype(F32)
    hat, inverse = centre(stream_ref[0])
    total = mid_ref[0] + norm_back(grad, line(gain_ref), hat, inverse)
    in_ref[0] = total.astype(BF16)
    seg = seg_ref[pl.ds(pl.program_id(0) + start, 1)]
    slots = lax.broadcasted_iota(jnp.int32, (SEGS, seg.shape[-1]), 0) == seg
    onehot = slots.astype(F32).astype(BF16)
    shift_ref[0] = dot(jnp.concatenate([onehot, onehot], axis=1), split_low(total))

    @pl.when(pl.program_id(0) == 0)
    def _():
        sums_ref[...] = jnp.zeros_like(sums_ref)

    sums_ref[0:1] += jnp.sum(grad * hat, axis=0, keepdims=True)
    sums_ref[1:2] += jnp.sum(grad, axis=0, keepdims=True)


def norm1_back(start, count, own, near, far, stream, mid, gain, seg, held=(), deps=()):
    rows, shard, model = stream.shape
    block, own_block = along((1, shard, model), 0, start), along((1, shard, model))
    return call(
        functools.partial(norm1_back_body, start), "norm1_back", (), (count,),
        [(own, own_block), (near, own_block), (far, own_block), (stream, block), (mid, block), (gain, fixed(gain.shape))]
        + [(seg, fixed(seg.shape))],
        [
            (stream.shape, BF16, block),
            ((count, SEGS, model), F32, along((1, SEGS, model))),
            ((8, model), F32, fixed((8, model))),
        ],
        held=[(array, 0) for array in held], deps=deps
    )


def exchange(own, one, far):
    return [own, swap(one, "c"), far, swap(far[1], "c")]


def tie(*values):
    return lax.optimization_barrier(values)


def cut(values, index, size, axis):
    return lax.dynamic_slice_in_dim(values, index * size, size, axis)


def add_low(kept, sent):
    return (kept.astype(F32) + sent.astype(F32)).astype(BF16)


def ordered(at, own, other, axis):
    return jnp.where(at == 0, jnp.concatenate([own, other], axis), jnp.concatenate([other, own], axis))


def finish_body(blocks, at_ref, d0, d1, u0, u1, l0, l1, down_ref, up_ref, qkv_ref, out_ref):
    c_at = at_ref[0]
    width = up_ref.shape[1] // (4 * blocks)
    size = d0.shape[0]
    for c in range(2):
        mine = c_at == c
        down_ref[c * size : (c + 1) * size] = jnp.where(mine, d0[...], d1[...]).astype(F32)
        up = jnp.where(mine, u0[...], u1[...]).astype(F32)
        for b in range(2 * blocks):
            up_ref[:, (2 * b + c) * width : (2 * b + c + 1) * width] = up[:, b * width : (b + 1) * width]
        late = jnp.where(mine, l0[...], l1[...]).astype(F32)
        half = out_ref.shape[1] // 2
        wide = half // 2
        out_ref[:, c * half : (c + 1) * half] = late[:, 6 * wide :]
        for y in range(2):
            for n in range(3):
                at = n * 4 * wide + (2 * y + c) * wide
                qkv_ref[:, at : at + wide] = late[:, (3 * y + n) * wide : (3 * y + n + 1) * wide]


def finish(c_at, dp, piece, down, up, late, parts):
    rows, model = late[0].shape[0], down[0].shape[1]
    depth, size = dp // 2, down[0].shape[0]
    if piece % 128 == 0:
        at = c_at.astype(jnp.int32)[None]
        shapes = [(2 * size, model), (rows, 2 * dp * piece), (rows, 3 * model), (rows, model)]
        arrays = list(down) + list(up) + list(late)
        return call(
            functools.partial(finish_body, depth), "finish", (at,), (1,),
            [(array, fixed(array.shape)) for array in arrays], [(shape, F32, fixed(shape)) for shape in shapes],
        )
    down_done = ordered(c_at, *down, 0).astype(F32)
    up_done = ordered(c_at, up[0][None], up[1][None], 0).reshape(2, rows, dp, piece).transpose(1, 2, 0, 3)
    up_done = up_done.reshape(rows, 2 * dp * piece).astype(F32)
    both = ordered(c_at, late[0][None], late[1][None], 0)
    width = model // parts
    qkv_done = both[:, :, : 6 * width].reshape(2, rows, 2, 3, width).transpose(1, 3, 2, 0, 4)
    qkv_done = qkv_done.reshape(rows, 3 * model).astype(F32)
    out_done = jnp.concatenate([both[0, :, 6 * width :], both[1, :, 6 * width :]], axis=1).astype(F32)
    return down_done, up_done, qkv_done, out_done


def local(
    inputs, segment_ids, doc_times, time_weight, time_bias, norm1_gain, norm1_bias, qkv_weight, qkv_bias,
    out_weight, out_bias, norm2_gain, norm2_bias, up_weight, up_bias, down_weight, down_bias, cotangent,
    *, dp,
):
    rows, shard, model = inputs.shape
    parts = 4
    tokens = rows * shard
    hidden_width = up_weight.shape[1]
    width = model // parts
    depth = dp // 2
    half = hidden_width // 2
    piece = half // dp
    z_at, x_at, y_at, c_at = (lax.axis_index(name) for name in ("z", "x", "y", "c"))
    me = 2 * y_at + c_at

    seg_two = swap(segment_ids, "y")
    segs = jnp.stack([segment_ids, swap(segment_ids, "c"), seg_two, swap(seg_two, "c")], axis=1)

    groups = [(0, rows - 1), (rows - 1, 1)] if rows > 1 else [(0, 1)]
    features = time_features(doc_times.reshape(rows * SEGS), jnp.arange(TEMB), TEMB // 2)
    time_shift = dot(features, time_weight).reshape(rows, SEGS, model)
    stream, own1 = norm1(inputs, segment_ids, time_shift, (time_bias, norm1_gain, norm1_bias))
    own1, segs = tie(own1, segs)
    two1 = swap(own1, "y")
    one1 = swap(own1, "c")

    me, x_at, z_at, c_at, y_at, own1 = tie(me, x_at, z_at, c_at, y_at, own1)
    order = [me ^ i for i in range(parts)]
    order_list = jnp.stack(order).astype(jnp.int32)
    me_list = order_list[:1]
    low_id, high_id = segs.min(axis=2), segs.max(axis=2)
    act = (low_id[:, :, None] <= high_id[:, None, :]) & (low_id[:, None, :] <= high_id[:, :, None])
    places = jnp.arange(parts, dtype=jnp.int32)
    rank = jnp.cumsum(act.astype(jnp.int32), axis=2) - 1
    chosen = act[..., None] & (rank[..., None] == places)
    idx = jnp.sum(jnp.where(chosen, places[:, None], 0), axis=2).astype(jnp.int32).reshape(-1)
    cnt = jnp.sum(act.astype(jnp.int32), axis=2).reshape(-1)
    positions = jnp.stack([o * shard + jnp.arange(shard, dtype=jnp.int32) for o in order])
    cos_tab, sin_tab = rotary_tables(positions, HEAD_DIM)

    cot = cotangent.reshape(tokens, model)
    cot_other = swap(cot, "c")
    if piece % BLOCK == 0:
        blk = (jnp.arange(dp)[:, None] * 2 + c_at) * (piece // BLOCK) + jnp.arange(piece // BLOCK)
        blk = blk.reshape(-1).astype(jnp.int32)
        up_from, down_from = up_weight, down_weight
    else:
        blk = jnp.zeros((half // BLOCK,), jnp.int32)
        up_from = lax.dynamic_index_in_dim(up_weight.reshape(model, dp, 2, piece), c_at, 2, keepdims=False)
        down_from = lax.dynamic_index_in_dim(down_weight.reshape(dp, 2, piece, model), c_at, 1, keepdims=False)
        up_from, down_from = up_from.reshape(model, half), down_from.reshape(half, model)
    grad_act, up_own, down_own, cot_both = cot_down(
        blk, cot, cot_other, up_from, down_from, piece % BLOCK != 0, half
    )
    up_bias_own, bias_blk = up_bias.reshape(1, hidden_width), blk
    if piece % BLOCK:
        up_bias_own = lax.dynamic_index_in_dim(up_bias.reshape(dp, 2, piece), c_at, 1, keepdims=False)
        up_bias_own, bias_blk = up_bias_own.reshape(1, half), jnp.arange(half // BLOCK, dtype=jnp.int32)

    qkv_line = qkv_bias.reshape(1, 3 * model)
    qkv, qkv_own = project_qkv(0, parts, me_list, own1, one1, qkv_weight, qkv_line, cos_tab, sin_tab, (), (grad_act, cnt, idx))
    two1, qkv = tie(two1, qkv)
    three1 = swap(two1, "c")
    qkv, _ = project_qkv(1, parts, me_list, two1, three1, qkv_weight, qkv_line, cos_tab, sin_tab, (qkv,))
    o, lse, attended = None, None, []
    for start, count in groups:
        held = () if o is None else (o, lse)
        o, out_one, out_far, lse = attend(start, count, cnt, idx, qkv, segs, held)
        attended.append((out_one, swap(out_far, "y")))
    held, normed2, normed2_other = (), [], []
    for (start, count), values in zip(groups, attended):
        far, o = tie(values[1], o)
        values = exchange(o, values[0], far)
        middle, low, attended_all = middle_norm(
            start, count, order_list, values, out_weight, stream, (out_bias, norm2_gain, norm2_bias), held
        )
        held = (middle, attended_all)
        normed2.append(low)
        normed2_other.append(swap(low, "c"))

    active, grad_hidden, up_b, normed2_both, part2, part2_other = hidden_units(
        bias_blk, normed2 + normed2_other, grad_act, up_own, up_bias_own
    )
    part2_sent = swap(part2_other, "c")
    grad_middle, grad_middle_low, att0, att1, far, sums2 = middle_back(
        order_list, part2, part2_sent, middle, cotangent, norm2_gain, out_weight, parts
    )
    far = swap(far, "y")
    sums2 = sums2[:4]

    active, grad_hidden, att0 = tie(active, grad_hidden, att0)
    up_rows = model // dp
    small_blocks = piece % BLOCK != 0 or depth != model // BLOCK
    if small_blocks:
        up_grad = dot(normed2_both, grad_hidden, 0, 0).astype(BF16)
        down_out = dot(active, cot_both, 0, 0).astype(BF16).reshape(depth, 2, piece, model)
        down_kept = lax.dynamic_index_in_dim(down_out, x_at, 1, keepdims=False).reshape(half // 2, model)
        down_out = lax.dynamic_index_in_dim(down_out, 1 - x_at, 1, keepdims=False).reshape(half // 2, model)
    else:
        up_grad, down_out = sent_grads(
            1 - x_at[None].astype(jnp.int32), normed2_both, cot_both, grad_hidden, active, depth
        )
    up_grad, down_out, far = tie(up_grad, down_out, far)
    up_z = lax.psum_scatter(up_grad, "z", scatter_dimension=0, tiled=True)
    down_sent = swap(down_out[: half // 4], "x")
    if small_blocks:
        feed = dot(active, down_own).astype(BF16)
        feed, feed_other = feed[:tokens], feed[tokens:]
        out_grad = dot(attended_all.reshape(tokens, model), grad_middle_low.reshape(tokens, model), 0, 0).astype(BF16)
        out_grad = jnp.concatenate([cut(out_grad, o_at, width, 0) for o_at in order], axis=0)
        out_sent, out_grad = (cut(out_grad, at, model // 2, 1) for at in (1 - c_at, c_at))
    else:
        feed, feed_other, out_sent, out_grad, down_kept = feed_grads(
            order_list, active, down_own, attended_all.reshape(tokens, model), grad_middle_low.reshape(tokens, model),
            cot_both, c_at, x_at, (far, down_out),
        )
    feed, feed_other, out_sent, out_grad, down_kept, down_sent, down_out = tie(
        feed, feed_other, out_sent, out_grad, down_kept, down_sent, down_out
    )
    down_late = swap(down_out[half // 4 :], "x")
    out_sent, feed_sent = swap(out_sent, "c"), swap(feed_other, "c")
    grad_o = exchange(att0, att1, far)

    back = []
    (start, count), rest = groups[0], groups[1:]
    found = attend_back(start, count, cnt, idx, qkv, o, grad_o, lse, segs, cos_tab, sin_tab, qkv_own)
    *found, down_late, out_sent, feed_sent = tie(*found, down_late, out_sent, feed_sent)
    grad_qkv, own, one, two, three = found
    there = add_low(two, swap(three, "c"))
    down_x = add_low(down_kept, jnp.concatenate([down_sent, down_late], axis=0))
    down_z = lax.psum_scatter(down_x, "z", scatter_dimension=0, tiled=True)
    out_c = add_low(out_grad, out_sent).reshape(depth, 2 * up_rows, model // 2)
    out_sent = cut(out_c, 1 - x_at, up_rows, 1)
    there, down_x, out_sent = tie(there, down_x, out_sent)
    far, near = swap(there, "y"), swap(one, "c")
    out_sent = swap(out_sent, "x")
    if rest:
        (start, count), = rest
        found = attend_back(
            start, count, cnt, idx, qkv, o, grad_o, lse, segs, cos_tab, sin_tab, qkv_own, (grad_qkv,),
            (there, down_x),
        )
        *found, far, up_z, out_sent = tie(*found, far, up_z, out_sent)
        back.append((own, near, far))
        grad_qkv, own, one, two, three = found
        there, far = tie(add_low(two, swap(three, "c")), far)
        far, near = swap(there, "y"), swap(one, "c")
        grad_qkv, there = tie(grad_qkv, there)
    qkv_out, qkv_kept, qkv_b = qkv_grads(x_at, [own1, one1, two1, three1], grad_qkv, depth)
    qkv_out, qkv_kept, far, out_sent, out_c, up_z = tie(qkv_out, qkv_kept, far, out_sent, out_c, up_z)
    back.append((own, near, far))
    qkv_sent = swap(qkv_out, "x")
    out_x = add_low(cut(out_c, x_at, up_rows, 1), out_sent)
    out_sent = cut(out_x, 1 - y_at, width, 2)
    qkv_out, up_out = tie(qkv_out, cut(up_z, 1 - x_at, up_rows, 0))
    up_sent = swap(up_out, "x")
    held, grad_shift, sums1 = (), [], 0.0
    for (start, count), values in zip(groups, back):
        input_grad, found, sums = norm1_back(
            start, count, *values, stream, grad_middle, norm1_gain, segment_ids, held, (qkv_kept, up_out)
        )
        if not held:
            input_grad, out_sent = tie(input_grad, out_sent)
            out_sent = swap(out_sent, "y")
        held = (input_grad,)
        grad_shift.append(found.reshape(count * SEGS, model))
        sums1 = sums1 + sums[:2]

    up_b = up_b.reshape(dp, 1, piece)
    up_b = jnp.where(jnp.arange(2)[:, None] == c_at, up_b, 0.0).reshape(-1, model)
    qkv_b = jnp.where(jnp.arange(parts)[:, None] == me, qkv_b.reshape(3, 1, width), 0.0).reshape(3, model)
    times = doc_times.reshape(1, rows * SEGS)
    times = jnp.concatenate([times // 32, times % 32], axis=1).astype(F32)
    times = jnp.tile(jnp.pad(times, ((0, 0), (0, width - times.shape[1]))), (1, parts))
    small = jnp.concatenate(grad_shift + [sums1, sums2, qkv_b, up_b, times], axis=0).astype(BF16)
    small_sent = swap(cut(small, 1 - c_at, 2 * width, 1), "c")
    small = add_low(cut(small, c_at, 2 * width, 1), small_sent)
    small, qkv_sent, out_sent = tie(small, qkv_sent, out_sent)
    small = add_low(cut(small, y_at, width, 1), swap(cut(small, 1 - y_at, width, 1), "y"))
    out_x = add_low(cut(out_x, y_at, width, 2), out_sent)
    late = jnp.concatenate([add_low(qkv_kept, qkv_sent), out_x], axis=2)
    small = ordered(x_at, small[None], swap(small, "x")[None], 0)
    output = middle.reshape(tokens, model) + (feed.astype(F32) + feed_sent.astype(F32) + down_bias.astype(F32))
    output = output.astype(BF16).reshape(rows, shard, model)
    small, late = tie(small, late)
    if depth == 4:
        flat = small.reshape(2 * small.shape[1] * width // model, model)
        parts_z = [lax.dynamic_index_in_dim(late, z_at ^ n, 0, keepdims=False) for n in range(depth)]
        sent = [
            lax.ppermute(jnp.concatenate([parts_z[n], flat], axis=0), "z", [(i, i ^ n) for i in range(depth)])
            for n in range(1, depth)
        ]
        small, down_z, up_z, up_sent = tie(small, down_z, up_z, up_sent)
        up_x = add_low(cut(up_z, x_at, up_rows, 0), up_sent)
        down_sent, up_sent = swap(down_z, "y"), swap(up_x, "y")
        *sent, output, down_sent, up_sent = tie(*sent, output, down_sent, up_sent)
        late = sum(part[:up_rows].astype(F32) for part in sent) + parts_z[0].astype(F32)
        late = late.astype(BF16)
        small = jnp.stack([small] + [part[up_rows:].reshape(small.shape) for part in sent])
        small = jnp.stack([lax.dynamic_index_in_dim(small, z_at ^ n, 0, keepdims=False) for n in range(depth)])
    else:
        up_x = add_low(cut(up_z, x_at, up_rows, 0), up_sent)
        down_sent, up_sent = swap(down_z, "y"), swap(up_x, "y")
        late = lax.psum_scatter(late, "z", scatter_dimension=0, tiled=False)
        small = lax.all_gather(small, "z")
    small = small.reshape(dp, small.shape[2], width)

    late_sent = swap(late, "y")
    down_done, up_done = add_low(down_z, down_sent), add_low(up_x, up_sent)
    down_other, up_other = swap(down_done, "c"), swap(up_done, "c")
    both = ordered(y_at, late[None], late_sent[None], 0)
    late = jnp.concatenate([both[0, :, : 3 * width], both[1, :, : 3 * width], both[0, :, 3 * width :], both[1, :, 3 * width :]], axis=1)
    late_other = swap(late, "c")

    down_done, up_done, qkv_done, out_done = finish(
        c_at, dp, piece, (down_done, down_other), (up_done, up_other), (late, late_other), parts
    )

    dp_at = 2 * z_at + x_at
    all_times = small[:, -1, : 2 * rows * SEGS].astype(F32) * 0.25
    all_times = all_times[:, : rows * SEGS] * 32.0 + all_times[:, rows * SEGS :]
    shifts = small[:, : rows * SEGS].reshape(dp * rows * SEGS, width)
    columns = dp_at * (TEMB // dp) + jnp.arange(TEMB // dp)
    wanted = time_features(all_times.reshape(-1), columns, TEMB // 2)
    sums = jnp.sum(small[:, rows * SEGS : -1].astype(F32), axis=0)
    full = [dot(wanted, shifts, 0, 0), sums, jnp.sum(shifts.astype(F32), axis=0, keepdims=True)]
    full = jnp.concatenate(full, axis=0).astype(BF16)
    count = full.shape[0]
    full = jnp.pad(full, ((0, -count % 16), (0, 0)))
    full = ordered(y_at, full[None], swap(full, "y")[None], 0)
    full = ordered(c_at, full[None], swap(full, "c")[None], 0)
    full = full.transpose(2, 0, 1, 3).reshape(-1, model).astype(F32)
    time_w_done, sums = full[: TEMB // dp], full[TEMB // dp : count]

    def share(vector):
        return cut(vector.reshape(-1), dp_at, vector.size // dp, 0)

    return (
        output, input_grad, time_w_done, share(sums[-1]), share(sums[0]), share(sums[1]), qkv_done, share(sums[6:9]),
        out_done, share(sums[4]), share(sums[2]), share(sums[3]), up_done, share(sums[9:-1]), down_done, share(sums[5]),
    )


def solution(mesh):
    dp, seq = mesh.shape["dp"], mesh.shape["seq"]
    fine = Mesh(mesh.devices.reshape(dp // 2, 2, seq // 2, 2), ("z", "x", "y", "c"))
    rows, seqs = ("z", "x"), ("y", "c")
    placed = (P(rows, seqs, None), P(rows, seqs), P(rows, None)) + (P(),) * 14 + (P(rows, seqs, None),)
    vec, mat = P(rows), P(rows, None)
    return jax.shard_map(
        functools.partial(local, dp=dp),
        mesh=fine,
        in_specs=placed,
        out_specs=(
            P(rows, seqs, None), P(rows, seqs, None), mat, vec, vec, vec, mat, vec, mat, vec, vec, vec, mat, vec, mat, vec,
        ),
        check_vma=False,
    )
```

```python
import functools
import math

import jax
import jax.numpy as jnp
from jax import lax
from jax.experimental import pallas as pl
from jax.experimental.pallas import tpu as pltpu
from jax.sharding import Mesh, PartitionSpec as P

HEADS = 16
HEAD_DIM = 64
TEMB = 256
SEGS = 8
EPSILON = 1e-05
F32 = jnp.float32
BF16 = jnp.bfloat16
NEG = -1e30
LOG2E = math.log2(math.e)
GELU_A = math.sqrt(2.0 / math.pi)
GELU_B = GELU_A * 0.044715
BLOCK = 256
VMEM = 60 * 1024 * 1024


def swap(value, axis):
    return lax.ppermute(value, axis, [(0, 1), (1, 0)])


def time_features(doc_times, column, half_size):
    frequency = jnp.exp(-math.log(10000.0) * (column % half_size).astype(F32) / half_size)
    angles = doc_times.astype(F32)[..., None] * frequency
    return jnp.where(column < half_size, jnp.sin(angles), jnp.cos(angles)).astype(BF16)


def rotary_tables(positions, head_size):
    half_size = head_size // 2
    frequency = jnp.exp(-math.log(10000.0) * 2.0 * jnp.arange(half_size, dtype=F32) / head_size)
    angles = positions.astype(F32)[..., None] * frequency
    cos_tab, sin_tab = jnp.cos(angles), jnp.sin(angles)
    return (
        jnp.concatenate([cos_tab] * 4, axis=-1),
        jnp.concatenate([-sin_tab, sin_tab, -sin_tab, sin_tab], axis=-1),
    )


def dot(left_op, right_op, left_dim=1, right_dim=0):
    return lax.dot_general(
        left_op, right_op, (((left_dim,), (right_dim,)), ((), ())), preferred_element_type=F32
    )


def turn(values, cos_tab, sin_tab):
    slabs = []
    lane = lax.broadcasted_iota(jnp.int32, (values.shape[0], 128), 1)
    first = lane % HEAD_DIM < HEAD_DIM // 2
    for start in range(0, values.shape[1], 128):
        slab = values[:, start : start + 128]
        partner = jnp.where(
            first, pltpu.roll(slab, 128 - HEAD_DIM // 2, 1), pltpu.roll(slab, HEAD_DIM // 2, 1)
        )
        slabs.append(slab * cos_tab + partner * sin_tab)
    return jnp.concatenate(slabs, axis=1)


def split_low(values):
    high = values.astype(BF16)
    return jnp.concatenate([high, (values - high.astype(F32)).astype(BF16)], axis=0)


def centre(values):
    scale = 1.0 / values.shape[-1]
    centred = values - jnp.sum(values, axis=-1, keepdims=True) * scale
    spread = jnp.sum(centred * centred, axis=-1, keepdims=True) * scale
    inverse = lax.rsqrt(spread + EPSILON)
    return centred * inverse, inverse


def norm_back(grad, gain, hat, inverse):
    scale = 1.0 / grad.shape[-1]
    scaled = grad * gain
    mean = jnp.sum(scaled, axis=-1, keepdims=True) * scale
    along = jnp.sum(scaled * hat, axis=-1, keepdims=True) * scale
    return inverse * (scaled - mean - hat * along)


def call(body, name, prefetch, grid, ins, outs, scratch=(), deps=(), held=()):
    count = len(prefetch) + len(ins)
    extra = [array for array, _ in held] + list(deps)

    def kernel(*refs):
        body(*refs[:count], *refs[count + len(extra) :])

    return pl.pallas_call(
        kernel,
        grid_spec=pltpu.PrefetchScalarGridSpec(
            num_scalar_prefetch=len(prefetch),
            grid=grid,
            in_specs=[spec for _, spec in ins] + [pl.BlockSpec(memory_space=pl.ANY)] * len(extra),
            out_specs=[spec for _, _, spec in outs],
            scratch_shapes=list(scratch),
        ),
        out_shape=[jax.ShapeDtypeStruct(shape, kind) for shape, kind, _ in outs],
        input_output_aliases={count + n: out for n, (_, out) in enumerate(held)},
        compiler_params=pltpu.CompilerParams(vmem_limit_bytes=VMEM),
        name=name,
    )(*prefetch, *[array for array, _ in ins], *extra)


def line(ref):
    return ref[...].astype(F32).reshape(1, -1)


def fixed(shape):
    return pl.BlockSpec(shape, lambda *_: (0,) * len(shape))


def along(shape, axis=0, start=0):
    return pl.BlockSpec(shape, lambda g, *_: tuple(start + g if n == axis else 0 for n in range(len(shape))))


def norm1_body(start, x_ref, seg_ref, shift_ref, time_ref, gain_ref, bias_ref, stream_ref, low_ref):
    seg = seg_ref[pl.ds(pl.program_id(0) + start, 1)]
    slots = lax.broadcasted_iota(jnp.int32, (SEGS, seg.shape[-1]), 0) == seg
    onehot = slots.astype(F32).astype(BF16)
    shift = shift_ref[0] + line(time_ref)
    added = dot(jnp.concatenate([onehot, onehot], axis=0), split_low(shift), 0, 0)
    stream = x_ref[0].astype(F32) + added
    hat, _ = centre(stream)
    stream_ref[0] = stream
    low_ref[0] = (hat * line(gain_ref) + line(bias_ref)).astype(BF16)


def norm1(start, count, x, seg, shift, vecs, held=()):
    rows, shard, model = x.shape
    block = along((1, shard, model), 0, start)
    return call(
        functools.partial(norm1_body, start), "norm1", (), (count,),
        [(x, block), (seg, fixed(seg.shape)), (shift, along((1, SEGS, model), 0, start))]
        + [(vec, fixed(vec.shape)) for vec in vecs],
        [(x.shape, F32, block), ((count, shard, model), BF16, along((1, shard, model)))],
        held=[(array, 0) for array in held],
    )


def qkv_body(sizes, me_ref, *refs):
    count = 2 * len(sizes)
    pieces, (w_ref, bias_ref, cos_ref, sin_ref, out_ref), own = refs[:count], refs[count : count + 5], refs[count + 5 :]
    places = [(n, sum(sizes[:g]) + r, n * len(sizes) + g, r) for n in range(2) for g, size in enumerate(sizes) for r in range(size)]
    step = pl.program_id(0)

    def run(turned):
        w = w_ref[...]
        bias = bias_ref[...].astype(F32)
        later = dot(pieces[0][0], w)
        for at, (n, r, _, _) in enumerate(places):
            values = later + bias
            if at + 1 < len(places):
                later = dot(pieces[places[at + 1][2]][places[at + 1][3]], w)
            if turned:
                values = turn(values, cos_ref[n], sin_ref[n]) * jnp.where(step == 0, LOG2E * HEAD_DIM**-0.5, 1.0)
            out_ref[0, n, r] = values.astype(BF16)

    for ref in own:
        ref[...] = w_ref[...].T

    @pl.when(step < 2)
    def _():
        run(True)

    @pl.when(step == 2)
    def _():
        run(False)


def project_qkv(pair, start, parts, rows, me, pieces, weight, bias, cos_tab, sin_tab, held=(), deps=()):
    _, shard, model = pieces[0][0].shape
    sizes = [piece.shape[0] for piece in pieces[0]]
    count = sum(sizes)
    width = model // parts
    place = pl.BlockSpec((1, 2, count, shard, width), lambda g, m: (g, pair, start // count, 0, 0))
    outs = [((3, parts, rows, shard, width), BF16, place)]
    if not held:
        outs.append(((3 * width, model), BF16, along((width, model))))
    return call(
        functools.partial(qkv_body, sizes), "qkv", (me,), (3,),
        [(piece, fixed(piece.shape)) for group in pieces for piece in group]
        + [
            (weight, pl.BlockSpec((model, width), lambda g, m: (0, g * parts + m[0]))),
            (bias, pl.BlockSpec((1, width), lambda g, m: (0, g * parts + m[0]))),
            (cos_tab, pl.BlockSpec((2, shard, 128), lambda g, m: (pair, 0, 0))),
            (sin_tab, pl.BlockSpec((2, shard, 128), lambda g, m: (pair, 0, 0))),
        ],
        outs, held=[(array, n) for n, array in enumerate(held)], deps=deps,
    )


def qkv_grads(x_at, pieces, grad, blocks, deps=()):
    shard, model = pieces[0][0].shape[1:]
    parts, rows, _, columns = grad.shape
    size = model // (2 * blocks)
    flat = [(n, piece) for n, group in enumerate(pieces) for piece in group]

    def body(at_ref, *refs):
        g_ref, out_ref, keep_ref, sum_ref = refs[len(flat) :]
        total, sums, start = 0.0, 0.0, [0] * parts
        for (n, piece), x_ref in zip(flat, refs):
            count = piece.shape[0]
            g = g_ref[n, start[n] : start[n] + count].reshape(count * shard, g_ref.shape[3])
            start[n] += count
            total = total + dot(x_ref[...].reshape(count * shard, model), g, 0, 0)
            sums = sums + jnp.sum(g.astype(F32), axis=0, keepdims=True)
        low = total.astype(BF16)
        for x in range(2):
            for b in range(blocks):
                values = low[(2 * b + x) * size : (2 * b + x + 1) * size]

                @pl.when(at_ref[0] == x)
                def _():
                    keep_ref[b] = values

                @pl.when(at_ref[0] != x)
                def _():
                    out_ref[b] = values

        sum_ref[...] = sums

    block = along((blocks, size, BLOCK), 2)
    shape = (blocks, size, columns)
    return call(
        body, "qkv_grads", (x_at.astype(jnp.int32)[None],), (columns // BLOCK,),
        [(x, fixed(x.shape)) for _, x in flat] + [(grad, along((parts, rows, shard, BLOCK), 3))],
        [(shape, BF16, block), (shape, BF16, block), ((1, columns), F32, along((1, BLOCK), 1))],
        deps=deps,
    )


def seg_columns(segq_all, segk):
    pieces, shard, _ = segk.shape
    for j in range(pieces):
        row = jnp.broadcast_to(segq_all[j:j+1].astype(F32), (128, shard))
        segk[j] = row.T

def attend_body(start, cnt_ref, idx_ref, qkv_ref, seg_ref, o_ref, one_ref, far_ref, lse_ref, vt, segk, qmt, acc):
    row = pl.program_id(0) + start
    _, pieces, _, shard, width = qkv_ref.shape
    heads = width // HEAD_DIM

    @pl.when(pl.program_id(0) == 0)
    def _():
        qmt[...] = jnp.zeros_like(qmt)

    for j in range(pieces):
        vt[j] = qkv_ref[2, j, 0].T
        qt = qkv_ref[0, j, 0].T
        for h in range(heads):
            at = slice(h * HEAD_DIM, (h + 1) * HEAD_DIM)
            qmt[j, at, h * shard : (h + 1) * shard] = qt[at]
    seg_columns(seg_ref[0], segk)

    @pl.loop(0, pieces)
    def _(piece):
        attend_piece(row * pieces + piece, piece, cnt_ref, idx_ref, qkv_ref.at[1], seg_ref, lse_ref, vt, segk, qmt, acc)

    for j in range(pieces):
        o_ref[j, 0] = acc[j].T.astype(BF16)
    one_ref[0] = o_ref[1, 0]
    far_ref[:, 0] = o_ref[2:, 0]


def attend_piece(at_q, piece, cnt_ref, idx_ref, k_ref, seg_ref, lse_ref, vt, segk, qmt, acc):
    pieces, _, shard, width = k_ref.shape
    heads = width // HEAD_DIM
    seg_q = seg_ref[0, pl.ds(piece, 1)].astype(F32)

    def run(count):
        @pl.when(cnt_ref[at_q] == count)
        def _():
            qm = qmt[piece]
            places = [idx_ref[at_q * pieces + t] for t in range(count)]
            top, tot, out = [None] * heads, [None] * heads, [None] * heads
            later = dot(k_ref[places[0], 0], qm)
            for t in range(count):
                s = later
                if t + 1 < count:
                    later = dot(k_ref[places[t + 1], 0], qm)
                col = segk[places[t]]
                same = jnp.concatenate([col] * (shard // 128), axis=1) == seg_q
                for h in range(heads):
                    at = slice(h * HEAD_DIM, (h + 1) * HEAD_DIM)
                    sh = jnp.where(same, s[:, h * shard : (h + 1) * shard], NEG)
                    best = jnp.max(sh, axis=0, keepdims=True)
                    if t:
                        best = jnp.maximum(top[h], best)
                        fade = jnp.exp2(top[h] - best)
                    p = jnp.exp2(sh - best)
                    values = jnp.concatenate([vt[places[t], at], jnp.ones((16, shard), BF16)], axis=0)
                    found = dot(values, p.astype(BF16))
                    total, found = found[HEAD_DIM : HEAD_DIM + 1], found[:HEAD_DIM]
                    if t:
                        total = tot[h] * fade + total
                        found = out[h] * fade + found
                    top[h], tot[h], out[h] = best, total, found
            for h in range(heads):
                acc[piece, h * HEAD_DIM : (h + 1) * HEAD_DIM] = out[h] / tot[h]
                lse_ref[0, piece, h : h + 1] = top[h] + jnp.log2(tot[h])

    for count in range(1, pieces + 1):
        run(count)


def attend(start, count, cnt, idx, qkv, seg, held=()):
    _, pieces, rows, shard, width = qkv.shape
    heads = width // HEAD_DIM
    pairs = count * (pieces * shard) ** 2
    return call(
        functools.partial(attend_body, start), "attend", (cnt, idx), (count,),
        [(qkv, along((3, pieces, 1, shard, width), 2, start)), (seg, along((1, pieces, shard), 0, start))],
        [
            ((pieces, rows, shard, width), BF16, along((pieces, 1, shard, width), 1, start)),
            ((count, shard, width), BF16, along((1, shard, width))),
            ((2, count, shard, width), BF16, along((2, 1, shard, width), 1)),
            ((rows, pieces, 8, shard), F32, along((1, pieces, 8, shard), 0, start)),
        ],
        [
            pltpu.VMEM((pieces, width, shard), BF16),
            pltpu.VMEM((pieces, shard, 128), F32),
            pltpu.VMEM((pieces, width, heads * shard), BF16),
            pltpu.VMEM((pieces, width, shard), F32),
        ],
        held=list(zip(held, (0, 3)))
    )


def attend_back_body(
    start, cnt_ref, idx_ref, qkv_ref, o_ref, do0, do1, do2, do3, lse_ref, seg_ref, cos_ref, sin_ref, w_ref,
    g_ref, p0_ref, p1_ref, p2_ref, p3_ref, kt, segk, dk, dv, dqt, qmt, gmt, qst, gst, low,
):
    row = pl.program_id(0) + start
    _, pieces, _, shard, width = qkv_ref.shape
    heads = width // HEAD_DIM

    @pl.when(pl.program_id(0) == 0)
    def _():
        qmt[...] = jnp.zeros_like(qmt)
        gmt[...] = jnp.zeros_like(gmt)

    seg_columns(seg_ref[0], segk)
    dk[...] = jnp.zeros_like(dk)
    dv[...] = jnp.zeros_like(dv)
    lane = lax.broadcasted_iota(jnp.int32, (shard, width), 1) // HEAD_DIM
    chosen = lax.broadcasted_iota(jnp.int32, (8, width), 1) // HEAD_DIM
    chosen = (chosen == lax.broadcasted_iota(jnp.int32, (8, width), 0)).astype(BF16)
    for j, do_ref in enumerate((do0, do1, do2, do3)):
        kt[j] = qkv_ref[1, j, 0].T
        q, do = qkv_ref[0, j, 0], do_ref[...].reshape(shard, width)
        qt, gt = q.T, do.T
        for h in range(heads):
            at, qa = slice(h * HEAD_DIM, (h + 1) * HEAD_DIM), slice(h * shard, (h + 1) * shard)
            qmt[j, at, qa] = qt[at]
            gmt[j, at, qa] = gt[at]
            qst[j, qa] = jnp.where(lane == h, q, jnp.zeros_like(q))
            gst[j, qa] = jnp.where(lane == h, do, jnp.zeros_like(do))
        prod = do.astype(F32) * o_ref[j, 0].astype(F32)
        high = prod.astype(BF16)
        low[j] = dot(chosen, high, 1, 1) + dot(chosen, (prod - high.astype(F32)).astype(BF16), 1, 1)

    @pl.loop(0, pieces)
    def _(piece):
        back_piece(
            row * pieces + piece, piece, cnt_ref, idx_ref, qkv_ref.at[1], qkv_ref.at[2], lse_ref, seg_ref,
            kt, segk, dk, dv, dqt, qmt, gmt, qst, gst, low,
        )

    for j, ref in ((1, p1_ref), (3, p3_ref), (0, p0_ref), (2, p2_ref)):
        grad_q = turn(dqt[j].T * HEAD_DIM**-0.5, cos_ref[j], -sin_ref[j]).astype(BF16)
        grad_k = turn(dk[j] * (1 / LOG2E), cos_ref[j], -sin_ref[j]).astype(BF16)
        grad = jnp.concatenate([grad_q, grad_k, dv[j].astype(BF16)], axis=1)
        g_ref[j, 0] = grad
        ref[0] = dot(grad, w_ref[...]).astype(BF16)


def back_piece(
    at_q, piece, cnt_ref, idx_ref, k_ref, v_ref, lse_ref, seg_ref, kt, segk, dk, dv, dqt, qmt, gmt, qst, gst, low
):
    pieces, _, shard, width = k_ref.shape
    heads = width // HEAD_DIM
    lse, delta = lse_ref[0, piece], low[piece]
    seg_q = seg_ref[0, pl.ds(piece, 1)].astype(F32)

    def run(count):
        @pl.when(cnt_ref[at_q] == count)
        def _():
            places = [idx_ref[at_q * pieces + t] for t in range(count)]
            qm, gm = qmt[piece], gmt[piece]
            later = dot(k_ref[places[0], 0], qm), dot(v_ref[places[0], 0], gm)
            out = [None] * heads
            for t in range(count):
                s, dp = later
                j = places[t]
                if t + 1 < count:
                    later = dot(k_ref[places[t + 1], 0], qm), dot(v_ref[places[t + 1], 0], gm)
                col = segk[j]
                same = jnp.concatenate([col] * (shard // 128), axis=1) == seg_q
                ps, dss = [], []
                for h in range(heads):
                    at, qa = slice(h * HEAD_DIM, (h + 1) * HEAD_DIM), slice(h * shard, (h + 1) * shard)
                    p = jnp.exp2(jnp.where(same, s[:, qa] - lse[h : h + 1], NEG))
                    ds = (p * (dp[:, qa] - delta[h : h + 1])).astype(BF16)
                    ps.append(p.astype(BF16))
                    dss.append(ds)
                    found = dot(kt[j, at], ds)
                    out[h] = found if t == 0 else out[h] + found
                dv[j] += dot(jnp.concatenate(ps, axis=1), gst[piece])
                dk[j] += dot(jnp.concatenate(dss, axis=1), qst[piece])
            for h in range(heads):
                dqt[piece, h * HEAD_DIM : (h + 1) * HEAD_DIM] = out[h]

    for count in range(1, pieces + 1):
        run(count)


def attend_back(start, count, cnt, idx, qkv, o, do, lse, seg, cos_tab, sin_tab, weight, held=(), deps=()):
    _, pieces, rows, shard, width = qkv.shape
    model = weight.shape[1]
    heads = width // HEAD_DIM
    table = fixed((pieces, shard, 128))
    pairs = count * (pieces * shard) ** 2
    square, wide = (pieces, width, heads * shard), (pieces, shard, width)
    one = along((1, shard, width), 0, start)
    return call(
        functools.partial(attend_back_body, start), "attend_back", (cnt, idx), (count,),
        [(qkv, along((3, pieces, 1, shard, width), 2, start)), (o, along((pieces, 1, shard, width), 1, start))]
        + [(do[0], one), (do[1], one), (do[2], along((1, 1, shard, width), 1, start)), (do[3], one)]
        + [(lse, along((1, pieces, 8, shard), 0, start)), (seg, along((1, pieces, shard), 0, start))]
        + [(cos_tab, table), (sin_tab, table), (weight, fixed(weight.shape))],
        [((pieces, rows, shard, 3 * width), BF16, along((pieces, 1, shard, 3 * width), 1, start))]
        + [((count, shard, model), BF16, along((1, shard, model)))] * pieces,
        [
            pltpu.VMEM((pieces, width, shard), BF16),
            pltpu.VMEM((pieces, shard, 128), F32),
            pltpu.VMEM(wide, F32),
            pltpu.VMEM(wide, F32),
            pltpu.VMEM((pieces, width, shard), F32),
            pltpu.VMEM(square, BF16),
            pltpu.VMEM(square, BF16),
            pltpu.VMEM((pieces, heads * shard, width), BF16),
            pltpu.VMEM((pieces, heads * shard, width), BF16),
            pltpu.VMEM((pieces, 8, shard), F32),
        ],
        held=[(array, 0) for array in held], deps=deps
    )


def middle_body(
    order_ref, a0, a1, a2, a3, w0, w1, w2, w3, stream_ref, bias_ref, gain_ref, shift_ref, mid_ref, low_ref, all_ref,
):
    _, shard, model = stream_ref.shape
    total = 0.0
    for n, (a, w) in enumerate(((a0, w0), (a1, w1), (a2, w2), (a3, w3))):
        values = a[...].reshape(shard, a.shape[-1])
        total = total + dot(values, w[...])
        all_ref[0, :, n * a.shape[-1] : (n + 1) * a.shape[-1]] = values
    mid = stream_ref[0] + (total + line(bias_ref))
    hat, _ = centre(mid)
    mid_ref[0] = mid
    low_ref[0] = (hat * line(gain_ref) + line(shift_ref)).astype(BF16)


def out_blocks(weight, parts):
    width = weight.shape[0] // parts

    def block(i):
        return pl.BlockSpec((width, weight.shape[1]), lambda g, o: (o[i], 0))

    return [(weight, block(i)) for i in range(parts)]


def middle_norm(start, count, order, attended, weight, stream, vecs, held=()):
    rows, shard, model = stream.shape
    parts = len(attended)
    width = model // parts
    block, one = along((1, shard, model), 0, start), along((1, shard, width))
    first = [along((1, 1, shard, width), 1, start), one, along((1, 1, shard, width), 1), one]
    return call(
        middle_body, "middle", (order,), (count,),
        list(zip(attended, first)) + out_blocks(weight, parts) + [(stream, block)]
        + [(vec, fixed(vec.shape)) for vec in vecs],
        [
            (stream.shape, F32, block),
            ((count, shard, model), BF16, along((1, shard, model))),
            (stream.shape, BF16, block),
        ],
        held=list(zip(held, (0, 2)))
    )


def cot_body(blk_ref, a_ref, b_ref, up_ref, down_ref, g_ref, up_out, down_out, both_ref):
    tokens = a_ref.shape[0]
    down = down_ref[...]

    @pl.when(pl.program_id(0) == 0)
    def _():
        both_ref[0:tokens] = a_ref[...]
        both_ref[tokens:] = b_ref[...]

    g_ref[0:tokens] = dot(a_ref[...], down, 1, 1).astype(BF16)
    g_ref[tokens:] = dot(b_ref[...], down, 1, 1).astype(BF16)
    up_out[...] = up_ref[...]
    down_out[...] = down


def cot_down(blk, own, other, up, down, picked, half):
    tokens, model = own.shape
    steps = half // BLOCK
    column = along((2 * tokens, BLOCK), 1)
    if picked:
        up_at, down_at = along((model, BLOCK), 1), along((BLOCK, model))
    else:
        up_at = pl.BlockSpec((model, BLOCK), lambda g, b: (0, b[g]))
        down_at = pl.BlockSpec((BLOCK, model), lambda g, b: (b[g], 0))
    return call(
        cot_body, "cot_down", (blk,), (steps,),
        [(own, fixed(own.shape)), (other, fixed(own.shape)), (up, up_at), (down, down_at)],
        [
            ((2 * tokens, half), BF16, column),
            ((model, half), BF16, along((model, BLOCK), 1)),
            ((half, model), BF16, along((BLOCK, model))),
            ((2 * tokens, model), BF16, fixed((2 * tokens, model))),
        ]
    )


def hidden_body(blocks, blk_ref, *refs):
    pieces, refs = refs[:-11], refs[-11:]
    g_ref, up_ref, row_ref, bias_ref, act_ref, grad_ref, sum_ref, both_ref, part_ref, other_ref, held = refs
    sizes = [ref.shape[0] * ref.shape[1] for ref in pieces]
    starts = [sum(sizes[:n]) for n in range(len(sizes))]
    step = pl.program_id(0)

    @pl.when(step == 0)
    def _():
        for ref, at, size in zip(pieces, starts, sizes):
            both_ref[at : at + size] = ref[...].reshape(size, ref.shape[2])

    @pl.when(step < blocks)
    def _():
        up = up_ref[...]
        bias = bias_ref[...].astype(F32)
        total = 0.0
        later = dot(pieces[0][...].reshape(sizes[0], -1), up)
        for n, (start, size) in enumerate(zip(starts, sizes)):
            at = slice(start, start + size)
            v = later + bias
            if n + 1 < len(pieces):
                later = dot(pieces[n + 1][...].reshape(sizes[n + 1], -1), up)
            square = v * v
            tanh = jnp.tanh(v * (GELU_A + GELU_B * square))
            gate = 0.5 + 0.5 * tanh
            act = v * gate
            slope = gate + act * ((1.0 - tanh) * (GELU_A + 3.0 * GELU_B * square))
            grad = (slope * g_ref[at].astype(F32)).astype(BF16)
            act_ref[at] = act.astype(BF16)
            grad_ref[at] = grad
            held[step, at] = grad
            total = total + jnp.sum(grad.astype(F32), axis=0, keepdims=True)
        sum_ref[...] = total

    @pl.when(step >= blocks)
    def _():
        grad = jnp.concatenate([held[n] for n in range(blocks)], axis=1)
        found = dot(grad, row_ref[...], 1, 1).astype(BF16)
        part_ref[...] = found[: part_ref.shape[0]]
        other_ref[...] = found[part_ref.shape[0] :]


def hidden_units(blk, pieces, grads, up, bias):
    model = pieces[0].shape[2]
    tokens, half = grads.shape
    blocks, more = half // BLOCK, model // BLOCK

    def first(g):
        return jnp.minimum(g, blocks - 1)

    def second(g):
        return jnp.maximum(g - blocks, 0)

    column = pl.BlockSpec((tokens, BLOCK), lambda g, b: (0, first(g)))
    line = pl.BlockSpec((1, BLOCK), lambda g, b: (0, first(g)))
    return call(
        functools.partial(hidden_body, blocks), "hidden", (blk,), (blocks + more,),
        [(piece, fixed(piece.shape)) for piece in pieces]
        + [
            (grads, column),
            (up, pl.BlockSpec((model, BLOCK), lambda g, b: (0, first(g)))),
            (up, pl.BlockSpec((BLOCK, half), lambda g, b: (second(g), 0))),
            (bias, pl.BlockSpec((1, BLOCK), lambda g, b: (0, b[first(g)]))),
        ],
        [
            (grads.shape, BF16, column),
            (grads.shape, BF16, column),
            ((1, half), F32, line),
            ((tokens, model), BF16, fixed((tokens, model))),
            ((tokens // 2, model), BF16, pl.BlockSpec((tokens // 2, BLOCK), lambda g, b: (0, second(g)))),
            ((tokens // 2, model), BF16, pl.BlockSpec((tokens // 2, BLOCK), lambda g, b: (0, second(g)))),
        ],
        [pltpu.VMEM((blocks, tokens, BLOCK), BF16)]
    )


def sent_body(other_ref, tok_ref, cot_ref, grad_ref, act_ref, up_ref, down_ref):
    up_ref[...] = dot(tok_ref[...], grad_ref[...], 0, 0).astype(BF16)
    down_ref[...] = dot(act_ref[...], cot_ref[...], 0, 0).astype(BF16)


def sent_grads(other, tokens, cot, grad, act, steps):
    count, model = tokens.shape
    half = grad.shape[1]
    size = half // (2 * steps)
    wide = half // steps
    return call(
        sent_body, "sent_grads", (other,), (steps,),
        [
            (tokens, fixed(tokens.shape)),
            (cot, fixed(cot.shape)),
            (grad, along((count, wide), 1)),
            (act, pl.BlockSpec((count, size), lambda g, o: (0, 2 * g + o[0]))),
        ],
        [((model, half), BF16, along((model, wide), 1)), ((half // 2, model), BF16, along((size, model)))],
    )


def feed_body(order_ref, act_ref, down_ref, att_ref, low_ref, half_ref, cot_ref, feed_ref, other_ref, out_ref, keep_ref, kept_ref):
    parts = order_ref.shape[0]
    width = att_ref.shape[1] // parts
    feed = dot(act_ref[...], down_ref[...]).astype(BF16)
    feed_ref[...] = feed[: feed_ref.shape[0]]
    other_ref[...] = feed[feed_ref.shape[0] :]
    kept_ref[...] = dot(half_ref[...], cot_ref[...], 0, 0).astype(BF16)
    grad = dot(att_ref[...], low_ref[...], 0, 0).astype(BF16)
    step, steps = pl.program_id(0), pl.num_programs(0)

    def write(ref):
        for n in range(parts):
            at = pl.multiple_of(order_ref[n] * width, width)
            ref[pl.ds(at, width)] = grad[n * width : (n + 1) * width]

    @pl.when(2 * step < steps)
    def _():
        write(out_ref)

    @pl.when(2 * step >= steps)
    def _():
        write(keep_ref)


def feed_grads(order, act, down, attended, low, cot, c_at, x_at, deps=()):
    tokens, half = act.shape
    own, model = attended.shape
    steps = model // BLOCK
    place = jnp.concatenate([order, jnp.stack([c_at, x_at]).astype(jnp.int32)])
    size = half // (2 * steps)

    def body(place_ref, *refs):
        feed_body(place_ref.at[0 : order.shape[0]], *refs)

    def low_at(g, p):
        c = p[order.shape[0]]
        mine = 2 * g >= steps
        return 0, jnp.where(mine, c * (steps // 2) + g - steps // 2, (1 - c) * (steps // 2) + g)

    return call(
        body, "feed_grads", (place,), (steps,),
        [
            (act, fixed(act.shape)),
            (down, along((half, BLOCK), 1)),
            (attended, fixed(attended.shape)),
            (low, pl.BlockSpec((own, BLOCK), low_at)),
            (act, pl.BlockSpec((tokens, size), lambda g, p: (0, 2 * g + p[order.shape[0] + 1]))),
            (cot, fixed(cot.shape)),
        ],
        [
            ((own, model), BF16, along((own, BLOCK), 1)),
            ((own, model), BF16, along((own, BLOCK), 1)),
            ((model, model // 2), BF16, pl.BlockSpec((model, BLOCK), lambda g, p: (0, jnp.minimum(g, steps // 2 - 1)))),
            ((model, model // 2), BF16, pl.BlockSpec((model, BLOCK), lambda g, p: (0, jnp.maximum(g - steps // 2, 0)))),
            ((half // 2, model), BF16, along((size, model))),
        ],
        deps=deps,
    )


def middle_back_body(
    order_ref, part_ref, sent_ref, mid_ref, cot_ref, gain_ref, w0, w1, w2, w3,
    grad_ref, low_ref, att0_ref, att1_ref, far_ref, sums_ref,
):
    grad = part_ref[...].astype(F32) + sent_ref[...].astype(F32)
    hat, inverse = centre(mid_ref[0])
    cot = cot_ref[0].astype(F32)
    total = cot + norm_back(grad, line(gain_ref), hat, inverse)
    low = total.astype(BF16)
    grad_ref[0] = total
    low_ref[0] = low
    far_ref[0, 0] = dot(low, w2[...], 1, 1).astype(BF16)
    far_ref[1, 0] = dot(low, w3[...], 1, 1).astype(BF16)
    att1_ref[0] = dot(low, w1[...], 1, 1).astype(BF16)
    att0_ref[0] = dot(low, w0[...], 1, 1).astype(BF16)

    @pl.when(pl.program_id(0) == 0)
    def _():
        sums_ref[...] = jnp.zeros_like(sums_ref)

    sums_ref[0:1] += jnp.sum(grad * hat, axis=0, keepdims=True)
    sums_ref[1:2] += jnp.sum(grad, axis=0, keepdims=True)
    sums_ref[2:3] += jnp.sum(low.astype(F32), axis=0, keepdims=True)
    sums_ref[3:4] += jnp.sum(cot, axis=0, keepdims=True)


def middle_back(order, both, sent, mid, cot, gain, weight, parts, deps=()):
    rows, shard, model = mid.shape
    width = model // parts
    block, one = along((1, shard, model)), along((1, shard, width))
    flat = pl.BlockSpec((shard, model), lambda g, o: (g, 0))
    return call(
        middle_back_body, "middle_back", (order,), (rows,),
        [(both, flat), (sent, flat), (mid, block), (cot, block), (gain, fixed(gain.shape))] + out_blocks(weight, parts),
        [
            (mid.shape, F32, block),
            (mid.shape, BF16, block),
            ((rows, shard, width), BF16, one),
            ((rows, shard, width), BF16, one),
            ((2, rows, shard, width), BF16, along((2, 1, shard, width), 1)),
            ((8, model), F32, fixed((8, model))),
        ],
        deps=deps
    )


def norm1_back_body(start, part_ref, near_ref, far_ref, stream_ref, mid_ref, gain_ref, seg_ref, in_ref, shift_ref, sums_ref):
    grad = part_ref[0].astype(F32) + near_ref[0].astype(F32) + far_ref[0].astype(F32)
    hat, inverse = centre(stream_ref[0])
    total = mid_ref[0] + norm_back(grad, line(gain_ref), hat, inverse)
    in_ref[0] = total.astype(BF16)
    seg = seg_ref[pl.ds(pl.program_id(0) + start, 1)]
    slots = lax.broadcasted_iota(jnp.int32, (SEGS, seg.shape[-1]), 0) == seg
    onehot = slots.astype(F32).astype(BF16)
    shift_ref[0] = dot(jnp.concatenate([onehot, onehot], axis=1), split_low(total))

    @pl.when(pl.program_id(0) == 0)
    def _():
        sums_ref[...] = jnp.zeros_like(sums_ref)

    sums_ref[0:1] += jnp.sum(grad * hat, axis=0, keepdims=True)
    sums_ref[1:2] += jnp.sum(grad, axis=0, keepdims=True)


def norm1_back(start, count, own, near, far, stream, mid, gain, seg, held=(), deps=()):
    rows, shard, model = stream.shape
    block, own_block = along((1, shard, model), 0, start), along((1, shard, model))
    return call(
        functools.partial(norm1_back_body, start), "norm1_back", (), (count,),
        [(own, own_block), (near, own_block), (far, own_block), (stream, block), (mid, block), (gain, fixed(gain.shape))]
        + [(seg, fixed(seg.shape))],
        [
            (stream.shape, BF16, block),
            ((count, SEGS, model), F32, along((1, SEGS, model))),
            ((8, model), F32, fixed((8, model))),
        ],
        held=[(array, 0) for array in held], deps=deps
    )


def exchange(own, one, far):
    return [own, swap(one, "c"), far, swap(far[1], "c")]


def tie(*values):
    return lax.optimization_barrier(values)


def cut(values, index, size, axis):
    return lax.dynamic_slice_in_dim(values, index * size, size, axis)


def add_low(kept, sent):
    return (kept.astype(F32) + sent.astype(F32)).astype(BF16)


def ordered(at, own, other, axis):
    return jnp.where(at == 0, jnp.concatenate([own, other], axis), jnp.concatenate([other, own], axis))


def finish_body(blocks, at_ref, d0, d1, u0, u1, l0, l1, down_ref, up_ref, qkv_ref, out_ref):
    c_at = at_ref[0]
    width = up_ref.shape[1] // (4 * blocks)
    size = d0.shape[0]
    for c in range(2):
        mine = c_at == c
        down_ref[c * size : (c + 1) * size] = jnp.where(mine, d0[...], d1[...]).astype(F32)
        up = jnp.where(mine, u0[...], u1[...]).astype(F32)
        for b in range(2 * blocks):
            up_ref[:, (2 * b + c) * width : (2 * b + c + 1) * width] = up[:, b * width : (b + 1) * width]
        late = jnp.where(mine, l0[...], l1[...]).astype(F32)
        half = out_ref.shape[1] // 2
        wide = half // 2
        out_ref[:, c * half : (c + 1) * half] = late[:, 6 * wide :]
        for y in range(2):
            for n in range(3):
                at = n * 4 * wide + (2 * y + c) * wide
                qkv_ref[:, at : at + wide] = late[:, (3 * y + n) * wide : (3 * y + n + 1) * wide]


def finish(c_at, dp, piece, down, up, late, parts):
    rows, model = late[0].shape[0], down[0].shape[1]
    depth, size = dp // 2, down[0].shape[0]
    if piece % 128 == 0:
        at = c_at.astype(jnp.int32)[None]
        shapes = [(2 * size, model), (rows, 2 * dp * piece), (rows, 3 * model), (rows, model)]
        arrays = list(down) + list(up) + list(late)
        return call(
            functools.partial(finish_body, depth), "finish", (at,), (1,),
            [(array, fixed(array.shape)) for array in arrays], [(shape, F32, fixed(shape)) for shape in shapes],
        )
    down_done = ordered(c_at, *down, 0).astype(F32)
    up_done = ordered(c_at, up[0][None], up[1][None], 0).reshape(2, rows, dp, piece).transpose(1, 2, 0, 3)
    up_done = up_done.reshape(rows, 2 * dp * piece).astype(F32)
    both = ordered(c_at, late[0][None], late[1][None], 0)
    width = model // parts
    qkv_done = both[:, :, : 6 * width].reshape(2, rows, 2, 3, width).transpose(1, 3, 2, 0, 4)
    qkv_done = qkv_done.reshape(rows, 3 * model).astype(F32)
    out_done = jnp.concatenate([both[0, :, 6 * width :], both[1, :, 6 * width :]], axis=1).astype(F32)
    return down_done, up_done, qkv_done, out_done


def local(
    inputs, segment_ids, doc_times, time_weight, time_bias, norm1_gain, norm1_bias, qkv_weight, qkv_bias,
    out_weight, out_bias, norm2_gain, norm2_bias, up_weight, up_bias, down_weight, down_bias, cotangent,
    *, dp,
):
    rows, shard, model = inputs.shape
    parts = 4
    tokens = rows * shard
    hidden_width = up_weight.shape[1]
    width = model // parts
    depth = dp // 2
    half = hidden_width // 2
    piece = half // dp
    z_at, x_at, y_at, c_at = (lax.axis_index(name) for name in ("z", "x", "y", "c"))
    me = 2 * y_at + c_at

    groups = [(0, rows - 1), (rows - 1, 1)] if rows > 1 else [(0, 1)]
    seg_one, seg_two = swap(segment_ids, "c"), swap(segment_ids, "y")
    seg_three = swap(seg_two, "c")
    features = time_features(doc_times.reshape(rows * SEGS), jnp.arange(TEMB), TEMB // 2)
    time_shift = dot(features, time_weight).reshape(rows, SEGS, model)
    own1, one1, two1, stream = [], [], [], None
    for start, count in groups:
        held = () if stream is None else (stream,)
        stream, low = norm1(
            start, count, inputs, segment_ids, time_shift, (time_bias, norm1_gain, norm1_bias), held
        )
        if stream is not None and not own1:
            low, seg_one, seg_two, seg_three = tie(low, seg_one, seg_two, seg_three)
        own1.append(low)
        two1.append(swap(low, "y"))
        one1.append(swap(low, "c"))
    segs = jnp.stack([segment_ids, seg_one, seg_two, seg_three], axis=1)

    me, x_at, z_at, c_at, y_at, own1[-1], segs = tie(me, x_at, z_at, c_at, y_at, own1[-1], segs)
    order = [me ^ i for i in range(parts)]
    order_list = jnp.stack(order).astype(jnp.int32)
    me_list = order_list[:1]
    low_id, high_id = segs.min(axis=2), segs.max(axis=2)
    act = (low_id[:, :, None] <= high_id[:, None, :]) & (low_id[:, None, :] <= high_id[:, :, None])
    places = jnp.arange(parts, dtype=jnp.int32)
    rank = jnp.cumsum(act.astype(jnp.int32), axis=2) - 1
    chosen = act[..., None] & (rank[..., None] == places)
    idx = jnp.sum(jnp.where(chosen, places[:, None], 0), axis=2).astype(jnp.int32).reshape(-1)
    cnt = jnp.sum(act.astype(jnp.int32), axis=2).reshape(-1)
    positions = jnp.stack([o * shard + jnp.arange(shard, dtype=jnp.int32) for o in order])
    cos_tab, sin_tab = rotary_tables(positions, HEAD_DIM)

    cot = cotangent.reshape(tokens, model)
    cot_other = swap(cot, "c")
    if piece % BLOCK == 0:
        blk = (jnp.arange(dp)[:, None] * 2 + c_at) * (piece // BLOCK) + jnp.arange(piece // BLOCK)
        blk = blk.reshape(-1).astype(jnp.int32)
        up_from, down_from = up_weight, down_weight
    else:
        blk = jnp.zeros((half // BLOCK,), jnp.int32)
        up_from = lax.dynamic_index_in_dim(up_weight.reshape(model, dp, 2, piece), c_at, 2, keepdims=False)
        down_from = lax.dynamic_index_in_dim(down_weight.reshape(dp, 2, piece, model), c_at, 1, keepdims=False)
        up_from, down_from = up_from.reshape(model, half), down_from.reshape(half, model)
    grad_act, up_own, down_own, cot_both = cot_down(
        blk, cot, cot_other, up_from, down_from, piece % BLOCK != 0, half
    )
    up_bias_own, bias_blk = up_bias.reshape(1, hidden_width), blk
    if piece % BLOCK:
        up_bias_own = lax.dynamic_index_in_dim(up_bias.reshape(dp, 2, piece), c_at, 1, keepdims=False)
        up_bias_own, bias_blk = up_bias_own.reshape(1, half), jnp.arange(half // BLOCK, dtype=jnp.int32)

    qkv_line = qkv_bias.reshape(1, 3 * model)
    near = (own1, one1)
    qkv, qkv_own = project_qkv(
        0, 0, parts, rows, me_list, near, qkv_weight, qkv_line, cos_tab, sin_tab, (), (grad_act, cnt, idx)
    )
    o, lse, attended, three1 = None, None, [], []
    for n, (start, count) in enumerate(groups):
        if n == 0:
            two1[0], qkv = tie(two1[0], qkv)
        else:
            two1[n], o = tie(two1[n], o)
        three1.append(swap(two1[n], "c"))
        (qkv,) = project_qkv(
            1, start, parts, rows, me_list, ([two1[n]], [three1[n]]), qkv_weight, qkv_line, cos_tab, sin_tab, (qkv,),
            () if o is None else (o,),
        )
        held = () if o is None else (o, lse)
        o, out_one, out_far, lse = attend(start, count, cnt, idx, qkv, segs, held)
        attended.append((out_one, swap(out_far, "y")))
    held, normed2, normed2_other = (), [], []
    for (start, count), values in zip(groups, attended):
        far, o = tie(values[1], o)
        values = exchange(o, values[0], far)
        middle, low, attended_all = middle_norm(
            start, count, order_list, values, out_weight, stream, (out_bias, norm2_gain, norm2_bias), held
        )
        held = (middle, attended_all)
        normed2.append(low)
        normed2_other.append(swap(low, "c"))

    active, grad_hidden, up_b, normed2_both, part2, part2_other = hidden_units(
        bias_blk, normed2 + normed2_other, grad_act, up_own, up_bias_own
    )
    part2_sent = swap(part2_other, "c")
    grad_middle, grad_middle_low, att0, att1, far, sums2 = middle_back(
        order_list, part2, part2_sent, middle, cotangent, norm2_gain, out_weight, parts
    )
    far = swap(far, "y")
    sums2 = sums2[:4]

    active, grad_hidden, att0 = tie(active, grad_hidden, att0)
    up_rows = model // dp
    small_blocks = piece % BLOCK != 0 or depth != model // BLOCK
    if small_blocks:
        up_grad = dot(normed2_both, grad_hidden, 0, 0).astype(BF16)
        down_out = dot(active, cot_both, 0, 0).astype(BF16).reshape(depth, 2, piece, model)
        down_kept = lax.dynamic_index_in_dim(down_out, x_at, 1, keepdims=False).reshape(half // 2, model)
        down_out = lax.dynamic_index_in_dim(down_out, 1 - x_at, 1, keepdims=False).reshape(half // 2, model)
    else:
        up_grad, down_out = sent_grads(
            1 - x_at[None].astype(jnp.int32), normed2_both, cot_both, grad_hidden, active, depth
        )
    up_grad, down_out, far = tie(up_grad, down_out, far)
    up_z = lax.psum_scatter(up_grad, "z", scatter_dimension=0, tiled=True)
    down_sent = swap(down_out[: half // 4], "x")
    if small_blocks:
        feed = dot(active, down_own).astype(BF16)
        feed, feed_other = feed[:tokens], feed[tokens:]
        out_grad = dot(attended_all.reshape(tokens, model), grad_middle_low.reshape(tokens, model), 0, 0).astype(BF16)
        out_grad = jnp.concatenate([cut(out_grad, o_at, width, 0) for o_at in order], axis=0)
        out_sent, out_grad = (cut(out_grad, at, model // 2, 1) for at in (1 - c_at, c_at))
    else:
        feed, feed_other, out_sent, out_grad, down_kept = feed_grads(
            order_list, active, down_own, attended_all.reshape(tokens, model), grad_middle_low.reshape(tokens, model),
            cot_both, c_at, x_at, (far, down_out),
        )
    feed, feed_other, out_sent, out_grad, down_kept, down_sent, down_out = tie(
        feed, feed_other, out_sent, out_grad, down_kept, down_sent, down_out
    )
    down_late = swap(down_out[half // 4 :], "x")
    out_sent, feed_sent = swap(out_sent, "c"), swap(feed_other, "c")
    grad_o = exchange(att0, att1, far)

    back = []
    (start, count), rest = groups[0], groups[1:]
    found = attend_back(start, count, cnt, idx, qkv, o, grad_o, lse, segs, cos_tab, sin_tab, qkv_own)
    *found, down_late, out_sent, feed_sent = tie(*found, down_late, out_sent, feed_sent)
    grad_qkv, own, one, two, three = found
    there = add_low(two, swap(three, "c"))
    down_x = add_low(down_kept, jnp.concatenate([down_sent, down_late], axis=0))
    down_z = lax.psum_scatter(down_x, "z", scatter_dimension=0, tiled=True)
    out_c = add_low(out_grad, out_sent).reshape(depth, 2 * up_rows, model // 2)
    out_sent = cut(out_c, 1 - x_at, up_rows, 1)
    there, down_x, out_sent = tie(there, down_x, out_sent)
    far, near = swap(there, "y"), swap(one, "c")
    out_sent = swap(out_sent, "x")
    if rest:
        (start, count), = rest
        found = attend_back(
            start, count, cnt, idx, qkv, o, grad_o, lse, segs, cos_tab, sin_tab, qkv_own, (grad_qkv,),
            (there, down_x),
        )
        *found, far, up_z, out_sent = tie(*found, far, up_z, out_sent)
        back.append((own, near, far))
        grad_qkv, own, one, two, three = found
        there, far = tie(add_low(two, swap(three, "c")), far)
        far, near = swap(there, "y"), swap(one, "c")
        grad_qkv, there = tie(grad_qkv, there)
    qkv_out, qkv_kept, qkv_b = qkv_grads(x_at, [own1, one1, two1, three1], grad_qkv, depth)
    qkv_out, qkv_kept, far, out_sent, out_c, up_z = tie(qkv_out, qkv_kept, far, out_sent, out_c, up_z)
    back.append((own, near, far))
    qkv_sent = swap(qkv_out, "x")
    out_x = add_low(cut(out_c, x_at, up_rows, 1), out_sent)
    out_sent = cut(out_x, 1 - y_at, width, 2)
    qkv_out, up_out = tie(qkv_out, cut(up_z, 1 - x_at, up_rows, 0))
    up_sent = swap(up_out, "x")
    held, grad_shift, sums1 = (), [], 0.0
    for (start, count), values in zip(groups, back):
        input_grad, found, sums = norm1_back(
            start, count, *values, stream, grad_middle, norm1_gain, segment_ids, held, (qkv_kept, up_out)
        )
        if not held:
            input_grad, out_sent = tie(input_grad, out_sent)
            out_sent = swap(out_sent, "y")
        held = (input_grad,)
        grad_shift.append(found.reshape(count * SEGS, model))
        sums1 = sums1 + sums[:2]

    up_b = up_b.reshape(dp, 1, piece)
    up_b = jnp.where(jnp.arange(2)[:, None] == c_at, up_b, 0.0).reshape(-1, model)
    qkv_b = jnp.where(jnp.arange(parts)[:, None] == me, qkv_b.reshape(3, 1, width), 0.0).reshape(3, model)
    times = doc_times.reshape(1, rows * SEGS)
    times = jnp.concatenate([times // 32, times % 32], axis=1).astype(F32)
    times = jnp.tile(jnp.pad(times, ((0, 0), (0, width - times.shape[1]))), (1, parts))
    small = jnp.concatenate(grad_shift + [sums1, sums2, qkv_b, up_b, times], axis=0).astype(BF16)
    small_sent = swap(cut(small, 1 - c_at, 2 * width, 1), "c")
    small = add_low(cut(small, c_at, 2 * width, 1), small_sent)
    small, qkv_sent, out_sent = tie(small, qkv_sent, out_sent)
    small = add_low(cut(small, y_at, width, 1), swap(cut(small, 1 - y_at, width, 1), "y"))
    small = ordered(x_at, small[None], swap(small, "x")[None], 0)
    out_x = add_low(cut(out_x, y_at, width, 2), out_sent)
    late = jnp.concatenate([add_low(qkv_kept, qkv_sent), out_x], axis=2)
    output = middle.reshape(tokens, model) + (feed.astype(F32) + feed_sent.astype(F32) + down_bias.astype(F32))
    output = output.astype(BF16).reshape(rows, shard, model)
    small, late = tie(small, late)
    if depth == 4:
        flat = small.reshape(2 * small.shape[1] * width // model, model)
        parts_z = [lax.dynamic_index_in_dim(late, z_at ^ n, 0, keepdims=False) for n in range(depth)]
        sent = [
            lax.ppermute(jnp.concatenate([parts_z[n], flat], axis=0), "z", [(i, i ^ n) for i in range(depth)])
            for n in range(1, depth)
        ]
        small, down_z, up_z, up_sent = tie(small, down_z, up_z, up_sent)
        up_x = add_low(cut(up_z, x_at, up_rows, 0), up_sent)
        down_sent, up_sent = swap(down_z, "y"), swap(up_x, "y")
        *sent, output, down_sent, up_sent = tie(*sent, output, down_sent, up_sent)
        late = sum(part[:up_rows].astype(F32) for part in sent) + parts_z[0].astype(F32)
        late = late.astype(BF16)
        small = jnp.stack([small] + [part[up_rows:].reshape(small.shape) for part in sent])
        small = jnp.stack([lax.dynamic_index_in_dim(small, z_at ^ n, 0, keepdims=False) for n in range(depth)])
    else:
        up_x = add_low(cut(up_z, x_at, up_rows, 0), up_sent)
        down_sent, up_sent = swap(down_z, "y"), swap(up_x, "y")
        late = lax.psum_scatter(late, "z", scatter_dimension=0, tiled=False)
        small = lax.all_gather(small, "z")
    small = small.reshape(dp, small.shape[2], width)

    late_sent = swap(late, "y")
    down_done, up_done = add_low(down_z, down_sent), add_low(up_x, up_sent)
    down_other, up_other = swap(down_done, "c"), swap(up_done, "c")
    both = ordered(y_at, late[None], late_sent[None], 0)
    late = jnp.concatenate([both[0, :, : 3 * width], both[1, :, : 3 * width], both[0, :, 3 * width :], both[1, :, 3 * width :]], axis=1)
    late_other = swap(late, "c")

    down_done, up_done, qkv_done, out_done = finish(
        c_at, dp, piece, (down_done, down_other), (up_done, up_other), (late, late_other), parts
    )

    dp_at = 2 * z_at + x_at
    all_times = small[:, -1, : 2 * rows * SEGS].astype(F32) * 0.25
    all_times = all_times[:, : rows * SEGS] * 32.0 + all_times[:, rows * SEGS :]
    shifts = small[:, : rows * SEGS].reshape(dp * rows * SEGS, width)
    columns = dp_at * (TEMB // dp) + jnp.arange(TEMB // dp)
    wanted = time_features(all_times.reshape(-1), columns, TEMB // 2)
    sums = jnp.sum(small[:, rows * SEGS : -1].astype(F32), axis=0)
    full = [dot(wanted, shifts, 0, 0), sums, jnp.sum(shifts.astype(F32), axis=0, keepdims=True)]
    full = jnp.concatenate(full, axis=0).astype(BF16)
    count = full.shape[0]
    full = jnp.pad(full, ((0, -count % 16), (0, 0)))
    full = ordered(y_at, full[None], swap(full, "y")[None], 0)
    full = ordered(c_at, full[None], swap(full, "c")[None], 0)
    full = full.transpose(2, 0, 1, 3).reshape(-1, model).astype(F32)
    time_w_done, sums = full[: TEMB // dp], full[TEMB // dp : count]

    def share(vector):
        return cut(vector.reshape(-1), dp_at, vector.size // dp, 0)

    return (
        output, input_grad, time_w_done, share(sums[-1]), share(sums[0]), share(sums[1]), qkv_done, share(sums[6:9]),
        out_done, share(sums[4]), share(sums[2]), share(sums[3]), up_done, share(sums[9:-1]), down_done, share(sums[5]),
    )


def solution(mesh):
    dp, seq = mesh.shape["dp"], mesh.shape["seq"]
    fine = Mesh(mesh.devices.reshape(dp // 2, 2, seq // 2, 2), ("z", "x", "y", "c"))
    rows, seqs = ("z", "x"), ("y", "c")
    placed = (P(rows, seqs, None), P(rows, seqs), P(rows, None)) + (P(),) * 14 + (P(rows, seqs, None),)
    vec, mat = P(rows), P(rows, None)
    return jax.shard_map(
        functools.partial(local, dp=dp),
        mesh=fine,
        in_specs=placed,
        out_specs=(
            P(rows, seqs, None), P(rows, seqs, None), mat, vec, vec, vec, mat, vec, mat, vec, vec, vec, mat, vec, mat, vec,
        ),
        check_vma=False,
    )
```

```python
import functools
import math

import jax
import jax.numpy as jnp
from jax import lax
from jax.experimental import pallas as pl
from jax.experimental.pallas import tpu as pltpu
from jax.sharding import Mesh, PartitionSpec as P

HEADS = 16
HEAD_DIM = 64
TEMB = 256
SEGS = 8
EPSILON = 1e-05
F32 = jnp.float32
BF16 = jnp.bfloat16
NEG = -1e30
LOG2E = math.log2(math.e)
GELU_A = math.sqrt(2.0 / math.pi)
GELU_B = GELU_A * 0.044715
BLOCK = 256
VMEM = 60 * 1024 * 1024


def swap(value, axis):
    return lax.ppermute(value, axis, [(0, 1), (1, 0)])


def time_features(doc_times, column, half_size):
    frequency = jnp.exp(-math.log(10000.0) * (column % half_size).astype(F32) / half_size)
    angles = doc_times.astype(F32)[..., None] * frequency
    return jnp.where(column < half_size, jnp.sin(angles), jnp.cos(angles)).astype(BF16)


def rotary_tables(positions, head_size):
    half_size = head_size // 2
    frequency = jnp.exp(-math.log(10000.0) * 2.0 * jnp.arange(half_size, dtype=F32) / head_size)
    angles = positions.astype(F32)[..., None] * frequency
    cos_tab, sin_tab = jnp.cos(angles), jnp.sin(angles)
    return (
        jnp.concatenate([cos_tab] * 4, axis=-1),
        jnp.concatenate([-sin_tab, sin_tab, -sin_tab, sin_tab], axis=-1),
    )


def dot(left_op, right_op, left_dim=1, right_dim=0):
    return lax.dot_general(
        left_op, right_op, (((left_dim,), (right_dim,)), ((), ())), preferred_element_type=F32
    )


def turn(values, cos_tab, sin_tab):
    slabs = []
    lane = lax.broadcasted_iota(jnp.int32, (values.shape[0], 128), 1)
    first = lane % HEAD_DIM < HEAD_DIM // 2
    for start in range(0, values.shape[1], 128):
        slab = values[:, start : start + 128]
        partner = jnp.where(
            first, pltpu.roll(slab, 128 - HEAD_DIM // 2, 1), pltpu.roll(slab, HEAD_DIM // 2, 1)
        )
        slabs.append(slab * cos_tab + partner * sin_tab)
    return jnp.concatenate(slabs, axis=1)


def split_low(values):
    high = values.astype(BF16)
    return jnp.concatenate([high, (values - high.astype(F32)).astype(BF16)], axis=0)


def centre(values):
    scale = 1.0 / values.shape[-1]
    centred = values - jnp.sum(values, axis=-1, keepdims=True) * scale
    spread = jnp.sum(centred * centred, axis=-1, keepdims=True) * scale
    inverse = lax.rsqrt(spread + EPSILON)
    return centred * inverse, inverse


def norm_back(grad, gain, hat, inverse):
    scale = 1.0 / grad.shape[-1]
    scaled = grad * gain
    mean = jnp.sum(scaled, axis=-1, keepdims=True) * scale
    along = jnp.sum(scaled * hat, axis=-1, keepdims=True) * scale
    return inverse * (scaled - mean - hat * along)


def call(body, name, prefetch, grid, ins, outs, scratch=(), deps=(), held=()):
    count = len(prefetch) + len(ins)
    extra = [array for array, _ in held] + list(deps)

    def kernel(*refs):
        body(*refs[:count], *refs[count + len(extra) :])

    return pl.pallas_call(
        kernel,
        grid_spec=pltpu.PrefetchScalarGridSpec(
            num_scalar_prefetch=len(prefetch),
            grid=grid,
            in_specs=[spec for _, spec in ins] + [pl.BlockSpec(memory_space=pl.ANY)] * len(extra),
            out_specs=[spec for _, _, spec in outs],
            scratch_shapes=list(scratch),
        ),
        out_shape=[jax.ShapeDtypeStruct(shape, kind) for shape, kind, _ in outs],
        input_output_aliases={count + n: out for n, (_, out) in enumerate(held)},
        compiler_params=pltpu.CompilerParams(vmem_limit_bytes=VMEM),
        name=name,
    )(*prefetch, *[array for array, _ in ins], *extra)


def line(ref):
    return ref[...].astype(F32).reshape(1, -1)


def fixed(shape):
    return pl.BlockSpec(shape, lambda *_: (0,) * len(shape))


def along(shape, axis=0, start=0):
    return pl.BlockSpec(shape, lambda g, *_: tuple(start + g if n == axis else 0 for n in range(len(shape))))


def norm1_body(start, x_ref, seg_ref, shift_ref, time_ref, gain_ref, bias_ref, stream_ref, low_ref):
    seg = seg_ref[pl.ds(pl.program_id(0) + start, 1)]
    slots = lax.broadcasted_iota(jnp.int32, (SEGS, seg.shape[-1]), 0) == seg
    onehot = slots.astype(F32).astype(BF16)
    shift = shift_ref[0] + line(time_ref)
    added = dot(jnp.concatenate([onehot, onehot], axis=0), split_low(shift), 0, 0)
    stream = x_ref[0].astype(F32) + added
    hat, _ = centre(stream)
    stream_ref[0] = stream
    low_ref[0] = (hat * line(gain_ref) + line(bias_ref)).astype(BF16)


def norm1(start, count, x, seg, shift, vecs, held=()):
    rows, shard, model = x.shape
    block = along((1, shard, model), 0, start)
    return call(
        functools.partial(norm1_body, start), "norm1", (), (count,),
        [(x, block), (seg, fixed(seg.shape)), (shift, along((1, SEGS, model), 0, start))]
        + [(vec, fixed(vec.shape)) for vec in vecs],
        [(x.shape, F32, block), ((count, shard, model), BF16, along((1, shard, model)))],
        held=[(array, 0) for array in held],
    )


def qkv_body(sizes, me_ref, *refs):
    count = 2 * len(sizes)
    pieces, (w_ref, bias_ref, cos_ref, sin_ref, out_ref), own = refs[:count], refs[count : count + 5], refs[count + 5 :]
    places = [(n, sum(sizes[:g]) + r, n * len(sizes) + g, r) for n in range(2) for g, size in enumerate(sizes) for r in range(size)]
    step = pl.program_id(0)

    def run(turned):
        w = w_ref[...]
        bias = bias_ref[...].astype(F32)
        later = dot(pieces[0][0], w)
        for at, (n, r, _, _) in enumerate(places):
            values = later + bias
            if at + 1 < len(places):
                later = dot(pieces[places[at + 1][2]][places[at + 1][3]], w)
            if turned:
                values = turn(values, cos_ref[n], sin_ref[n]) * jnp.where(step == 0, LOG2E * HEAD_DIM**-0.5, 1.0)
            out_ref[0, n, r] = values.astype(BF16)

    for ref in own:
        ref[...] = w_ref[...].T

    @pl.when(step < 2)
    def _():
        run(True)

    @pl.when(step == 2)
    def _():
        run(False)


def project_qkv(pair, start, parts, rows, me, pieces, weight, bias, cos_tab, sin_tab, held=(), deps=()):
    _, shard, model = pieces[0][0].shape
    sizes = [piece.shape[0] for piece in pieces[0]]
    count = sum(sizes)
    width = model // parts
    place = pl.BlockSpec((1, 2, count, shard, width), lambda g, m: (g, pair, start // count, 0, 0))
    outs = [((3, parts, rows, shard, width), BF16, place)]
    if not held:
        outs.append(((3 * width, model), BF16, along((width, model))))
    return call(
        functools.partial(qkv_body, sizes), "qkv", (me,), (3,),
        [(piece, fixed(piece.shape)) for group in pieces for piece in group]
        + [
            (weight, pl.BlockSpec((model, width), lambda g, m: (0, g * parts + m[0]))),
            (bias, pl.BlockSpec((1, width), lambda g, m: (0, g * parts + m[0]))),
            (cos_tab, pl.BlockSpec((2, shard, 128), lambda g, m: (pair, 0, 0))),
            (sin_tab, pl.BlockSpec((2, shard, 128), lambda g, m: (pair, 0, 0))),
        ],
        outs, held=[(array, n) for n, array in enumerate(held)], deps=deps,
    )


def qkv_grads(x_at, pieces, grad, blocks, deps=()):
    shard, model = pieces[0][0].shape[1:]
    parts, rows, _, columns = grad.shape
    size = model // (2 * blocks)
    flat = [(n, piece) for n, group in enumerate(pieces) for piece in group]

    def body(at_ref, *refs):
        g_ref, out_ref, keep_ref, sum_ref = refs[len(flat) :]
        total, sums, start = 0.0, 0.0, [0] * parts
        for (n, piece), x_ref in zip(flat, refs):
            count = piece.shape[0]
            g = g_ref[n, start[n] : start[n] + count].reshape(count * shard, g_ref.shape[3])
            start[n] += count
            total = total + dot(x_ref[...].reshape(count * shard, model), g, 0, 0)
            sums = sums + jnp.sum(g.astype(F32), axis=0, keepdims=True)
        low = total.astype(BF16)
        for x in range(2):
            for b in range(blocks):
                values = low[(2 * b + x) * size : (2 * b + x + 1) * size]

                @pl.when(at_ref[0] == x)
                def _():
                    keep_ref[b] = values

                @pl.when(at_ref[0] != x)
                def _():
                    out_ref[b] = values

        sum_ref[...] = sums

    block = along((blocks, size, BLOCK), 2)
    shape = (blocks, size, columns)
    return call(
        body, "qkv_grads", (x_at.astype(jnp.int32)[None],), (columns // BLOCK,),
        [(x, fixed(x.shape)) for _, x in flat] + [(grad, along((parts, rows, shard, BLOCK), 3))],
        [(shape, BF16, block), (shape, BF16, block), ((1, columns), F32, along((1, BLOCK), 1))],
        deps=deps,
    )


def seg_columns(segq_all, segk):
    pieces, shard, _ = segk.shape
    for j in range(pieces):
        row = jnp.broadcast_to(segq_all[j:j+1].astype(F32), (128, shard))
        segk[j] = row.T

def attend_body(start, cnt_ref, idx_ref, qkv_ref, seg_ref, o_ref, one_ref, far_ref, lse_ref, vt, segk, qmt, acc):
    row = pl.program_id(0) + start
    _, pieces, _, shard, width = qkv_ref.shape
    heads = width // HEAD_DIM

    @pl.when(pl.program_id(0) == 0)
    def _():
        qmt[...] = jnp.zeros_like(qmt)

    for j in range(pieces):
        vt[j] = qkv_ref[2, j, 0].T
        qt = qkv_ref[0, j, 0].T
        for h in range(heads):
            at = slice(h * HEAD_DIM, (h + 1) * HEAD_DIM)
            qmt[j, at, h * shard : (h + 1) * shard] = qt[at]
    seg_columns(seg_ref[0], segk)

    @pl.loop(0, pieces)
    def _(piece):
        attend_piece(row * pieces + piece, piece, cnt_ref, idx_ref, qkv_ref.at[1], seg_ref, lse_ref, vt, segk, qmt, acc)

    for j in range(pieces):
        o_ref[j, 0] = acc[j].T.astype(BF16)
    one_ref[0] = o_ref[1, 0]
    far_ref[:, 0] = o_ref[2:, 0]


def attend_piece(at_q, piece, cnt_ref, idx_ref, k_ref, seg_ref, lse_ref, vt, segk, qmt, acc):
    pieces, _, shard, width = k_ref.shape
    heads = width // HEAD_DIM
    seg_q = seg_ref[0, pl.ds(piece, 1)].astype(F32)

    def run(count):
        @pl.when(cnt_ref[at_q] == count)
        def _():
            qm = qmt[piece]
            places = [idx_ref[at_q * pieces + t] for t in range(count)]
            top, tot, out = [None] * heads, [None] * heads, [None] * heads
            later = dot(k_ref[places[0], 0], qm)
            for t in range(count):
                s = later
                if t + 1 < count:
                    later = dot(k_ref[places[t + 1], 0], qm)
                col = segk[places[t]]
                same = jnp.concatenate([col] * (shard // 128), axis=1) == seg_q
                for h in range(heads):
                    at = slice(h * HEAD_DIM, (h + 1) * HEAD_DIM)
                    sh = jnp.where(same, s[:, h * shard : (h + 1) * shard], NEG)
                    best = jnp.max(sh, axis=0, keepdims=True)
                    if t:
                        best = jnp.maximum(top[h], best)
                        fade = jnp.exp2(top[h] - best)
                    p = jnp.exp2(sh - best)
                    values = jnp.concatenate([vt[places[t], at], jnp.ones((16, shard), BF16)], axis=0)
                    found = dot(values, p.astype(BF16))
                    total, found = found[HEAD_DIM : HEAD_DIM + 1], found[:HEAD_DIM]
                    if t:
                        total = tot[h] * fade + total
                        found = out[h] * fade + found
                    top[h], tot[h], out[h] = best, total, found
            for h in range(heads):
                acc[piece, h * HEAD_DIM : (h + 1) * HEAD_DIM] = out[h] / tot[h]
                lse_ref[0, piece, h : h + 1] = top[h] + jnp.log2(tot[h])

    for count in range(1, pieces + 1):
        run(count)


def attend(start, count, cnt, idx, qkv, seg, held=()):
    _, pieces, rows, shard, width = qkv.shape
    heads = width // HEAD_DIM
    pairs = count * (pieces * shard) ** 2
    return call(
        functools.partial(attend_body, start), "attend", (cnt, idx), (count,),
        [(qkv, along((3, pieces, 1, shard, width), 2, start)), (seg, along((1, pieces, shard), 0, start))],
        [
            ((pieces, rows, shard, width), BF16, along((pieces, 1, shard, width), 1, start)),
            ((count, shard, width), BF16, along((1, shard, width))),
            ((2, count, shard, width), BF16, along((2, 1, shard, width), 1)),
            ((rows, pieces, 8, shard), F32, along((1, pieces, 8, shard), 0, start)),
        ],
        [
            pltpu.VMEM((pieces, width, shard), BF16),
            pltpu.VMEM((pieces, shard, 128), F32),
            pltpu.VMEM((pieces, width, heads * shard), BF16),
            pltpu.VMEM((pieces, width, shard), F32),
        ],
        held=list(zip(held, (0, 3)))
    )


def attend_back_body(
    start, cnt_ref, idx_ref, qkv_ref, o_ref, do0, do1, do2, do3, lse_ref, seg_ref, cos_ref, sin_ref, w_ref,
    g_ref, p0_ref, p1_ref, p2_ref, p3_ref, kt, segk, dk, dv, dqt, qmt, gmt, qst, gst, low,
):
    row = pl.program_id(0) + start
    _, pieces, _, shard, width = qkv_ref.shape
    heads = width // HEAD_DIM

    @pl.when(pl.program_id(0) == 0)
    def _():
        qmt[...] = jnp.zeros_like(qmt)
        gmt[...] = jnp.zeros_like(gmt)

    seg_columns(seg_ref[0], segk)
    dk[...] = jnp.zeros_like(dk)
    dv[...] = jnp.zeros_like(dv)
    lane = lax.broadcasted_iota(jnp.int32, (shard, width), 1) // HEAD_DIM
    chosen = lax.broadcasted_iota(jnp.int32, (8, width), 1) // HEAD_DIM
    chosen = (chosen == lax.broadcasted_iota(jnp.int32, (8, width), 0)).astype(BF16)
    for j, do_ref in enumerate((do0, do1, do2, do3)):
        kt[j] = qkv_ref[1, j, 0].T
        q, do = qkv_ref[0, j, 0], do_ref[...].reshape(shard, width)
        qt, gt = q.T, do.T
        for h in range(heads):
            at, qa = slice(h * HEAD_DIM, (h + 1) * HEAD_DIM), slice(h * shard, (h + 1) * shard)
            qmt[j, at, qa] = qt[at]
            gmt[j, at, qa] = gt[at]
            qst[j, qa] = jnp.where(lane == h, q, jnp.zeros_like(q))
            gst[j, qa] = jnp.where(lane == h, do, jnp.zeros_like(do))
        prod = do.astype(F32) * o_ref[j, 0].astype(F32)
        high = prod.astype(BF16)
        low[j] = dot(chosen, high, 1, 1) + dot(chosen, (prod - high.astype(F32)).astype(BF16), 1, 1)

    @pl.loop(0, pieces)
    def _(piece):
        back_piece(
            row * pieces + piece, piece, cnt_ref, idx_ref, qkv_ref.at[1], qkv_ref.at[2], lse_ref, seg_ref,
            kt, segk, dk, dv, dqt, qmt, gmt, qst, gst, low,
        )

    for j, ref in ((1, p1_ref), (3, p3_ref), (0, p0_ref), (2, p2_ref)):
        grad_q = turn(dqt[j].T * HEAD_DIM**-0.5, cos_ref[j], -sin_ref[j]).astype(BF16)
        grad_k = turn(dk[j] * (1 / LOG2E), cos_ref[j], -sin_ref[j]).astype(BF16)
        grad = jnp.concatenate([grad_q, grad_k, dv[j].astype(BF16)], axis=1)
        g_ref[j, 0] = grad
        ref[0] = dot(grad, w_ref[...]).astype(BF16)


def back_piece(
    at_q, piece, cnt_ref, idx_ref, k_ref, v_ref, lse_ref, seg_ref, kt, segk, dk, dv, dqt, qmt, gmt, qst, gst, low
):
    pieces, _, shard, width = k_ref.shape
    heads = width // HEAD_DIM
    lse, delta = lse_ref[0, piece], low[piece]
    seg_q = seg_ref[0, pl.ds(piece, 1)].astype(F32)

    def run(count):
        @pl.when(cnt_ref[at_q] == count)
        def _():
            places = [idx_ref[at_q * pieces + t] for t in range(count)]
            qm, gm = qmt[piece], gmt[piece]
            later = dot(k_ref[places[0], 0], qm), dot(v_ref[places[0], 0], gm)
            out = [None] * heads
            for t in range(count):
                s, dp = later
                j = places[t]
                if t + 1 < count:
                    later = dot(k_ref[places[t + 1], 0], qm), dot(v_ref[places[t + 1], 0], gm)
                col = segk[j]
                same = jnp.concatenate([col] * (shard // 128), axis=1) == seg_q
                ps, dss = [], []
                for h in range(heads):
                    at, qa = slice(h * HEAD_DIM, (h + 1) * HEAD_DIM), slice(h * shard, (h + 1) * shard)
                    p = jnp.exp2(jnp.where(same, s[:, qa] - lse[h : h + 1], NEG))
                    ds = (p * (dp[:, qa] - delta[h : h + 1])).astype(BF16)
                    ps.append(p.astype(BF16))
                    dss.append(ds)
                    found = dot(kt[j, at], ds)
                    out[h] = found if t == 0 else out[h] + found
                dv[j] += dot(jnp.concatenate(ps, axis=1), gst[piece])
                dk[j] += dot(jnp.concatenate(dss, axis=1), qst[piece])
            for h in range(heads):
                dqt[piece, h * HEAD_DIM : (h + 1) * HEAD_DIM] = out[h]

    for count in range(1, pieces + 1):
        run(count)


def attend_back(start, count, cnt, idx, qkv, o, do, lse, seg, cos_tab, sin_tab, weight, held=(), deps=()):
    _, pieces, rows, shard, width = qkv.shape
    model = weight.shape[1]
    heads = width // HEAD_DIM
    table = fixed((pieces, shard, 128))
    pairs = count * (pieces * shard) ** 2
    square, wide = (pieces, width, heads * shard), (pieces, shard, width)
    one = along((1, shard, width), 0, start)
    return call(
        functools.partial(attend_back_body, start), "attend_back", (cnt, idx), (count,),
        [(qkv, along((3, pieces, 1, shard, width), 2, start)), (o, along((pieces, 1, shard, width), 1, start))]
        + [(do[0], one), (do[1], one), (do[2], along((1, 1, shard, width), 1, start)), (do[3], one)]
        + [(lse, along((1, pieces, 8, shard), 0, start)), (seg, along((1, pieces, shard), 0, start))]
        + [(cos_tab, table), (sin_tab, table), (weight, fixed(weight.shape))],
        [((pieces, rows, shard, 3 * width), BF16, along((pieces, 1, shard, 3 * width), 1, start))]
        + [((count, shard, model), BF16, along((1, shard, model)))] * pieces,
        [
            pltpu.VMEM((pieces, width, shard), BF16),
            pltpu.VMEM((pieces, shard, 128), F32),
            pltpu.VMEM(wide, F32),
            pltpu.VMEM(wide, F32),
            pltpu.VMEM((pieces, width, shard), F32),
            pltpu.VMEM(square, BF16),
            pltpu.VMEM(square, BF16),
            pltpu.VMEM((pieces, heads * shard, width), BF16),
            pltpu.VMEM((pieces, heads * shard, width), BF16),
            pltpu.VMEM((pieces, 8, shard), F32),
        ],
        held=[(array, 0) for array in held], deps=deps
    )


def middle_body(
    order_ref, a0, a1, a2, a3, w0, w1, w2, w3, stream_ref, bias_ref, gain_ref, shift_ref, mid_ref, low_ref, all_ref,
):
    _, shard, model = stream_ref.shape
    total = 0.0
    for n, (a, w) in enumerate(((a0, w0), (a1, w1), (a2, w2), (a3, w3))):
        values = a[...].reshape(shard, a.shape[-1])
        total = total + dot(values, w[...])
        all_ref[0, :, n * a.shape[-1] : (n + 1) * a.shape[-1]] = values
    mid = stream_ref[0] + (total + line(bias_ref))
    hat, _ = centre(mid)
    mid_ref[0] = mid
    low_ref[0] = (hat * line(gain_ref) + line(shift_ref)).astype(BF16)


def out_blocks(weight, parts):
    width = weight.shape[0] // parts

    def block(i):
        return pl.BlockSpec((width, weight.shape[1]), lambda g, o: (o[i], 0))

    return [(weight, block(i)) for i in range(parts)]


def middle_norm(start, count, order, attended, weight, stream, vecs, held=()):
    rows, shard, model = stream.shape
    parts = len(attended)
    width = model // parts
    block, one = along((1, shard, model), 0, start), along((1, shard, width))
    first = [along((1, 1, shard, width), 1, start), one, along((1, 1, shard, width), 1), one]
    return call(
        middle_body, "middle", (order,), (count,),
        list(zip(attended, first)) + out_blocks(weight, parts) + [(stream, block)]
        + [(vec, fixed(vec.shape)) for vec in vecs],
        [
            (stream.shape, F32, block),
            ((count, shard, model), BF16, along((1, shard, model))),
            (stream.shape, BF16, block),
        ],
        held=list(zip(held, (0, 2)))
    )


def cot_body(blk_ref, a_ref, b_ref, up_ref, down_ref, g_ref, up_out, down_out, both_ref):
    tokens = a_ref.shape[0]
    down = down_ref[...]

    @pl.when(pl.program_id(0) == 0)
    def _():
        both_ref[0:tokens] = a_ref[...]
        both_ref[tokens:] = b_ref[...]

    g_ref[0:tokens] = dot(a_ref[...], down, 1, 1).astype(BF16)
    g_ref[tokens:] = dot(b_ref[...], down, 1, 1).astype(BF16)
    up_out[...] = up_ref[...]
    down_out[...] = down


def cot_down(blk, own, other, up, down, picked, half):
    tokens, model = own.shape
    steps = half // BLOCK
    column = along((2 * tokens, BLOCK), 1)
    if picked:
        up_at, down_at = along((model, BLOCK), 1), along((BLOCK, model))
    else:
        up_at = pl.BlockSpec((model, BLOCK), lambda g, b: (0, b[g]))
        down_at = pl.BlockSpec((BLOCK, model), lambda g, b: (b[g], 0))
    return call(
        cot_body, "cot_down", (blk,), (steps,),
        [(own, fixed(own.shape)), (other, fixed(own.shape)), (up, up_at), (down, down_at)],
        [
            ((2 * tokens, half), BF16, column),
            ((model, half), BF16, along((model, BLOCK), 1)),
            ((half, model), BF16, along((BLOCK, model))),
            ((2 * tokens, model), BF16, fixed((2 * tokens, model))),
        ]
    )


def hidden_body(blocks, blk_ref, *refs):
    pieces, refs = refs[:-11], refs[-11:]
    g_ref, up_ref, row_ref, bias_ref, act_ref, grad_ref, sum_ref, both_ref, part_ref, other_ref, held = refs
    sizes = [ref.shape[0] * ref.shape[1] for ref in pieces]
    starts = [sum(sizes[:n]) for n in range(len(sizes))]
    step = pl.program_id(0)

    @pl.when(step == 0)
    def _():
        for ref, at, size in zip(pieces, starts, sizes):
            both_ref[at : at + size] = ref[...].reshape(size, ref.shape[2])

    @pl.when(step < blocks)
    def _():
        up = up_ref[...]
        bias = bias_ref[...].astype(F32)
        total = 0.0
        later = dot(pieces[0][...].reshape(sizes[0], -1), up)
        for n, (start, size) in enumerate(zip(starts, sizes)):
            at = slice(start, start + size)
            v = later + bias
            if n + 1 < len(pieces):
                later = dot(pieces[n + 1][...].reshape(sizes[n + 1], -1), up)
            square = v * v
            tanh = jnp.tanh(v * (GELU_A + GELU_B * square))
            gate = 0.5 + 0.5 * tanh
            act = v * gate
            slope = gate + act * ((1.0 - tanh) * (GELU_A + 3.0 * GELU_B * square))
            grad = (slope * g_ref[at].astype(F32)).astype(BF16)
            act_ref[at] = act.astype(BF16)
            grad_ref[at] = grad
            held[step, at] = grad
            total = total + jnp.sum(grad.astype(F32), axis=0, keepdims=True)
        sum_ref[...] = total

    @pl.when(step >= blocks)
    def _():
        grad = jnp.concatenate([held[n] for n in range(blocks)], axis=1)
        found = dot(grad, row_ref[...], 1, 1).astype(BF16)
        part_ref[...] = found[: part_ref.shape[0]]
        other_ref[...] = found[part_ref.shape[0] :]


def hidden_units(blk, pieces, grads, up, bias):
    model = pieces[0].shape[2]
    tokens, half = grads.shape
    blocks, more = half // BLOCK, model // BLOCK

    def first(g):
        return jnp.minimum(g, blocks - 1)

    def second(g):
        return jnp.maximum(g - blocks, 0)

    column = pl.BlockSpec((tokens, BLOCK), lambda g, b: (0, first(g)))
    line = pl.BlockSpec((1, BLOCK), lambda g, b: (0, first(g)))
    return call(
        functools.partial(hidden_body, blocks), "hidden", (blk,), (blocks + more,),
        [(piece, fixed(piece.shape)) for piece in pieces]
        + [
            (grads, column),
            (up, pl.BlockSpec((model, BLOCK), lambda g, b: (0, first(g)))),
            (up, pl.BlockSpec((BLOCK, half), lambda g, b: (second(g), 0))),
            (bias, pl.BlockSpec((1, BLOCK), lambda g, b: (0, b[first(g)]))),
        ],
        [
            (grads.shape, BF16, column),
            (grads.shape, BF16, column),
            ((1, half), F32, line),
            ((tokens, model), BF16, fixed((tokens, model))),
            ((tokens // 2, model), BF16, pl.BlockSpec((tokens // 2, BLOCK), lambda g, b: (0, second(g)))),
            ((tokens // 2, model), BF16, pl.BlockSpec((tokens // 2, BLOCK), lambda g, b: (0, second(g)))),
        ],
        [pltpu.VMEM((blocks, tokens, BLOCK), BF16)]
    )


def sent_body(other_ref, tok_ref, cot_ref, grad_ref, act_ref, up_ref, down_ref):
    up_ref[...] = dot(tok_ref[...], grad_ref[...], 0, 0).astype(BF16)
    down_ref[...] = dot(act_ref[...], cot_ref[...], 0, 0).astype(BF16)


def sent_grads(other, tokens, cot, grad, act, steps):
    count, model = tokens.shape
    half = grad.shape[1]
    size = half // (2 * steps)
    wide = half // steps
    return call(
        sent_body, "sent_grads", (other,), (steps,),
        [
            (tokens, fixed(tokens.shape)),
            (cot, fixed(cot.shape)),
            (grad, along((count, wide), 1)),
            (act, pl.BlockSpec((count, size), lambda g, o: (0, 2 * g + o[0]))),
        ],
        [((model, half), BF16, along((model, wide), 1)), ((half // 2, model), BF16, along((size, model)))],
    )


def feed_body(order_ref, act_ref, down_ref, att_ref, low_ref, half_ref, cot_ref, feed_ref, other_ref, out_ref, keep_ref, kept_ref):
    parts = order_ref.shape[0]
    width = att_ref.shape[1] // parts
    feed = dot(act_ref[...], down_ref[...]).astype(BF16)
    feed_ref[...] = feed[: feed_ref.shape[0]]
    other_ref[...] = feed[feed_ref.shape[0] :]
    kept_ref[...] = dot(half_ref[...], cot_ref[...], 0, 0).astype(BF16)
    grad = dot(att_ref[...], low_ref[...], 0, 0).astype(BF16)
    step, steps = pl.program_id(0), pl.num_programs(0)

    def write(ref):
        for n in range(parts):
            at = pl.multiple_of(order_ref[n] * width, width)
            ref[pl.ds(at, width)] = grad[n * width : (n + 1) * width]

    @pl.when(2 * step < steps)
    def _():
        write(out_ref)

    @pl.when(2 * step >= steps)
    def _():
        write(keep_ref)


def feed_grads(order, act, down, attended, low, cot, c_at, x_at, deps=()):
    tokens, half = act.shape
    own, model = attended.shape
    steps = model // BLOCK
    place = jnp.concatenate([order, jnp.stack([c_at, x_at]).astype(jnp.int32)])
    size = half // (2 * steps)

    def body(place_ref, *refs):
        feed_body(place_ref.at[0 : order.shape[0]], *refs)

    def low_at(g, p):
        c = p[order.shape[0]]
        mine = 2 * g >= steps
        return 0, jnp.where(mine, c * (steps // 2) + g - steps // 2, (1 - c) * (steps // 2) + g)

    return call(
        body, "feed_grads", (place,), (steps,),
        [
            (act, fixed(act.shape)),
            (down, along((half, BLOCK), 1)),
            (attended, fixed(attended.shape)),
            (low, pl.BlockSpec((own, BLOCK), low_at)),
            (act, pl.BlockSpec((tokens, size), lambda g, p: (0, 2 * g + p[order.shape[0] + 1]))),
            (cot, fixed(cot.shape)),
        ],
        [
            ((own, model), BF16, along((own, BLOCK), 1)),
            ((own, model), BF16, along((own, BLOCK), 1)),
            ((model, model // 2), BF16, pl.BlockSpec((model, BLOCK), lambda g, p: (0, jnp.minimum(g, steps // 2 - 1)))),
            ((model, model // 2), BF16, pl.BlockSpec((model, BLOCK), lambda g, p: (0, jnp.maximum(g - steps // 2, 0)))),
            ((half // 2, model), BF16, along((size, model))),
        ],
        deps=deps,
    )


def middle_back_body(
    order_ref, part_ref, sent_ref, mid_ref, cot_ref, gain_ref, w0, w1, w2, w3,
    grad_ref, low_ref, att0_ref, att1_ref, far_ref, sums_ref,
):
    grad = part_ref[...].astype(F32) + sent_ref[...].astype(F32)
    hat, inverse = centre(mid_ref[0])
    cot = cot_ref[0].astype(F32)
    total = cot + norm_back(grad, line(gain_ref), hat, inverse)
    low = total.astype(BF16)
    grad_ref[0] = total
    low_ref[0] = low
    far_ref[0, 0] = dot(low, w2[...], 1, 1).astype(BF16)
    far_ref[1, 0] = dot(low, w3[...], 1, 1).astype(BF16)
    att1_ref[0] = dot(low, w1[...], 1, 1).astype(BF16)
    att0_ref[0] = dot(low, w0[...], 1, 1).astype(BF16)

    @pl.when(pl.program_id(0) == 0)
    def _():
        sums_ref[...] = jnp.zeros_like(sums_ref)

    sums_ref[0:1] += jnp.sum(grad * hat, axis=0, keepdims=True)
    sums_ref[1:2] += jnp.sum(grad, axis=0, keepdims=True)
    sums_ref[2:3] += jnp.sum(low.astype(F32), axis=0, keepdims=True)
    sums_ref[3:4] += jnp.sum(cot, axis=0, keepdims=True)


def middle_back(order, both, sent, mid, cot, gain, weight, parts, deps=()):
    rows, shard, model = mid.shape
    width = model // parts
    block, one = along((1, shard, model)), along((1, shard, width))
    flat = pl.BlockSpec((shard, model), lambda g, o: (g, 0))
    return call(
        middle_back_body, "middle_back", (order,), (rows,),
        [(both, flat), (sent, flat), (mid, block), (cot, block), (gain, fixed(gain.shape))] + out_blocks(weight, parts),
        [
            (mid.shape, F32, block),
            (mid.shape, BF16, block),
            ((rows, shard, width), BF16, one),
            ((rows, shard, width), BF16, one),
            ((2, rows, shard, width), BF16, along((2, 1, shard, width), 1)),
            ((8, model), F32, fixed((8, model))),
        ],
        deps=deps
    )


def norm1_back_body(start, part_ref, near_ref, far_ref, stream_ref, mid_ref, gain_ref, seg_ref, in_ref, shift_ref, sums_ref):
    grad = part_ref[0].astype(F32) + near_ref[0].astype(F32) + far_ref[0].astype(F32)
    hat, inverse = centre(stream_ref[0])
    total = mid_ref[0] + norm_back(grad, line(gain_ref), hat, inverse)
    in_ref[0] = total.astype(BF16)
    seg = seg_ref[pl.ds(pl.program_id(0) + start, 1)]
    slots = lax.broadcasted_iota(jnp.int32, (SEGS, seg.shape[-1]), 0) == seg
    onehot = slots.astype(F32).astype(BF16)
    shift_ref[0] = dot(jnp.concatenate([onehot, onehot], axis=1), split_low(total))

    @pl.when(pl.program_id(0) == 0)
    def _():
        sums_ref[...] = jnp.zeros_like(sums_ref)

    sums_ref[0:1] += jnp.sum(grad * hat, axis=0, keepdims=True)
    sums_ref[1:2] += jnp.sum(grad, axis=0, keepdims=True)


def norm1_back(start, count, own, near, far, stream, mid, gain, seg, held=(), deps=()):
    rows, shard, model = stream.shape
    block, own_block = along((1, shard, model), 0, start), along((1, shard, model))
    return call(
        functools.partial(norm1_back_body, start), "norm1_back", (), (count,),
        [(own, own_block), (near, own_block), (far, own_block), (stream, block), (mid, block), (gain, fixed(gain.shape))]
        + [(seg, fixed(seg.shape))],
        [
            (stream.shape, BF16, block),
            ((count, SEGS, model), F32, along((1, SEGS, model))),
            ((8, model), F32, fixed((8, model))),
        ],
        held=[(array, 0) for array in held], deps=deps
    )


def exchange(own, one, far):
    return [own, swap(one, "c"), far, swap(far[1], "c")]


def tie(*values):
    return lax.optimization_barrier(values)


def cut(values, index, size, axis):
    return lax.dynamic_slice_in_dim(values, index * size, size, axis)


def add_low(kept, sent):
    return (kept.astype(F32) + sent.astype(F32)).astype(BF16)


def ordered(at, own, other, axis):
    return jnp.where(at == 0, jnp.concatenate([own, other], axis), jnp.concatenate([other, own], axis))


def finish_body(blocks, at_ref, d0, d1, u0, u1, l0, l1, down_ref, up_ref, qkv_ref, out_ref):
    c_at = at_ref[0]
    width = up_ref.shape[1] // (4 * blocks)
    size = d0.shape[0]
    for c in range(2):
        mine = c_at == c
        down_ref[c * size : (c + 1) * size] = jnp.where(mine, d0[...], d1[...]).astype(F32)
        up = jnp.where(mine, u0[...], u1[...]).astype(F32)
        for b in range(2 * blocks):
            up_ref[:, (2 * b + c) * width : (2 * b + c + 1) * width] = up[:, b * width : (b + 1) * width]
        late = jnp.where(mine, l0[...], l1[...]).astype(F32)
        half = out_ref.shape[1] // 2
        wide = half // 2
        out_ref[:, c * half : (c + 1) * half] = late[:, 6 * wide :]
        for y in range(2):
            for n in range(3):
                at = n * 4 * wide + (2 * y + c) * wide
                qkv_ref[:, at : at + wide] = late[:, (3 * y + n) * wide : (3 * y + n + 1) * wide]


def finish(c_at, dp, piece, down, up, late, parts):
    rows, model = late[0].shape[0], down[0].shape[1]
    depth, size = dp // 2, down[0].shape[0]
    if piece % 128 == 0:
        at = c_at.astype(jnp.int32)[None]
        shapes = [(2 * size, model), (rows, 2 * dp * piece), (rows, 3 * model), (rows, model)]
        arrays = list(down) + list(up) + list(late)
        return call(
            functools.partial(finish_body, depth), "finish", (at,), (1,),
            [(array, fixed(array.shape)) for array in arrays], [(shape, F32, fixed(shape)) for shape in shapes],
        )
    down_done = ordered(c_at, *down, 0).astype(F32)
    up_done = ordered(c_at, up[0][None], up[1][None], 0).reshape(2, rows, dp, piece).transpose(1, 2, 0, 3)
    up_done = up_done.reshape(rows, 2 * dp * piece).astype(F32)
    both = ordered(c_at, late[0][None], late[1][None], 0)
    width = model // parts
    qkv_done = both[:, :, : 6 * width].reshape(2, rows, 2, 3, width).transpose(1, 3, 2, 0, 4)
    qkv_done = qkv_done.reshape(rows, 3 * model).astype(F32)
    out_done = jnp.concatenate([both[0, :, 6 * width :], both[1, :, 6 * width :]], axis=1).astype(F32)
    return down_done, up_done, qkv_done, out_done


def local(
    inputs, segment_ids, doc_times, time_weight, time_bias, norm1_gain, norm1_bias, qkv_weight, qkv_bias,
    out_weight, out_bias, norm2_gain, norm2_bias, up_weight, up_bias, down_weight, down_bias, cotangent,
    *, dp,
):
    rows, shard, model = inputs.shape
    parts = 4
    tokens = rows * shard
    hidden_width = up_weight.shape[1]
    width = model // parts
    depth = dp // 2
    half = hidden_width // 2
    piece = half // dp
    z_at, x_at, y_at, c_at = (lax.axis_index(name) for name in ("z", "x", "y", "c"))
    me = 2 * y_at + c_at

    groups = [(0, rows - 1), (rows - 1, 1)] if rows > 1 else [(0, 1)]
    seg_one, seg_two = swap(segment_ids, "c"), swap(segment_ids, "y")
    seg_three = swap(seg_two, "c")
    features = time_features(doc_times.reshape(rows * SEGS), jnp.arange(TEMB), TEMB // 2)
    time_shift = dot(features, time_weight).reshape(rows, SEGS, model)
    own1, one1, two1, stream = [], [], [], None
    for start, count in groups:
        held = () if stream is None else (stream,)
        stream, low = norm1(
            start, count, inputs, segment_ids, time_shift, (time_bias, norm1_gain, norm1_bias), held
        )
        if stream is not None and not own1:
            low, seg_one, seg_two, seg_three = tie(low, seg_one, seg_two, seg_three)
        own1.append(low)
        two1.append(swap(low, "y"))
        one1.append(swap(low, "c"))
    segs = jnp.stack([segment_ids, seg_one, seg_two, seg_three], axis=1)

    me, x_at, z_at, c_at, y_at, own1[-1], segs = tie(me, x_at, z_at, c_at, y_at, own1[-1], segs)
    order = [me ^ i for i in range(parts)]
    order_list = jnp.stack(order).astype(jnp.int32)
    me_list = order_list[:1]
    low_id, high_id = segs.min(axis=2), segs.max(axis=2)
    act = (low_id[:, :, None] <= high_id[:, None, :]) & (low_id[:, None, :] <= high_id[:, :, None])
    places = jnp.arange(parts, dtype=jnp.int32)
    rank = jnp.cumsum(act.astype(jnp.int32), axis=2) - 1
    chosen = act[..., None] & (rank[..., None] == places)
    idx = jnp.sum(jnp.where(chosen, places[:, None], 0), axis=2).astype(jnp.int32).reshape(-1)
    cnt = jnp.sum(act.astype(jnp.int32), axis=2).reshape(-1)
    positions = jnp.stack([o * shard + jnp.arange(shard, dtype=jnp.int32) for o in order])
    cos_tab, sin_tab = rotary_tables(positions, HEAD_DIM)

    cot = cotangent.reshape(tokens, model)
    cot_other = swap(cot, "c")
    if piece % BLOCK == 0:
        blk = (jnp.arange(dp)[:, None] * 2 + c_at) * (piece // BLOCK) + jnp.arange(piece // BLOCK)
        blk = blk.reshape(-1).astype(jnp.int32)
        up_from, down_from = up_weight, down_weight
    else:
        blk = jnp.zeros((half // BLOCK,), jnp.int32)
        up_from = lax.dynamic_index_in_dim(up_weight.reshape(model, dp, 2, piece), c_at, 2, keepdims=False)
        down_from = lax.dynamic_index_in_dim(down_weight.reshape(dp, 2, piece, model), c_at, 1, keepdims=False)
        up_from, down_from = up_from.reshape(model, half), down_from.reshape(half, model)
    grad_act, up_own, down_own, cot_both = cot_down(
        blk, cot, cot_other, up_from, down_from, piece % BLOCK != 0, half
    )
    up_bias_own, bias_blk = up_bias.reshape(1, hidden_width), blk
    if piece % BLOCK:
        up_bias_own = lax.dynamic_index_in_dim(up_bias.reshape(dp, 2, piece), c_at, 1, keepdims=False)
        up_bias_own, bias_blk = up_bias_own.reshape(1, half), jnp.arange(half // BLOCK, dtype=jnp.int32)

    qkv_line = qkv_bias.reshape(1, 3 * model)
    near = (own1, one1)
    qkv, qkv_own = project_qkv(
        0, 0, parts, rows, me_list, near, qkv_weight, qkv_line, cos_tab, sin_tab, (), (grad_act, cnt, idx)
    )
    o, lse, attended, three1 = None, None, [], []
    for n, (start, count) in enumerate(groups):
        if n == 0:
            two1[0], qkv = tie(two1[0], qkv)
        else:
            two1[n], o = tie(two1[n], o)
        three1.append(swap(two1[n], "c"))
        (qkv,) = project_qkv(
            1, start, parts, rows, me_list, ([two1[n]], [three1[n]]), qkv_weight, qkv_line, cos_tab, sin_tab, (qkv,),
            () if o is None else (o,),
        )
        held = () if o is None else (o, lse)
        o, out_one, out_far, lse = attend(start, count, cnt, idx, qkv, segs, held)
        attended.append((out_one, swap(out_far, "y")))
    held, normed2, normed2_other = (), [], []
    for (start, count), values in zip(groups, attended):
        far, o = tie(values[1], o)
        values = exchange(o, values[0], far)
        middle, low, attended_all = middle_norm(
            start, count, order_list, values, out_weight, stream, (out_bias, norm2_gain, norm2_bias), held
        )
        held = (middle, attended_all)
        normed2.append(low)
        normed2_other.append(swap(low, "c"))

    active, grad_hidden, up_b, normed2_both, part2, part2_other = hidden_units(
        bias_blk, normed2 + normed2_other, grad_act, up_own, up_bias_own
    )
    part2_sent = swap(part2_other, "c")
    grad_middle, grad_middle_low, att0, att1, far, sums2 = middle_back(
        order_list, part2, part2_sent, middle, cotangent, norm2_gain, out_weight, parts
    )
    far = swap(far, "y")
    sums2 = sums2[:4]

    active, grad_hidden, att0 = tie(active, grad_hidden, att0)
    up_rows = model // dp
    small_blocks = piece % BLOCK != 0 or depth != model // BLOCK
    if small_blocks:
        up_grad = dot(normed2_both, grad_hidden, 0, 0).astype(BF16)
        down_out = dot(active, cot_both, 0, 0).astype(BF16).reshape(depth, 2, piece, model)
        down_kept = lax.dynamic_index_in_dim(down_out, x_at, 1, keepdims=False).reshape(half // 2, model)
        down_out = lax.dynamic_index_in_dim(down_out, 1 - x_at, 1, keepdims=False).reshape(half // 2, model)
    else:
        up_grad, down_out = sent_grads(
            1 - x_at[None].astype(jnp.int32), normed2_both, cot_both, grad_hidden, active, depth
        )
    up_grad, down_out, far = tie(up_grad, down_out, far)
    grad_o = exchange(att0, att1, far)
    up_z = lax.psum_scatter(up_grad, "z", scatter_dimension=0, tiled=True)
    down_sent = swap(down_out[: half // 4], "x")
    if small_blocks:
        feed = dot(active, down_own).astype(BF16)
        feed, feed_other = feed[:tokens], feed[tokens:]
        out_grad = dot(attended_all.reshape(tokens, model), grad_middle_low.reshape(tokens, model), 0, 0).astype(BF16)
        out_grad = jnp.concatenate([cut(out_grad, o_at, width, 0) for o_at in order], axis=0)
        out_sent, out_grad = (cut(out_grad, at, model // 2, 1) for at in (1 - c_at, c_at))
    else:
        feed, feed_other, out_sent, out_grad, down_kept = feed_grads(
            order_list, active, down_own, attended_all.reshape(tokens, model), grad_middle_low.reshape(tokens, model),
            cot_both, c_at, x_at, (far, down_out),
        )
    feed, feed_other, out_sent, out_grad, down_kept, down_sent, down_out, *grad_o = tie(
        feed, feed_other, out_sent, out_grad, down_kept, down_sent, down_out, *grad_o
    )
    down_late = swap(down_out[half // 4 :], "x")
    out_sent, feed_sent = swap(out_sent, "c"), swap(feed_other, "c")

    back = []
    (start, count), rest = groups[0], groups[1:]
    found = attend_back(start, count, cnt, idx, qkv, o, grad_o, lse, segs, cos_tab, sin_tab, qkv_own)
    *found, down_late, out_sent, feed_sent = tie(*found, down_late, out_sent, feed_sent)
    grad_qkv, own, one, two, three = found
    there = add_low(two, swap(three, "c"))
    down_x = add_low(down_kept, jnp.concatenate([down_sent, down_late], axis=0))
    down_z = lax.psum_scatter(down_x, "z", scatter_dimension=0, tiled=True)
    out_c = add_low(out_grad, out_sent).reshape(depth, 2 * up_rows, model // 2)
    out_sent = cut(out_c, 1 - x_at, up_rows, 1)
    there, down_x, out_sent = tie(there, down_x, out_sent)
    far, near = swap(there, "y"), swap(one, "c")
    out_sent = swap(out_sent, "x")
    if rest:
        (start, count), = rest
        found = attend_back(
            start, count, cnt, idx, qkv, o, grad_o, lse, segs, cos_tab, sin_tab, qkv_own, (grad_qkv,),
            (there, down_x),
        )
        *found, far, up_z, out_sent = tie(*found, far, up_z, out_sent)
        back.append((own, near, far))
        grad_qkv, own, one, two, three = found
        there, far = tie(add_low(two, swap(three, "c")), far)
        far, near = swap(there, "y"), swap(one, "c")
        grad_qkv, there = tie(grad_qkv, there)
    qkv_out, qkv_kept, qkv_b = qkv_grads(x_at, [own1, one1, two1, three1], grad_qkv, depth)
    qkv_out, qkv_kept, far, out_sent, out_c, up_z = tie(qkv_out, qkv_kept, far, out_sent, out_c, up_z)
    back.append((own, near, far))
    qkv_sent = swap(qkv_out, "x")
    out_x = add_low(cut(out_c, x_at, up_rows, 1), out_sent)
    out_sent = cut(out_x, 1 - y_at, width, 2)
    qkv_out, up_out = tie(qkv_out, cut(up_z, 1 - x_at, up_rows, 0))
    up_sent = swap(up_out, "x")
    held, grad_shift, sums1 = (), [], 0.0
    for (start, count), values in zip(groups, back):
        input_grad, found, sums = norm1_back(
            start, count, *values, stream, grad_middle, norm1_gain, segment_ids, held, (qkv_kept, up_out)
        )
        if not held:
            input_grad, out_sent = tie(input_grad, out_sent)
            out_sent = swap(out_sent, "y")
        held = (input_grad,)
        grad_shift.append(found.reshape(count * SEGS, model))
        sums1 = sums1 + sums[:2]

    up_b = up_b.reshape(dp, 1, piece)
    up_b = jnp.where(jnp.arange(2)[:, None] == c_at, up_b, 0.0).reshape(-1, model)
    qkv_b = jnp.where(jnp.arange(parts)[:, None] == me, qkv_b.reshape(3, 1, width), 0.0).reshape(3, model)
    times = doc_times.reshape(1, rows * SEGS)
    times = jnp.concatenate([times // 32, times % 32], axis=1).astype(F32)
    times = jnp.tile(jnp.pad(times, ((0, 0), (0, width - times.shape[1]))), (1, parts))
    small = jnp.concatenate(grad_shift + [sums1, sums2, qkv_b, up_b, times], axis=0).astype(BF16)
    small_sent = swap(cut(small, 1 - c_at, 2 * width, 1), "c")
    small = add_low(cut(small, c_at, 2 * width, 1), small_sent)
    small, qkv_sent, out_sent = tie(small, qkv_sent, out_sent)
    small = add_low(cut(small, y_at, width, 1), swap(cut(small, 1 - y_at, width, 1), "y"))
    small = ordered(x_at, small[None], swap(small, "x")[None], 0)
    out_x = add_low(cut(out_x, y_at, width, 2), out_sent)
    late = jnp.concatenate([add_low(qkv_kept, qkv_sent), out_x], axis=2)
    output = middle.reshape(tokens, model) + (feed.astype(F32) + feed_sent.astype(F32) + down_bias.astype(F32))
    output = output.astype(BF16).reshape(rows, shard, model)
    small, late = tie(small, late)
    if depth == 4:
        flat = small.reshape(2 * small.shape[1] * width // model, model)
        parts_z = [lax.dynamic_index_in_dim(late, z_at ^ n, 0, keepdims=False) for n in range(depth)]
        sent = [
            lax.ppermute(jnp.concatenate([parts_z[n], flat], axis=0), "z", [(i, i ^ n) for i in range(depth)])
            for n in range(1, depth)
        ]
        small, down_z, up_z, up_sent = tie(small, down_z, up_z, up_sent)
        up_x = add_low(cut(up_z, x_at, up_rows, 0), up_sent)
        down_sent, up_sent = swap(down_z, "y"), swap(up_x, "y")
        *sent, output, down_sent, up_sent = tie(*sent, output, down_sent, up_sent)
        late = sum(part[:up_rows].astype(F32) for part in sent) + parts_z[0].astype(F32)
        late = late.astype(BF16)
        small = jnp.stack([small] + [part[up_rows:].reshape(small.shape) for part in sent])
        small = jnp.stack([lax.dynamic_index_in_dim(small, z_at ^ n, 0, keepdims=False) for n in range(depth)])
    else:
        up_x = add_low(cut(up_z, x_at, up_rows, 0), up_sent)
        down_sent, up_sent = swap(down_z, "y"), swap(up_x, "y")
        late = lax.psum_scatter(late, "z", scatter_dimension=0, tiled=False)
        small = lax.all_gather(small, "z")
    small = small.reshape(dp, small.shape[2], width)

    late_sent = swap(late, "y")
    down_done, up_done = add_low(down_z, down_sent), add_low(up_x, up_sent)
    down_other, up_other = swap(down_done, "c"), swap(up_done, "c")
    both = ordered(y_at, late[None], late_sent[None], 0)
    late = jnp.concatenate([both[0, :, : 3 * width], both[1, :, : 3 * width], both[0, :, 3 * width :], both[1, :, 3 * width :]], axis=1)
    late_other = swap(late, "c")

    down_done, up_done, qkv_done, out_done = finish(
        c_at, dp, piece, (down_done, down_other), (up_done, up_other), (late, late_other), parts
    )

    dp_at = 2 * z_at + x_at
    all_times = small[:, -1, : 2 * rows * SEGS].astype(F32) * 0.25
    all_times = all_times[:, : rows * SEGS] * 32.0 + all_times[:, rows * SEGS :]
    shifts = small[:, : rows * SEGS].reshape(dp * rows * SEGS, width)
    columns = dp_at * (TEMB // dp) + jnp.arange(TEMB // dp)
    wanted = time_features(all_times.reshape(-1), columns, TEMB // 2)
    sums = jnp.sum(small[:, rows * SEGS : -1].astype(F32), axis=0)
    full = [dot(wanted, shifts, 0, 0), sums, jnp.sum(shifts.astype(F32), axis=0, keepdims=True)]
    full = jnp.concatenate(full, axis=0).astype(BF16)
    count = full.shape[0]
    full = jnp.pad(full, ((0, -count % 16), (0, 0)))
    full = ordered(y_at, full[None], swap(full, "y")[None], 0)
    full = ordered(c_at, full[None], swap(full, "c")[None], 0)
    full = full.transpose(2, 0, 1, 3).reshape(-1, model).astype(F32)
    time_w_done, sums = full[: TEMB // dp], full[TEMB // dp : count]

    def share(vector):
        return cut(vector.reshape(-1), dp_at, vector.size // dp, 0)

    return (
        output, input_grad, time_w_done, share(sums[-1]), share(sums[0]), share(sums[1]), qkv_done, share(sums[6:9]),
        out_done, share(sums[4]), share(sums[2]), share(sums[3]), up_done, share(sums[9:-1]), down_done, share(sums[5]),
    )


def solution(mesh):
    dp, seq = mesh.shape["dp"], mesh.shape["seq"]
    fine = Mesh(mesh.devices.reshape(dp // 2, 2, seq // 2, 2), ("z", "x", "y", "c"))
    rows, seqs = ("z", "x"), ("y", "c")
    placed = (P(rows, seqs, None), P(rows, seqs), P(rows, None)) + (P(),) * 14 + (P(rows, seqs, None),)
    vec, mat = P(rows), P(rows, None)
    return jax.shard_map(
        functools.partial(local, dp=dp),
        mesh=fine,
        in_specs=placed,
        out_specs=(
            P(rows, seqs, None), P(rows, seqs, None), mat, vec, vec, vec, mat, vec, mat, vec, vec, vec, mat, vec, mat, vec,
        ),
        check_vma=False,
    )
```

```python
import functools
import math

import jax
import jax.numpy as jnp
from jax import lax
from jax.experimental import pallas as pl
from jax.experimental.pallas import tpu as pltpu
from jax.sharding import Mesh, PartitionSpec as P

HEADS = 16
HEAD_DIM = 64
TEMB = 256
SEGS = 8
EPSILON = 1e-05
F32 = jnp.float32
BF16 = jnp.bfloat16
NEG = -1e30
LOG2E = math.log2(math.e)
GELU_A = math.sqrt(2.0 / math.pi)
GELU_B = GELU_A * 0.044715
BLOCK = 256
VMEM = 60 * 1024 * 1024


def swap(value, axis):
    return lax.ppermute(value, axis, [(0, 1), (1, 0)])


def time_features(doc_times, column, half_size):
    frequency = jnp.exp(-math.log(10000.0) * (column % half_size).astype(F32) / half_size)
    angles = doc_times.astype(F32)[..., None] * frequency
    return jnp.where(column < half_size, jnp.sin(angles), jnp.cos(angles)).astype(BF16)


def rotary_tables(positions, head_size):
    half_size = head_size // 2
    frequency = jnp.exp(-math.log(10000.0) * 2.0 * jnp.arange(half_size, dtype=F32) / head_size)
    angles = positions.astype(F32)[..., None] * frequency
    cos_tab, sin_tab = jnp.cos(angles), jnp.sin(angles)
    return (
        jnp.concatenate([cos_tab] * 4, axis=-1),
        jnp.concatenate([-sin_tab, sin_tab, -sin_tab, sin_tab], axis=-1),
    )


def dot(left_op, right_op, left_dim=1, right_dim=0):
    return lax.dot_general(
        left_op, right_op, (((left_dim,), (right_dim,)), ((), ())), preferred_element_type=F32
    )


def turn(values, cos_tab, sin_tab):
    slabs = []
    lane = lax.broadcasted_iota(jnp.int32, (values.shape[0], 128), 1)
    first = lane % HEAD_DIM < HEAD_DIM // 2
    for start in range(0, values.shape[1], 128):
        slab = values[:, start : start + 128]
        partner = jnp.where(
            first, pltpu.roll(slab, 128 - HEAD_DIM // 2, 1), pltpu.roll(slab, HEAD_DIM // 2, 1)
        )
        slabs.append(slab * cos_tab + partner * sin_tab)
    return jnp.concatenate(slabs, axis=1)


def split_low(values):
    high = values.astype(BF16)
    return jnp.concatenate([high, (values - high.astype(F32)).astype(BF16)], axis=0)


def centre(values):
    scale = 1.0 / values.shape[-1]
    centred = values - jnp.sum(values, axis=-1, keepdims=True) * scale
    spread = jnp.sum(centred * centred, axis=-1, keepdims=True) * scale
    inverse = lax.rsqrt(spread + EPSILON)
    return centred * inverse, inverse


def norm_back(grad, gain, hat, inverse):
    scale = 1.0 / grad.shape[-1]
    scaled = grad * gain
    mean = jnp.sum(scaled, axis=-1, keepdims=True) * scale
    along = jnp.sum(scaled * hat, axis=-1, keepdims=True) * scale
    return inverse * (scaled - mean - hat * along)


def call(body, name, prefetch, grid, ins, outs, scratch=(), deps=(), held=()):
    count = len(prefetch) + len(ins)
    extra = [array for array, _ in held] + list(deps)

    def kernel(*refs):
        body(*refs[:count], *refs[count + len(extra) :])

    return pl.pallas_call(
        kernel,
        grid_spec=pltpu.PrefetchScalarGridSpec(
            num_scalar_prefetch=len(prefetch),
            grid=grid,
            in_specs=[spec for _, spec in ins] + [pl.BlockSpec(memory_space=pl.ANY)] * len(extra),
            out_specs=[spec for _, _, spec in outs],
            scratch_shapes=list(scratch),
        ),
        out_shape=[jax.ShapeDtypeStruct(shape, kind) for shape, kind, _ in outs],
        input_output_aliases={count + n: out for n, (_, out) in enumerate(held)},
        compiler_params=pltpu.CompilerParams(vmem_limit_bytes=VMEM),
        name=name,
    )(*prefetch, *[array for array, _ in ins], *extra)


def line(ref):
    return ref[...].astype(F32).reshape(1, -1)


def fixed(shape):
    return pl.BlockSpec(shape, lambda *_: (0,) * len(shape))


def along(shape, axis=0, start=0):
    return pl.BlockSpec(shape, lambda g, *_: tuple(start + g if n == axis else 0 for n in range(len(shape))))


def norm1_body(start, x_ref, seg_ref, shift_ref, time_ref, gain_ref, bias_ref, stream_ref, low_ref):
    seg = seg_ref[pl.ds(pl.program_id(0) + start, 1)]
    slots = lax.broadcasted_iota(jnp.int32, (SEGS, seg.shape[-1]), 0) == seg
    onehot = slots.astype(F32).astype(BF16)
    shift = shift_ref[0] + line(time_ref)
    added = dot(jnp.concatenate([onehot, onehot], axis=0), split_low(shift), 0, 0)
    stream = x_ref[0].astype(F32) + added
    hat, _ = centre(stream)
    stream_ref[0] = stream
    low_ref[0] = (hat * line(gain_ref) + line(bias_ref)).astype(BF16)


def norm1(start, count, x, seg, shift, vecs, held=()):
    rows, shard, model = x.shape
    block = along((1, shard, model), 0, start)
    return call(
        functools.partial(norm1_body, start), "norm1", (), (count,),
        [(x, block), (seg, fixed(seg.shape)), (shift, along((1, SEGS, model), 0, start))]
        + [(vec, fixed(vec.shape)) for vec in vecs],
        [(x.shape, F32, block), ((count, shard, model), BF16, along((1, shard, model)))],
        held=[(array, 0) for array in held],
    )


def qkv_body(sizes, me_ref, *refs):
    count = 2 * len(sizes)
    pieces, (w_ref, bias_ref, cos_ref, sin_ref, out_ref), own = refs[:count], refs[count : count + 5], refs[count + 5 :]
    places = [(n, sum(sizes[:g]) + r, n * len(sizes) + g, r) for n in range(2) for g, size in enumerate(sizes) for r in range(size)]
    step = pl.program_id(0)

    def run(turned):
        w = w_ref[...]
        bias = bias_ref[...].astype(F32)
        later = dot(pieces[0][0], w)
        for at, (n, r, _, _) in enumerate(places):
            values = later + bias
            if at + 1 < len(places):
                later = dot(pieces[places[at + 1][2]][places[at + 1][3]], w)
            if turned:
                values = turn(values, cos_ref[n], sin_ref[n]) * jnp.where(step == 0, LOG2E * HEAD_DIM**-0.5, 1.0)
            out_ref[0, n, r] = values.astype(BF16)

    for ref in own:
        ref[...] = w_ref[...].T

    @pl.when(step < 2)
    def _():
        run(True)

    @pl.when(step == 2)
    def _():
        run(False)


def project_qkv(pair, start, parts, rows, me, pieces, weight, bias, cos_tab, sin_tab, held=(), deps=()):
    _, shard, model = pieces[0][0].shape
    sizes = [piece.shape[0] for piece in pieces[0]]
    count = sum(sizes)
    width = model // parts
    place = pl.BlockSpec((1, 2, count, shard, width), lambda g, m: (g, pair, start // count, 0, 0))
    outs = [((3, parts, rows, shard, width), BF16, place)]
    if not held:
        outs.append(((3 * width, model), BF16, along((width, model))))
    return call(
        functools.partial(qkv_body, sizes), "qkv", (me,), (3,),
        [(piece, fixed(piece.shape)) for group in pieces for piece in group]
        + [
            (weight, pl.BlockSpec((model, width), lambda g, m: (0, g * parts + m[0]))),
            (bias, pl.BlockSpec((1, width), lambda g, m: (0, g * parts + m[0]))),
            (cos_tab, pl.BlockSpec((2, shard, 128), lambda g, m: (pair, 0, 0))),
            (sin_tab, pl.BlockSpec((2, shard, 128), lambda g, m: (pair, 0, 0))),
        ],
        outs, held=[(array, n) for n, array in enumerate(held)], deps=deps,
    )


def qkv_grads(x_at, pieces, grad, blocks, deps=()):
    shard, model = pieces[0][0].shape[1:]
    parts, rows, _, columns = grad.shape
    size = model // (2 * blocks)
    flat = [(n, piece) for n, group in enumerate(pieces) for piece in group]

    def body(at_ref, *refs):
        g_ref, out_ref, keep_ref, sum_ref = refs[len(flat) :]
        total, sums, start = 0.0, 0.0, [0] * parts
        for (n, piece), x_ref in zip(flat, refs):
            count = piece.shape[0]
            g = g_ref[n, start[n] : start[n] + count].reshape(count * shard, g_ref.shape[3])
            start[n] += count
            total = total + dot(x_ref[...].reshape(count * shard, model), g, 0, 0)
            sums = sums + jnp.sum(g.astype(F32), axis=0, keepdims=True)
        low = total.astype(BF16)
        for x in range(2):
            for b in range(blocks):
                values = low[(2 * b + x) * size : (2 * b + x + 1) * size]

                @pl.when(at_ref[0] == x)
                def _():
                    keep_ref[b] = values

                @pl.when(at_ref[0] != x)
                def _():
                    out_ref[b] = values

        sum_ref[...] = sums

    block = along((blocks, size, BLOCK), 2)
    shape = (blocks, size, columns)
    return call(
        body, "qkv_grads", (x_at.astype(jnp.int32)[None],), (columns // BLOCK,),
        [(x, fixed(x.shape)) for _, x in flat] + [(grad, along((parts, rows, shard, BLOCK), 3))],
        [(shape, BF16, block), (shape, BF16, block), ((1, columns), F32, along((1, BLOCK), 1))],
        deps=deps,
    )


def seg_columns(segq_all, segk):
    pieces, shard, _ = segk.shape
    for j in range(pieces):
        row = jnp.broadcast_to(segq_all[j:j+1].astype(F32), (128, shard))
        segk[j] = row.T

def attend_body(start, cnt_ref, idx_ref, qkv_ref, seg_ref, o_ref, one_ref, far_ref, lse_ref, vt, segk, qmt, acc):
    row = pl.program_id(0) + start
    _, pieces, _, shard, width = qkv_ref.shape
    heads = width // HEAD_DIM

    @pl.when(pl.program_id(0) == 0)
    def _():
        qmt[...] = jnp.zeros_like(qmt)

    for j in range(pieces):
        vt[j] = qkv_ref[2, j, 0].T
        qt = qkv_ref[0, j, 0].T
        for h in range(heads):
            at = slice(h * HEAD_DIM, (h + 1) * HEAD_DIM)
            qmt[j, at, h * shard : (h + 1) * shard] = qt[at]
    seg_columns(seg_ref[0], segk)

    @pl.loop(0, pieces)
    def _(piece):
        attend_piece(row * pieces + piece, piece, cnt_ref, idx_ref, qkv_ref.at[1], seg_ref, lse_ref, vt, segk, qmt, acc)

    for j in range(pieces):
        o_ref[j, 0] = acc[j].T.astype(BF16)
    one_ref[0] = o_ref[1, 0]
    far_ref[:, 0] = o_ref[2:, 0]


def attend_piece(at_q, piece, cnt_ref, idx_ref, k_ref, seg_ref, lse_ref, vt, segk, qmt, acc):
    pieces, _, shard, width = k_ref.shape
    heads = width // HEAD_DIM
    seg_q = seg_ref[0, pl.ds(piece, 1)].astype(F32)

    def run(count):
        @pl.when(cnt_ref[at_q] == count)
        def _():
            qm = qmt[piece]
            places = [idx_ref[at_q * pieces + t] for t in range(count)]
            top, tot, out = [None] * heads, [None] * heads, [None] * heads
            later = dot(k_ref[places[0], 0], qm)
            for t in range(count):
                s = later
                if t + 1 < count:
                    later = dot(k_ref[places[t + 1], 0], qm)
                col = segk[places[t]]
                same = jnp.concatenate([col] * (shard // 128), axis=1) == seg_q
                for h in range(heads):
                    at = slice(h * HEAD_DIM, (h + 1) * HEAD_DIM)
                    sh = jnp.where(same, s[:, h * shard : (h + 1) * shard], NEG)
                    best = jnp.max(sh, axis=0, keepdims=True)
                    if t:
                        best = jnp.maximum(top[h], best)
                        fade = jnp.exp2(top[h] - best)
                    p = jnp.exp2(sh - best)
                    values = jnp.concatenate([vt[places[t], at], jnp.ones((16, shard), BF16)], axis=0)
                    found = dot(values, p.astype(BF16))
                    total, found = found[HEAD_DIM : HEAD_DIM + 1], found[:HEAD_DIM]
                    if t:
                        total = tot[h] * fade + total
                        found = out[h] * fade + found
                    top[h], tot[h], out[h] = best, total, found
            for h in range(heads):
                acc[piece, h * HEAD_DIM : (h + 1) * HEAD_DIM] = out[h] / tot[h]
                lse_ref[0, piece, h : h + 1] = top[h] + jnp.log2(tot[h])

    for count in range(1, pieces + 1):
        run(count)


def attend(start, count, cnt, idx, qkv, seg, held=()):
    _, pieces, rows, shard, width = qkv.shape
    heads = width // HEAD_DIM
    pairs = count * (pieces * shard) ** 2
    return call(
        functools.partial(attend_body, start), "attend", (cnt, idx), (count,),
        [(qkv, along((3, pieces, 1, shard, width), 2, start)), (seg, along((1, pieces, shard), 0, start))],
        [
            ((pieces, rows, shard, width), BF16, along((pieces, 1, shard, width), 1, start)),
            ((count, shard, width), BF16, along((1, shard, width))),
            ((2, count, shard, width), BF16, along((2, 1, shard, width), 1)),
            ((rows, pieces, 8, shard), F32, along((1, pieces, 8, shard), 0, start)),
        ],
        [
            pltpu.VMEM((pieces, width, shard), BF16),
            pltpu.VMEM((pieces, shard, 128), F32),
            pltpu.VMEM((pieces, width, heads * shard), BF16),
            pltpu.VMEM((pieces, width, shard), F32),
        ],
        held=list(zip(held, (0, 3)))
    )


def attend_back_body(
    start, cnt_ref, idx_ref, qkv_ref, o_ref, do0, do1, do2, do3, lse_ref, seg_ref, cos_ref, sin_ref, w_ref,
    g_ref, p0_ref, p1_ref, p2_ref, p3_ref, kt, segk, dk, dv, dqt, qmt, gmt, qst, gst, low,
):
    row = pl.program_id(0) + start
    _, pieces, _, shard, width = qkv_ref.shape
    heads = width // HEAD_DIM

    @pl.when(pl.program_id(0) == 0)
    def _():
        qmt[...] = jnp.zeros_like(qmt)
        gmt[...] = jnp.zeros_like(gmt)

    seg_columns(seg_ref[0], segk)
    dk[...] = jnp.zeros_like(dk)
    dv[...] = jnp.zeros_like(dv)
    lane = lax.broadcasted_iota(jnp.int32, (shard, width), 1) // HEAD_DIM
    chosen = lax.broadcasted_iota(jnp.int32, (8, width), 1) // HEAD_DIM
    chosen = (chosen == lax.broadcasted_iota(jnp.int32, (8, width), 0)).astype(BF16)
    for j, do_ref in enumerate((do0, do1, do2, do3)):
        kt[j] = qkv_ref[1, j, 0].T
        q, do = qkv_ref[0, j, 0], do_ref[...].reshape(shard, width)
        qt, gt = q.T, do.T
        for h in range(heads):
            at, qa = slice(h * HEAD_DIM, (h + 1) * HEAD_DIM), slice(h * shard, (h + 1) * shard)
            qmt[j, at, qa] = qt[at]
            gmt[j, at, qa] = gt[at]
            qst[j, qa] = jnp.where(lane == h, q, jnp.zeros_like(q))
            gst[j, qa] = jnp.where(lane == h, do, jnp.zeros_like(do))
        prod = do.astype(F32) * o_ref[j, 0].astype(F32)
        high = prod.astype(BF16)
        low[j] = dot(chosen, high, 1, 1) + dot(chosen, (prod - high.astype(F32)).astype(BF16), 1, 1)

    @pl.loop(0, pieces)
    def _(piece):
        back_piece(
            row * pieces + piece, piece, cnt_ref, idx_ref, qkv_ref.at[1], qkv_ref.at[2], lse_ref, seg_ref,
            kt, segk, dk, dv, dqt, qmt, gmt, qst, gst, low,
        )

    for j, ref in ((1, p1_ref), (3, p3_ref), (0, p0_ref), (2, p2_ref)):
        grad_q = turn(dqt[j].T * HEAD_DIM**-0.5, cos_ref[j], -sin_ref[j]).astype(BF16)
        grad_k = turn(dk[j] * (1 / LOG2E), cos_ref[j], -sin_ref[j]).astype(BF16)
        grad = jnp.concatenate([grad_q, grad_k, dv[j].astype(BF16)], axis=1)
        g_ref[j, 0] = grad
        ref[0] = dot(grad, w_ref[...]).astype(BF16)


def back_piece(
    at_q, piece, cnt_ref, idx_ref, k_ref, v_ref, lse_ref, seg_ref, kt, segk, dk, dv, dqt, qmt, gmt, qst, gst, low
):
    pieces, _, shard, width = k_ref.shape
    heads = width // HEAD_DIM
    lse, delta = lse_ref[0, piece], low[piece]
    seg_q = seg_ref[0, pl.ds(piece, 1)].astype(F32)

    def run(count):
        @pl.when(cnt_ref[at_q] == count)
        def _():
            places = [idx_ref[at_q * pieces + t] for t in range(count)]
            qm, gm = qmt[piece], gmt[piece]
            later = dot(k_ref[places[0], 0], qm), dot(v_ref[places[0], 0], gm)
            out = [None] * heads
            for t in range(count):
                s, dp = later
                j = places[t]
                if t + 1 < count:
                    later = dot(k_ref[places[t + 1], 0], qm), dot(v_ref[places[t + 1], 0], gm)
                col = segk[j]
                same = jnp.concatenate([col] * (shard // 128), axis=1) == seg_q
                ps, dss = [], []
                for h in range(heads):
                    at, qa = slice(h * HEAD_DIM, (h + 1) * HEAD_DIM), slice(h * shard, (h + 1) * shard)
                    p = jnp.exp2(jnp.where(same, s[:, qa] - lse[h : h + 1], NEG))
                    ds = (p * (dp[:, qa] - delta[h : h + 1])).astype(BF16)
                    ps.append(p.astype(BF16))
                    dss.append(ds)
                    found = dot(kt[j, at], ds)
                    out[h] = found if t == 0 else out[h] + found
                dv[j] += dot(jnp.concatenate(ps, axis=1), gst[piece])
                dk[j] += dot(jnp.concatenate(dss, axis=1), qst[piece])
            for h in range(heads):
                dqt[piece, h * HEAD_DIM : (h + 1) * HEAD_DIM] = out[h]

    for count in range(1, pieces + 1):
        run(count)


def attend_back(start, count, cnt, idx, qkv, o, do, lse, seg, cos_tab, sin_tab, weight, held=(), deps=()):
    _, pieces, rows, shard, width = qkv.shape
    model = weight.shape[1]
    heads = width // HEAD_DIM
    table = fixed((pieces, shard, 128))
    pairs = count * (pieces * shard) ** 2
    square, wide = (pieces, width, heads * shard), (pieces, shard, width)
    one = along((1, shard, width), 0, start)
    return call(
        functools.partial(attend_back_body, start), "attend_back", (cnt, idx), (count,),
        [(qkv, along((3, pieces, 1, shard, width), 2, start)), (o, along((pieces, 1, shard, width), 1, start))]
        + [(do[0], one), (do[1], one), (do[2], along((1, 1, shard, width), 1, start)), (do[3], one)]
        + [(lse, along((1, pieces, 8, shard), 0, start)), (seg, along((1, pieces, shard), 0, start))]
        + [(cos_tab, table), (sin_tab, table), (weight, fixed(weight.shape))],
        [((pieces, rows, shard, 3 * width), BF16, along((pieces, 1, shard, 3 * width), 1, start))]
        + [((count, shard, model), BF16, along((1, shard, model)))] * pieces,
        [
            pltpu.VMEM((pieces, width, shard), BF16),
            pltpu.VMEM((pieces, shard, 128), F32),
            pltpu.VMEM(wide, F32),
            pltpu.VMEM(wide, F32),
            pltpu.VMEM((pieces, width, shard), F32),
            pltpu.VMEM(square, BF16),
            pltpu.VMEM(square, BF16),
            pltpu.VMEM((pieces, heads * shard, width), BF16),
            pltpu.VMEM((pieces, heads * shard, width), BF16),
            pltpu.VMEM((pieces, 8, shard), F32),
        ],
        held=[(array, 0) for array in held], deps=deps
    )


def middle_body(
    order_ref, a0, a1, a2, a3, w0, w1, w2, w3, stream_ref, bias_ref, gain_ref, shift_ref, mid_ref, low_ref, all_ref,
):
    _, shard, model = stream_ref.shape
    total = 0.0
    for n, (a, w) in enumerate(((a0, w0), (a1, w1), (a2, w2), (a3, w3))):
        values = a[...].reshape(shard, a.shape[-1])
        total = total + dot(values, w[...])
        all_ref[0, :, n * a.shape[-1] : (n + 1) * a.shape[-1]] = values
    mid = stream_ref[0] + (total + line(bias_ref))
    hat, _ = centre(mid)
    mid_ref[0] = mid
    low_ref[0] = (hat * line(gain_ref) + line(shift_ref)).astype(BF16)


def out_blocks(weight, parts):
    width = weight.shape[0] // parts

    def block(i):
        return pl.BlockSpec((width, weight.shape[1]), lambda g, o: (o[i], 0))

    return [(weight, block(i)) for i in range(parts)]


def middle_norm(start, count, order, attended, weight, stream, vecs, held=()):
    rows, shard, model = stream.shape
    parts = len(attended)
    width = model // parts
    block, one = along((1, shard, model), 0, start), along((1, shard, width))
    first = [along((1, 1, shard, width), 1, start), one, along((1, 1, shard, width), 1), one]
    return call(
        middle_body, "middle", (order,), (count,),
        list(zip(attended, first)) + out_blocks(weight, parts) + [(stream, block)]
        + [(vec, fixed(vec.shape)) for vec in vecs],
        [
            (stream.shape, F32, block),
            ((count, shard, model), BF16, along((1, shard, model))),
            (stream.shape, BF16, block),
        ],
        held=list(zip(held, (0, 2)))
    )


def cot_body(blk_ref, a_ref, b_ref, up_ref, down_ref, g_ref, up_out, down_out, both_ref):
    tokens = a_ref.shape[0]
    down = down_ref[...]

    @pl.when(pl.program_id(0) == 0)
    def _():
        both_ref[0:tokens] = a_ref[...]
        both_ref[tokens:] = b_ref[...]

    g_ref[0:tokens] = dot(a_ref[...], down, 1, 1).astype(BF16)
    g_ref[tokens:] = dot(b_ref[...], down, 1, 1).astype(BF16)
    up_out[...] = up_ref[...]
    down_out[...] = down


def cot_down(blk, own, other, up, down, picked, half):
    tokens, model = own.shape
    steps = half // BLOCK
    column = along((2 * tokens, BLOCK), 1)
    if picked:
        up_at, down_at = along((model, BLOCK), 1), along((BLOCK, model))
    else:
        up_at = pl.BlockSpec((model, BLOCK), lambda g, b: (0, b[g]))
        down_at = pl.BlockSpec((BLOCK, model), lambda g, b: (b[g], 0))
    return call(
        cot_body, "cot_down", (blk,), (steps,),
        [(own, fixed(own.shape)), (other, fixed(own.shape)), (up, up_at), (down, down_at)],
        [
            ((2 * tokens, half), BF16, column),
            ((model, half), BF16, along((model, BLOCK), 1)),
            ((half, model), BF16, along((BLOCK, model))),
            ((2 * tokens, model), BF16, fixed((2 * tokens, model))),
        ]
    )


def hidden_body(blocks, blk_ref, *refs):
    pieces, refs = refs[:-11], refs[-11:]
    g_ref, up_ref, row_ref, bias_ref, act_ref, grad_ref, sum_ref, both_ref, part_ref, other_ref, held = refs
    sizes = [ref.shape[0] * ref.shape[1] for ref in pieces]
    starts = [sum(sizes[:n]) for n in range(len(sizes))]
    step = pl.program_id(0)

    @pl.when(step == 0)
    def _():
        for ref, at, size in zip(pieces, starts, sizes):
            both_ref[at : at + size] = ref[...].reshape(size, ref.shape[2])

    @pl.when(step < blocks)
    def _():
        up = up_ref[...]
        bias = bias_ref[...].astype(F32)
        total = 0.0
        later = dot(pieces[0][...].reshape(sizes[0], -1), up)
        for n, (start, size) in enumerate(zip(starts, sizes)):
            at = slice(start, start + size)
            v = later + bias
            if n + 1 < len(pieces):
                later = dot(pieces[n + 1][...].reshape(sizes[n + 1], -1), up)
            square = v * v
            tanh = jnp.tanh(v * (GELU_A + GELU_B * square))
            gate = 0.5 + 0.5 * tanh
            act = v * gate
            slope = gate + act * ((1.0 - tanh) * (GELU_A + 3.0 * GELU_B * square))
            grad = (slope * g_ref[at].astype(F32)).astype(BF16)
            act_ref[at] = act.astype(BF16)
            grad_ref[at] = grad
            held[step, at] = grad
            total = total + jnp.sum(grad.astype(F32), axis=0, keepdims=True)
        sum_ref[...] = total

    @pl.when(step >= blocks)
    def _():
        grad = jnp.concatenate([held[n] for n in range(blocks)], axis=1)
        found = dot(grad, row_ref[...], 1, 1).astype(BF16)
        part_ref[...] = found[: part_ref.shape[0]]
        other_ref[...] = found[part_ref.shape[0] :]


def hidden_units(blk, pieces, grads, up, bias):
    model = pieces[0].shape[2]
    tokens, half = grads.shape
    blocks, more = half // BLOCK, model // BLOCK

    def first(g):
        return jnp.minimum(g, blocks - 1)

    def second(g):
        return jnp.maximum(g - blocks, 0)

    column = pl.BlockSpec((tokens, BLOCK), lambda g, b: (0, first(g)))
    line = pl.BlockSpec((1, BLOCK), lambda g, b: (0, first(g)))
    return call(
        functools.partial(hidden_body, blocks), "hidden", (blk,), (blocks + more,),
        [(piece, fixed(piece.shape)) for piece in pieces]
        + [
            (grads, column),
            (up, pl.BlockSpec((model, BLOCK), lambda g, b: (0, first(g)))),
            (up, pl.BlockSpec((BLOCK, half), lambda g, b: (second(g), 0))),
            (bias, pl.BlockSpec((1, BLOCK), lambda g, b: (0, b[first(g)]))),
        ],
        [
            (grads.shape, BF16, column),
            (grads.shape, BF16, column),
            ((1, half), F32, line),
            ((tokens, model), BF16, fixed((tokens, model))),
            ((tokens // 2, model), BF16, pl.BlockSpec((tokens // 2, BLOCK), lambda g, b: (0, second(g)))),
            ((tokens // 2, model), BF16, pl.BlockSpec((tokens // 2, BLOCK), lambda g, b: (0, second(g)))),
        ],
        [pltpu.VMEM((blocks, tokens, BLOCK), BF16)]
    )


def sent_body(other_ref, tok_ref, cot_ref, grad_ref, act_ref, up_ref, down_ref):
    up_ref[...] = dot(tok_ref[...], grad_ref[...], 0, 0).astype(BF16)
    down_ref[...] = dot(act_ref[...], cot_ref[...], 0, 0).astype(BF16)


def sent_grads(other, tokens, cot, grad, act, steps):
    count, model = tokens.shape
    half = grad.shape[1]
    size = half // (2 * steps)
    wide = half // steps
    return call(
        sent_body, "sent_grads", (other,), (steps,),
        [
            (tokens, fixed(tokens.shape)),
            (cot, fixed(cot.shape)),
            (grad, along((count, wide), 1)),
            (act, pl.BlockSpec((count, size), lambda g, o: (0, 2 * g + o[0]))),
        ],
        [((model, half), BF16, along((model, wide), 1)), ((half // 2, model), BF16, along((size, model)))],
    )


def feed_body(order_ref, act_ref, down_ref, att_ref, low_ref, half_ref, cot_ref, feed_ref, other_ref, out_ref, keep_ref, kept_ref):
    parts = order_ref.shape[0]
    width = att_ref.shape[1] // parts
    feed = dot(act_ref[...], down_ref[...]).astype(BF16)
    feed_ref[...] = feed[: feed_ref.shape[0]]
    other_ref[...] = feed[feed_ref.shape[0] :]
    kept_ref[...] = dot(half_ref[...], cot_ref[...], 0, 0).astype(BF16)
    grad = dot(att_ref[...], low_ref[...], 0, 0).astype(BF16)
    step, steps = pl.program_id(0), pl.num_programs(0)

    def write(ref):
        for n in range(parts):
            at = pl.multiple_of(order_ref[n] * width, width)
            ref[pl.ds(at, width)] = grad[n * width : (n + 1) * width]

    @pl.when(2 * step < steps)
    def _():
        write(out_ref)

    @pl.when(2 * step >= steps)
    def _():
        write(keep_ref)


def feed_grads(order, act, down, attended, low, cot, c_at, x_at, deps=()):
    tokens, half = act.shape
    own, model = attended.shape
    steps = model // BLOCK
    place = jnp.concatenate([order, jnp.stack([c_at, x_at]).astype(jnp.int32)])
    size = half // (2 * steps)

    def body(place_ref, *refs):
        feed_body(place_ref.at[0 : order.shape[0]], *refs)

    def low_at(g, p):
        c = p[order.shape[0]]
        mine = 2 * g >= steps
        return 0, jnp.where(mine, c * (steps // 2) + g - steps // 2, (1 - c) * (steps // 2) + g)

    return call(
        body, "feed_grads", (place,), (steps,),
        [
            (act, fixed(act.shape)),
            (down, along((half, BLOCK), 1)),
            (attended, fixed(attended.shape)),
            (low, pl.BlockSpec((own, BLOCK), low_at)),
            (act, pl.BlockSpec((tokens, size), lambda g, p: (0, 2 * g + p[order.shape[0] + 1]))),
            (cot, fixed(cot.shape)),
        ],
        [
            ((own, model), BF16, along((own, BLOCK), 1)),
            ((own, model), BF16, along((own, BLOCK), 1)),
            ((model, model // 2), BF16, pl.BlockSpec((model, BLOCK), lambda g, p: (0, jnp.minimum(g, steps // 2 - 1)))),
            ((model, model // 2), BF16, pl.BlockSpec((model, BLOCK), lambda g, p: (0, jnp.maximum(g - steps // 2, 0)))),
            ((half // 2, model), BF16, along((size, model))),
        ],
        deps=deps,
    )


def middle_back_body(
    order_ref, part_ref, sent_ref, mid_ref, cot_ref, gain_ref, w0, w1, w2, w3,
    grad_ref, low_ref, att0_ref, att1_ref, far_ref, sums_ref,
):
    grad = part_ref[...].astype(F32) + sent_ref[...].astype(F32)
    hat, inverse = centre(mid_ref[0])
    cot = cot_ref[0].astype(F32)
    total = cot + norm_back(grad, line(gain_ref), hat, inverse)
    low = total.astype(BF16)
    grad_ref[0] = total
    low_ref[0] = low
    far_ref[0, 0] = dot(low, w2[...], 1, 1).astype(BF16)
    far_ref[1, 0] = dot(low, w3[...], 1, 1).astype(BF16)
    att1_ref[0] = dot(low, w1[...], 1, 1).astype(BF16)
    att0_ref[0] = dot(low, w0[...], 1, 1).astype(BF16)

    @pl.when(pl.program_id(0) == 0)
    def _():
        sums_ref[...] = jnp.zeros_like(sums_ref)

    sums_ref[0:1] += jnp.sum(grad * hat, axis=0, keepdims=True)
    sums_ref[1:2] += jnp.sum(grad, axis=0, keepdims=True)
    sums_ref[2:3] += jnp.sum(low.astype(F32), axis=0, keepdims=True)
    sums_ref[3:4] += jnp.sum(cot, axis=0, keepdims=True)


def middle_back(order, both, sent, mid, cot, gain, weight, parts, deps=()):
    rows, shard, model = mid.shape
    width = model // parts
    block, one = along((1, shard, model)), along((1, shard, width))
    flat = pl.BlockSpec((shard, model), lambda g, o: (g, 0))
    return call(
        middle_back_body, "middle_back", (order,), (rows,),
        [(both, flat), (sent, flat), (mid, block), (cot, block), (gain, fixed(gain.shape))] + out_blocks(weight, parts),
        [
            (mid.shape, F32, block),
            (mid.shape, BF16, block),
            ((rows, shard, width), BF16, one),
            ((rows, shard, width), BF16, one),
            ((2, rows, shard, width), BF16, along((2, 1, shard, width), 1)),
            ((8, model), F32, fixed((8, model))),
        ],
        deps=deps
    )


def norm1_back_body(start, part_ref, near_ref, far_ref, stream_ref, mid_ref, gain_ref, seg_ref, in_ref, shift_ref, sums_ref):
    grad = part_ref[0].astype(F32) + near_ref[0].astype(F32) + far_ref[0].astype(F32)
    hat, inverse = centre(stream_ref[0])
    total = mid_ref[0] + norm_back(grad, line(gain_ref), hat, inverse)
    in_ref[0] = total.astype(BF16)
    seg = seg_ref[pl.ds(pl.program_id(0) + start, 1)]
    slots = lax.broadcasted_iota(jnp.int32, (SEGS, seg.shape[-1]), 0) == seg
    onehot = slots.astype(F32).astype(BF16)
    shift_ref[0] = dot(jnp.concatenate([onehot, onehot], axis=1), split_low(total))

    @pl.when(pl.program_id(0) == 0)
    def _():
        sums_ref[...] = jnp.zeros_like(sums_ref)

    sums_ref[0:1] += jnp.sum(grad * hat, axis=0, keepdims=True)
    sums_ref[1:2] += jnp.sum(grad, axis=0, keepdims=True)


def norm1_back(start, count, own, near, far, stream, mid, gain, seg, held=(), deps=()):
    rows, shard, model = stream.shape
    block, own_block = along((1, shard, model), 0, start), along((1, shard, model))
    return call(
        functools.partial(norm1_back_body, start), "norm1_back", (), (count,),
        [(own, own_block), (near, own_block), (far, own_block), (stream, block), (mid, block), (gain, fixed(gain.shape))]
        + [(seg, fixed(seg.shape))],
        [
            (stream.shape, BF16, block),
            ((count, SEGS, model), F32, along((1, SEGS, model))),
            ((8, model), F32, fixed((8, model))),
        ],
        held=[(array, 0) for array in held], deps=deps
    )


def exchange(own, one, far):
    return [own, swap(one, "c"), far, swap(far[1], "c")]


def tie(*values):
    return lax.optimization_barrier(values)


def cut(values, index, size, axis):
    return lax.dynamic_slice_in_dim(values, index * size, size, axis)


def add_low(kept, sent):
    return (kept.astype(F32) + sent.astype(F32)).astype(BF16)


def ordered(at, own, other, axis):
    return jnp.where(at == 0, jnp.concatenate([own, other], axis), jnp.concatenate([other, own], axis))


def wide_body(blocks, at_ref, d0, d1, u0, u1, down_ref, up_ref):
    c_at = at_ref[0]
    width = up_ref.shape[1] // (4 * blocks)
    size = d0.shape[0]
    for c in range(2):
        mine = c_at == c
        down_ref[c * size : (c + 1) * size] = jnp.where(mine, d0[...], d1[...]).astype(F32)
        up = jnp.where(mine, u0[...], u1[...]).astype(F32)
        for b in range(2 * blocks):
            up_ref[:, (2 * b + c) * width : (2 * b + c + 1) * width] = up[:, b * width : (b + 1) * width]


def finish_wide(c_at, dp, piece, down, up, deps=()):
    rows, model = up[0].shape[0], down[0].shape[1]
    depth, size = dp // 2, down[0].shape[0]
    if piece % 128 == 0:
        shapes = [(2 * size, model), (rows, 2 * dp * piece)]
        return call(
            functools.partial(wide_body, depth), "finish_wide", (c_at.astype(jnp.int32)[None],), (1,),
            [(array, fixed(array.shape)) for array in (*down, *up)], [(shape, F32, fixed(shape)) for shape in shapes],
            deps=deps,
        )
    down_done = ordered(c_at, *down, 0).astype(F32)
    up_done = ordered(c_at, up[0][None], up[1][None], 0).reshape(2, rows, dp, piece).transpose(1, 2, 0, 3)
    return down_done, up_done.reshape(rows, 2 * dp * piece).astype(F32)


def late_body(at_ref, l0, l1, qkv_ref, out_ref):
    half = out_ref.shape[1] // 2
    wide = half // 2
    for c in range(2):
        late = jnp.where(at_ref[0] == c, l0[...], l1[...]).astype(F32)
        out_ref[:, c * half : (c + 1) * half] = late[:, 6 * wide :]
        for y in range(2):
            for n in range(3):
                at = n * 4 * wide + (2 * y + c) * wide
                qkv_ref[:, at : at + wide] = late[:, (3 * y + n) * wide : (3 * y + n + 1) * wide]


def finish_late(c_at, model, piece, late, parts):
    rows = late[0].shape[0]
    if piece % 128 == 0:
        return call(
            late_body, "finish_late", (c_at.astype(jnp.int32)[None],), (1,),
            [(array, fixed(array.shape)) for array in late],
            [((rows, size), F32, fixed((rows, size))) for size in (3 * model, model)],
        )
    both = ordered(c_at, late[0][None], late[1][None], 0)
    width = model // parts
    qkv_done = both[:, :, : 6 * width].reshape(2, rows, 2, 3, width).transpose(1, 3, 2, 0, 4)
    qkv_done = qkv_done.reshape(rows, 3 * model).astype(F32)
    return qkv_done, jnp.concatenate([both[0, :, 6 * width :], both[1, :, 6 * width :]], axis=1).astype(F32)


def local(
    inputs, segment_ids, doc_times, time_weight, time_bias, norm1_gain, norm1_bias, qkv_weight, qkv_bias,
    out_weight, out_bias, norm2_gain, norm2_bias, up_weight, up_bias, down_weight, down_bias, cotangent,
    *, dp,
):
    rows, shard, model = inputs.shape
    parts = 4
    tokens = rows * shard
    hidden_width = up_weight.shape[1]
    width = model // parts
    depth = dp // 2
    half = hidden_width // 2
    piece = half // dp
    z_at, x_at, y_at, c_at = (lax.axis_index(name) for name in ("z", "x", "y", "c"))
    me = 2 * y_at + c_at

    groups = [(0, rows - 1), (rows - 1, 1)] if rows > 1 else [(0, 1)]
    seg_one, seg_two = swap(segment_ids, "c"), swap(segment_ids, "y")
    seg_three = swap(seg_two, "c")
    features = time_features(doc_times.reshape(rows * SEGS), jnp.arange(TEMB), TEMB // 2)
    time_shift = dot(features, time_weight).reshape(rows, SEGS, model)
    own1, one1, two1, stream = [], [], [], None
    for start, count in groups:
        held = () if stream is None else (stream,)
        stream, low = norm1(
            start, count, inputs, segment_ids, time_shift, (time_bias, norm1_gain, norm1_bias), held
        )
        if stream is not None and not own1:
            low, seg_one, seg_two, seg_three = tie(low, seg_one, seg_two, seg_three)
        own1.append(low)
        two1.append(swap(low, "y"))
        one1.append(swap(low, "c"))
    segs = jnp.stack([segment_ids, seg_one, seg_two, seg_three], axis=1)

    me, x_at, z_at, c_at, y_at, own1[-1], segs = tie(me, x_at, z_at, c_at, y_at, own1[-1], segs)
    order = [me ^ i for i in range(parts)]
    order_list = jnp.stack(order).astype(jnp.int32)
    me_list = order_list[:1]
    low_id, high_id = segs.min(axis=2), segs.max(axis=2)
    act = (low_id[:, :, None] <= high_id[:, None, :]) & (low_id[:, None, :] <= high_id[:, :, None])
    places = jnp.arange(parts, dtype=jnp.int32)
    rank = jnp.cumsum(act.astype(jnp.int32), axis=2) - 1
    chosen = act[..., None] & (rank[..., None] == places)
    idx = jnp.sum(jnp.where(chosen, places[:, None], 0), axis=2).astype(jnp.int32).reshape(-1)
    cnt = jnp.sum(act.astype(jnp.int32), axis=2).reshape(-1)
    positions = jnp.stack([o * shard + jnp.arange(shard, dtype=jnp.int32) for o in order])
    cos_tab, sin_tab = rotary_tables(positions, HEAD_DIM)

    cot = cotangent.reshape(tokens, model)
    cot_other = swap(cot, "c")
    if piece % BLOCK == 0:
        blk = (jnp.arange(dp)[:, None] * 2 + c_at) * (piece // BLOCK) + jnp.arange(piece // BLOCK)
        blk = blk.reshape(-1).astype(jnp.int32)
        up_from, down_from = up_weight, down_weight
    else:
        blk = jnp.zeros((half // BLOCK,), jnp.int32)
        up_from = lax.dynamic_index_in_dim(up_weight.reshape(model, dp, 2, piece), c_at, 2, keepdims=False)
        down_from = lax.dynamic_index_in_dim(down_weight.reshape(dp, 2, piece, model), c_at, 1, keepdims=False)
        up_from, down_from = up_from.reshape(model, half), down_from.reshape(half, model)
    grad_act, up_own, down_own, cot_both = cot_down(
        blk, cot, cot_other, up_from, down_from, piece % BLOCK != 0, half
    )
    up_bias_own, bias_blk = up_bias.reshape(1, hidden_width), blk
    if piece % BLOCK:
        up_bias_own = lax.dynamic_index_in_dim(up_bias.reshape(dp, 2, piece), c_at, 1, keepdims=False)
        up_bias_own, bias_blk = up_bias_own.reshape(1, half), jnp.arange(half // BLOCK, dtype=jnp.int32)

    qkv_line = qkv_bias.reshape(1, 3 * model)
    near = (own1, one1)
    qkv, qkv_own = project_qkv(
        0, 0, parts, rows, me_list, near, qkv_weight, qkv_line, cos_tab, sin_tab, (), (grad_act, cnt, idx)
    )
    o, lse, attended, three1 = None, None, [], []
    for n, (start, count) in enumerate(groups):
        if n == 0:
            two1[0], qkv = tie(two1[0], qkv)
        else:
            two1[n], o = tie(two1[n], o)
        three1.append(swap(two1[n], "c"))
        (qkv,) = project_qkv(
            1, start, parts, rows, me_list, ([two1[n]], [three1[n]]), qkv_weight, qkv_line, cos_tab, sin_tab, (qkv,),
            () if o is None else (o,),
        )
        held = () if o is None else (o, lse)
        o, out_one, out_far, lse = attend(start, count, cnt, idx, qkv, segs, held)
        attended.append((out_one, swap(out_far, "y")))
    held, normed2, normed2_other = (), [], []
    for (start, count), values in zip(groups, attended):
        far, o = tie(values[1], o)
        values = exchange(o, values[0], far)
        middle, low, attended_all = middle_norm(
            start, count, order_list, values, out_weight, stream, (out_bias, norm2_gain, norm2_bias), held
        )
        held = (middle, attended_all)
        normed2.append(low)
        normed2_other.append(swap(low, "c"))

    active, grad_hidden, up_b, normed2_both, part2, part2_other = hidden_units(
        bias_blk, normed2 + normed2_other, grad_act, up_own, up_bias_own
    )
    part2_sent = swap(part2_other, "c")
    grad_middle, grad_middle_low, att0, att1, far, sums2 = middle_back(
        order_list, part2, part2_sent, middle, cotangent, norm2_gain, out_weight, parts
    )
    far = swap(far, "y")
    sums2 = sums2[:4]

    active, grad_hidden, att0 = tie(active, grad_hidden, att0)
    up_rows = model // dp
    small_blocks = piece % BLOCK != 0 or depth != model // BLOCK
    if small_blocks:
        up_grad = dot(normed2_both, grad_hidden, 0, 0).astype(BF16)
        down_out = dot(active, cot_both, 0, 0).astype(BF16).reshape(depth, 2, piece, model)
        down_kept = lax.dynamic_index_in_dim(down_out, x_at, 1, keepdims=False).reshape(half // 2, model)
        down_out = lax.dynamic_index_in_dim(down_out, 1 - x_at, 1, keepdims=False).reshape(half // 2, model)
    else:
        up_grad, down_out = sent_grads(
            1 - x_at[None].astype(jnp.int32), normed2_both, cot_both, grad_hidden, active, depth
        )
    up_grad, down_out, far = tie(up_grad, down_out, far)
    grad_o = exchange(att0, att1, far)
    up_z = lax.psum_scatter(up_grad, "z", scatter_dimension=0, tiled=True)
    down_sent = swap(down_out[: half // 4], "x")
    if small_blocks:
        feed = dot(active, down_own).astype(BF16)
        feed, feed_other = feed[:tokens], feed[tokens:]
        out_grad = dot(attended_all.reshape(tokens, model), grad_middle_low.reshape(tokens, model), 0, 0).astype(BF16)
        out_grad = jnp.concatenate([cut(out_grad, o_at, width, 0) for o_at in order], axis=0)
        out_sent, out_grad = (cut(out_grad, at, model // 2, 1) for at in (1 - c_at, c_at))
    else:
        feed, feed_other, out_sent, out_grad, down_kept = feed_grads(
            order_list, active, down_own, attended_all.reshape(tokens, model), grad_middle_low.reshape(tokens, model),
            cot_both, c_at, x_at, (far, down_out),
        )
    feed, feed_other, out_sent, out_grad, down_kept, down_sent, down_out, *grad_o = tie(
        feed, feed_other, out_sent, out_grad, down_kept, down_sent, down_out, *grad_o
    )
    down_late = swap(down_out[half // 4 :], "x")
    out_sent, feed_sent = swap(out_sent, "c"), swap(feed_other, "c")

    back = []
    (start, count), rest = groups[0], groups[1:]
    found = attend_back(start, count, cnt, idx, qkv, o, grad_o, lse, segs, cos_tab, sin_tab, qkv_own)
    *found, down_late, out_sent, feed_sent = tie(*found, down_late, out_sent, feed_sent)
    grad_qkv, own, one, two, three = found
    there = add_low(two, swap(three, "c"))
    down_x = add_low(down_kept, jnp.concatenate([down_sent, down_late], axis=0))
    down_z = lax.psum_scatter(down_x, "z", scatter_dimension=0, tiled=True)
    out_c = add_low(out_grad, out_sent).reshape(depth, 2 * up_rows, model // 2)
    out_sent = cut(out_c, 1 - x_at, up_rows, 1)
    there, down_x, out_sent = tie(there, down_x, out_sent)
    far, near = swap(there, "y"), swap(one, "c")
    out_sent = swap(out_sent, "x")
    if rest:
        (start, count), = rest
        found = attend_back(
            start, count, cnt, idx, qkv, o, grad_o, lse, segs, cos_tab, sin_tab, qkv_own, (grad_qkv,),
            (there, down_x),
        )
        *found, far, up_z, out_sent = tie(*found, far, up_z, out_sent)
        back.append((own, near, far))
        grad_qkv, own, one, two, three = found
        there, far = tie(add_low(two, swap(three, "c")), far)
        far, near = swap(there, "y"), swap(one, "c")
        grad_qkv, there = tie(grad_qkv, there)
    qkv_out, qkv_kept, qkv_b = qkv_grads(x_at, [own1, one1, two1, three1], grad_qkv, depth)
    qkv_out, qkv_kept, far, out_sent, out_c, up_z = tie(qkv_out, qkv_kept, far, out_sent, out_c, up_z)
    back.append((own, near, far))
    qkv_sent = swap(qkv_out, "x")
    out_x = add_low(cut(out_c, x_at, up_rows, 1), out_sent)
    out_sent = cut(out_x, 1 - y_at, width, 2)
    qkv_out, up_out = tie(qkv_out, cut(up_z, 1 - x_at, up_rows, 0))
    up_sent = swap(up_out, "x")
    held, grad_shift, sums1 = (), [], 0.0
    for (start, count), values in zip(groups, back):
        input_grad, found, sums = norm1_back(
            start, count, *values, stream, grad_middle, norm1_gain, segment_ids, held, (qkv_kept, up_out)
        )
        if not held:
            input_grad, out_sent = tie(input_grad, out_sent)
            out_sent = swap(out_sent, "y")
        held = (input_grad,)
        grad_shift.append(found.reshape(count * SEGS, model))
        sums1 = sums1 + sums[:2]

    up_b = up_b.reshape(dp, 1, piece)
    up_b = jnp.where(jnp.arange(2)[:, None] == c_at, up_b, 0.0).reshape(-1, model)
    qkv_b = jnp.where(jnp.arange(parts)[:, None] == me, qkv_b.reshape(3, 1, width), 0.0).reshape(3, model)
    times = doc_times.reshape(1, rows * SEGS)
    times = jnp.concatenate([times // 32, times % 32], axis=1).astype(F32)
    times = jnp.tile(jnp.pad(times, ((0, 0), (0, width - times.shape[1]))), (1, parts))
    small = jnp.concatenate(grad_shift + [sums1, sums2, qkv_b, up_b, times], axis=0).astype(BF16)
    small_sent = swap(cut(small, 1 - c_at, 2 * width, 1), "c")
    small = add_low(cut(small, c_at, 2 * width, 1), small_sent)
    small, qkv_sent, out_sent = tie(small, qkv_sent, out_sent)
    small = add_low(cut(small, y_at, width, 1), swap(cut(small, 1 - y_at, width, 1), "y"))
    small = ordered(x_at, small[None], swap(small, "x")[None], 0)
    out_x = add_low(cut(out_x, y_at, width, 2), out_sent)
    late = jnp.concatenate([add_low(qkv_kept, qkv_sent), out_x], axis=2)
    output = middle.reshape(tokens, model) + (feed.astype(F32) + feed_sent.astype(F32) + down_bias.astype(F32))
    output = output.astype(BF16).reshape(rows, shard, model)
    small, late = tie(small, late)
    if depth == 4:
        flat = small.reshape(2 * small.shape[1] * width // model, model)
        parts_z = [lax.dynamic_index_in_dim(late, z_at ^ n, 0, keepdims=False) for n in range(depth)]
        sent = [
            lax.ppermute(jnp.concatenate([parts_z[n], flat], axis=0), "z", [(i, i ^ n) for i in range(depth)])
            for n in range(1, depth)
        ]
        small, down_z, up_z, up_sent = tie(small, down_z, up_z, up_sent)
        up_x = add_low(cut(up_z, x_at, up_rows, 0), up_sent)
        down_sent, up_sent = swap(down_z, "y"), swap(up_x, "y")
        *sent, output, down_sent, up_sent = tie(*sent, output, down_sent, up_sent)
        late = sum(part[:up_rows].astype(F32) for part in sent) + parts_z[0].astype(F32)
        late = late.astype(BF16)
        small = jnp.stack([small] + [part[up_rows:].reshape(small.shape) for part in sent])
        small = jnp.stack([lax.dynamic_index_in_dim(small, z_at ^ n, 0, keepdims=False) for n in range(depth)])
    else:
        up_x = add_low(cut(up_z, x_at, up_rows, 0), up_sent)
        down_sent, up_sent = swap(down_z, "y"), swap(up_x, "y")
        late = lax.psum_scatter(late, "z", scatter_dimension=0, tiled=False)
        small = lax.all_gather(small, "z")
    small = small.reshape(dp, small.shape[2], width)

    late_sent = swap(late, "y")
    down_done, up_done = add_low(down_z, down_sent), add_low(up_x, up_sent)
    down_other, up_other = swap(down_done, "c"), swap(up_done, "c")
    dp_at = 2 * z_at + x_at
    all_times = small[:, -1, : 2 * rows * SEGS].astype(F32) * 0.25
    all_times = all_times[:, : rows * SEGS] * 32.0 + all_times[:, rows * SEGS :]
    shifts = small[:, : rows * SEGS].reshape(dp * rows * SEGS, width)
    columns = dp_at * (TEMB // dp) + jnp.arange(TEMB // dp)
    wanted = time_features(all_times.reshape(-1), columns, TEMB // 2)
    sums = jnp.sum(small[:, rows * SEGS : -1].astype(F32), axis=0)
    full = [dot(wanted, shifts, 0, 0), sums, jnp.sum(shifts.astype(F32), axis=0, keepdims=True)]
    full = jnp.concatenate(full, axis=0).astype(BF16)
    count = full.shape[0]
    full = jnp.pad(full, ((0, -count % 16), (0, 0)))
    full = ordered(y_at, full[None], swap(full, "y")[None], 0)
    full = ordered(c_at, full[None], swap(full, "c")[None], 0)
    full = full.transpose(2, 0, 1, 3).reshape(-1, model).astype(F32)
    time_w_done, sums = full[: TEMB // dp], full[TEMB // dp : count]

    def share(vector):
        return cut(vector.reshape(-1), dp_at, vector.size // dp, 0)

    vectors = [share(sums[n]) for n in (-1, 0, 1)] + [share(sums[6:9])]
    vectors += [share(sums[n]) for n in (4, 2, 3)] + [share(sums[9:-1]), share(sums[5])]
    both = ordered(y_at, late[None], late_sent[None], 0)
    late = jnp.concatenate([both[0, :, : 3 * width], both[1, :, : 3 * width], both[0, :, 3 * width :], both[1, :, 3 * width :]], axis=1)
    late_other = swap(late, "c")
    wide = finish_wide(c_at, dp, piece, (down_done, down_other), (up_done, up_other), (late, *vectors))
    down_done, up_done, late_other = tie(*wide, late_other)

    qkv_done, out_done = finish_late(c_at, model, piece, (late, late_other), parts)

    time_b_done, gain1_done, bias1_done, qkv_b_done, out_b_done, gain2_done, bias2_done, up_b_done, down_b_done = vectors
    return (
        output, input_grad, time_w_done, time_b_done, gain1_done, bias1_done, qkv_done, qkv_b_done,
        out_done, out_b_done, gain2_done, bias2_done, up_done, up_b_done, down_done, down_b_done,
    )


def solution(mesh):
    dp, seq = mesh.shape["dp"], mesh.shape["seq"]
    fine = Mesh(mesh.devices.reshape(dp // 2, 2, seq // 2, 2), ("z", "x", "y", "c"))
    rows, seqs = ("z", "x"), ("y", "c")
    placed = (P(rows, seqs, None), P(rows, seqs), P(rows, None)) + (P(),) * 14 + (P(rows, seqs, None),)
    vec, mat = P(rows), P(rows, None)
    return jax.shard_map(
        functools.partial(local, dp=dp),
        mesh=fine,
        in_specs=placed,
        out_specs=(
            P(rows, seqs, None), P(rows, seqs, None), mat, vec, vec, vec, mat, vec, mat, vec, vec, vec, mat, vec, mat, vec,
        ),
        check_vma=False,
    )
```

```python
import functools
import math

import jax
import jax.numpy as jnp
from jax import lax
from jax.experimental import pallas as pl
from jax.experimental.pallas import tpu as pltpu
from jax.sharding import Mesh, PartitionSpec as P

HEADS = 16
HEAD_DIM = 64
TEMB = 256
SEGS = 8
EPSILON = 1e-05
F32 = jnp.float32
BF16 = jnp.bfloat16
NEG = -1e30
LOG2E = math.log2(math.e)
GELU_A = math.sqrt(2.0 / math.pi)
GELU_B = GELU_A * 0.044715
BLOCK = 256
VMEM = 60 * 1024 * 1024


def swap(value, axis):
    return lax.ppermute(value, axis, [(0, 1), (1, 0)])


def time_features(doc_times, column, half_size):
    frequency = jnp.exp(-math.log(10000.0) * (column % half_size).astype(F32) / half_size)
    angles = doc_times.astype(F32)[..., None] * frequency
    return jnp.where(column < half_size, jnp.sin(angles), jnp.cos(angles)).astype(BF16)


def rotary_tables(positions, head_size):
    half_size = head_size // 2
    frequency = jnp.exp(-math.log(10000.0) * 2.0 * jnp.arange(half_size, dtype=F32) / head_size)
    angles = positions.astype(F32)[..., None] * frequency
    cos_tab, sin_tab = jnp.cos(angles), jnp.sin(angles)
    return (
        jnp.concatenate([cos_tab] * 4, axis=-1),
        jnp.concatenate([-sin_tab, sin_tab, -sin_tab, sin_tab], axis=-1),
    )


def dot(left_op, right_op, left_dim=1, right_dim=0):
    return lax.dot_general(
        left_op, right_op, (((left_dim,), (right_dim,)), ((), ())), preferred_element_type=F32
    )


def turn(values, cos_tab, sin_tab):
    slabs = []
    lane = lax.broadcasted_iota(jnp.int32, (values.shape[0], 128), 1)
    first = lane % HEAD_DIM < HEAD_DIM // 2
    for start in range(0, values.shape[1], 128):
        slab = values[:, start : start + 128]
        partner = jnp.where(
            first, pltpu.roll(slab, 128 - HEAD_DIM // 2, 1), pltpu.roll(slab, HEAD_DIM // 2, 1)
        )
        slabs.append(slab * cos_tab + partner * sin_tab)
    return jnp.concatenate(slabs, axis=1)


def split_low(values):
    high = values.astype(BF16)
    return jnp.concatenate([high, (values - high.astype(F32)).astype(BF16)], axis=0)


def centre(values):
    scale = 1.0 / values.shape[-1]
    centred = values - jnp.sum(values, axis=-1, keepdims=True) * scale
    spread = jnp.sum(centred * centred, axis=-1, keepdims=True) * scale
    inverse = lax.rsqrt(spread + EPSILON)
    return centred * inverse, inverse


def norm_back(grad, gain, hat, inverse):
    scale = 1.0 / grad.shape[-1]
    scaled = grad * gain
    mean = jnp.sum(scaled, axis=-1, keepdims=True) * scale
    along = jnp.sum(scaled * hat, axis=-1, keepdims=True) * scale
    return inverse * (scaled - mean - hat * along)


def call(body, name, prefetch, grid, ins, outs, scratch=(), deps=(), held=()):
    count = len(prefetch) + len(ins)
    extra = [array for array, _ in held] + list(deps)

    def kernel(*refs):
        body(*refs[:count], *refs[count + len(extra) :])

    return pl.pallas_call(
        kernel,
        grid_spec=pltpu.PrefetchScalarGridSpec(
            num_scalar_prefetch=len(prefetch),
            grid=grid,
            in_specs=[spec for _, spec in ins] + [pl.BlockSpec(memory_space=pl.ANY)] * len(extra),
            out_specs=[spec for _, _, spec in outs],
            scratch_shapes=list(scratch),
        ),
        out_shape=[jax.ShapeDtypeStruct(shape, kind) for shape, kind, _ in outs],
        input_output_aliases={count + n: out for n, (_, out) in enumerate(held)},
        compiler_params=pltpu.CompilerParams(vmem_limit_bytes=VMEM),
        name=name,
    )(*prefetch, *[array for array, _ in ins], *extra)


def line(ref):
    return ref[...].astype(F32).reshape(1, -1)


def fixed(shape):
    return pl.BlockSpec(shape, lambda *_: (0,) * len(shape))


def along(shape, axis=0, start=0):
    return pl.BlockSpec(shape, lambda g, *_: tuple(start + g if n == axis else 0 for n in range(len(shape))))


def norm1_body(start, x_ref, seg_ref, shift_ref, time_ref, gain_ref, bias_ref, stream_ref, low_ref):
    seg = seg_ref[pl.ds(pl.program_id(0) + start, 1)]
    slots = lax.broadcasted_iota(jnp.int32, (SEGS, seg.shape[-1]), 0) == seg
    onehot = slots.astype(F32).astype(BF16)
    shift = shift_ref[0] + line(time_ref)
    added = dot(jnp.concatenate([onehot, onehot], axis=0), split_low(shift), 0, 0)
    stream = x_ref[0].astype(F32) + added
    hat, _ = centre(stream)
    stream_ref[0] = stream
    low_ref[0] = (hat * line(gain_ref) + line(bias_ref)).astype(BF16)


def norm1(start, count, x, seg, shift, vecs, held=()):
    rows, shard, model = x.shape
    block = along((1, shard, model), 0, start)
    return call(
        functools.partial(norm1_body, start), "norm1", (), (count,),
        [(x, block), (seg, fixed(seg.shape)), (shift, along((1, SEGS, model), 0, start))]
        + [(vec, fixed(vec.shape)) for vec in vecs],
        [(x.shape, F32, block), ((count, shard, model), BF16, along((1, shard, model)))],
        held=[(array, 0) for array in held],
    )


def qkv_body(sizes, me_ref, *refs):
    count = 2 * len(sizes)
    pieces, (w_ref, bias_ref, cos_ref, sin_ref, out_ref), own = refs[:count], refs[count : count + 5], refs[count + 5 :]
    places = [(n, sum(sizes[:g]) + r, n * len(sizes) + g, r) for n in range(2) for g, size in enumerate(sizes) for r in range(size)]
    step = pl.program_id(0)

    def run(turned):
        w = w_ref[...]
        bias = bias_ref[...].astype(F32)
        later = dot(pieces[0][0], w)
        for at, (n, r, _, _) in enumerate(places):
            values = later + bias
            if at + 1 < len(places):
                later = dot(pieces[places[at + 1][2]][places[at + 1][3]], w)
            if turned:
                values = turn(values, cos_ref[n], sin_ref[n]) * jnp.where(step == 0, LOG2E * HEAD_DIM**-0.5, 1.0)
            out_ref[0, n, r] = values.astype(BF16)

    for ref in own:
        ref[...] = w_ref[...].T

    @pl.when(step < 2)
    def _():
        run(True)

    @pl.when(step == 2)
    def _():
        run(False)


def project_qkv(pair, start, parts, rows, me, pieces, weight, bias, cos_tab, sin_tab, held=(), deps=()):
    _, shard, model = pieces[0][0].shape
    sizes = [piece.shape[0] for piece in pieces[0]]
    count = sum(sizes)
    width = model // parts
    place = pl.BlockSpec((1, 2, count, shard, width), lambda g, m: (g, pair, start // count, 0, 0))
    outs = [((3, parts, rows, shard, width), BF16, place)]
    if not held:
        outs.append(((3 * width, model), BF16, along((width, model))))
    return call(
        functools.partial(qkv_body, sizes), "qkv", (me,), (3,),
        [(piece, fixed(piece.shape)) for group in pieces for piece in group]
        + [
            (weight, pl.BlockSpec((model, width), lambda g, m: (0, g * parts + m[0]))),
            (bias, pl.BlockSpec((1, width), lambda g, m: (0, g * parts + m[0]))),
            (cos_tab, pl.BlockSpec((2, shard, 128), lambda g, m: (pair, 0, 0))),
            (sin_tab, pl.BlockSpec((2, shard, 128), lambda g, m: (pair, 0, 0))),
        ],
        outs, held=[(array, n) for n, array in enumerate(held)], deps=deps,
    )


def qkv_grads(x_at, pieces, grad, blocks, deps=()):
    shard, model = pieces[0][0].shape[1:]
    parts, rows, _, columns = grad.shape
    size = model // (2 * blocks)
    flat = [(n, piece) for n, group in enumerate(pieces) for piece in group]

    def body(at_ref, *refs):
        g_ref, out_ref, keep_ref, sum_ref = refs[len(flat) :]
        total, sums, start = 0.0, 0.0, [0] * parts
        for (n, piece), x_ref in zip(flat, refs):
            count = piece.shape[0]
            g = g_ref[n, start[n] : start[n] + count].reshape(count * shard, g_ref.shape[3])
            start[n] += count
            total = total + dot(x_ref[...].reshape(count * shard, model), g, 0, 0)
            sums = sums + jnp.sum(g.astype(F32), axis=0, keepdims=True)
        low = total.astype(BF16)
        for x in range(2):
            for b in range(blocks):
                values = low[(2 * b + x) * size : (2 * b + x + 1) * size]

                @pl.when(at_ref[0] == x)
                def _():
                    keep_ref[b] = values

                @pl.when(at_ref[0] != x)
                def _():
                    out_ref[b] = values

        sum_ref[...] = sums

    block = along((blocks, size, BLOCK), 2)
    shape = (blocks, size, columns)
    return call(
        body, "qkv_grads", (x_at.astype(jnp.int32)[None],), (columns // BLOCK,),
        [(x, fixed(x.shape)) for _, x in flat] + [(grad, along((parts, rows, shard, BLOCK), 3))],
        [(shape, BF16, block), (shape, BF16, block), ((1, columns), F32, along((1, BLOCK), 1))],
        deps=deps,
    )


def seg_columns(segq_all, segk):
    pieces, shard, _ = segk.shape
    for j in range(pieces):
        row = jnp.broadcast_to(segq_all[j:j+1].astype(F32), (128, shard))
        segk[j] = row.T

def attend_body(start, cnt_ref, idx_ref, qkv_ref, seg_ref, o_ref, one_ref, far_ref, lse_ref, vt, segk, qmt, acc):
    row = pl.program_id(0) + start
    _, pieces, _, shard, width = qkv_ref.shape
    heads = width // HEAD_DIM

    @pl.when(pl.program_id(0) == 0)
    def _():
        qmt[...] = jnp.zeros_like(qmt)

    for j in range(pieces):
        vt[j] = qkv_ref[2, j, 0].T
        qt = qkv_ref[0, j, 0].T
        for h in range(heads):
            at = slice(h * HEAD_DIM, (h + 1) * HEAD_DIM)
            qmt[j, at, h * shard : (h + 1) * shard] = qt[at]
    seg_columns(seg_ref[0], segk)

    @pl.loop(0, pieces)
    def _(piece):
        attend_piece(row * pieces + piece, piece, cnt_ref, idx_ref, qkv_ref.at[1], seg_ref, lse_ref, vt, segk, qmt, acc)

    for j in range(pieces):
        o_ref[j, 0] = acc[j].T.astype(BF16)
    one_ref[0] = o_ref[1, 0]
    far_ref[:, 0] = o_ref[2:, 0]


def attend_piece(at_q, piece, cnt_ref, idx_ref, k_ref, seg_ref, lse_ref, vt, segk, qmt, acc):
    pieces, _, shard, width = k_ref.shape
    heads = width // HEAD_DIM
    seg_q = seg_ref[0, pl.ds(piece, 1)].astype(F32)

    def run(count):
        @pl.when(cnt_ref[at_q] == count)
        def _():
            qm = qmt[piece]
            places = [idx_ref[at_q * pieces + t] for t in range(count)]
            top, tot, out = [None] * heads, [None] * heads, [None] * heads
            later = dot(k_ref[places[0], 0], qm)
            for t in range(count):
                s = later
                if t + 1 < count:
                    later = dot(k_ref[places[t + 1], 0], qm)
                col = segk[places[t]]
                same = jnp.concatenate([col] * (shard // 128), axis=1) == seg_q
                for h in range(heads):
                    at = slice(h * HEAD_DIM, (h + 1) * HEAD_DIM)
                    sh = jnp.where(same, s[:, h * shard : (h + 1) * shard], NEG)
                    best = jnp.max(sh, axis=0, keepdims=True)
                    if t:
                        best = jnp.maximum(top[h], best)
                        fade = jnp.exp2(top[h] - best)
                    p = jnp.exp2(sh - best)
                    values = jnp.concatenate([vt[places[t], at], jnp.ones((16, shard), BF16)], axis=0)
                    found = dot(values, p.astype(BF16))
                    total, found = found[HEAD_DIM : HEAD_DIM + 1], found[:HEAD_DIM]
                    if t:
                        total = tot[h] * fade + total
                        found = out[h] * fade + found
                    top[h], tot[h], out[h] = best, total, found
            for h in range(heads):
                acc[piece, h * HEAD_DIM : (h + 1) * HEAD_DIM] = out[h] / tot[h]
                lse_ref[0, piece, h : h + 1] = top[h] + jnp.log2(tot[h])

    for count in range(1, pieces + 1):
        run(count)


def attend(start, count, cnt, idx, qkv, seg, held=()):
    _, pieces, rows, shard, width = qkv.shape
    heads = width // HEAD_DIM
    pairs = count * (pieces * shard) ** 2
    return call(
        functools.partial(attend_body, start), "attend", (cnt, idx), (count,),
        [(qkv, along((3, pieces, 1, shard, width), 2, start)), (seg, along((1, pieces, shard), 0, start))],
        [
            ((pieces, rows, shard, width), BF16, along((pieces, 1, shard, width), 1, start)),
            ((count, shard, width), BF16, along((1, shard, width))),
            ((2, count, shard, width), BF16, along((2, 1, shard, width), 1)),
            ((rows, pieces, 8, shard), F32, along((1, pieces, 8, shard), 0, start)),
        ],
        [
            pltpu.VMEM((pieces, width, shard), BF16),
            pltpu.VMEM((pieces, shard, 128), F32),
            pltpu.VMEM((pieces, width, heads * shard), BF16),
            pltpu.VMEM((pieces, width, shard), F32),
        ],
        held=list(zip(held, (0, 3)))
    )


def attend_back_body(
    start, cnt_ref, idx_ref, qkv_ref, o_ref, do0, do1, do2, do3, lse_ref, seg_ref, cos_ref, sin_ref, w_ref,
    g_ref, p0_ref, p1_ref, p2_ref, p3_ref, kt, segk, dk, dv, dqt, qmt, gmt, qst, gst, low,
):
    row = pl.program_id(0) + start
    _, pieces, _, shard, width = qkv_ref.shape
    heads = width // HEAD_DIM

    @pl.when(pl.program_id(0) == 0)
    def _():
        qmt[...] = jnp.zeros_like(qmt)
        gmt[...] = jnp.zeros_like(gmt)

    seg_columns(seg_ref[0], segk)
    dk[...] = jnp.zeros_like(dk)
    dv[...] = jnp.zeros_like(dv)
    lane = lax.broadcasted_iota(jnp.int32, (shard, width), 1) // HEAD_DIM
    chosen = lax.broadcasted_iota(jnp.int32, (8, width), 1) // HEAD_DIM
    chosen = (chosen == lax.broadcasted_iota(jnp.int32, (8, width), 0)).astype(BF16)
    for j, do_ref in enumerate((do0, do1, do2, do3)):
        kt[j] = qkv_ref[1, j, 0].T
        q, do = qkv_ref[0, j, 0], do_ref[...].reshape(shard, width)
        qt, gt = q.T, do.T
        for h in range(heads):
            at, qa = slice(h * HEAD_DIM, (h + 1) * HEAD_DIM), slice(h * shard, (h + 1) * shard)
            qmt[j, at, qa] = qt[at]
            gmt[j, at, qa] = gt[at]
            qst[j, qa] = jnp.where(lane == h, q, jnp.zeros_like(q))
            gst[j, qa] = jnp.where(lane == h, do, jnp.zeros_like(do))
        prod = do.astype(F32) * o_ref[j, 0].astype(F32)
        high = prod.astype(BF16)
        low[j] = dot(chosen, high, 1, 1) + dot(chosen, (prod - high.astype(F32)).astype(BF16), 1, 1)

    @pl.loop(0, pieces)
    def _(piece):
        back_piece(
            row * pieces + piece, piece, cnt_ref, idx_ref, qkv_ref.at[1], qkv_ref.at[2], lse_ref, seg_ref,
            kt, segk, dk, dv, dqt, qmt, gmt, qst, gst, low,
        )

    for j, ref in ((1, p1_ref), (3, p3_ref), (0, p0_ref), (2, p2_ref)):
        grad_q = turn(dqt[j].T * HEAD_DIM**-0.5, cos_ref[j], -sin_ref[j]).astype(BF16)
        grad_k = turn(dk[j] * (1 / LOG2E), cos_ref[j], -sin_ref[j]).astype(BF16)
        grad = jnp.concatenate([grad_q, grad_k, dv[j].astype(BF16)], axis=1)
        g_ref[j, 0] = grad
        ref[0] = dot(grad, w_ref[...]).astype(BF16)


def back_piece(
    at_q, piece, cnt_ref, idx_ref, k_ref, v_ref, lse_ref, seg_ref, kt, segk, dk, dv, dqt, qmt, gmt, qst, gst, low
):
    pieces, _, shard, width = k_ref.shape
    heads = width // HEAD_DIM
    lse, delta = lse_ref[0, piece], low[piece]
    seg_q = seg_ref[0, pl.ds(piece, 1)].astype(F32)

    def run(count):
        @pl.when(cnt_ref[at_q] == count)
        def _():
            places = [idx_ref[at_q * pieces + t] for t in range(count)]
            qm, gm = qmt[piece], gmt[piece]
            later = dot(k_ref[places[0], 0], qm), dot(v_ref[places[0], 0], gm)
            out = [None] * heads
            for t in range(count):
                s, dp = later
                j = places[t]
                if t + 1 < count:
                    later = dot(k_ref[places[t + 1], 0], qm), dot(v_ref[places[t + 1], 0], gm)
                col = segk[j]
                same = jnp.concatenate([col] * (shard // 128), axis=1) == seg_q
                ps, dss = [], []
                for h in range(heads):
                    at, qa = slice(h * HEAD_DIM, (h + 1) * HEAD_DIM), slice(h * shard, (h + 1) * shard)
                    p = jnp.exp2(jnp.where(same, s[:, qa] - lse[h : h + 1], NEG))
                    ds = (p * (dp[:, qa] - delta[h : h + 1])).astype(BF16)
                    ps.append(p.astype(BF16))
                    dss.append(ds)
                    found = dot(kt[j, at], ds)
                    out[h] = found if t == 0 else out[h] + found
                dv[j] += dot(jnp.concatenate(ps, axis=1), gst[piece])
                dk[j] += dot(jnp.concatenate(dss, axis=1), qst[piece])
            for h in range(heads):
                dqt[piece, h * HEAD_DIM : (h + 1) * HEAD_DIM] = out[h]

    for count in range(1, pieces + 1):
        run(count)


def attend_back(start, count, cnt, idx, qkv, o, do, lse, seg, cos_tab, sin_tab, weight, held=(), deps=()):
    _, pieces, rows, shard, width = qkv.shape
    model = weight.shape[1]
    heads = width // HEAD_DIM
    table = fixed((pieces, shard, 128))
    pairs = count * (pieces * shard) ** 2
    square, wide = (pieces, width, heads * shard), (pieces, shard, width)
    one = along((1, shard, width), 0, start)
    return call(
        functools.partial(attend_back_body, start), "attend_back", (cnt, idx), (count,),
        [(qkv, along((3, pieces, 1, shard, width), 2, start)), (o, along((pieces, 1, shard, width), 1, start))]
        + [(do[0], one), (do[1], one), (do[2], along((1, 1, shard, width), 1, start)), (do[3], one)]
        + [(lse, along((1, pieces, 8, shard), 0, start)), (seg, along((1, pieces, shard), 0, start))]
        + [(cos_tab, table), (sin_tab, table), (weight, fixed(weight.shape))],
        [((pieces, rows, shard, 3 * width), BF16, along((pieces, 1, shard, 3 * width), 1, start))]
        + [((count, shard, model), BF16, along((1, shard, model)))] * pieces,
        [
            pltpu.VMEM((pieces, width, shard), BF16),
            pltpu.VMEM((pieces, shard, 128), F32),
            pltpu.VMEM(wide, F32),
            pltpu.VMEM(wide, F32),
            pltpu.VMEM((pieces, width, shard), F32),
            pltpu.VMEM(square, BF16),
            pltpu.VMEM(square, BF16),
            pltpu.VMEM((pieces, heads * shard, width), BF16),
            pltpu.VMEM((pieces, heads * shard, width), BF16),
            pltpu.VMEM((pieces, 8, shard), F32),
        ],
        held=[(array, 0) for array in held], deps=deps
    )


def middle_body(
    order_ref, a0, a1, a2, a3, w0, w1, w2, w3, stream_ref, bias_ref, gain_ref, shift_ref, mid_ref, low_ref, all_ref,
):
    _, shard, model = stream_ref.shape
    total = 0.0
    for n, (a, w) in enumerate(((a0, w0), (a1, w1), (a2, w2), (a3, w3))):
        values = a[...].reshape(shard, a.shape[-1])
        total = total + dot(values, w[...])
        all_ref[0, :, n * a.shape[-1] : (n + 1) * a.shape[-1]] = values
    mid = stream_ref[0] + (total + line(bias_ref))
    hat, _ = centre(mid)
    mid_ref[0] = mid
    low_ref[0] = (hat * line(gain_ref) + line(shift_ref)).astype(BF16)


def out_blocks(weight, parts):
    width = weight.shape[0] // parts

    def block(i):
        return pl.BlockSpec((width, weight.shape[1]), lambda g, o: (o[i], 0))

    return [(weight, block(i)) for i in range(parts)]


def middle_norm(start, count, order, attended, weight, stream, vecs, held=()):
    rows, shard, model = stream.shape
    parts = len(attended)
    width = model // parts
    block, one = along((1, shard, model), 0, start), along((1, shard, width))
    first = [along((1, 1, shard, width), 1, start), one, along((1, 1, shard, width), 1), one]
    return call(
        middle_body, "middle", (order,), (count,),
        list(zip(attended, first)) + out_blocks(weight, parts) + [(stream, block)]
        + [(vec, fixed(vec.shape)) for vec in vecs],
        [
            (stream.shape, F32, block),
            ((count, shard, model), BF16, along((1, shard, model))),
            (stream.shape, BF16, block),
        ],
        held=list(zip(held, (0, 2)))
    )


def cot_body(blk_ref, a_ref, b_ref, up_ref, down_ref, g_ref, up_out, down_out, both_ref):
    tokens = a_ref.shape[0]
    down = down_ref[...]

    @pl.when(pl.program_id(0) == 0)
    def _():
        both_ref[0:tokens] = a_ref[...]
        both_ref[tokens:] = b_ref[...]

    g_ref[0:tokens] = dot(a_ref[...], down, 1, 1).astype(BF16)
    g_ref[tokens:] = dot(b_ref[...], down, 1, 1).astype(BF16)
    up_out[...] = up_ref[...]
    down_out[...] = down


def cot_down(blk, own, other, up, down, picked, half):
    tokens, model = own.shape
    steps = half // BLOCK
    column = along((2 * tokens, BLOCK), 1)
    if picked:
        up_at, down_at = along((model, BLOCK), 1), along((BLOCK, model))
    else:
        up_at = pl.BlockSpec((model, BLOCK), lambda g, b: (0, b[g]))
        down_at = pl.BlockSpec((BLOCK, model), lambda g, b: (b[g], 0))
    return call(
        cot_body, "cot_down", (blk,), (steps,),
        [(own, fixed(own.shape)), (other, fixed(own.shape)), (up, up_at), (down, down_at)],
        [
            ((2 * tokens, half), BF16, column),
            ((model, half), BF16, along((model, BLOCK), 1)),
            ((half, model), BF16, along((BLOCK, model))),
            ((2 * tokens, model), BF16, fixed((2 * tokens, model))),
        ]
    )


def hidden_body(blocks, blk_ref, *refs):
    pieces, refs = refs[:-11], refs[-11:]
    g_ref, up_ref, row_ref, bias_ref, act_ref, grad_ref, sum_ref, both_ref, part_ref, other_ref, held = refs
    sizes = [ref.shape[0] * ref.shape[1] for ref in pieces]
    starts = [sum(sizes[:n]) for n in range(len(sizes))]
    step = pl.program_id(0)

    @pl.when(step == 0)
    def _():
        for ref, at, size in zip(pieces, starts, sizes):
            both_ref[at : at + size] = ref[...].reshape(size, ref.shape[2])

    @pl.when(step < blocks)
    def _():
        up = up_ref[...]
        bias = bias_ref[...].astype(F32)
        total = 0.0
        later = dot(pieces[0][...].reshape(sizes[0], -1), up)
        for n, (start, size) in enumerate(zip(starts, sizes)):
            at = slice(start, start + size)
            v = later + bias
            if n + 1 < len(pieces):
                later = dot(pieces[n + 1][...].reshape(sizes[n + 1], -1), up)
            square = v * v
            tanh = jnp.tanh(v * (GELU_A + GELU_B * square))
            gate = 0.5 + 0.5 * tanh
            act = v * gate
            slope = gate + act * ((1.0 - tanh) * (GELU_A + 3.0 * GELU_B * square))
            grad = (slope * g_ref[at].astype(F32)).astype(BF16)
            act_ref[at] = act.astype(BF16)
            grad_ref[at] = grad
            held[step, at] = grad
            total = total + jnp.sum(grad.astype(F32), axis=0, keepdims=True)
        sum_ref[...] = total

    @pl.when(step >= blocks)
    def _():
        grad = jnp.concatenate([held[n] for n in range(blocks)], axis=1)
        found = dot(grad, row_ref[...], 1, 1).astype(BF16)
        part_ref[...] = found[: part_ref.shape[0]]
        other_ref[...] = found[part_ref.shape[0] :]


def hidden_units(blk, pieces, grads, up, bias):
    model = pieces[0].shape[2]
    tokens, half = grads.shape
    blocks, more = half // BLOCK, model // BLOCK

    def first(g):
        return jnp.minimum(g, blocks - 1)

    def second(g):
        return jnp.maximum(g - blocks, 0)

    column = pl.BlockSpec((tokens, BLOCK), lambda g, b: (0, first(g)))
    line = pl.BlockSpec((1, BLOCK), lambda g, b: (0, first(g)))
    return call(
        functools.partial(hidden_body, blocks), "hidden", (blk,), (blocks + more,),
        [(piece, fixed(piece.shape)) for piece in pieces]
        + [
            (grads, column),
            (up, pl.BlockSpec((model, BLOCK), lambda g, b: (0, first(g)))),
            (up, pl.BlockSpec((BLOCK, half), lambda g, b: (second(g), 0))),
            (bias, pl.BlockSpec((1, BLOCK), lambda g, b: (0, b[first(g)]))),
        ],
        [
            (grads.shape, BF16, column),
            (grads.shape, BF16, column),
            ((1, half), F32, line),
            ((tokens, model), BF16, fixed((tokens, model))),
            ((tokens // 2, model), BF16, pl.BlockSpec((tokens // 2, BLOCK), lambda g, b: (0, second(g)))),
            ((tokens // 2, model), BF16, pl.BlockSpec((tokens // 2, BLOCK), lambda g, b: (0, second(g)))),
        ],
        [pltpu.VMEM((blocks, tokens, BLOCK), BF16)]
    )


def sent_body(other_ref, tok_ref, cot_ref, grad_ref, act_ref, up_ref, down_ref):
    up_ref[...] = dot(tok_ref[...], grad_ref[...], 0, 0).astype(BF16)
    down_ref[...] = dot(act_ref[...], cot_ref[...], 0, 0).astype(BF16)


def sent_grads(other, tokens, cot, grad, act, steps):
    count, model = tokens.shape
    half = grad.shape[1]
    size = half // (2 * steps)
    wide = half // steps
    return call(
        sent_body, "sent_grads", (other,), (steps,),
        [
            (tokens, fixed(tokens.shape)),
            (cot, fixed(cot.shape)),
            (grad, along((count, wide), 1)),
            (act, pl.BlockSpec((count, size), lambda g, o: (0, 2 * g + o[0]))),
        ],
        [((model, half), BF16, along((model, wide), 1)), ((half // 2, model), BF16, along((size, model)))],
    )


def feed_body(order_ref, act_ref, down_ref, att_ref, low_ref, half_ref, cot_ref, feed_ref, other_ref, out_ref, keep_ref, kept_ref):
    parts = order_ref.shape[0]
    width = att_ref.shape[1] // parts
    feed = dot(act_ref[...], down_ref[...]).astype(BF16)
    feed_ref[...] = feed[: feed_ref.shape[0]]
    other_ref[...] = feed[feed_ref.shape[0] :]
    kept_ref[...] = dot(half_ref[...], cot_ref[...], 0, 0).astype(BF16)
    grad = dot(att_ref[...], low_ref[...], 0, 0).astype(BF16)
    step, steps = pl.program_id(0), pl.num_programs(0)

    def write(ref):
        for n in range(parts):
            at = pl.multiple_of(order_ref[n] * width, width)
            ref[pl.ds(at, width)] = grad[n * width : (n + 1) * width]

    @pl.when(2 * step < steps)
    def _():
        write(out_ref)

    @pl.when(2 * step >= steps)
    def _():
        write(keep_ref)


def feed_grads(order, act, down, attended, low, cot, c_at, x_at, deps=()):
    tokens, half = act.shape
    own, model = attended.shape
    steps = model // BLOCK
    place = jnp.concatenate([order, jnp.stack([c_at, x_at]).astype(jnp.int32)])
    size = half // (2 * steps)

    def body(place_ref, *refs):
        feed_body(place_ref.at[0 : order.shape[0]], *refs)

    def low_at(g, p):
        c = p[order.shape[0]]
        mine = 2 * g >= steps
        return 0, jnp.where(mine, c * (steps // 2) + g - steps // 2, (1 - c) * (steps // 2) + g)

    return call(
        body, "feed_grads", (place,), (steps,),
        [
            (act, fixed(act.shape)),
            (down, along((half, BLOCK), 1)),
            (attended, fixed(attended.shape)),
            (low, pl.BlockSpec((own, BLOCK), low_at)),
            (act, pl.BlockSpec((tokens, size), lambda g, p: (0, 2 * g + p[order.shape[0] + 1]))),
            (cot, fixed(cot.shape)),
        ],
        [
            ((own, model), BF16, along((own, BLOCK), 1)),
            ((own, model), BF16, along((own, BLOCK), 1)),
            ((model, model // 2), BF16, pl.BlockSpec((model, BLOCK), lambda g, p: (0, jnp.minimum(g, steps // 2 - 1)))),
            ((model, model // 2), BF16, pl.BlockSpec((model, BLOCK), lambda g, p: (0, jnp.maximum(g - steps // 2, 0)))),
            ((half // 2, model), BF16, along((size, model))),
        ],
        deps=deps,
    )


def middle_back_body(
    order_ref, part_ref, sent_ref, mid_ref, cot_ref, gain_ref, w0, w1, w2, w3,
    grad_ref, low_ref, att0_ref, att1_ref, far_ref, sums_ref,
):
    grad = part_ref[...].astype(F32) + sent_ref[...].astype(F32)
    hat, inverse = centre(mid_ref[0])
    cot = cot_ref[0].astype(F32)
    total = cot + norm_back(grad, line(gain_ref), hat, inverse)
    low = total.astype(BF16)
    grad_ref[0] = total
    low_ref[0] = low
    far_ref[0, 0] = dot(low, w2[...], 1, 1).astype(BF16)
    far_ref[1, 0] = dot(low, w3[...], 1, 1).astype(BF16)
    att1_ref[0] = dot(low, w1[...], 1, 1).astype(BF16)
    att0_ref[0] = dot(low, w0[...], 1, 1).astype(BF16)

    @pl.when(pl.program_id(0) == 0)
    def _():
        sums_ref[...] = jnp.zeros_like(sums_ref)

    sums_ref[0:1] += jnp.sum(grad * hat, axis=0, keepdims=True)
    sums_ref[1:2] += jnp.sum(grad, axis=0, keepdims=True)
    sums_ref[2:3] += jnp.sum(low.astype(F32), axis=0, keepdims=True)
    sums_ref[3:4] += jnp.sum(cot, axis=0, keepdims=True)


def middle_back(order, both, sent, mid, cot, gain, weight, parts, deps=()):
    rows, shard, model = mid.shape
    width = model // parts
    block, one = along((1, shard, model)), along((1, shard, width))
    flat = pl.BlockSpec((shard, model), lambda g, o: (g, 0))
    return call(
        middle_back_body, "middle_back", (order,), (rows,),
        [(both, flat), (sent, flat), (mid, block), (cot, block), (gain, fixed(gain.shape))] + out_blocks(weight, parts),
        [
            (mid.shape, F32, block),
            (mid.shape, BF16, block),
            ((rows, shard, width), BF16, one),
            ((rows, shard, width), BF16, one),
            ((2, rows, shard, width), BF16, along((2, 1, shard, width), 1)),
            ((8, model), F32, fixed((8, model))),
        ],
        deps=deps
    )


def norm1_back_body(start, part_ref, near_ref, far_ref, stream_ref, mid_ref, gain_ref, seg_ref, in_ref, shift_ref, sums_ref):
    grad = part_ref[0].astype(F32) + near_ref[0].astype(F32) + far_ref[0].astype(F32)
    hat, inverse = centre(stream_ref[0])
    total = mid_ref[0] + norm_back(grad, line(gain_ref), hat, inverse)
    in_ref[0] = total.astype(BF16)
    seg = seg_ref[pl.ds(pl.program_id(0) + start, 1)]
    slots = lax.broadcasted_iota(jnp.int32, (SEGS, seg.shape[-1]), 0) == seg
    onehot = slots.astype(F32).astype(BF16)
    shift_ref[0] = dot(jnp.concatenate([onehot, onehot], axis=1), split_low(total))

    @pl.when(pl.program_id(0) == 0)
    def _():
        sums_ref[...] = jnp.zeros_like(sums_ref)

    sums_ref[0:1] += jnp.sum(grad * hat, axis=0, keepdims=True)
    sums_ref[1:2] += jnp.sum(grad, axis=0, keepdims=True)


def norm1_back(start, count, own, near, far, stream, mid, gain, seg, held=(), deps=()):
    rows, shard, model = stream.shape
    block, own_block = along((1, shard, model), 0, start), along((1, shard, model))
    return call(
        functools.partial(norm1_back_body, start), "norm1_back", (), (count,),
        [(own, own_block), (near, own_block), (far, own_block), (stream, block), (mid, block), (gain, fixed(gain.shape))]
        + [(seg, fixed(seg.shape))],
        [
            (stream.shape, BF16, block),
            ((count, SEGS, model), F32, along((1, SEGS, model))),
            ((8, model), F32, fixed((8, model))),
        ],
        held=[(array, 0) for array in held], deps=deps
    )


def exchange(own, one, far):
    return [own, swap(one, "c"), far, swap(far[1], "c")]


def tie(*values):
    return lax.optimization_barrier(values)


def cut(values, index, size, axis):
    return lax.dynamic_slice_in_dim(values, index * size, size, axis)


def add_low(kept, sent):
    return (kept.astype(F32) + sent.astype(F32)).astype(BF16)


def ordered(at, own, other, axis):
    return jnp.where(at == 0, jnp.concatenate([own, other], axis), jnp.concatenate([other, own], axis))


def wide_body(blocks, at_ref, d0, d1, u0, u1, down_ref, up_ref):
    c_at = at_ref[0]
    width = up_ref.shape[1] // (4 * blocks)
    size = d0.shape[0]
    for c in range(2):
        mine = c_at == c
        down_ref[c * size : (c + 1) * size] = jnp.where(mine, d0[...], d1[...]).astype(F32)
        up = jnp.where(mine, u0[...], u1[...]).astype(F32)
        for b in range(2 * blocks):
            up_ref[:, (2 * b + c) * width : (2 * b + c + 1) * width] = up[:, b * width : (b + 1) * width]


def finish_wide(c_at, dp, piece, down, up, deps=()):
    rows, model = up[0].shape[0], down[0].shape[1]
    depth, size = dp // 2, down[0].shape[0]
    if piece % 128 == 0:
        shapes = [(2 * size, model), (rows, 2 * dp * piece)]
        return call(
            functools.partial(wide_body, depth), "finish_wide", (c_at.astype(jnp.int32)[None],), (1,),
            [(array, fixed(array.shape)) for array in (*down, *up)], [(shape, F32, fixed(shape)) for shape in shapes],
            deps=deps,
        )
    down_done = ordered(c_at, *down, 0).astype(F32)
    up_done = ordered(c_at, up[0][None], up[1][None], 0).reshape(2, rows, dp, piece).transpose(1, 2, 0, 3)
    return down_done, up_done.reshape(rows, 2 * dp * piece).astype(F32)


def late_body(at_ref, l0, l1, qkv_ref, out_ref):
    half = out_ref.shape[1] // 2
    wide = half // 2
    for c in range(2):
        late = jnp.where(at_ref[0] == c, l0[...], l1[...]).astype(F32)
        out_ref[:, c * half : (c + 1) * half] = late[:, 6 * wide :]
        for y in range(2):
            for n in range(3):
                at = n * 4 * wide + (2 * y + c) * wide
                qkv_ref[:, at : at + wide] = late[:, (3 * y + n) * wide : (3 * y + n + 1) * wide]


def finish_late(c_at, model, piece, late, parts):
    rows = late[0].shape[0]
    if piece % 128 == 0:
        return call(
            late_body, "finish_late", (c_at.astype(jnp.int32)[None],), (1,),
            [(array, fixed(array.shape)) for array in late],
            [((rows, size), F32, fixed((rows, size))) for size in (3 * model, model)],
        )
    both = ordered(c_at, late[0][None], late[1][None], 0)
    width = model // parts
    qkv_done = both[:, :, : 6 * width].reshape(2, rows, 2, 3, width).transpose(1, 3, 2, 0, 4)
    qkv_done = qkv_done.reshape(rows, 3 * model).astype(F32)
    return qkv_done, jnp.concatenate([both[0, :, 6 * width :], both[1, :, 6 * width :]], axis=1).astype(F32)


def local(
    inputs, segment_ids, doc_times, time_weight, time_bias, norm1_gain, norm1_bias, qkv_weight, qkv_bias,
    out_weight, out_bias, norm2_gain, norm2_bias, up_weight, up_bias, down_weight, down_bias, cotangent,
    *, dp,
):
    rows, shard, model = inputs.shape
    parts = 4
    tokens = rows * shard
    hidden_width = up_weight.shape[1]
    width = model // parts
    depth = dp // 2
    half = hidden_width // 2
    piece = half // dp
    z_at, x_at, y_at, c_at = (lax.axis_index(name) for name in ("z", "x", "y", "c"))
    me = 2 * y_at + c_at

    groups = [(0, rows - 1), (rows - 1, 1)] if rows > 1 else [(0, 1)]
    seg_one, seg_two = swap(segment_ids, "c"), swap(segment_ids, "y")
    seg_three = swap(seg_two, "c")
    features = time_features(doc_times.reshape(rows * SEGS), jnp.arange(TEMB), TEMB // 2)
    time_shift = dot(features, time_weight).reshape(rows, SEGS, model)
    own1, one1, two1, stream = [], [], [], None
    for start, count in groups:
        held = () if stream is None else (stream,)
        stream, low = norm1(
            start, count, inputs, segment_ids, time_shift, (time_bias, norm1_gain, norm1_bias), held
        )
        if stream is not None and not own1:
            low, seg_one, seg_two, seg_three = tie(low, seg_one, seg_two, seg_three)
        own1.append(low)
        two1.append(swap(low, "y"))
        one1.append(swap(low, "c"))
    segs = jnp.stack([segment_ids, seg_one, seg_two, seg_three], axis=1)

    me, x_at, z_at, c_at, y_at, own1[-1], segs = tie(me, x_at, z_at, c_at, y_at, own1[-1], segs)
    order = [me ^ i for i in range(parts)]
    order_list = jnp.stack(order).astype(jnp.int32)
    me_list = order_list[:1]
    low_id, high_id = segs.min(axis=2), segs.max(axis=2)
    act = (low_id[:, :, None] <= high_id[:, None, :]) & (low_id[:, None, :] <= high_id[:, :, None])
    places = jnp.arange(parts, dtype=jnp.int32)
    rank = jnp.cumsum(act.astype(jnp.int32), axis=2) - 1
    chosen = act[..., None] & (rank[..., None] == places)
    idx = jnp.sum(jnp.where(chosen, places[:, None], 0), axis=2).astype(jnp.int32).reshape(-1)
    cnt = jnp.sum(act.astype(jnp.int32), axis=2).reshape(-1)
    positions = jnp.stack([o * shard + jnp.arange(shard, dtype=jnp.int32) for o in order])
    cos_tab, sin_tab = rotary_tables(positions, HEAD_DIM)

    cot = cotangent.reshape(tokens, model)
    cot_other = swap(cot, "c")
    if piece % BLOCK == 0:
        blk = (jnp.arange(dp)[:, None] * 2 + c_at) * (piece // BLOCK) + jnp.arange(piece // BLOCK)
        blk = blk.reshape(-1).astype(jnp.int32)
        up_from, down_from = up_weight, down_weight
    else:
        blk = jnp.zeros((half // BLOCK,), jnp.int32)
        up_from = lax.dynamic_index_in_dim(up_weight.reshape(model, dp, 2, piece), c_at, 2, keepdims=False)
        down_from = lax.dynamic_index_in_dim(down_weight.reshape(dp, 2, piece, model), c_at, 1, keepdims=False)
        up_from, down_from = up_from.reshape(model, half), down_from.reshape(half, model)
    grad_act, up_own, down_own, cot_both = cot_down(
        blk, cot, cot_other, up_from, down_from, piece % BLOCK != 0, half
    )
    up_bias_own, bias_blk = up_bias.reshape(1, hidden_width), blk
    if piece % BLOCK:
        up_bias_own = lax.dynamic_index_in_dim(up_bias.reshape(dp, 2, piece), c_at, 1, keepdims=False)
        up_bias_own, bias_blk = up_bias_own.reshape(1, half), jnp.arange(half // BLOCK, dtype=jnp.int32)

    qkv_line = qkv_bias.reshape(1, 3 * model)
    near = (own1, one1)
    qkv, qkv_own = project_qkv(
        0, 0, parts, rows, me_list, near, qkv_weight, qkv_line, cos_tab, sin_tab, (), (grad_act, cnt, idx)
    )
    o, lse, attended, three1 = None, None, [], []
    for n, (start, count) in enumerate(groups):
        if n == 0:
            two1[0], qkv = tie(two1[0], qkv)
        else:
            two1[n], o = tie(two1[n], o)
        three1.append(swap(two1[n], "c"))
        (qkv,) = project_qkv(
            1, start, parts, rows, me_list, ([two1[n]], [three1[n]]), qkv_weight, qkv_line, cos_tab, sin_tab, (qkv,),
            () if o is None else (o,),
        )
        held = () if o is None else (o, lse)
        o, out_one, out_far, lse = attend(start, count, cnt, idx, qkv, segs, held)
        attended.append((out_one, swap(out_far, "y")))
    held, normed2, normed2_other = (), [], []
    for (start, count), values in zip(groups, attended):
        far, o = tie(values[1], o)
        values = exchange(o, values[0], far)
        middle, low, attended_all = middle_norm(
            start, count, order_list, values, out_weight, stream, (out_bias, norm2_gain, norm2_bias), held
        )
        held = (middle, attended_all)
        normed2.append(low)
        normed2_other.append(swap(low, "c"))

    active, grad_hidden, up_b, normed2_both, part2, part2_other = hidden_units(
        bias_blk, normed2 + normed2_other, grad_act, up_own, up_bias_own
    )
    part2_sent = swap(part2_other, "c")
    grad_middle, grad_middle_low, att0, att1, far, sums2 = middle_back(
        order_list, part2, part2_sent, middle, cotangent, norm2_gain, out_weight, parts
    )
    far = swap(far, "y")
    sums2 = sums2[:4]

    active, grad_hidden, att0 = tie(active, grad_hidden, att0)
    up_rows = model // dp
    small_blocks = piece % BLOCK != 0 or depth != model // BLOCK
    if small_blocks:
        up_grad = dot(normed2_both, grad_hidden, 0, 0).astype(BF16)
        down_out = dot(active, cot_both, 0, 0).astype(BF16).reshape(depth, 2, piece, model)
        down_kept = lax.dynamic_index_in_dim(down_out, x_at, 1, keepdims=False).reshape(half // 2, model)
        down_out = lax.dynamic_index_in_dim(down_out, 1 - x_at, 1, keepdims=False).reshape(half // 2, model)
    else:
        up_grad, down_out = sent_grads(
            1 - x_at[None].astype(jnp.int32), normed2_both, cot_both, grad_hidden, active, depth
        )
    up_b = up_b.reshape(dp, 1, piece)
    up_b = jnp.where(jnp.arange(2)[:, None] == c_at, up_b, 0.0).reshape(-1, model)
    times = doc_times.reshape(1, rows * SEGS)
    times = jnp.concatenate([times // 32, times % 32], axis=1).astype(F32)
    times = jnp.tile(jnp.pad(times, ((0, 0), (0, width - times.shape[1]))), (1, parts))
    early = jnp.concatenate([sums2, up_b, times], axis=0).astype(BF16)
    up_grad, down_out, far, early = tie(up_grad, down_out, far, early)
    grad_o = exchange(att0, att1, far)
    up_z = lax.psum_scatter(up_grad, "z", scatter_dimension=0, tiled=True)
    down_sent = swap(down_out[: half // 4], "x")
    if small_blocks:
        feed = dot(active, down_own).astype(BF16)
        feed, feed_other = feed[:tokens], feed[tokens:]
        out_grad = dot(attended_all.reshape(tokens, model), grad_middle_low.reshape(tokens, model), 0, 0).astype(BF16)
        out_grad = jnp.concatenate([cut(out_grad, o_at, width, 0) for o_at in order], axis=0)
        out_sent, out_grad = (cut(out_grad, at, model // 2, 1) for at in (1 - c_at, c_at))
    else:
        feed, feed_other, out_sent, out_grad, down_kept = feed_grads(
            order_list, active, down_own, attended_all.reshape(tokens, model), grad_middle_low.reshape(tokens, model),
            cot_both, c_at, x_at, (far, down_out),
        )
    feed, feed_other, out_sent, out_grad, down_kept, down_sent, down_out, *grad_o = tie(
        feed, feed_other, out_sent, out_grad, down_kept, down_sent, down_out, *grad_o
    )
    down_late = swap(down_out[half // 4 :], "x")
    out_sent, feed_sent = swap(out_sent, "c"), swap(feed_other, "c")

    back = []
    (start, count), rest = groups[0], groups[1:]
    found = attend_back(start, count, cnt, idx, qkv, o, grad_o, lse, segs, cos_tab, sin_tab, qkv_own)
    *found, down_late, out_sent, feed_sent = tie(*found, down_late, out_sent, feed_sent)
    grad_qkv, own, one, two, three = found
    there = add_low(two, swap(three, "c"))
    down_x = add_low(down_kept, jnp.concatenate([down_sent, down_late], axis=0))
    down_z = lax.psum_scatter(down_x, "z", scatter_dimension=0, tiled=True)
    out_c = add_low(out_grad, out_sent).reshape(depth, 2 * up_rows, model // 2)
    out_sent = cut(out_c, 1 - x_at, up_rows, 1)
    there, down_x, out_sent = tie(there, down_x, out_sent)
    far, near = swap(there, "y"), swap(one, "c")
    out_sent = swap(out_sent, "x")
    if rest:
        (start, count), = rest
        found = attend_back(
            start, count, cnt, idx, qkv, o, grad_o, lse, segs, cos_tab, sin_tab, qkv_own, (grad_qkv,),
            (there, down_x),
        )
        *found, far, up_z, out_sent = tie(*found, far, up_z, out_sent)
        back.append((own, near, far))
        grad_qkv, own, one, two, three = found
        there, far = tie(add_low(two, swap(three, "c")), far)
        far, near = swap(there, "y"), swap(one, "c")
        grad_qkv, there = tie(grad_qkv, there)
    qkv_out, qkv_kept, qkv_b = qkv_grads(x_at, [own1, one1, two1, three1], grad_qkv, depth)
    qkv_out, qkv_kept, far, out_sent, out_c, up_z = tie(qkv_out, qkv_kept, far, out_sent, out_c, up_z)
    back.append((own, near, far))
    qkv_sent = swap(qkv_out, "x")
    out_x = add_low(cut(out_c, x_at, up_rows, 1), out_sent)
    out_sent = cut(out_x, 1 - y_at, width, 2)
    qkv_out, up_out = tie(qkv_out, cut(up_z, 1 - x_at, up_rows, 0))
    up_sent = swap(up_out, "x")
    held, grad_shift, sums1 = (), [], 0.0
    for (start, count), values in zip(groups, back):
        input_grad, found, sums = norm1_back(
            start, count, *values, stream, grad_middle, norm1_gain, segment_ids, held, (qkv_kept, up_out)
        )
        if not held:
            input_grad, out_sent = tie(input_grad, out_sent)
            out_sent = swap(out_sent, "y")
        held = (input_grad,)
        grad_shift.append(found.reshape(count * SEGS, model))
        sums1 = sums1 + sums[:2]

    qkv_b = jnp.where(jnp.arange(parts)[:, None] == me, qkv_b.reshape(3, 1, width), 0.0).reshape(3, model)
    small = jnp.concatenate(grad_shift + [sums1, qkv_b], axis=0).astype(BF16)
    small = jnp.concatenate([small, early], axis=0)
    small_sent = swap(cut(small, 1 - c_at, 2 * width, 1), "c")
    small = add_low(cut(small, c_at, 2 * width, 1), small_sent)
    small, qkv_sent, out_sent = tie(small, qkv_sent, out_sent)
    small = add_low(cut(small, y_at, width, 1), swap(cut(small, 1 - y_at, width, 1), "y"))
    small = ordered(x_at, small[None], swap(small, "x")[None], 0)
    out_x = add_low(cut(out_x, y_at, width, 2), out_sent)
    late = jnp.concatenate([add_low(qkv_kept, qkv_sent), out_x], axis=2)
    output = middle.reshape(tokens, model) + (feed.astype(F32) + feed_sent.astype(F32) + down_bias.astype(F32))
    output = output.astype(BF16).reshape(rows, shard, model)
    small, late = tie(small, late)
    if depth == 4:
        flat = small.reshape(2 * small.shape[1] * width // model, model)
        parts_z = [lax.dynamic_index_in_dim(late, z_at ^ n, 0, keepdims=False) for n in range(depth)]
        sent = [
            lax.ppermute(jnp.concatenate([parts_z[n], flat], axis=0), "z", [(i, i ^ n) for i in range(depth)])
            for n in range(1, depth)
        ]
        small, down_z, up_z, up_sent = tie(small, down_z, up_z, up_sent)
        up_x = add_low(cut(up_z, x_at, up_rows, 0), up_sent)
        down_sent, up_sent = swap(down_z, "y"), swap(up_x, "y")
        *sent, output, down_sent, up_sent = tie(*sent, output, down_sent, up_sent)
        late = sum(part[:up_rows].astype(F32) for part in sent) + parts_z[0].astype(F32)
        late = late.astype(BF16)
        small = jnp.stack([small] + [part[up_rows:].reshape(small.shape) for part in sent])
        small = jnp.stack([lax.dynamic_index_in_dim(small, z_at ^ n, 0, keepdims=False) for n in range(depth)])
    else:
        up_x = add_low(cut(up_z, x_at, up_rows, 0), up_sent)
        down_sent, up_sent = swap(down_z, "y"), swap(up_x, "y")
        late = lax.psum_scatter(late, "z", scatter_dimension=0, tiled=False)
        small = lax.all_gather(small, "z")
    small = small.reshape(dp, small.shape[2], width)

    late_sent = swap(late, "y")
    down_done, up_done = add_low(down_z, down_sent), add_low(up_x, up_sent)
    down_other, up_other = swap(down_done, "c"), swap(up_done, "c")
    dp_at = 2 * z_at + x_at
    all_times = small[:, -1, : 2 * rows * SEGS].astype(F32) * 0.25
    all_times = all_times[:, : rows * SEGS] * 32.0 + all_times[:, rows * SEGS :]
    shifts = small[:, : rows * SEGS].reshape(dp * rows * SEGS, width)
    columns = dp_at * (TEMB // dp) + jnp.arange(TEMB // dp)
    wanted = time_features(all_times.reshape(-1), columns, TEMB // 2)
    sums = jnp.sum(small[:, rows * SEGS : -1].astype(F32), axis=0)
    full = [dot(wanted, shifts, 0, 0), sums, jnp.sum(shifts.astype(F32), axis=0, keepdims=True)]
    full = jnp.concatenate(full, axis=0).astype(BF16)
    count = full.shape[0]
    full = jnp.pad(full, ((0, -count % 16), (0, 0)))
    full = ordered(y_at, full[None], swap(full, "y")[None], 0)
    full = ordered(c_at, full[None], swap(full, "c")[None], 0)
    full = full.transpose(2, 0, 1, 3).reshape(-1, model).astype(F32)
    time_w_done, sums = full[: TEMB // dp], full[TEMB // dp : count]

    def share(vector):
        return cut(vector.reshape(-1), dp_at, vector.size // dp, 0)

    vectors = [share(sums[n]) for n in (-1, 0, 1)] + [share(sums[2:5])]
    vectors += [share(sums[n]) for n in (7, 5, 6)] + [share(sums[9:-1]), share(sums[8])]
    both = ordered(y_at, late[None], late_sent[None], 0)
    late = jnp.concatenate([both[0, :, : 3 * width], both[1, :, : 3 * width], both[0, :, 3 * width :], both[1, :, 3 * width :]], axis=1)
    late_other = swap(late, "c")
    wide = finish_wide(c_at, dp, piece, (down_done, down_other), (up_done, up_other), (late, *vectors))
    down_done, up_done, late_other = tie(*wide, late_other)

    qkv_done, out_done = finish_late(c_at, model, piece, (late, late_other), parts)

    time_b_done, gain1_done, bias1_done, qkv_b_done, out_b_done, gain2_done, bias2_done, up_b_done, down_b_done = vectors
    return (
        output, input_grad, time_w_done, time_b_done, gain1_done, bias1_done, qkv_done, qkv_b_done,
        out_done, out_b_done, gain2_done, bias2_done, up_done, up_b_done, down_done, down_b_done,
    )


def solution(mesh):
    dp, seq = mesh.shape["dp"], mesh.shape["seq"]
    fine = Mesh(mesh.devices.reshape(dp // 2, 2, seq // 2, 2), ("z", "x", "y", "c"))
    rows, seqs = ("z", "x"), ("y", "c")
    placed = (P(rows, seqs, None), P(rows, seqs), P(rows, None)) + (P(),) * 14 + (P(rows, seqs, None),)
    vec, mat = P(rows), P(rows, None)
    return jax.shard_map(
        functools.partial(local, dp=dp),
        mesh=fine,
        in_specs=placed,
        out_specs=(
            P(rows, seqs, None), P(rows, seqs, None), mat, vec, vec, vec, mat, vec, mat, vec, vec, vec, mat, vec, mat, vec,
        ),
        check_vma=False,
    )
```
